32 devices in a mesh: groups: 2 (over y), dom: 4 (over z), sub: 4 (over x, core).
Axes of the slice: x: 2, y: 2, z: 4, core: 2. Of those that a mesh axis runs over, the one named last changes fastest.
Arguments:
- grid_lat: bfloat16 [4096, 512], P(('groups', 'dom'), 'sub'), parts along dimension 0, may hold values from -6 to 6
- mesh_lat: bfloat16 [4096, 512], P(('groups', 'dom'), 'sub'), parts along dimension 0, may hold values from -6 to 6
- grid_send: int32 [4, 4, 64], P('dom'), may hold values from 0 to 511, as said below
- mesh_send: int32 [4, 4, 32], P('dom'), may hold values from 0 to 511, as said below
- enc_edges: int32 [2, 16384], P(None, ('dom', 'sub')), may hold values from 0 to 767, as said below
- enc_geom: float32 [4, 16384], P(None, ('dom', 'sub')), may hold values from -6 to 6
- enc_blocks: int32 [4], P('dom'), may hold values from 16 to 32, as said below
- proc_edges: int32 [2, 32768], P(None, ('dom', 'sub')), may hold values from 0 to 639, as said below
- proc_geom: float32 [4, 32768], P(None, ('dom', 'sub')), may hold values from -6 to 6
- proc_blocks: int32 [4], P('dom'), may hold values from 32 to 64, as said below
- enc_geo: float32 [4, 512], replicated, may hold values from -3 to 3
- proc_geo: float32 [4, 512], replicated, may hold values from -3 to 3
- enc_edge_in: bfloat16 [1536, 512], P('sub'), may hold values from -0.15625 to 0.15625
- enc_edge_out: bfloat16 [512, 512], P('sub'), may hold values from -0.25 to 0.25
- enc_node_in: bfloat16 [1024, 512], P('sub'), may hold values from -0.1875 to 0.1875
- enc_node_out: bfloat16 [512, 512], P('sub'), may hold values from -0.25 to 0.25
- proc_edge_in: bfloat16 [1536, 512], P('sub'), may hold values from -0.15625 to 0.15625
- proc_edge_out: bfloat16 [512, 512], P('sub'), may hold values from -0.25 to 0.25
- proc_node_in: bfloat16 [1024, 512], P('sub'), may hold values from -0.1875 to 0.1875
- proc_node_out: bfloat16 [512, 512], P('sub'), may hold values from -0.25 to 0.25
- enc_edge_gain: float32 [512], replicated, may hold values from 0.25 to 1.75
- enc_node_gain: float32 [512], replicated, may hold values from 0.25 to 1.75
- proc_edge_gain: float32 [512], replicated, may hold values from 0.25 to 1.75
- proc_node_gain: float32 [512], replicated, may hold values from 0.25 to 1.75
Outputs:
- mesh_out: bfloat16 [4096, 512], P(('groups', 'dom', 'sub')), parts along dimension 0
The draws below stay inside these ranges and needn't reach their ends.
There are 2 independent parts, one for each index of `groups`. The reference program is written for one: setup_inputs(seed, part) draws one part's arguments, and reference() takes and returns one part's arrays. A program takes and returns all parts, laid end to end along the dimension named above; an argument that names none is the same for every part. Nothing has to cross between parts.
Inputs may be any that keep to these rules, and one draw needn't show every extreme that they name: grid_send[q, r, :] are 64 distinct local grid rows of partition q, the ones partition q + o[r] reads, o = (-2, -1, 1, 2). mesh_send[q, r, :] are 32 distinct local mesh rows of partition q, the ones partition q + o[r] reads. `enc_edges`: row 0 is a sender, a place in its partition's grid_table, never in a list r whose partition p + o[r] lies outside 0 to 3; row 1 is a receiver, a local mesh row of the partition, below 512. `proc_edges`: row 0 is a sender, a place in its partition's mesh_table, never in a list whose partition lies outside 0 to 3; row 1 is a receiver, a local mesh row of the partition. `enc_blocks`: some partition has all 32 blocks live. `proc_blocks`: some partition has all 64 blocks live.
All inputs are finite; a program needn't handle non-finite values.
Results may differ from the reference program's by a relative error of at most 0.0095.
Values may be sent and summed in bfloat16 or wider, within the bound.
No kernel may reach another device: no remote copies, remote signals or barrier semaphores. Data moves between devices by JAX's collectives and lax.ppermute only.
A program may use at most 64 MiB of HBM per device.

```python
import jax
import jax.numpy as jnp
from jax import lax

D = 512
FF = 512
GRID_DEV = 512
MESH_DEV = 512
GRID_SEND = 64
MESH_SEND = 32
BLOCK = 128
ENC_CAP = 32
PROC_CAP = 64
PARTS_SIZE = 4
GRID = 2048
MESH = 2048
ENC_EDGES = 16384
PROC_EDGES = 32768


def bring_to(shuffled, target, position):
    current = shuffled[position]
    shuffled = jnp.where(shuffled == target, current, shuffled)
    return shuffled.at[position].set(target)


def send_lists(key, node_rows, slot_count):
    key_list = jax.random.split(key, PARTS_SIZE * 4)

    def make_list(subkey):
        shuffled = jax.random.permutation(subkey, node_rows)
        shuffled = bring_to(shuffled, node_rows - 1, 0)
        shuffled = bring_to(shuffled, 0, 1)
        return shuffled[:slot_count]
    return jax.vmap(make_list)(key_list).reshape(PARTS_SIZE, 4, slot_count).astype(jnp.int32)


def random_edges(key, capacity, node_rows, slot_count):
    per_part = capacity * BLOCK
    edge_total = PARTS_SIZE * per_part
    first_key, second_key = jax.random.split(key)
    senders = jax.random.randint(first_key, (edge_total,), 0, node_rows + 4 * slot_count)
    receivers = jax.random.randint(second_key, (edge_total,), 0, MESH_DEV)
    partition = jnp.arange(edge_total) // per_part
    region = jnp.clip((senders - node_rows) // slot_count, 0, 3)
    offset = jnp.array([-2, -1, 1, 2])[region]
    source = partition + offset
    missing = (senders >= node_rows) & ((source < 0) | (source >= PARTS_SIZE))
    senders = jnp.where(missing, senders % node_rows, senders)
    senders = senders.at[0].set(node_rows + 4 * slot_count - 1).at[1].set(0)
    receivers = receivers.at[0].set(MESH_DEV - 1).at[1].set(0)
    return jnp.stack([senders, receivers]).astype(jnp.int32)


def block_counts(key, capacity):
    first_key, second_key, third_key = jax.random.split(key, 3)
    counts = jax.random.randint(first_key, (PARTS_SIZE,), capacity // 2, capacity + 1)
    busiest = jax.random.randint(second_key, (), 0, PARTS_SIZE)
    lightest = (busiest + 1 + jax.random.randint(third_key, (), 0, PARTS_SIZE - 1)) % PARTS_SIZE
    return counts.at[busiest].set(capacity).at[lightest].set(capacity // 2).astype(jnp.int32)


def draw_grid_send(key, part):
    key = jax.random.fold_in(key, 11)
    return send_lists(key, GRID_DEV, GRID_SEND)


def draw_mesh_send(key, part):
    key = jax.random.fold_in(key, 12)
    return send_lists(key, MESH_DEV, MESH_SEND)


def draw_enc_edges(key, part):
    key = jax.random.fold_in(key, 13)
    return random_edges(key, ENC_CAP, GRID_DEV, GRID_SEND)


def draw_proc_edges(key, part):
    key = jax.random.fold_in(key, 14)
    return random_edges(key, PROC_CAP, MESH_DEV, MESH_SEND)


def draw_enc_blocks(key, part):
    key = jax.random.fold_in(key, 15)
    return block_counts(key, ENC_CAP)


def draw_proc_blocks(key, part):
    key = jax.random.fold_in(key, 16)
    return block_counts(key, PROC_CAP)


def block_scale(own_key, shape, cuts, least, top_value):
    def one(dim, parts):
        draws = jax.random.uniform(jax.random.fold_in(jax.random.fold_in(own_key, 6), dim), (parts,), jnp.float32, least / len(cuts), top_value / len(cuts))
        return jnp.repeat(jnp.exp(draws), shape[dim] // parts).reshape((-1,) + (1,) * (len(shape) - dim - 1))

    gain = one(*cuts[0])
    for cut in cuts[1:]:
        gain = gain * one(*cut)
    return gain


def centred(key, dims, deviation, limit, cuts=(), held_as=jnp.bfloat16):
    result = deviation * jax.random.normal(key, dims, jnp.float32)
    if cuts:
        result = result * block_scale(key, dims, cuts, -0.22, 0.18)
    return jnp.clip(result, -limit, limit).astype(held_as)


def setup_inputs(seed: int = 0, part: int = 0) -> dict:
    seeds = jax.random.split(jax.random.key(seed), 25)
    own_keys = jax.random.split(jax.random.fold_in(seeds[24], part), 25)
    grid_lat = centred(own_keys[0], (GRID, D), 1.0, 6.0, ((0, 4), (1, 4)))
    mesh_lat = centred(own_keys[1], (MESH, D), 1.0, 6.0, ((0, 4), (1, 4)))
    grid_send = draw_grid_send(jax.random.fold_in(seeds[24], 71), part)
    mesh_send = draw_mesh_send(jax.random.fold_in(seeds[24], 71), part)
    enc_edges = draw_enc_edges(jax.random.fold_in(seeds[24], 71), part)
    enc_geom = centred(seeds[5], (4, ENC_EDGES), 1.0, 6.0, ((1, 16),), jnp.float32)
    enc_blocks = draw_enc_blocks(jax.random.fold_in(seeds[24], 71), part)
    proc_edges = draw_proc_edges(jax.random.fold_in(seeds[24], 71), part)
    proc_geom = centred(seeds[8], (4, PROC_EDGES), 1.0, 6.0, ((1, 16),), jnp.float32)
    proc_blocks = draw_proc_blocks(jax.random.fold_in(seeds[24], 71), part)
    enc_geo = centred(seeds[10], (4, D), 4 ** -0.5, 3.0, (), jnp.float32)
    proc_geo = centred(seeds[11], (4, D), 4 ** -0.5, 3.0, (), jnp.float32)
    enc_edge_in = centred(seeds[12], (3 * D, FF), (3 * D) ** -0.5, 0.15625, ((0, 4),))
    enc_edge_out = centred(seeds[13], (FF, D), FF ** -0.5, 0.25, ((0, 4),))
    enc_node_in = centred(seeds[14], (2 * D, FF), (2 * D) ** -0.5, 0.1875, ((0, 4),))
    enc_node_out = centred(seeds[15], (FF, D), FF ** -0.5, 0.25, ((0, 4),))
    proc_edge_in = centred(seeds[16], (3 * D, FF), (3 * D) ** -0.5, 0.15625, ((0, 4),))
    proc_edge_out = centred(seeds[17], (FF, D), FF ** -0.5, 0.25, ((0, 4),))
    proc_node_in = centred(seeds[18], (2 * D, FF), (2 * D) ** -0.5, 0.1875, ((0, 4),))
    proc_node_out = centred(seeds[19], (FF, D), FF ** -0.5, 0.25, ((0, 4),))
    enc_edge_gain = jnp.clip(1.0 + 0.15 * jax.random.normal(seeds[20], (D,), jnp.float32), 0.25, 1.75)
    enc_node_gain = jnp.clip(1.0 + 0.15 * jax.random.normal(seeds[21], (D,), jnp.float32), 0.25, 1.75)
    proc_edge_gain = jnp.clip(1.0 + 0.15 * jax.random.normal(seeds[22], (D,), jnp.float32), 0.25, 1.75)
    proc_node_gain = jnp.clip(1.0 + 0.15 * jax.random.normal(seeds[23], (D,), jnp.float32), 0.25, 1.75)
    return {"grid_lat": grid_lat, "mesh_lat": mesh_lat, "grid_send": grid_send, "mesh_send": mesh_send, "enc_edges": enc_edges, "enc_geom": enc_geom, "enc_blocks": enc_blocks, "proc_edges": proc_edges, "proc_geom": proc_geom, "proc_blocks": proc_blocks, "enc_geo": enc_geo, "proc_geo": proc_geo, "enc_edge_in": enc_edge_in, "enc_edge_out": enc_edge_out, "enc_node_in": enc_node_in, "enc_node_out": enc_node_out, "proc_edge_in": proc_edge_in, "proc_edge_out": proc_edge_out, "proc_node_in": proc_node_in, "proc_node_out": proc_node_out, "enc_edge_gain": enc_edge_gain, "enc_node_gain": enc_node_gain, "proc_edge_gain": proc_edge_gain, "proc_node_gain": proc_node_gain}


OFFSETS = (-2, -1, 1, 2)

def layer_norm(values, scales):
    average = lax.optimization_barrier(jnp.mean(values, axis=-1, keepdims=True))
    centered = values - average
    spread = lax.optimization_barrier(jnp.mean(centered * centered, axis=-1, keepdims=True))
    return centered / jnp.sqrt(spread + 1e-05) * scales

def extended_index(send_table, node_rows):
    partitions = jnp.arange(PARTS_SIZE, dtype=jnp.int32)
    pieces = [partitions[:, None] * node_rows + jnp.arange(node_rows, dtype=jnp.int32)[None, :]]
    for region in range(4):
        source = partitions + OFFSETS[region]
        inside = (source >= 0) & (source < PARTS_SIZE)
        clipped = jnp.clip(source, 0, PARTS_SIZE - 1).astype(jnp.int32)
        listed = send_table[clipped, 3 - region, :] + clipped[:, None] * node_rows
        pieces.append(jnp.where(inside[:, None], listed, 0).astype(jnp.int32))
    return jnp.concatenate(pieces, axis=1)

def edge_pass(edge_lists, geometry, live_blocks, node_source, node_target, send_table, node_rows, geo_weight, weights_in, weights_out, edge_gain, capacity):
    per_part = capacity * BLOCK
    lookup = extended_index(send_table, node_rows)
    edges_split = edge_lists.reshape(2, PARTS_SIZE, per_part).transpose(1, 0, 2)
    geometry_split = geometry.reshape(4, PARTS_SIZE, per_part).transpose(1, 0, 2)
    positions = jnp.arange(per_part, dtype=jnp.int32)

    def visit(totals, inputs):
        edges_here, geometry_here, lookup_here, live_here, partition = inputs
        senders = lookup_here[edges_here[0]]
        receivers = edges_here[1] + partition * MESH_DEV
        embedded = jax.nn.silu(jnp.dot(geometry_here.T, geo_weight, precision=lax.Precision.HIGHEST)).astype(jnp.bfloat16)
        stacked = jnp.concatenate([embedded, node_source[senders], node_target[receivers]], axis=1)
        hidden = jax.nn.silu(jnp.dot(stacked, weights_in, preferred_element_type=jnp.float32)).astype(jnp.bfloat16)
        message = layer_norm(jnp.dot(hidden, weights_out, preferred_element_type=jnp.float32), edge_gain)
        message = jnp.where((positions < live_here * BLOCK)[:, None], message, 0.0)
        return (totals.at[receivers].add(message), None)
    totals = jnp.zeros((PARTS_SIZE * MESH_DEV, node_target.shape[1]), jnp.float32)
    totals, ignored = lax.scan(visit, totals, (edges_split, geometry_split, lookup, live_blocks, jnp.arange(PARTS_SIZE, dtype=jnp.int32)))
    return totals

def node_pass(latent, totals, weights_in, weights_out, node_gain):
    stacked = jnp.concatenate([latent, totals.astype(jnp.bfloat16)], axis=1)
    hidden = jax.nn.silu(jnp.dot(stacked, weights_in, preferred_element_type=jnp.float32)).astype(jnp.bfloat16)
    update = layer_norm(jnp.dot(hidden, weights_out, preferred_element_type=jnp.float32), node_gain)
    return (latent.astype(jnp.float32) + update).astype(jnp.bfloat16)

def reference(grid_lat, mesh_lat, grid_send, mesh_send, enc_edges, enc_geom, enc_blocks, proc_edges, proc_geom, proc_blocks, enc_geo, proc_geo, enc_edge_in, enc_edge_out, enc_node_in, enc_node_out, proc_edge_in, proc_edge_out, proc_node_in, proc_node_out, enc_edge_gain, enc_node_gain, proc_edge_gain, proc_node_gain):
    totals = edge_pass(enc_edges, enc_geom, enc_blocks, grid_lat, mesh_lat, grid_send, GRID_DEV, enc_geo, enc_edge_in, enc_edge_out, enc_edge_gain, ENC_CAP)
    middle = node_pass(mesh_lat, totals, enc_node_in, enc_node_out, enc_node_gain)
    totals = edge_pass(proc_edges, proc_geom, proc_blocks, middle, middle, mesh_send, MESH_DEV, proc_geo, proc_edge_in, proc_edge_out, proc_edge_gain, PROC_CAP)
    return node_pass(middle, totals, proc_node_in, proc_node_out, proc_node_gain)
```

```python
import functools

import jax
import jax.numpy as jnp
from jax import lax
from jax.experimental import pallas as pl
from jax.experimental.pallas import tpu as pltpu
from jax.sharding import PartitionSpec as P

BLOCK = 128
OFFSETS = (-2, -1, 1, 2)
STEP = 256
VMEM_BYTES = 48 * 1024 * 1024
BF16 = jnp.bfloat16
F32 = jnp.float32


def silu(v):
    h = 0.5 * v
    return h + h * jnp.tanh(h)


def region_of(delta):
    return jnp.where(delta < 0, delta + 2, delta + 1)


def halo_plan(count):
    plan = []
    if count == 4:
        for bit in (1, 2, 3):
            pairs = [(d, d ^ bit) for d in range(4) if abs((d ^ bit) - d) <= 2]
            regions = [(OFFSETS.index((d ^ bit) - d) if abs((d ^ bit) - d) <= 2 else -1) for d in range(4)]
            plan.append((pairs, regions, regions))
    else:
        for region, offset in enumerate(OFFSETS):
            pairs = [(d, d + offset) for d in range(count) if 0 <= d + offset < count]
            plan.append((pairs, region, 3 - region))
    return plan


def by_index(choice, index):
    if isinstance(choice, int):
        return choice
    picked = jnp.int32(choice[0])
    for place in range(1, len(choice)):
        picked = jnp.where(index == place, choice[place], picked)
    return picked


def whole_refs(count):
    return [pl.BlockSpec(memory_space=pltpu.VMEM)] * count


def call(body, outs, args, scratch=(), flops=0, smem=0):
    moved = sum(a.size * a.dtype.itemsize for a in args) + sum(
        o.size * jnp.dtype(o.dtype).itemsize for o in outs
    )
    specs = whole_refs(len(args) - smem) + [pl.BlockSpec(memory_space=pltpu.SMEM)] * smem
    return pl.pallas_call(
        body,
        out_shape=tuple(outs),
        in_specs=specs,
        out_specs=tuple(whole_refs(len(outs))),
        scratch_shapes=list(scratch),
        compiler_params=pltpu.CompilerParams(vmem_limit_bytes=VMEM_BYTES),
        cost_estimate=pl.CostEstimate(flops=int(flops), bytes_accessed=int(moved), transcendentals=0),
    )(*args)


def dot(a, b):
    return jnp.dot(a, b, preferred_element_type=F32)


def dot_first(a, b):
    return lax.dot_general(a, b, (((0,), (0,)), ((), ())), preferred_element_type=F32)


def three_parts(v):
    a = v.astype(BF16)
    rest = v - a.astype(F32)
    b = rest.astype(BF16)
    c = (rest - b.astype(F32)).astype(BF16)
    return a, b, c


def embed_rows(geom, geo):
    a1, a2, a3 = three_parts(geom)
    b1, b2, b3 = three_parts(geo)
    left = jnp.concatenate([a1, a1, a2, a1, a2, a3], axis=0)
    right = jnp.concatenate([b1, b2, b1, b3, b2, b1], axis=0)
    return silu(dot_first(left, right)).astype(BF16)


def embed_kernel(egeom, egeo, pgeom, pgeo, eout, pout):
    for geom, geo, out in ((egeom, egeo, eout), (pgeom, pgeo, pout)):
        for first in range(0, out.shape[0], STEP):
            out[first : first + STEP, :] = embed_rows(geom[:, first : first + STEP], geo[...])


def layer_norm(v):
    width = v.shape[-1]
    centered = v - jnp.sum(v, axis=-1, keepdims=True) * (1.0 / width)
    spread = jnp.sum(centered * centered, axis=-1, keepdims=True) * (1.0 / width)
    return centered * lax.rsqrt(spread + 1e-05)


def pick_rows(table, listed):
    rows = lax.broadcasted_iota(jnp.int32, (table.shape[0], listed.shape[1]), 0)
    return dot_first((rows == listed).astype(F32).astype(BF16), table).astype(BF16)


def place_shards(shards, steps, target, rows, first_row=0):
    quarter = lax.axis_index("sub")
    for shard, step in zip(shards, steps):
        place = pl.multiple_of(lax.bitwise_xor(quarter, step) * rows, rows)
        target[pl.ds(place, rows), :] = shard[first_row : first_row + rows, :]


def pack_kernel(grid, mesh, w_in, w_out, lat, weights):
    n = grid.shape[0]
    lat[:n, :] = grid[...]
    lat[n:, :] = mesh[...]
    k = w_in.shape[0]
    weights[:k, :] = w_in[...]
    weights[k:, :] = w_out[...]


XOR_STEPS = (0, 2, 1, 3)


def spread_kernel(plan, rows, l0, l1, l2, l3, send, full, *outs):
    quarter = lax.axis_index("sub")
    here = lax.axis_index("dom")
    width = l0.shape[1]
    for shard, step in zip((l0, l1, l2, l3), XOR_STEPS):
        place = pl.multiple_of(lax.bitwise_xor(quarter, step) * width, width)
        full[:, pl.ds(place, width)] = shard[...]
    table = full[:rows, :]
    for (pairs, sent, received), out in zip(plan, outs):
        region = jnp.maximum(by_index(sent, here), 0)
        out[...] = pick_rows(table, send[0, pl.ds(region, 1), :])


def halo_targets(plan, slots, node_rows, width):
    here = lax.axis_index("dom")
    lane = lax.broadcasted_iota(jnp.int32, (1, width), 1)
    target = jnp.full((1, width), -1, jnp.int32)
    for place, (pairs, sent, received) in enumerate(plan):
        region = by_index(received, here)
        first = jnp.where(region < 0, -4 * node_rows, node_rows + region * slots)
        inside = (lane >= place * slots) & (lane < (place + 1) * slots)
        target = jnp.where(inside, lane - place * slots + first, target)
    return target


def edge_blocks(edges, live_edges, count, targets, node_rows, out_rows, first_stage, w_out, totals):
    lane = lax.broadcasted_iota(jnp.int32, (1, node_rows), 1)
    row = lax.broadcasted_iota(jnp.int32, (out_rows, 1), 0)
    quarter = lax.axis_index("sub")
    zero = jnp.zeros((6, STEP), jnp.int32)
    total = None
    for block in range(count // STEP):
        first = block * STEP
        pair = edges[:, first : first + STEP]
        upright = jnp.transpose(jnp.concatenate([pair, zero], axis=0).astype(F32)).astype(jnp.int32)
        senders = upright[:, 0:1]
        receivers = upright[:, 1:2]
        summed = first_stage(block, senders, receivers, lane)
        hidden = silu(summed).astype(BF16)
        message = layer_norm(dot(hidden, w_out[...]))
        place = lax.broadcasted_iota(jnp.int32, (STEP, 1), 0) + (first + quarter * count)
        message = jnp.where(place < live_edges, message, 0.0).astype(BF16)
        collect = (row == pair[1:2, :]).astype(F32).astype(BF16)
        part = dot(collect, message)
        if block == 0:
            totals[...] = part
        else:
            totals[...] += part
    return total


def hot(cond):
    return cond.astype(F32).astype(BF16)


def hand_out(totals, gain, keep, give):
    rows = totals.shape[0] // 4
    core = lax.rem(lax.axis_index("sub"), 2)
    for half in range(2):
        for out, which in ((keep, core), (give, 1 - core)):
            place = pl.multiple_of((2 * half + which) * rows, rows)
            out[half * rows : (half + 1) * rows, :] = (totals[pl.ds(place, rows), :] * gain[...]).astype(BF16)


def enc_kernel(plan, slots, node_rows, n_halo, emb, full, edges, gain, w0, w1, w2, w3, *rest):
    halos = rest[:n_halo]
    live, keep, give, w_in, w_out, table, totals = rest[n_halo:]
    d = full.shape[1]
    k = w_in.shape[0] // 4
    shards = (w0, w1, w2, w3)
    place_shards(shards, XOR_STEPS, w_in, k)
    place_shards(shards, XOR_STEPS, w_out, w_out.shape[0] // 4, k)
    mesh_rows = full.shape[0] - node_rows
    table[:node_rows, :] = dot(full[:node_rows, :], w_in[d : 2 * d, :]).astype(BF16)
    table[node_rows : node_rows + mesh_rows, :] = dot(full[node_rows:, :], w_in[2 * d :, :]).astype(BF16)
    base = node_rows + mesh_rows
    got = jnp.concatenate([h[...] for h in halos], axis=0)
    table[base : base + got.shape[0], :] = dot(got, w_in[d : 2 * d, :]).astype(BF16)
    if base + got.shape[0] < table.shape[0]:
        table[base + got.shape[0] :, :] = jnp.zeros((table.shape[0] - base - got.shape[0], d), BF16)
    targets = halo_targets(plan, slots, node_rows, table.shape[0] - base)

    def first_stage(block, senders, receivers, lane):
        chosen = jnp.concatenate(
            [hot(lane == senders), hot(lane == receivers), hot(targets == senders)], axis=1
        )
        return dot(emb[block * STEP : (block + 1) * STEP, :], w_in[:d, :]) + dot(chosen, table[...])

    edge_blocks(
        edges, live[0] * BLOCK, edges.shape[1], targets, node_rows, mesh_rows, first_stage, w_out, totals
    )
    hand_out(totals, gain, keep, give)


def shard_rows(ref, first, rows, place):
    step = ref.shape[0] // 4
    start = (0, 2, 1, 3).index(place) * step + first
    return ref[start : start + rows, :]


def node_kernel(rows_total, first_in, rows_in, rows_out, mesh, mine, theirs, gain, weights, out):
    d = gain.shape[1]
    shares = (mine[...].astype(F32) + theirs[...].astype(F32)).astype(BF16)
    stacked = jnp.concatenate([mesh[...], shares], axis=1)
    w_in = jnp.concatenate([shard_rows(weights, first_in, rows_in, p) for p in range(4)], axis=0)
    w_out = jnp.concatenate([shard_rows(weights, first_in + rows_in, rows_out, p) for p in range(4)], axis=0)
    hidden = silu(dot(stacked, w_in)).astype(BF16)
    update = layer_norm(dot(hidden, w_out)) * gain[...]
    out[...] = (mesh[...].astype(F32) + update).astype(BF16)


def core_rows_kernel(first_row, full, out):
    rows = out.shape[0] // 2
    core = lax.rem(lax.axis_index("sub"), 2)
    for half in range(2):
        place = pl.multiple_of(first_row + (2 * half + core) * rows, rows)
        out[half * rows : (half + 1) * rows, :] = full[pl.ds(place, rows), :]


def middle_kernel(plan, mine, theirs, send, full, *outs):
    rows = mine.shape[0] // 2
    core = lax.rem(lax.axis_index("sub"), 2)
    here = lax.axis_index("dom")
    for half in range(2):
        for part, which in ((mine, core), (theirs, 1 - core)):
            place = pl.multiple_of((2 * half + which) * rows, rows)
            full[pl.ds(place, rows), :] = part[half * rows : (half + 1) * rows, :]
    table = full[...]
    for (pairs, sent, received), out in zip(plan, outs):
        region = jnp.maximum(by_index(sent, here), 0)
        out[...] = pick_rows(table, send[0, pl.ds(region, 1), :])


def proc_first_kernel(emb, full, edges, weights, pre, table):
    d = full.shape[1]
    node_rows = full.shape[0]
    step = weights.shape[0] // 4
    w_in = jnp.concatenate([shard_rows(weights, 0, 3 * d // 4, p) for p in range(4)], axis=0)
    table[:node_rows, :] = dot(full[...], w_in[d : 2 * d, :]).astype(BF16)
    table[node_rows:, :] = dot(full[...], w_in[2 * d :, :]).astype(BF16)
    lane = lax.broadcasted_iota(jnp.int32, (1, node_rows), 1)
    zero = jnp.zeros((6, STEP), jnp.int32)
    for block in range(edges.shape[1] // STEP):
        first = block * STEP
        pair = edges[:, first : first + STEP]
        upright = jnp.transpose(jnp.concatenate([pair, zero], axis=0).astype(F32)).astype(jnp.int32)
        chosen = jnp.concatenate([hot(lane == upright[:, 0:1]), hot(lane == upright[:, 1:2])], axis=1)
        pre[first : first + STEP, :] = dot(emb[first : first + STEP, :], w_in[:d, :]) + dot(chosen, table[...])


def proc_second_kernel(plan, slots, node_rows, n_halo, pre, edges, gain, weights, *rest):
    halos = rest[:n_halo]
    live, keep, give, w_out, table, totals = rest[n_halo:]
    d = pre.shape[1]
    for place in range(4):
        k = 3 * d // 4
        w_out[place * d // 4 : (place + 1) * d // 4, :] = shard_rows(weights, k, d // 4, place)
    w_source = jnp.concatenate([shard_rows(weights, 0, 3 * d // 4, p) for p in range(4)], axis=0)[d : 2 * d, :]
    got = jnp.concatenate([h[...] for h in halos], axis=0)
    table[: got.shape[0], :] = dot(got, w_source).astype(BF16)
    if got.shape[0] < table.shape[0]:
        table[got.shape[0] :, :] = jnp.zeros((table.shape[0] - got.shape[0], d), BF16)
    targets = halo_targets(plan, slots, node_rows, table.shape[0])

    def first_stage(block, senders, receivers, lane):
        return pre[block * STEP : (block + 1) * STEP, :] + dot(hot(targets == senders), table[...])

    edge_blocks(
        edges, live[0] * BLOCK, edges.shape[1], targets, node_rows, node_rows, first_stage, w_out, totals
    )
    hand_out(totals, gain, keep, give)


def fold_kernel(mine, theirs, keep, give):
    rows = mine.shape[0] // 2
    chip = lax.div(lax.axis_index("sub"), 2)
    for out, which in ((keep, chip), (give, 1 - chip)):
        place = pl.multiple_of(which * rows, rows)
        out[...] = (mine[pl.ds(place, rows), :].astype(F32) + theirs[pl.ds(place, rows), :].astype(F32)).astype(BF16)


def add_kernel(mine, theirs, out):
    out[...] = (mine[...].astype(F32) + theirs[...].astype(F32)).astype(BF16)


def out_kernel(first_in, rows_in, rows_out, full, mine, theirs, gain, weights, out):
    rows = mine.shape[0]
    place = pl.multiple_of(lax.axis_index("sub") * rows, rows)
    node_kernel(rows, first_in, rows_in, rows_out, full.at[pl.ds(place, rows), :], mine, theirs, gain, weights, out)


def to_chip(v):
    return lax.ppermute(v, "sub", [(i, i ^ 2) for i in range(4)])


def to_core(v):
    return lax.ppermute(v, "sub", [(i, i ^ 1) for i in range(4)])


def spread(v):
    across = to_chip(v)
    beside = to_core(v)
    return v, across, beside, to_core(across)


def gathered(v):
    pair = lax.all_gather(v, "sub", axis=0, tiled=True, axis_index_groups=[[0, 2], [1, 3]])
    return lax.all_gather(pair, "sub", axis=0, tiled=True, axis_index_groups=[[0, 1], [2, 3]])


def shape(rows, width, dtype=BF16):
    return jax.ShapeDtypeStruct((rows, width), dtype)


def padded(rows):
    return -(-rows // 128) * 128


def local(
    grid_lat,
    mesh_lat,
    grid_send,
    mesh_send,
    enc_edges,
    enc_geom,
    enc_blocks,
    proc_edges,
    proc_geom,
    proc_blocks,
    enc_geo,
    proc_geo,
    enc_edge_in,
    enc_edge_out,
    enc_node_in,
    enc_node_out,
    proc_edge_in,
    proc_edge_out,
    proc_node_in,
    proc_node_out,
    enc_edge_gain,
    enc_node_gain,
    proc_edge_gain,
    proc_node_gain,
):
    plan = halo_plan(lax.axis_size("dom"))
    d = enc_geo.shape[1]
    grid_rows, mesh_rows = grid_lat.shape[0], mesh_lat.shape[0]
    n_enc, n_proc = enc_edges.shape[1], proc_edges.shape[1]
    enc_edge_gain, enc_node_gain, proc_edge_gain, proc_node_gain = (
        g.reshape(1, d) for g in (enc_edge_gain, enc_node_gain, proc_edge_gain, proc_node_gain)
    )
    k_in, k_out = enc_edge_in.shape[0], enc_edge_out.shape[0]

    lat, enc_w = call(
        pack_kernel,
        [shape(grid_rows + mesh_rows, grid_lat.shape[1]), shape(k_in + k_out, d)],
        [grid_lat, mesh_lat, enc_edge_in, enc_edge_out],
    )
    lat_parts = spread(lat)
    enc_w_parts = spread(enc_w)
    enc_node_w = gathered(jnp.concatenate([enc_node_in, enc_node_out], axis=0))
    proc_w = gathered(jnp.concatenate([proc_edge_in, proc_edge_out, proc_node_in, proc_node_out], axis=0))

    enc_emb, proc_emb = call(
        embed_kernel,
        [shape(n_enc, d), shape(n_proc, d)],
        [enc_geom, enc_geo, proc_geom, proc_geo],
        flops=2 * (n_enc + n_proc) * d * 128,
    )
    slots = grid_send.shape[2]
    full, *outgoing = call(
        functools.partial(spread_kernel, plan, grid_rows),
        [shape(grid_rows + mesh_rows, d)] + [shape(slots, d)] * len(plan),
        [*lat_parts, grid_send],
        flops=2 * len(plan) * slots * grid_rows * d,
    )
    halos = [lax.ppermute(v, "dom", entry[0]) for v, entry in zip(outgoing, plan)]
    halo_rows = padded(len(plan) * slots)
    half = mesh_rows // 2
    keep, give = call(
        functools.partial(enc_kernel, plan, slots, grid_rows, len(plan)),
        [shape(half, d), shape(half, d)],
        [enc_emb, full, enc_edges, enc_edge_gain, *enc_w_parts, *halos, enc_blocks],
        scratch=[
            pltpu.VMEM((3 * d, d), BF16),
            pltpu.VMEM((d, d), BF16),
            pltpu.VMEM((grid_rows + mesh_rows + halo_rows, d), BF16),
            pltpu.VMEM((mesh_rows, d), F32),
        ],
        flops=2 * n_enc * d * (3 * d + grid_rows + mesh_rows + halo_rows),
        smem=1,
    )
    (own_mesh,) = call(functools.partial(core_rows_kernel, grid_rows), [shape(half, d)], [full])
    (chip_sum,) = call(add_kernel, [shape(half, d)], [keep, to_core(give)])
    (mid_half,) = call(
        functools.partial(node_kernel, half, 0, enc_node_in.shape[0], enc_node_out.shape[0]),
        [shape(half, d)],
        [own_mesh, chip_sum, to_chip(chip_sum), enc_node_gain, enc_node_w],
        flops=2 * half * d * 3 * d,
    )
    slots = mesh_send.shape[2]
    mid, *outgoing = call(
        functools.partial(middle_kernel, plan),
        [shape(mesh_rows, d)] + [shape(slots, d)] * len(plan),
        [mid_half, to_core(mid_half), mesh_send],
        flops=2 * len(plan) * slots * mesh_rows * d,
    )
    halos = [lax.ppermute(v, "dom", entry[0]) for v, entry in zip(outgoing, plan)]
    halo_rows = padded(len(plan) * slots)
    (pre,) = call(
        proc_first_kernel,
        [shape(n_proc, d, F32)],
        [proc_emb, mid, proc_edges, proc_w],
        scratch=[pltpu.VMEM((2 * mesh_rows, d), BF16)],
        flops=2 * n_proc * d * (d + 2 * mesh_rows),
    )
    keep, give = call(
        functools.partial(proc_second_kernel, plan, slots, mesh_rows, len(plan)),
        [shape(half, d), shape(half, d)],
        [pre, proc_edges, proc_edge_gain, proc_w, *halos, proc_blocks],
        scratch=[
            pltpu.VMEM((d, d), BF16),
            pltpu.VMEM((halo_rows, d), BF16),
            pltpu.VMEM((mesh_rows, d), F32),
        ],
        flops=2 * n_proc * d * (d + mesh_rows + halo_rows),
        smem=1,
    )
    quarter = mesh_rows // 4
    mine, other = call(fold_kernel, [shape(quarter, d)] * 2, [keep, to_core(give)])
    (result,) = call(
        functools.partial(out_kernel, k_in + k_out, proc_node_in.shape[0], proc_node_out.shape[0]),
        [shape(quarter, d)],
        [mid, mine, to_chip(other), proc_node_gain, proc_w],
        flops=2 * quarter * d * 3 * d,
    )
    return result


def solution(mesh):
    placed = (
        P(("groups", "dom"), "sub"),
        P(("groups", "dom"), "sub"),
        P("dom", None, None),
        P("dom", None, None),
        P(None, ("dom", "sub")),
        P(None, ("dom", "sub")),
        P("dom"),
        P(None, ("dom", "sub")),
        P(None, ("dom", "sub")),
        P("dom"),
        P(),
        P(),
        P("sub", None),
        P("sub", None),
        P("sub", None),
        P("sub", None),
        P("sub", None),
        P("sub", None),
        P("sub", None),
        P("sub", None),
        P(),
        P(),
        P(),
        P(),
    )
    return jax.shard_map(
        local,
        mesh=mesh,
        in_specs=placed,
        out_specs=P(("groups", "dom", "sub"), None),
        check_vma=False,
    )
```

```python
import functools

import jax
import jax.numpy as jnp
from jax import lax
from jax.experimental import pallas as pl
from jax.experimental.pallas import tpu as pltpu
from jax.sharding import PartitionSpec as P

BLOCK = 128
OFFSETS = (-2, -1, 1, 2)
STEP = 512
GATHERED = 1024
VMEM_BYTES = 24 * 1024 * 1024
I16 = jnp.int16
BF16 = jnp.bfloat16
F32 = jnp.float32


def silu(v):
    h = 0.5 * v
    return h + h * jnp.tanh(h)


def region_of(delta):
    return jnp.where(delta < 0, delta + 2, delta + 1)


def halo_plan(count):
    plan = []
    if count == 4:
        for bit in (1, 2, 3):
            pairs = [(d, d ^ bit) for d in range(4) if abs((d ^ bit) - d) <= 2]
            regions = [(OFFSETS.index((d ^ bit) - d) if abs((d ^ bit) - d) <= 2 else -1) for d in range(4)]
            plan.append((pairs, regions, regions))
    else:
        for region, offset in enumerate(OFFSETS):
            pairs = [(d, d + offset) for d in range(count) if 0 <= d + offset < count]
            plan.append((pairs, region, 3 - region))
    return plan


def by_index(choice, index):
    if isinstance(choice, int):
        return choice
    picked = jnp.int32(choice[0])
    for place in range(1, len(choice)):
        picked = jnp.where(index == place, choice[place], picked)
    return picked


def whole_refs(count):
    return [pl.BlockSpec(memory_space=pltpu.VMEM)] * count


def call(body, outs, args, scratch=(), flops=0, smem=0):
    moved = sum(a.size * a.dtype.itemsize for a in args) + sum(
        o.size * jnp.dtype(o.dtype).itemsize for o in outs
    )
    specs = whole_refs(len(args) - smem) + [pl.BlockSpec(memory_space=pltpu.SMEM)] * smem
    return pl.pallas_call(
        body,
        out_shape=tuple(outs),
        in_specs=specs,
        out_specs=tuple(whole_refs(len(outs))),
        scratch_shapes=list(scratch),
        compiler_params=pltpu.CompilerParams(vmem_limit_bytes=VMEM_BYTES),
        cost_estimate=pl.CostEstimate(flops=int(flops), bytes_accessed=int(moved), transcendentals=0),
    )(*args)


def dot(a, b):
    return jnp.dot(a, b, preferred_element_type=F32)


def dot_first(a, b):
    return lax.dot_general(a, b, (((0,), (0,)), ((), ())), preferred_element_type=F32)


def three_parts(v):
    a = v.astype(BF16)
    rest = v - a.astype(F32)
    b = rest.astype(BF16)
    c = (rest - b.astype(F32)).astype(BF16)
    return a, b, c


def embed_rows(geom, geo):
    a1, a2, a3 = three_parts(geom)
    b1, b2, b3 = three_parts(geo)
    left = jnp.concatenate([a1, a1, a2, a1, a2, a3], axis=0)
    right = jnp.concatenate([b1, b2, b1, b3, b2, b1], axis=0)
    return silu(dot_first(left, right)).astype(BF16)


def embed_kernel(egeom, egeo, pgeom, pgeo, after, eout, pout):
    for geom, geo, out in ((egeom, egeo, eout), (pgeom, pgeo, pout)):
        for first in range(0, out.shape[0], STEP):
            out[first : first + STEP, :] = embed_rows(geom[:, first : first + STEP], geo[...])


def layer_norm(v):
    width = v.shape[-1]
    centered = v - jnp.sum(v, axis=-1, keepdims=True) * (1.0 / width)
    spread = jnp.sum(centered * centered, axis=-1, keepdims=True) * (1.0 / width)
    return centered * lax.rsqrt(spread + 1e-05)


def hot(cond):
    return jnp.where(cond, BF16(1), BF16(0))


def pick_rows(table, listed):
    rows = lax.broadcasted_iota(I16, (table.shape[0], 1), 0)
    return dot_first(hot(rows == listed.astype(I16)), table).astype(BF16)


def pick_lists(plan, table, send, outs):
    here = lax.axis_index("dom")
    for (pairs, sent, received), out in zip(plan, outs):
        region = jnp.maximum(by_index(sent, here), 0)
        out[...] = pick_rows(table, send[0, pl.ds(region, 1), :])


def half_of(whole, half):
    rows = half.shape[0]
    half[...] = whole[pl.ds(pl.multiple_of(lax.axis_index("groups") * rows, rows), rows), :]


def stack_into(out, parts):
    first = 0
    for part in parts:
        out[first : first + part.shape[0], :] = part[...]
        first += part.shape[0]


def first_pack_kernel(plan, grid, send, w_in, w_out, weights, half, *outs):
    stack_into(weights, (w_in, w_out))
    half_of(weights, half)
    pick_lists(plan, grid[...], send, outs)


def second_pack_kernel(e_in, e_out, p_in, p_out, after, weights, e_half, p_half):
    stack_into(weights, (e_in, e_out, p_in, p_out))
    rows = e_in.shape[0] + e_out.shape[0]
    half_of(weights.at[:rows, :], e_half)
    half_of(weights.at[rows:, :], p_half)


def concat_kernel(*refs):
    stack_into(refs[-1], refs[:-1])


def place_shards(target, refs, first=0):
    own, beside, *halves = refs
    quarter = lax.axis_index("sub")
    group = lax.axis_index("groups")
    rows = target.shape[0] // 4
    for ref, step in ((own, 0), (beside, 1)):
        place = pl.multiple_of(lax.bitwise_xor(quarter, step) * rows, rows)
        target[pl.ds(place, rows), :] = ref[first : first + rows, :]
    if len(halves) == 2:
        for ref, step in zip(halves, (2, 3)):
            place = pl.multiple_of(lax.bitwise_xor(quarter, step) * rows, rows)
            target[pl.ds(place, rows), :] = ref[...]
    else:
        half = rows // 2
        for ref, step, other in zip(halves, (2, 2, 3, 3), (0, 1, 0, 1)):
            which = lax.bitwise_xor(group, other)
            place = pl.multiple_of(lax.bitwise_xor(quarter, step) * rows + which * half, half)
            target[pl.ds(place, half), :] = ref[...]


def joined(stack, first, rows):
    step = stack.shape[0] // 4
    return jnp.concatenate([stack[k * step + first : k * step + first + rows, :] for k in range(4)], axis=0)


def halo_targets(plan, slots, node_rows, width):
    here = lax.axis_index("dom")
    lane = lax.broadcasted_iota(jnp.int32, (1, width), 1)
    target = jnp.full((1, width), -1, jnp.int32)
    for place, (pairs, sent, received) in enumerate(plan):
        region = by_index(received, here)
        first = jnp.where(region < 0, -4 * node_rows, node_rows + region * slots)
        inside = (lane >= place * slots) & (lane < (place + 1) * slots)
        target = jnp.where(inside, lane - place * slots + first, target)
    return target.astype(I16)


def columns(edges, first):
    pair = edges[:, first : first + STEP]
    zero = jnp.zeros((8 - pair.shape[0], STEP), jnp.int32)
    upright = jnp.transpose(jnp.concatenate([pair, zero], axis=0).astype(F32)).astype(jnp.int32).astype(I16)
    return upright[:, 0:1], upright[:, 1:2]


def edge_blocks(edges, live_edges, first_stage, w_out, messages, totals):
    count = edges.shape[1]
    row = lax.broadcasted_iota(I16, (totals.shape[0], 1), 0)
    quarter = lax.axis_index("sub")
    for first in range(0, count, STEP):
        hidden = silu(first_stage(first)).astype(BF16)
        message = layer_norm(dot(hidden, w_out))
        place = lax.broadcasted_iota(jnp.int32, (STEP, 1), 0) + (first + quarter * count)
        messages[first : first + STEP, :] = jnp.where(place < live_edges, message, 0.0).astype(BF16)
        done = first + STEP
        if done % GATHERED == 0 or done == count:
            begin = (first // GATHERED) * GATHERED
            collect = hot(row == edges[1:2, begin:done].astype(I16))
            part = dot(collect, messages[begin:done, :])
            if begin == 0:
                totals[...] = part
            else:
                totals[...] += part


def hand_out(totals, gain, keep, give):
    rows = totals.shape[0] // 4
    core = lax.rem(lax.axis_index("sub"), 2)
    for half in range(2):
        for out, which in ((keep, core), (give, 1 - core)):
            place = pl.multiple_of((2 * half + which) * rows, rows)
            out[half * rows : (half + 1) * rows, :] = (totals[pl.ds(place, rows), :] * gain[...]).astype(BF16)


def enc_kernel(
    plan, slots, grid_rows, mesh_rows, k_in, emb, edges, gain, l0, l1, l2, l3, w0, w1, w2, w3, w4, w5,
    live, keep, give, own_mesh, full, stack, table, messages, totals,
):
    d = gain.shape[1]
    quarter = lax.axis_index("sub")
    width = l0.shape[1]
    for shard, step in zip((l0, l1, l2, l3), (0, 2, 1, 3)):
        place = pl.multiple_of(lax.bitwise_xor(quarter, step) * width, width)
        full[:, pl.ds(place, width)] = shard[...]
    place_shards(stack, (w0, w1, w2, w3, w4, w5))
    rows = mesh_rows // 4
    core = lax.rem(quarter, 2)
    for half in range(2):
        place = pl.multiple_of(grid_rows + (2 * half + core) * rows, rows)
        own_mesh[half * rows : (half + 1) * rows, :] = full[pl.ds(place, rows), :]

    w_in = joined(stack, 0, k_in)
    halo_first, got = grid_rows + mesh_rows, full.shape[0] - grid_rows - mesh_rows
    table[:d, :] = w_in[:d, :]
    table[d : d + grid_rows, :] = dot(full[:grid_rows, :], w_in[d : 2 * d, :]).astype(BF16)
    base = d + grid_rows + mesh_rows
    table[d + grid_rows : base, :] = dot(full[grid_rows:halo_first, :], w_in[2 * d :, :]).astype(BF16)
    table[base : base + got, :] = dot(full[halo_first:, :], w_in[d : 2 * d, :]).astype(BF16)
    if base + got < table.shape[0]:
        table[base + got :, :] = jnp.zeros((table.shape[0] - base - got, d), BF16)
    targets = halo_targets(plan, slots, grid_rows, table.shape[0] - base)
    own = lax.broadcasted_iota(I16, (1, grid_rows), 1)
    mesh = lax.broadcasted_iota(I16, (1, mesh_rows), 1)

    def first_stage(first):
        senders, receivers = columns(edges, first)
        chosen = [emb[first : first + STEP, :], hot(own == senders), hot(mesh == receivers), hot(targets == senders)]
        return dot(jnp.concatenate(chosen, axis=1), table[...])

    edge_blocks(edges, live[0] * BLOCK, first_stage, joined(stack, k_in, d // 4), messages, totals)
    hand_out(totals, gain, keep, give)


def node_update(mesh, shares, w_in, w_out, gain):
    stacked = jnp.concatenate([mesh, shares], axis=1)
    hidden = silu(dot(stacked, w_in)).astype(BF16)
    update = layer_norm(dot(hidden, w_out)) * gain
    return (mesh.astype(F32) + update).astype(BF16)


def add(mine, theirs):
    return (mine.astype(F32) + theirs.astype(F32)).astype(BF16)


def add_kernel(mine, theirs, out):
    out[...] = add(mine[...], theirs[...])


def node_kernel(k_in, k_out, mesh, mine, theirs, gain, n_in, n_out, w0, w1, w2, w3, w4, w5, out, packed, stack):
    place_shards(stack, (w0, w1, w2, w3, w4, w5))
    w_in, w_out = joined(stack, 0, k_in), joined(stack, k_in, k_out)
    out[...] = node_update(mesh[...], add(mine[...], theirs[...]), w_in, w_out, gain[...])
    stack_into(packed, (n_in, n_out))


def middle_kernel(plan, mine, theirs, send, full, *outs):
    rows = mine.shape[0] // 2
    core = lax.rem(lax.axis_index("sub"), 2)
    for half in range(2):
        for part, which in ((mine, core), (theirs, 1 - core)):
            place = pl.multiple_of((2 * half + which) * rows, rows)
            full[pl.ds(place, rows), :] = part[half * rows : (half + 1) * rows, :]
    pick_lists(plan, full[...], send, outs)


def proc_first_kernel(k_in, first_row, emb, full, edges, w0, w1, w2, w3, w4, w5, table, pre, w_source, w_out, stack):
    d = full.shape[1]
    node_rows = full.shape[0]
    place_shards(stack, (w0, w1, w2, w3, w4, w5), first_row)
    w_in = joined(stack, 0, k_in)
    w_out[...] = joined(stack, k_in, d // 4)
    w_source[...] = w_in[d : 2 * d, :]
    table[:d, :] = w_in[:d, :]
    table[d : d + node_rows, :] = dot(full[...], w_in[d : 2 * d, :]).astype(BF16)
    table[d + node_rows :, :] = dot(full[...], w_in[2 * d :, :]).astype(BF16)
    lane = lax.broadcasted_iota(I16, (1, node_rows), 1)
    for first in range(0, pre.shape[0], STEP):
        pre[first : first + STEP, :] = dot(own_chosen(emb, edges, lane, first), table[...])


def own_chosen(emb, edges, lane, first):
    senders, receivers = columns(edges, first)
    return jnp.concatenate([emb[first : first + STEP, :], hot(lane == senders), hot(lane == receivers)], axis=1)


def proc_second_kernel(
    plan, slots, node_rows, n_halo, emb, edges, gain, table, pre, w_source, w_out, *rest
):
    halos = rest[:n_halo]
    live, keep, give, halo_table, messages, totals = rest[n_halo:]
    d = pre.shape[1]
    got = jnp.concatenate([h[...] for h in halos], axis=0)
    halo_table[: got.shape[0], :] = dot(got, w_source[...]).astype(BF16)
    if got.shape[0] < halo_table.shape[0]:
        halo_table[got.shape[0] :, :] = jnp.zeros((halo_table.shape[0] - got.shape[0], d), BF16)
    targets = halo_targets(plan, slots, node_rows, halo_table.shape[0])
    lane = lax.broadcasted_iota(I16, (1, node_rows), 1)

    def first_stage(first):
        senders, receivers = columns(edges, first)
        remote = dot(hot(targets == senders), halo_table[...])
        if first < pre.shape[0]:
            return pre[first : first + STEP, :] + remote
        return dot(own_chosen(emb, edges, lane, first), table[...]) + remote

    edge_blocks(edges, live[0] * BLOCK, first_stage, w_out[...], messages, totals)
    hand_out(totals, gain, keep, give)


def fold_kernel(mine, theirs, keep, give):
    rows = mine.shape[0] // 2
    chip = lax.div(lax.axis_index("sub"), 2)
    for out, which in ((keep, chip), (give, 1 - chip)):
        place = pl.multiple_of(which * rows, rows)
        out[...] = add(mine[pl.ds(place, rows), :], theirs[pl.ds(place, rows), :])


def out_kernel(k_in, k_out, full, mine, theirs, gain, w0, w1, w2, w3, out, stack):
    rows = mine.shape[0]
    mesh = full[pl.ds(pl.multiple_of(lax.axis_index("sub") * rows, rows), rows), :]
    place_shards(stack, (w0, w1, w2, w3))
    w_in, w_out = joined(stack, 0, k_in), joined(stack, k_in, k_out)
    out[...] = node_update(mesh, add(mine[...], theirs[...]), w_in, w_out, gain[...])


def to_chip(v):
    return lax.ppermute(v, "sub", [(i, i ^ 2) for i in range(4)])


def to_core(v):
    return lax.ppermute(v, "sub", [(i, i ^ 1) for i in range(4)])


def to_group(v):
    count = lax.axis_size("groups")
    return lax.ppermute(v, "groups", [(i, count - 1 - i) for i in range(count)])


def shape(rows, width, dtype=BF16):
    return jax.ShapeDtypeStruct((rows, width), dtype)


def padded(rows):
    return -(-rows // 128) * 128


def local(
    grid_lat,
    mesh_lat,
    grid_send,
    mesh_send,
    enc_edges,
    enc_geom,
    enc_blocks,
    proc_edges,
    proc_geom,
    proc_blocks,
    enc_geo,
    proc_geo,
    enc_edge_in,
    enc_edge_out,
    enc_node_in,
    enc_node_out,
    proc_edge_in,
    proc_edge_out,
    proc_node_in,
    proc_node_out,
    enc_edge_gain,
    enc_node_gain,
    proc_edge_gain,
    proc_node_gain,
):
    plan = halo_plan(lax.axis_size("dom"))
    d = enc_geo.shape[1]
    grid_rows, mesh_rows = grid_lat.shape[0], mesh_lat.shape[0]
    n_enc, n_proc = enc_edges.shape[1], proc_edges.shape[1]
    enc_edge_gain, enc_node_gain, proc_edge_gain, proc_node_gain = (
        g.reshape(1, d) for g in (enc_edge_gain, enc_node_gain, proc_edge_gain, proc_node_gain)
    )
    k_in, k_out = enc_edge_in.shape[0], enc_edge_out.shape[0]
    n_in, n_out = enc_node_in.shape[0], enc_node_out.shape[0]
    width = grid_lat.shape[1]

    slots = grid_send.shape[2]
    edge_w, edge_half, *outgoing = call(
        functools.partial(first_pack_kernel, plan),
        [shape(k_in + k_out, d), shape((k_in + k_out) // 2, d)] + [shape(slots, width)] * len(plan),
        [grid_lat, grid_send, enc_edge_in, enc_edge_out],
    )
    edge_across = to_chip(edge_half)
    halos = [lax.ppermute(v, "dom", entry[0]) for v, entry in zip(outgoing, plan)]
    got = len(plan) * slots
    (lat,) = call(concat_kernel, [shape(grid_rows + mesh_rows + got, width)], [grid_lat, mesh_lat, *halos])
    lat_across = to_chip(lat)
    lat_beside = to_core(lat)
    edge_beside = to_core(edge_w)
    enc_emb, proc_emb = call(
        embed_kernel,
        [shape(n_enc, d), shape(n_proc, d)],
        [enc_geom, enc_geo, proc_geom, proc_geo, lat],
        flops=2 * (n_enc + n_proc) * d * 128,
    )
    edge_round = to_group(edge_across)
    lat_both = to_core(lat_across)
    next_w, node_half, proc_half = call(
        second_pack_kernel,
        [shape(n_in + n_out + k_in + k_out, d), shape((n_in + n_out) // 2, d), shape((k_in + k_out) // 2, d)],
        [enc_node_in, enc_node_out, proc_edge_in, proc_edge_out, lat_across],
    )
    node_across, proc_across = to_chip(node_half), to_chip(proc_half)
    next_beside = to_core(next_w)

    halo_rows = padded(got)
    half = mesh_rows // 2
    keep, give, own_mesh = call(
        functools.partial(enc_kernel, plan, slots, grid_rows, mesh_rows, k_in),
        [shape(half, d)] * 3,
        [
            enc_emb, enc_edges, enc_edge_gain, lat, lat_across, lat_beside, lat_both,
            edge_w, edge_beside, edge_across, edge_round, to_core(edge_across), to_core(edge_round), enc_blocks,
        ],
        scratch=[
            pltpu.VMEM((grid_rows + mesh_rows + got, d), BF16),
            pltpu.VMEM((4 * (k_in + k_out), d), BF16),
            pltpu.VMEM((d + grid_rows + mesh_rows + halo_rows, d), BF16),
            pltpu.VMEM((n_enc, d), BF16),
            pltpu.VMEM((mesh_rows, d), F32),
        ],
        flops=2 * n_enc * d * (3 * d + grid_rows + mesh_rows + halo_rows),
        smem=1,
    )
    node_round, proc_round = to_group(node_across), to_group(proc_across)
    (chip_sum,) = call(add_kernel, [shape(half, d)], [keep, to_core(give)])
    mid_half, last_w = call(
        functools.partial(node_kernel, n_in, n_out),
        [shape(half, d), shape(n_in + n_out, d)],
        [
            own_mesh, chip_sum, to_chip(chip_sum), enc_node_gain, proc_node_in, proc_node_out,
            next_w, next_beside, node_across, node_round, to_core(node_across), to_core(node_round),
        ],
        scratch=[pltpu.VMEM((4 * (n_in + n_out), d), BF16)],
        flops=2 * half * d * 3 * d,
    )
    slots = mesh_send.shape[2]
    mid, *outgoing = call(
        functools.partial(middle_kernel, plan),
        [shape(mesh_rows, d)] + [shape(slots, d)] * len(plan),
        [mid_half, to_core(mid_half), mesh_send],
        flops=2 * len(plan) * slots * mesh_rows * d,
    )
    halos = [lax.ppermute(v, "dom", entry[0]) for v, entry in zip(outgoing, plan)]
    last_across, last_beside = to_chip(last_w), to_core(last_w)
    early = n_proc // 2
    table, pre, w_source, w_out = call(
        functools.partial(proc_first_kernel, k_in, n_in + n_out),
        [shape(d + 2 * mesh_rows, d), shape(early, d, F32), shape(d, d), shape(d, d)],
        [
            proc_emb, mid, proc_edges, next_w, next_beside, proc_across, proc_round,
            to_core(proc_across), to_core(proc_round),
        ],
        scratch=[pltpu.VMEM((4 * (k_in + k_out), d), BF16)],
        flops=2 * early * d * (d + 2 * mesh_rows),
    )
    halo_rows = padded(len(plan) * slots)
    keep, give = call(
        functools.partial(proc_second_kernel, plan, slots, mesh_rows, len(plan)),
        [shape(half, d), shape(half, d)],
        [proc_emb, proc_edges, proc_edge_gain, table, pre, w_source, w_out, *halos, proc_blocks],
        scratch=[
            pltpu.VMEM((halo_rows, d), BF16),
            pltpu.VMEM((n_proc, d), BF16),
            pltpu.VMEM((mesh_rows, d), F32),
        ],
        flops=2 * n_proc * d * (2 * d + mesh_rows + halo_rows),
        smem=1,
    )
    quarter = mesh_rows // 4
    mine, other = call(fold_kernel, [shape(quarter, d)] * 2, [keep, to_core(give)])
    (result,) = call(
        functools.partial(out_kernel, n_in, n_out),
        [shape(quarter, d)],
        [mid, mine, to_chip(other), proc_node_gain, last_w, last_beside, last_across, to_core(last_across)],
        scratch=[pltpu.VMEM((4 * (n_in + n_out), d), BF16)],
        flops=2 * quarter * d * 3 * d,
    )
    return result


def solution(mesh):
    placed = (
        P(("groups", "dom"), "sub"),
        P(("groups", "dom"), "sub"),
        P("dom", None, None),
        P("dom", None, None),
        P(None, ("dom", "sub")),
        P(None, ("dom", "sub")),
        P("dom"),
        P(None, ("dom", "sub")),
        P(None, ("dom", "sub")),
        P("dom"),
        P(),
        P(),
        P("sub", None),
        P("sub", None),
        P("sub", None),
        P("sub", None),
        P("sub", None),
        P("sub", None),
        P("sub", None),
        P("sub", None),
        P(),
        P(),
        P(),
        P(),
    )
    return jax.shard_map(
        local,
        mesh=mesh,
        in_specs=placed,
        out_specs=P(("groups", "dom", "sub"), None),
        check_vma=False,
    )
```

```python
import functools

import jax
import jax.numpy as jnp
from jax import lax
from jax.experimental import pallas as pl
from jax.experimental.pallas import tpu as pltpu
from jax.sharding import PartitionSpec as P

BLOCK = 128
OFFSETS = (-2, -1, 1, 2)
STEP = 512
GATHERED = 1024
VMEM_FULL = 64 * 1024 * 1024
VMEM_BYTES = 24 * 1024 * 1024
I16 = jnp.int16
BF16 = jnp.bfloat16
F32 = jnp.float32


def silu(v):
    h = 0.5 * v
    return h + h * jnp.tanh(h)


def region_of(delta):
    return jnp.where(delta < 0, delta + 2, delta + 1)


def halo_plan(count):
    plan = []
    if count == 4:
        for bit in (1, 2, 3):
            pairs = [(d, d ^ bit) for d in range(4) if abs((d ^ bit) - d) <= 2]
            regions = [(OFFSETS.index((d ^ bit) - d) if abs((d ^ bit) - d) <= 2 else -1) for d in range(4)]
            plan.append((pairs, regions, regions))
    else:
        for region, offset in enumerate(OFFSETS):
            pairs = [(d, d + offset) for d in range(count) if 0 <= d + offset < count]
            plan.append((pairs, region, 3 - region))
    return plan


def by_index(choice, index):
    if isinstance(choice, int):
        return choice
    picked = jnp.int32(choice[0])
    for place in range(1, len(choice)):
        picked = jnp.where(index == place, choice[place], picked)
    return picked


def whole_refs(count):
    return [pl.BlockSpec(memory_space=pltpu.VMEM)] * count


def call(body, outs, args, scratch=(), flops=0, smem=0, far=0, vmem=VMEM_BYTES):
    moved = sum(a.size * a.dtype.itemsize for a in args) + sum(
        o.size * jnp.dtype(o.dtype).itemsize for o in outs
    )
    specs = [pl.BlockSpec(memory_space=pltpu.HBM)] * far + whole_refs(len(args) - smem - far)
    specs += [pl.BlockSpec(memory_space=pltpu.SMEM)] * smem
    return pl.pallas_call(
        body,
        out_shape=tuple(outs),
        in_specs=specs,
        out_specs=tuple(whole_refs(len(outs))),
        scratch_shapes=list(scratch),
        compiler_params=pltpu.CompilerParams(vmem_limit_bytes=vmem),
        cost_estimate=pl.CostEstimate(flops=int(flops), bytes_accessed=int(moved), transcendentals=0),
    )(*args)


def dot(a, b):
    return jnp.dot(a, b, preferred_element_type=F32)


def dot_first(a, b):
    return lax.dot_general(a, b, (((0,), (0,)), ((), ())), preferred_element_type=F32)


def three_parts(v):
    a = v.astype(BF16)
    rest = v - a.astype(F32)
    b = rest.astype(BF16)
    c = (rest - b.astype(F32)).astype(BF16)
    return a, b, c


def embed_rows(geom, geo):
    a1, a2, a3 = three_parts(geom)
    b1, b2, b3 = three_parts(geo)
    left = jnp.concatenate([a1, a1, a2, a1, a2, a3], axis=0)
    right = jnp.concatenate([b1, b2, b1, b3, b2, b1], axis=0)
    return silu(dot_first(left, right)).astype(BF16)


def layer_norm(v):
    width = v.shape[-1]
    centered = v - jnp.sum(v, axis=-1, keepdims=True) * (1.0 / width)
    spread = jnp.sum(centered * centered, axis=-1, keepdims=True) * (1.0 / width)
    return centered * lax.rsqrt(spread + 1e-05)


def hot(cond):
    return jnp.where(cond, BF16(1), BF16(0))


def pick_rows(table, listed):
    rows = lax.broadcasted_iota(I16, (table.shape[0], 1), 0)
    return dot_first(hot(rows == listed.astype(I16)), table).astype(BF16)


def pick_lists(plan, table, send, outs):
    here = lax.axis_index("dom")
    for (pairs, sent, received), out in zip(plan, outs):
        region = jnp.maximum(by_index(sent, here), 0)
        out[...] = pick_rows(table, send[0, pl.ds(region, 1), :])


def stack_into(out, parts):
    first = 0
    for part in parts:
        out[first : first + part.shape[0], :] = part[...]
        first += part.shape[0]


def fetch(sems, moves):
    copies = [pltpu.make_async_copy(source, target, sems.at[k]) for k, (source, target) in enumerate(moves)]
    for copy in copies:
        copy.start()
    return copies


def own_half(ref):
    rows = ref.shape[0] // 2
    return ref.at[pl.ds(pl.multiple_of(lax.axis_index("groups") * rows, rows), rows), :]


def first_pack_kernel(plan, grid, send, w_in, w_out, half, *rest):
    outs = rest[: len(plan)]
    listed, table, sems = rest[len(plan) :]
    k, n = w_in.shape[0] // 2, w_out.shape[0] // 2
    copies = fetch(
        sems,
        [
            (send, listed),
            (grid, table),
            (own_half(w_in), half.at[pl.ds(0, k), :]),
            (own_half(w_out), half.at[pl.ds(k, n), :]),
        ],
    )
    copies[0].wait()
    copies[1].wait()
    pick_lists(plan, table[...], listed, outs)
    copies[2].wait()
    copies[3].wait()


def embed_kernel(e_in, e_out, p_in, p_out, egeom, egeo, pgeom, pgeo, after, weights, eout, pout):
    stack_into(weights, (e_in, e_out, p_in, p_out))
    for geom, geo, out in ((egeom, egeo, eout), (pgeom, pgeo, pout)):
        for begin in range(0, out.shape[0], STEP):
            out[begin : begin + STEP, :] = embed_rows(geom[:, begin : begin + STEP], geo[...])


def cross_kernel(rows_whole, k_in, weights, lat, crossing, lat_out):
    lat_out[...] = lat[...]
    crossing[:rows_whole, :] = weights[:rows_whole, :]
    first, place = rows_whole, rows_whole
    for rows in (k_in, weights.shape[0] - rows_whole - k_in):
        half = rows // 2
        begin = pl.multiple_of(first + lax.axis_index("groups") * half, 64)
        crossing[place : place + half, :] = weights[pl.ds(begin, half), :]
        first, place = first + rows, place + half


def split_kernel(source, after, *outs):
    first = 0
    for out in outs:
        out[...] = source[first : first + out.shape[0], :]
        first += out.shape[0]


def concat_kernel(*refs):
    stack_into(refs[-1], refs[:-1])


def put_shard(target, source, first, step, part=0, parts=1):
    rows = target.shape[0] // (4 * parts)
    place = (lax.bitwise_xor(lax.axis_index("sub"), step) * parts + part) * rows
    target[pl.ds(pl.multiple_of(place, rows), rows), :] = source[first : first + rows, :]


def put_half(target, k, source, first=0, step=0, other=0):
    rows = target.shape[0] // 4
    which = lax.bitwise_xor(lax.axis_index("groups"), other)
    begin = lax.bitwise_xor(lax.axis_index("sub"), step) * rows
    for base, count in ((0, k // 2), (k // 2, (rows - k) // 2)):
        place = pl.multiple_of(begin + 2 * base + which * count, 64)
        target[pl.ds(place, count), :] = source[first + base : first + base + count, :]


def joined(stack, first, rows):
    step = stack.shape[0] // 4
    return jnp.concatenate([stack[k * step + first : k * step + first + rows, :] for k in range(4)], axis=0)


def halo_targets(plan, slots, node_rows, width):
    here = lax.axis_index("dom")
    lane = lax.broadcasted_iota(jnp.int32, (1, width), 1)
    target = jnp.full((1, width), -1, jnp.int32)
    for place, (pairs, sent, received) in enumerate(plan):
        region = by_index(received, here)
        first = jnp.where(region < 0, -4 * node_rows, node_rows + region * slots)
        inside = (lane >= place * slots) & (lane < (place + 1) * slots)
        target = jnp.where(inside, lane - place * slots + first, target)
    return target.astype(I16)


def columns(edges, first):
    pair = edges[:, first : first + STEP]
    zero = jnp.zeros((8 - pair.shape[0], STEP), jnp.int32)
    upright = jnp.transpose(jnp.concatenate([pair, zero], axis=0).astype(F32)).astype(jnp.int32).astype(I16)
    return upright[:, 0:1], upright[:, 1:2]


def edge_blocks(edges, live_edges, first_stage, w_out, messages, totals):
    count = edges.shape[1]
    row = lax.broadcasted_iota(I16, (totals.shape[0], 1), 0)
    quarter = lax.axis_index("sub")
    for first in range(0, count, STEP):
        hidden = silu(first_stage(first)).astype(BF16)
        message = layer_norm(dot(hidden, w_out))
        place = lax.broadcasted_iota(jnp.int32, (STEP, 1), 0) + (first + quarter * count)
        messages[first : first + STEP, :] = jnp.where(place < live_edges, message, 0.0).astype(BF16)
        done = first + STEP
        if done % GATHERED == 0 or done == count:
            begin = (first // GATHERED) * GATHERED
            collect = hot(row == edges[1:2, begin:done].astype(I16))
            part = dot(collect, messages[begin:done, :])
            if begin == 0:
                totals[...] = part
            else:
                totals[...] += part


def hand_out(totals, gain, keep, give):
    rows = totals.shape[0] // 4
    core = lax.rem(lax.axis_index("sub"), 2)
    for half in range(2):
        for out, which in ((keep, core), (give, 1 - core)):
            place = pl.multiple_of((2 * half + which) * rows, rows)
            out[half * rows : (half + 1) * rows, :] = (totals[pl.ds(place, rows), :] * gain[...]).astype(BF16)


def enc_kernel(
    plan, slots, grid_rows, mesh_rows, k_in, emb, edges, gain, l0, l1, l2, l3, o_in, o_out, b_in, b_out,
    across, round_, both, round_both, live, keep, give, own_mesh, full, stack, table, messages, totals,
):
    d = gain.shape[1]
    quarter = lax.axis_index("sub")
    width = l0.shape[1]
    for shard, step in zip((l0, l1, l2, l3), (0, 2, 1, 3)):
        place = pl.multiple_of(lax.bitwise_xor(quarter, step) * width, width)
        full[:, pl.ds(place, width)] = shard[...]
    step = k_in + d // 4
    for first, second, bit in ((o_in, o_out, 0), (b_in, b_out, 1)):
        place = lax.bitwise_xor(quarter, bit) * step
        stack[pl.ds(pl.multiple_of(place, 128), k_in), :] = first[...]
        stack[pl.ds(pl.multiple_of(place + k_in, 128), d // 4), :] = second[...]
    put_half(stack, k_in, across, 0, 2, 0)
    put_half(stack, k_in, round_, 0, 2, 1)
    put_half(stack, k_in, both, 0, 3, 0)
    put_half(stack, k_in, round_both, 0, 3, 1)
    rows = mesh_rows // 4
    core = lax.rem(quarter, 2)
    for half in range(2):
        place = pl.multiple_of(grid_rows + (2 * half + core) * rows, rows)
        own_mesh[half * rows : (half + 1) * rows, :] = full[pl.ds(place, rows), :]

    w_in = joined(stack, 0, k_in)
    halo_first, got = grid_rows + mesh_rows, full.shape[0] - grid_rows - mesh_rows
    table[:d, :] = w_in[:d, :]
    table[d : d + grid_rows, :] = dot(full[:grid_rows, :], w_in[d : 2 * d, :]).astype(BF16)
    base = d + grid_rows + mesh_rows
    table[d + grid_rows : base, :] = dot(full[grid_rows:halo_first, :], w_in[2 * d :, :]).astype(BF16)
    table[base : base + got, :] = dot(full[halo_first:, :], w_in[d : 2 * d, :]).astype(BF16)
    if base + got < table.shape[0]:
        table[base + got :, :] = jnp.zeros((table.shape[0] - base - got, d), BF16)
    targets = halo_targets(plan, slots, grid_rows, table.shape[0] - base)
    own = lax.broadcasted_iota(I16, (1, grid_rows), 1)
    mesh = lax.broadcasted_iota(I16, (1, mesh_rows), 1)

    def first_stage(first):
        senders, receivers = columns(edges, first)
        chosen = [emb[first : first + STEP, :], hot(own == senders), hot(mesh == receivers), hot(targets == senders)]
        return dot(jnp.concatenate(chosen, axis=1), table[...])

    edge_blocks(edges, live[0] * BLOCK, first_stage, joined(stack, k_in, d // 4), messages, totals)
    hand_out(totals, gain, keep, give)


def node_update(mesh, shares, w_in, w_out, gain):
    stacked = jnp.concatenate([mesh, shares], axis=1)
    hidden = silu(dot(stacked, w_in)).astype(BF16)
    update = layer_norm(dot(hidden, w_out)) * gain
    return (mesh.astype(F32) + update).astype(BF16)


def add(mine, theirs):
    return (mine.astype(F32) + theirs.astype(F32)).astype(BF16)


def add_kernel(mine, theirs, out):
    out[...] = add(mine[...], theirs[...])


def node_kernel(k_in, k_out, mesh, mine, theirs, gain, n_in, n_out, w0, w1, w2, w3, w4, out, packed, stack):
    for shard, bit in zip((w0, w1, w2), (0, 1, 2)):
        put_shard(stack, shard, 0, bit)
    put_shard(stack, w3, 0, 3, 0, 2)
    put_shard(stack, w4, 0, 3, 1, 2)
    w_in, w_out = joined(stack, 0, k_in), joined(stack, k_in, k_out)
    out[...] = node_update(mesh[...], add(mine[...], theirs[...]), w_in, w_out, gain[...])
    stack_into(packed, (n_in, n_out))


def middle_kernel(plan, mine, theirs, send, full, *outs):
    rows = mine.shape[0] // 2
    core = lax.rem(lax.axis_index("sub"), 2)
    for half in range(2):
        for part, which in ((mine, core), (theirs, 1 - core)):
            place = pl.multiple_of((2 * half + which) * rows, rows)
            full[pl.ds(place, rows), :] = part[half * rows : (half + 1) * rows, :]
    pick_lists(plan, full[...], send, outs)


def proc_first_kernel(k_in, first_row, emb, full, edges, w0, w1, across, both, round_, round_both, table, pre, w_source, w_out, stack):
    d = full.shape[1]
    node_rows = full.shape[0]
    put_shard(stack, w0, first_row, 0)
    put_shard(stack, w1, first_row, 1)
    put_half(stack, k_in, across, 0, 2, 0)
    put_half(stack, k_in, both, 0, 3, 0)
    put_half(stack, k_in, round_, 0, 2, 1)
    put_half(stack, k_in, round_both, 0, 3, 1)
    w_in = joined(stack, 0, k_in)
    w_out[...] = joined(stack, k_in, d // 4)
    w_source[...] = w_in[d : 2 * d, :]
    table[:d, :] = w_in[:d, :]
    table[d : d + node_rows, :] = dot(full[...], w_in[d : 2 * d, :]).astype(BF16)
    table[d + node_rows :, :] = dot(full[...], w_in[2 * d :, :]).astype(BF16)
    lane = lax.broadcasted_iota(I16, (1, node_rows), 1)
    for first in range(0, pre.shape[0], STEP):
        pre[first : first + STEP, :] = dot(own_chosen(emb, edges, lane, first), table[...])


def own_chosen(emb, edges, lane, first):
    senders, receivers = columns(edges, first)
    return jnp.concatenate([emb[first : first + STEP, :], hot(lane == senders), hot(lane == receivers)], axis=1)


def proc_second_kernel(
    plan, slots, node_rows, n_halo, emb, edges, gain, table, pre, w_source, w_out, *rest
):
    halos = rest[:n_halo]
    live, keep, give, halo_table, messages, totals = rest[n_halo:]
    d = pre.shape[1]
    got = jnp.concatenate([h[...] for h in halos], axis=0)
    halo_table[: got.shape[0], :] = dot(got, w_source[...]).astype(BF16)
    if got.shape[0] < halo_table.shape[0]:
        halo_table[got.shape[0] :, :] = jnp.zeros((halo_table.shape[0] - got.shape[0], d), BF16)
    targets = halo_targets(plan, slots, node_rows, halo_table.shape[0])
    lane = lax.broadcasted_iota(I16, (1, node_rows), 1)

    def first_stage(first):
        senders, receivers = columns(edges, first)
        remote = dot(hot(targets == senders), halo_table[...])
        if first < pre.shape[0]:
            return pre[first : first + STEP, :] + remote
        return dot(own_chosen(emb, edges, lane, first), table[...]) + remote

    edge_blocks(edges, live[0] * BLOCK, first_stage, w_out[...], messages, totals)
    hand_out(totals, gain, keep, give)


def fold_kernel(mine, theirs, keep, give):
    rows = mine.shape[0] // 2
    chip = lax.div(lax.axis_index("sub"), 2)
    for out, which in ((keep, chip), (give, 1 - chip)):
        place = pl.multiple_of(which * rows, rows)
        out[...] = add(mine[pl.ds(place, rows), :], theirs[pl.ds(place, rows), :])


def out_kernel(k_in, k_out, full, mine, theirs, gain, w0, w1, w2, w3, out, stack):
    rows = mine.shape[0]
    mesh = full[pl.ds(pl.multiple_of(lax.axis_index("sub") * rows, rows), rows), :]
    for shard, bit in zip((w0, w1, w2, w3), (0, 1, 2, 3)):
        put_shard(stack, shard, 0, bit)
    w_in, w_out = joined(stack, 0, k_in), joined(stack, k_in, k_out)
    out[...] = node_update(mesh, add(mine[...], theirs[...]), w_in, w_out, gain[...])


def to_chip(v):
    return lax.ppermute(v, "sub", [(i, i ^ 2) for i in range(4)])


def to_core(v):
    return lax.ppermute(v, "sub", [(i, i ^ 1) for i in range(4)])


def to_group(v):
    count = lax.axis_size("groups")
    return lax.ppermute(v, "groups", [(i, count - 1 - i) for i in range(count)])


def shape(rows, width, dtype=BF16):
    return jax.ShapeDtypeStruct((rows, width), dtype)


def padded(rows):
    return -(-rows // 128) * 128


def local(
    grid_lat,
    mesh_lat,
    grid_send,
    mesh_send,
    enc_edges,
    enc_geom,
    enc_blocks,
    proc_edges,
    proc_geom,
    proc_blocks,
    enc_geo,
    proc_geo,
    enc_edge_in,
    enc_edge_out,
    enc_node_in,
    enc_node_out,
    proc_edge_in,
    proc_edge_out,
    proc_node_in,
    proc_node_out,
    enc_edge_gain,
    enc_node_gain,
    proc_edge_gain,
    proc_node_gain,
):
    plan = halo_plan(lax.axis_size("dom"))
    d = enc_geo.shape[1]
    grid_rows, mesh_rows = grid_lat.shape[0], mesh_lat.shape[0]
    n_enc, n_proc = enc_edges.shape[1], proc_edges.shape[1]
    enc_edge_gain, enc_node_gain, proc_edge_gain, proc_node_gain = (
        g.reshape(1, d) for g in (enc_edge_gain, enc_node_gain, proc_edge_gain, proc_node_gain)
    )
    k_in, k_out = enc_edge_in.shape[0], enc_edge_out.shape[0]
    n_in, n_out = enc_node_in.shape[0], enc_node_out.shape[0]
    width = grid_lat.shape[1]

    slots = grid_send.shape[2]
    edge_half, *outgoing = call(
        functools.partial(first_pack_kernel, plan),
        [shape((k_in + k_out) // 2, d)] + [shape(slots, width)] * len(plan),
        [grid_lat, grid_send, enc_edge_in, enc_edge_out],
        scratch=[
            pltpu.VMEM(grid_send.shape, jnp.int32),
            pltpu.VMEM(grid_lat.shape, BF16),
            pltpu.SemaphoreType.DMA((4,)),
        ],
        far=4,
        vmem=VMEM_FULL - 512 * 1024,
    )
    edge_across = to_chip(edge_half)
    halos = [lax.ppermute(v, "dom", entry[0]) for v, entry in zip(outgoing, plan)]
    got = len(plan) * slots
    (lat,) = call(
        concat_kernel,
        [shape(grid_rows + mesh_rows + got, width)],
        [grid_lat, mesh_lat, *halos],
    )
    lat_across = to_chip(lat)
    lat_beside = to_core(lat)
    edge_beside = [to_core(enc_edge_in), to_core(enc_edge_out)]
    edge_round = to_group(edge_across)
    next_w, enc_emb, proc_emb = call(
        embed_kernel,
        [shape(n_in + n_out + k_in + k_out, d), shape(n_enc, d), shape(n_proc, d)],
        [
            enc_node_in, enc_node_out, proc_edge_in, proc_edge_out,
            enc_geom, enc_geo, proc_geom, proc_geo, lat,
        ],
        flops=2 * (n_enc + n_proc) * d * 128,
    )
    crossing, lat_sent = call(
        functools.partial(cross_kernel, n_in + n_out, k_in),
        [shape(n_in + n_out + (k_in + k_out) // 2, d), shape(lat.shape[0], width)],
        [next_w, lat_across],
    )
    lat_both = to_core(lat_sent)
    next_across = to_chip(crossing)
    next_beside = to_core(next_w)

    halo_rows = padded(got)
    half = mesh_rows // 2
    keep, give, own_mesh = call(
        functools.partial(enc_kernel, plan, slots, grid_rows, mesh_rows, k_in),
        [shape(half, d)] * 3,
        [
            enc_emb, enc_edges, enc_edge_gain, lat, lat_across, lat_beside, lat_both,
            enc_edge_in, enc_edge_out, *edge_beside,
            edge_across, edge_round, to_core(edge_across), to_core(edge_round), enc_blocks,
        ],
        scratch=[
            pltpu.VMEM((grid_rows + mesh_rows + got, d), BF16),
            pltpu.VMEM((4 * (k_in + k_out), d), BF16),
            pltpu.VMEM((d + grid_rows + mesh_rows + halo_rows, d), BF16),
            pltpu.VMEM((n_enc, d), BF16),
            pltpu.VMEM((mesh_rows, d), F32),
        ],
        flops=2 * n_enc * d * (3 * d + grid_rows + mesh_rows + halo_rows),
        smem=1,
    )
    (chip_sum,) = call(add_kernel, [shape(half, d)], [keep, to_core(give)])
    *node_across, proc_across = call(
        split_kernel,
        [shape((n_in + n_out) // 2, d)] * 2 + [shape((k_in + k_out) // 2, d)],
        [next_across, chip_sum],
    )
    node_both = [to_core(v) for v in node_across]
    proc_round = to_group(proc_across)
    mid_half, last_w = call(
        functools.partial(node_kernel, n_in, n_out),
        [shape(half, d), shape(n_in + n_out, d)],
        [
            own_mesh, chip_sum, to_chip(chip_sum), enc_node_gain, proc_node_in, proc_node_out,
            next_w, next_beside, next_across, *node_both,
        ],
        scratch=[pltpu.VMEM((4 * (n_in + n_out), d), BF16)],
        flops=2 * half * d * 3 * d,
    )
    slots = mesh_send.shape[2]
    mid, *outgoing = call(
        functools.partial(middle_kernel, plan),
        [shape(mesh_rows, d)] + [shape(slots, d)] * len(plan),
        [mid_half, to_core(mid_half), mesh_send],
        flops=2 * len(plan) * slots * mesh_rows * d,
    )
    halos = [lax.ppermute(v, "dom", entry[0]) for v, entry in zip(outgoing, plan)]
    last_across, last_beside = to_chip(last_w), to_core(last_w)
    early = n_proc // 2
    table, pre, w_source, w_out = call(
        functools.partial(proc_first_kernel, k_in, n_in + n_out),
        [shape(d + 2 * mesh_rows, d), shape(early, d, F32), shape(d, d), shape(d, d)],
        [
            proc_emb, mid, proc_edges, next_w, next_beside, proc_across, to_core(proc_across),
            proc_round, to_core(proc_round),
        ],
        scratch=[pltpu.VMEM((4 * (k_in + k_out), d), BF16)],
        flops=2 * early * d * (d + 2 * mesh_rows),
    )
    halo_rows = padded(len(plan) * slots)
    keep, give = call(
        functools.partial(proc_second_kernel, plan, slots, mesh_rows, len(plan)),
        [shape(half, d), shape(half, d)],
        [proc_emb, proc_edges, proc_edge_gain, table, pre, w_source, w_out, *halos, proc_blocks],
        scratch=[
            pltpu.VMEM((halo_rows, d), BF16),
            pltpu.VMEM((n_proc, d), BF16),
            pltpu.VMEM((mesh_rows, d), F32),
        ],
        flops=2 * n_proc * d * (2 * d + mesh_rows + halo_rows),
        smem=1,
    )
    quarter = mesh_rows // 4
    mine, other = call(fold_kernel, [shape(quarter, d)] * 2, [keep, to_core(give)])
    (result,) = call(
        functools.partial(out_kernel, n_in, n_out),
        [shape(quarter, d)],
        [mid, mine, to_chip(other), proc_node_gain, last_w, last_beside, last_across, to_core(last_across)],
        scratch=[pltpu.VMEM((4 * (n_in + n_out), d), BF16)],
        flops=2 * quarter * d * 3 * d,
    )
    return result


def solution(mesh):
    placed = (
        P(("groups", "dom"), "sub"),
        P(("groups", "dom"), "sub"),
        P("dom", None, None),
        P("dom", None, None),
        P(None, ("dom", "sub")),
        P(None, ("dom", "sub")),
        P("dom"),
        P(None, ("dom", "sub")),
        P(None, ("dom", "sub")),
        P("dom"),
        P(),
        P(),
        P("sub", None),
        P("sub", None),
        P("sub", None),
        P("sub", None),
        P("sub", None),
        P("sub", None),
        P("sub", None),
        P("sub", None),
        P(),
        P(),
        P(),
        P(),
    )
    return jax.shard_map(
        local,
        mesh=mesh,
        in_specs=placed,
        out_specs=P(("groups", "dom", "sub"), None),
        check_vma=False,
    )
```

```python
import functools

import jax
import jax.numpy as jnp
from jax import lax
from jax.experimental import pallas as pl
from jax.experimental.pallas import tpu as pltpu
from jax.sharding import PartitionSpec as P

BLOCK = 128
OFFSETS = (-2, -1, 1, 2)
STEP = 512
GATHERED = 1024
LONG = 30 * 10**9
VMEM_BYTES = 24 * 1024 * 1024
I16 = jnp.int16
BF16 = jnp.bfloat16
F32 = jnp.float32


def silu(v):
    h = 0.5 * v
    return h + h * jnp.tanh(h)


def halo_plan(count):
    if count <= 5:
        return [("all", place) for place in range(count)]
    return [("region", region) for region in range(4)]


def sent_region(entry, here):
    kind, place = entry
    if kind == "region":
        return place, True
    delta = place - here
    region = jnp.where(delta < 0, delta + 2, delta + 1)
    return jnp.clip(region, 0, 3), (delta != 0) & (delta >= -2) & (delta <= 2)


def received_region(entry, here):
    kind, place = entry
    if kind == "region":
        return 3 - place, True
    return sent_region(entry, here)


def exchange(plan, lists):
    if plan[0][0] == "all":
        return lax.all_to_all(lists, "dom", split_axis=0, concat_axis=0, tiled=True)
    count = lax.axis_size("dom")
    rows = lists.shape[0] // len(plan)
    blocks = []
    for place, (kind, region) in enumerate(plan):
        step = OFFSETS[region]
        pairs = [(d, d + step) for d in range(count) if 0 <= d + step < count]
        blocks.append(lax.ppermute(lists[place * rows : (place + 1) * rows], "dom", pairs))
    return jnp.concatenate(blocks, axis=0)


def whole_refs(count):
    return [pl.BlockSpec(memory_space=pltpu.VMEM)] * count


def call(body, outs, args, scratch=(), flops=0, smem=0):
    moved = sum(a.size * a.dtype.itemsize for a in args) + sum(
        o.size * jnp.dtype(o.dtype).itemsize for o in outs
    )
    specs = whole_refs(len(args) - smem) + [pl.BlockSpec(memory_space=pltpu.SMEM)] * smem
    return pl.pallas_call(
        body,
        out_shape=tuple(outs),
        in_specs=specs,
        out_specs=tuple(whole_refs(len(outs))),
        scratch_shapes=list(scratch),
        compiler_params=pltpu.CompilerParams(vmem_limit_bytes=VMEM_BYTES),
        cost_estimate=pl.CostEstimate(flops=int(flops), bytes_accessed=int(moved), transcendentals=0),
    )(*args)


def dot(a, b):
    return jnp.dot(a, b, preferred_element_type=F32)


def dot_first(a, b):
    return lax.dot_general(a, b, (((0,), (0,)), ((), ())), preferred_element_type=F32)


def three_parts(v):
    a = v.astype(BF16)
    rest = v - a.astype(F32)
    b = rest.astype(BF16)
    c = (rest - b.astype(F32)).astype(BF16)
    return a, b, c


def embed_rows(geom, geo):
    a1, a2, a3 = three_parts(geom)
    b1, b2, b3 = three_parts(geo)
    left = jnp.concatenate([a1, a1, a2, a1, a2, a3], axis=0)
    right = jnp.concatenate([b1, b2, b1, b3, b2, b1], axis=0)
    return silu(dot_first(left, right)).astype(BF16)


def layer_norm(v):
    width = v.shape[-1]
    centered = v - jnp.sum(v, axis=-1, keepdims=True) * (1.0 / width)
    spread = jnp.sum(centered * centered, axis=-1, keepdims=True) * (1.0 / width)
    return centered * lax.rsqrt(spread + 1e-05)


def hot(cond):
    return jnp.where(cond, BF16(1), BF16(0))


def pick_rows(table, listed):
    rows = lax.broadcasted_iota(I16, (table.shape[0], 1), 0)
    return dot_first(hot(rows == listed.astype(I16)), table).astype(BF16)


def pick_lists(plan, table, send, out):
    here = lax.axis_index("dom")
    rows = out.shape[0] // len(plan)
    for place, entry in enumerate(plan):
        region, there = sent_region(entry, here)
        listed = jnp.where(there, send[0, pl.ds(region, 1), :], -1)
        out[place * rows : (place + 1) * rows, :] = pick_rows(table, listed)


def stack_into(out, parts):
    first = 0
    for part in parts:
        out[first : first + part.shape[0], :] = part[...]
        first += part.shape[0]


def begin_kernel(token):
    token[...] = jnp.zeros(token.shape, token.dtype)


def first_pack_kernel(plan, grid, send, w_in, w_out, token, half, out):
    place = 0
    for source in (w_in, w_out):
        rows = source.shape[0] // 2
        begin = pl.multiple_of(lax.axis_index("groups") * rows, 64)
        half[place : place + rows, :] = source[pl.ds(begin, rows), :]
        place += rows
    pick_lists(plan, grid[...], send, out)


def embed_kernel(e_in, e_out, p_in, p_out, egeom, egeo, pgeom, pgeo, after, weights, eout, pout):
    stack_into(weights, (e_in, e_out, p_in, p_out))
    for geom, geo, out in ((egeom, egeo, eout), (pgeom, pgeo, pout)):
        for begin in range(0, out.shape[0], STEP):
            out[begin : begin + STEP, :] = embed_rows(geom[:, begin : begin + STEP], geo[...])


def cross_kernel(rows_whole, k_in, weights, lat, crossing, lat_out):
    lat_out[...] = lat[...]
    crossing[:rows_whole, :] = weights[:rows_whole, :]
    first, place = rows_whole, rows_whole
    for rows in (k_in, weights.shape[0] - rows_whole - k_in):
        half = rows // 2
        begin = pl.multiple_of(first + lax.axis_index("groups") * half, 64)
        crossing[place : place + half, :] = weights[pl.ds(begin, half), :]
        first, place = first + rows, place + half


def split_kernel(source, after, *outs):
    first = 0
    for out in outs:
        out[...] = source[first : first + out.shape[0], :]
        first += out.shape[0]


def concat_kernel(*refs):
    stack_into(refs[-1], refs[:-1])


def put_shard(target, source, first, step, part=0, parts=1):
    rows = target.shape[0] // (4 * parts)
    place = (lax.bitwise_xor(lax.axis_index("sub"), step) * parts + part) * rows
    target[pl.ds(pl.multiple_of(place, rows), rows), :] = source[first : first + rows, :]


def put_half(target, k, source, first=0, step=0, other=0):
    rows = target.shape[0] // 4
    which = lax.bitwise_xor(lax.axis_index("groups"), other)
    begin = lax.bitwise_xor(lax.axis_index("sub"), step) * rows
    for base, count in ((0, k // 2), (k // 2, (rows - k) // 2)):
        place = pl.multiple_of(begin + 2 * base + which * count, 64)
        target[pl.ds(place, count), :] = source[first + base : first + base + count, :]


def joined(stack, first, rows):
    step = stack.shape[0] // 4
    return jnp.concatenate([stack[k * step + first : k * step + first + rows, :] for k in range(4)], axis=0)


def halo_targets(plan, slots, node_rows, width):
    here = lax.axis_index("dom")
    lane = lax.broadcasted_iota(jnp.int32, (1, width), 1)
    target = jnp.full((1, width), -1, jnp.int32)
    for place, entry in enumerate(plan):
        region, there = received_region(entry, here)
        first = jnp.where(there, node_rows + region * slots, -4 * node_rows)
        inside = (lane >= place * slots) & (lane < (place + 1) * slots)
        target = jnp.where(inside, lane - place * slots + first, target)
    return target.astype(I16)


def columns(edges, first):
    pair = edges[:, first : first + STEP]
    zero = jnp.zeros((8 - pair.shape[0], STEP), jnp.int32)
    upright = jnp.transpose(jnp.concatenate([pair, zero], axis=0).astype(F32)).astype(jnp.int32).astype(I16)
    return upright[:, 0:1], upright[:, 1:2]


def edge_blocks(edges, live_edges, first_stage, w_out, messages, totals):
    count = edges.shape[1]
    row = lax.broadcasted_iota(I16, (totals.shape[0], 1), 0)
    quarter = lax.axis_index("sub")
    for first in range(0, count, STEP):
        hidden = silu(first_stage(first)).astype(BF16)
        message = layer_norm(dot(hidden, w_out))
        place = lax.broadcasted_iota(jnp.int32, (STEP, 1), 0) + (first + quarter * count)
        messages[first : first + STEP, :] = jnp.where(place < live_edges, message, 0.0).astype(BF16)
        done = first + STEP
        if done % GATHERED == 0 or done == count:
            begin = (first // GATHERED) * GATHERED
            collect = hot(row == edges[1:2, begin:done].astype(I16))
            part = dot(collect, messages[begin:done, :])
            if begin == 0:
                totals[...] = part
            else:
                totals[...] += part


def hand_out(totals, gain, keep, give):
    rows = totals.shape[0] // 4
    core = lax.rem(lax.axis_index("sub"), 2)
    for half in range(2):
        for out, which in ((keep, core), (give, 1 - core)):
            place = pl.multiple_of((2 * half + which) * rows, rows)
            out[half * rows : (half + 1) * rows, :] = (totals[pl.ds(place, rows), :] * gain[...]).astype(BF16)


def enc_kernel(
    plan, slots, grid_rows, mesh_rows, k_in, emb, edges, gain, l0, l1, l2, l3, o_in, o_out, b_in, b_out,
    across, round_, both, round_both, live, keep, give, own_mesh, full, stack, table, messages, totals,
):
    d = gain.shape[1]
    quarter = lax.axis_index("sub")
    width = l0.shape[1]
    for shard, step in zip((l0, l1, l2, l3), (0, 2, 1, 3)):
        place = pl.multiple_of(lax.bitwise_xor(quarter, step) * width, width)
        full[:, pl.ds(place, width)] = shard[...]
    step = k_in + d // 4
    for first, second, bit in ((o_in, o_out, 0), (b_in, b_out, 1)):
        place = lax.bitwise_xor(quarter, bit) * step
        stack[pl.ds(pl.multiple_of(place, 128), k_in), :] = first[...]
        stack[pl.ds(pl.multiple_of(place + k_in, 128), d // 4), :] = second[...]
    put_half(stack, k_in, across, 0, 2, 0)
    put_half(stack, k_in, round_, 0, 2, 1)
    put_half(stack, k_in, both, 0, 3, 0)
    put_half(stack, k_in, round_both, 0, 3, 1)
    rows = mesh_rows // 4
    core = lax.rem(quarter, 2)
    for half in range(2):
        place = pl.multiple_of(grid_rows + (2 * half + core) * rows, rows)
        own_mesh[half * rows : (half + 1) * rows, :] = full[pl.ds(place, rows), :]

    w_in = joined(stack, 0, k_in)
    halo_first, got = grid_rows + mesh_rows, full.shape[0] - grid_rows - mesh_rows
    table[:d, :] = w_in[:d, :]
    table[d : d + grid_rows, :] = dot(full[:grid_rows, :], w_in[d : 2 * d, :]).astype(BF16)
    base = d + grid_rows + mesh_rows
    table[d + grid_rows : base, :] = dot(full[grid_rows:halo_first, :], w_in[2 * d :, :]).astype(BF16)
    table[base : base + got, :] = dot(full[halo_first:, :], w_in[d : 2 * d, :]).astype(BF16)
    if base + got < table.shape[0]:
        table[base + got :, :] = jnp.zeros((table.shape[0] - base - got, d), BF16)
    targets = halo_targets(plan, slots, grid_rows, table.shape[0] - base)
    own = lax.broadcasted_iota(I16, (1, grid_rows), 1)
    mesh = lax.broadcasted_iota(I16, (1, mesh_rows), 1)

    def first_stage(first):
        senders, receivers = columns(edges, first)
        chosen = [emb[first : first + STEP, :], hot(own == senders), hot(mesh == receivers), hot(targets == senders)]
        return dot(jnp.concatenate(chosen, axis=1), table[...])

    edge_blocks(edges, live[0] * BLOCK, first_stage, joined(stack, k_in, d // 4), messages, totals)
    hand_out(totals, gain, keep, give)


def node_update(mesh, shares, w_in, w_out, gain):
    stacked = jnp.concatenate([mesh, shares], axis=1)
    hidden = silu(dot(stacked, w_in)).astype(BF16)
    update = layer_norm(dot(hidden, w_out)) * gain
    return (mesh.astype(F32) + update).astype(BF16)


def add(mine, theirs):
    return (mine.astype(F32) + theirs.astype(F32)).astype(BF16)


def add_kernel(mine, theirs, out):
    out[...] = add(mine[...], theirs[...])


def node_kernel(k_in, k_out, mesh, mine, theirs, gain, n_in, n_out, w0, w1, w2, w3, w4, out, packed, stack):
    for shard, bit in zip((w0, w1, w2), (0, 1, 2)):
        put_shard(stack, shard, 0, bit)
    put_shard(stack, w3, 0, 3, 0, 2)
    put_shard(stack, w4, 0, 3, 1, 2)
    w_in, w_out = joined(stack, 0, k_in), joined(stack, k_in, k_out)
    out[...] = node_update(mesh[...], add(mine[...], theirs[...]), w_in, w_out, gain[...])
    stack_into(packed, (n_in, n_out))


def middle_kernel(plan, mine, theirs, send, full, out):
    rows = mine.shape[0] // 2
    core = lax.rem(lax.axis_index("sub"), 2)
    for half in range(2):
        for part, which in ((mine, core), (theirs, 1 - core)):
            place = pl.multiple_of((2 * half + which) * rows, rows)
            full[pl.ds(place, rows), :] = part[half * rows : (half + 1) * rows, :]
    pick_lists(plan, full[...], send, out)


def proc_first_kernel(k_in, first_row, emb, full, edges, w0, w1, across, both, round_, round_both, table, pre, w_source, w_out, stack):
    d = full.shape[1]
    node_rows = full.shape[0]
    put_shard(stack, w0, first_row, 0)
    put_shard(stack, w1, first_row, 1)
    put_half(stack, k_in, across, 0, 2, 0)
    put_half(stack, k_in, both, 0, 3, 0)
    put_half(stack, k_in, round_, 0, 2, 1)
    put_half(stack, k_in, round_both, 0, 3, 1)
    w_in = joined(stack, 0, k_in)
    w_out[...] = joined(stack, k_in, d // 4)
    w_source[...] = w_in[d : 2 * d, :]
    table[:d, :] = w_in[:d, :]
    table[d : d + node_rows, :] = dot(full[...], w_in[d : 2 * d, :]).astype(BF16)
    table[d + node_rows :, :] = dot(full[...], w_in[2 * d :, :]).astype(BF16)
    lane = lax.broadcasted_iota(I16, (1, node_rows), 1)
    for first in range(0, pre.shape[0], STEP):
        pre[first : first + STEP, :] = dot(own_chosen(emb, edges, lane, first), table[...])


def own_chosen(emb, edges, lane, first):
    senders, receivers = columns(edges, first)
    return jnp.concatenate([emb[first : first + STEP, :], hot(lane == senders), hot(lane == receivers)], axis=1)


def proc_second_kernel(
    plan, slots, node_rows, emb, edges, gain, table, pre, w_source, w_out, halos,
    live, keep, give, halo_table, messages, totals,
):
    d = pre.shape[1]
    got = halos[...]
    halo_table[: got.shape[0], :] = dot(got, w_source[...]).astype(BF16)
    if got.shape[0] < halo_table.shape[0]:
        halo_table[got.shape[0] :, :] = jnp.zeros((halo_table.shape[0] - got.shape[0], d), BF16)
    targets = halo_targets(plan, slots, node_rows, halo_table.shape[0])
    lane = lax.broadcasted_iota(I16, (1, node_rows), 1)

    def first_stage(first):
        senders, receivers = columns(edges, first)
        remote = dot(hot(targets == senders), halo_table[...])
        if first < pre.shape[0]:
            return pre[first : first + STEP, :] + remote
        return dot(own_chosen(emb, edges, lane, first), table[...]) + remote

    edge_blocks(edges, live[0] * BLOCK, first_stage, w_out[...], messages, totals)
    hand_out(totals, gain, keep, give)


def fold_kernel(mine, theirs, keep, give):
    rows = mine.shape[0] // 2
    chip = lax.div(lax.axis_index("sub"), 2)
    for out, which in ((keep, chip), (give, 1 - chip)):
        place = pl.multiple_of(which * rows, rows)
        out[...] = add(mine[pl.ds(place, rows), :], theirs[pl.ds(place, rows), :])


def out_kernel(k_in, k_out, full, mine, theirs, gain, w0, w1, w2, w3, out, stack):
    rows = mine.shape[0]
    mesh = full[pl.ds(pl.multiple_of(lax.axis_index("sub") * rows, rows), rows), :]
    for shard, bit in zip((w0, w1, w2, w3), (0, 1, 2, 3)):
        put_shard(stack, shard, 0, bit)
    w_in, w_out = joined(stack, 0, k_in), joined(stack, k_in, k_out)
    out[...] = node_update(mesh, add(mine[...], theirs[...]), w_in, w_out, gain[...])


def to_chip(v):
    return lax.ppermute(v, "sub", [(i, i ^ 2) for i in range(4)])


def to_core(v):
    return lax.ppermute(v, "sub", [(i, i ^ 1) for i in range(4)])


def to_group(v):
    count = lax.axis_size("groups")
    return lax.ppermute(v, "groups", [(i, count - 1 - i) for i in range(count)])


def shape(rows, width, dtype=BF16):
    return jax.ShapeDtypeStruct((rows, width), dtype)


def padded(rows):
    return -(-rows // 128) * 128


def local(
    grid_lat,
    mesh_lat,
    grid_send,
    mesh_send,
    enc_edges,
    enc_geom,
    enc_blocks,
    proc_edges,
    proc_geom,
    proc_blocks,
    enc_geo,
    proc_geo,
    enc_edge_in,
    enc_edge_out,
    enc_node_in,
    enc_node_out,
    proc_edge_in,
    proc_edge_out,
    proc_node_in,
    proc_node_out,
    enc_edge_gain,
    enc_node_gain,
    proc_edge_gain,
    proc_node_gain,
):
    plan = halo_plan(lax.axis_size("dom"))
    d = enc_geo.shape[1]
    grid_rows, mesh_rows = grid_lat.shape[0], mesh_lat.shape[0]
    n_enc, n_proc = enc_edges.shape[1], proc_edges.shape[1]
    enc_edge_gain, enc_node_gain, proc_edge_gain, proc_node_gain = (
        g.reshape(1, d) for g in (enc_edge_gain, enc_node_gain, proc_edge_gain, proc_node_gain)
    )
    k_in, k_out = enc_edge_in.shape[0], enc_edge_out.shape[0]
    n_in, n_out = enc_node_in.shape[0], enc_node_out.shape[0]
    width = grid_lat.shape[1]

    slots = grid_send.shape[2]
    (token,) = call(begin_kernel, [shape(16, 128)], [], flops=LONG)
    edge_half, outgoing = call(
        functools.partial(first_pack_kernel, plan),
        [shape((k_in + k_out) // 2, d), shape(len(plan) * slots, width)],
        [grid_lat, grid_send, enc_edge_in, enc_edge_out, token],
    )
    edge_across = to_chip(edge_half)
    halos = exchange(plan, outgoing)
    got = len(plan) * slots
    (lat,) = call(
        concat_kernel,
        [shape(grid_rows + mesh_rows + got, width)],
        [grid_lat, mesh_lat, halos],
    )
    lat_across = to_chip(lat)
    lat_beside = to_core(lat)
    edge_beside = [to_core(enc_edge_in), to_core(enc_edge_out)]
    edge_round = to_group(edge_across)
    next_w, enc_emb, proc_emb = call(
        embed_kernel,
        [shape(n_in + n_out + k_in + k_out, d), shape(n_enc, d), shape(n_proc, d)],
        [
            enc_node_in, enc_node_out, proc_edge_in, proc_edge_out,
            enc_geom, enc_geo, proc_geom, proc_geo, lat,
        ],
        flops=2 * (n_enc + n_proc) * d * 128,
    )
    crossing, lat_sent = call(
        functools.partial(cross_kernel, n_in + n_out, k_in),
        [shape(n_in + n_out + (k_in + k_out) // 2, d), shape(lat.shape[0], width)],
        [next_w, lat_across],
    )
    lat_both = to_core(lat_sent)
    next_across = to_chip(crossing)
    next_beside = to_core(next_w)

    halo_rows = padded(got)
    half = mesh_rows // 2
    keep, give, own_mesh = call(
        functools.partial(enc_kernel, plan, slots, grid_rows, mesh_rows, k_in),
        [shape(half, d)] * 3,
        [
            enc_emb, enc_edges, enc_edge_gain, lat, lat_across, lat_beside, lat_both,
            enc_edge_in, enc_edge_out, *edge_beside,
            edge_across, edge_round, to_core(edge_across), to_core(edge_round), enc_blocks,
        ],
        scratch=[
            pltpu.VMEM((grid_rows + mesh_rows + got, d), BF16),
            pltpu.VMEM((4 * (k_in + k_out), d), BF16),
            pltpu.VMEM((d + grid_rows + mesh_rows + halo_rows, d), BF16),
            pltpu.VMEM((n_enc, d), BF16),
            pltpu.VMEM((mesh_rows, d), F32),
        ],
        flops=2 * n_enc * d * (3 * d + grid_rows + mesh_rows + halo_rows),
        smem=1,
    )
    (chip_sum,) = call(add_kernel, [shape(half, d)], [keep, to_core(give)])
    *node_across, proc_across = call(
        split_kernel,
        [shape((n_in + n_out) // 2, d)] * 2 + [shape((k_in + k_out) // 2, d)],
        [next_across, chip_sum],
    )
    node_both = [to_core(v) for v in node_across]
    proc_round = to_group(proc_across)
    mid_half, last_w = call(
        functools.partial(node_kernel, n_in, n_out),
        [shape(half, d), shape(n_in + n_out, d)],
        [
            own_mesh, chip_sum, to_chip(chip_sum), enc_node_gain, proc_node_in, proc_node_out,
            next_w, next_beside, next_across, *node_both,
        ],
        scratch=[pltpu.VMEM((4 * (n_in + n_out), d), BF16)],
        flops=2 * half * d * 3 * d,
    )
    slots = mesh_send.shape[2]
    mid, outgoing = call(
        functools.partial(middle_kernel, plan),
        [shape(mesh_rows, d), shape(len(plan) * slots, d)],
        [mid_half, to_core(mid_half), mesh_send],
        flops=2 * len(plan) * slots * mesh_rows * d,
    )
    halos = exchange(plan, outgoing)
    last_across, last_beside = to_chip(last_w), to_core(last_w)
    early = n_proc // 2
    table, pre, w_source, w_out = call(
        functools.partial(proc_first_kernel, k_in, n_in + n_out),
        [shape(d + 2 * mesh_rows, d), shape(early, d, F32), shape(d, d), shape(d, d)],
        [
            proc_emb, mid, proc_edges, next_w, next_beside, proc_across, to_core(proc_across),
            proc_round, to_core(proc_round),
        ],
        scratch=[pltpu.VMEM((4 * (k_in + k_out), d), BF16)],
        flops=2 * early * d * (d + 2 * mesh_rows),
    )
    halo_rows = padded(len(plan) * slots)
    keep, give = call(
        functools.partial(proc_second_kernel, plan, slots, mesh_rows),
        [shape(half, d), shape(half, d)],
        [proc_emb, proc_edges, proc_edge_gain, table, pre, w_source, w_out, halos, proc_blocks],
        scratch=[
            pltpu.VMEM((halo_rows, d), BF16),
            pltpu.VMEM((n_proc, d), BF16),
            pltpu.VMEM((mesh_rows, d), F32),
        ],
        flops=2 * n_proc * d * (2 * d + mesh_rows + halo_rows),
        smem=1,
    )
    quarter = mesh_rows // 4
    mine, other = call(fold_kernel, [shape(quarter, d)] * 2, [keep, to_core(give)])
    (result,) = call(
        functools.partial(out_kernel, n_in, n_out),
        [shape(quarter, d)],
        [mid, mine, to_chip(other), proc_node_gain, last_w, last_beside, last_across, to_core(last_across)],
        scratch=[pltpu.VMEM((4 * (n_in + n_out), d), BF16)],
        flops=2 * quarter * d * 3 * d,
    )
    return result


def solution(mesh):
    placed = (
        P(("groups", "dom"), "sub"),
        P(("groups", "dom"), "sub"),
        P("dom", None, None),
        P("dom", None, None),
        P(None, ("dom", "sub")),
        P(None, ("dom", "sub")),
        P("dom"),
        P(None, ("dom", "sub")),
        P(None, ("dom", "sub")),
        P("dom"),
        P(),
        P(),
        P("sub", None),
        P("sub", None),
        P("sub", None),
        P("sub", None),
        P("sub", None),
        P("sub", None),
        P("sub", None),
        P("sub", None),
        P(),
        P(),
        P(),
        P(),
    )
    return jax.shard_map(
        local,
        mesh=mesh,
        in_specs=placed,
        out_specs=P(("groups", "dom", "sub"), None),
        check_vma=False,
    )
```

```python
import functools

import jax
import jax.numpy as jnp
from jax import lax
from jax.experimental import pallas as pl
from jax.experimental.pallas import tpu as pltpu
from jax.sharding import PartitionSpec as P

BLOCK = 128
OFFSETS = (-2, -1, 1, 2)
STEP = 512
GATHERED = 1024
LONG = 30 * 10**9
VMEM_BYTES = 24 * 1024 * 1024
I16 = jnp.int16
BF16 = jnp.bfloat16
F32 = jnp.float32


def silu(v):
    h = 0.5 * v
    return h + h * jnp.tanh(h)


def region_of(delta):
    return jnp.where(delta < 0, delta + 2, delta + 1)


def halo_plan(count):
    plan = []
    if count == 4:
        for bit in (1, 2, 3):
            pairs = [(d, d ^ bit) for d in range(4) if abs((d ^ bit) - d) <= 2]
            regions = [(OFFSETS.index((d ^ bit) - d) if abs((d ^ bit) - d) <= 2 else -1) for d in range(4)]
            plan.append((pairs, regions, regions))
    else:
        for region, offset in enumerate(OFFSETS):
            pairs = [(d, d + offset) for d in range(count) if 0 <= d + offset < count]
            plan.append((pairs, region, 3 - region))
    return plan


def by_index(choice, index):
    if isinstance(choice, int):
        return choice
    picked = jnp.int32(choice[0])
    for place in range(1, len(choice)):
        picked = jnp.where(index == place, choice[place], picked)
    return picked


def whole_refs(count):
    return [pl.BlockSpec(memory_space=pltpu.VMEM)] * count


def call(body, outs, args, scratch=(), flops=0, smem=0):
    moved = sum(a.size * a.dtype.itemsize for a in args) + sum(
        o.size * jnp.dtype(o.dtype).itemsize for o in outs
    )
    specs = whole_refs(len(args) - smem) + [pl.BlockSpec(memory_space=pltpu.SMEM)] * smem
    return pl.pallas_call(
        body,
        out_shape=tuple(outs),
        in_specs=specs,
        out_specs=tuple(whole_refs(len(outs))),
        scratch_shapes=list(scratch),
        compiler_params=pltpu.CompilerParams(vmem_limit_bytes=VMEM_BYTES),
        cost_estimate=pl.CostEstimate(flops=int(flops), bytes_accessed=int(moved), transcendentals=0),
    )(*args)


def dot(a, b):
    return jnp.dot(a, b, preferred_element_type=F32)


def dot_first(a, b):
    return lax.dot_general(a, b, (((0,), (0,)), ((), ())), preferred_element_type=F32)


def three_parts(v):
    a = v.astype(BF16)
    rest = v - a.astype(F32)
    b = rest.astype(BF16)
    c = (rest - b.astype(F32)).astype(BF16)
    return a, b, c


def embed_rows(geom, geo):
    a1, a2, a3 = three_parts(geom)
    b1, b2, b3 = three_parts(geo)
    left = jnp.concatenate([a1, a1, a2, a1, a2, a3], axis=0)
    right = jnp.concatenate([b1, b2, b1, b3, b2, b1], axis=0)
    return silu(dot_first(left, right)).astype(BF16)


def layer_norm(v):
    width = v.shape[-1]
    centered = v - jnp.sum(v, axis=-1, keepdims=True) * (1.0 / width)
    spread = jnp.sum(centered * centered, axis=-1, keepdims=True) * (1.0 / width)
    return centered * lax.rsqrt(spread + 1e-05)


def hot(cond):
    return jnp.where(cond, BF16(1), BF16(0))


def pick_rows(table, listed, rows=None):
    if rows is None:
        rows = lax.broadcasted_iota(I16, (table.shape[0], 1), 0)
    return dot_first(hot(rows == listed.astype(I16)), table).astype(BF16)


def pick_lists(plan, table, send, outs, rows=None):
    here = lax.axis_index("dom")
    for (pairs, sent, received), out in zip(plan, outs):
        region = jnp.maximum(by_index(sent, here), 0)
        out[...] = pick_rows(table, send[0, pl.ds(region, 1), :], rows)


def stack_into(out, parts):
    first = 0
    for part in parts:
        out[first : first + part.shape[0], :] = part[...]
        first += part.shape[0]


def begin_kernel(token):
    token[...] = jnp.zeros(token.shape, token.dtype)


def first_pack_kernel(plan, grid, send, w_in, w_out, token, half, *outs):
    place = 0
    for source in (w_in, w_out):
        rows = source.shape[0] // 2
        begin = pl.multiple_of(lax.axis_index("groups") * rows, 64)
        half[place : place + rows, :] = source[pl.ds(begin, rows), :]
        place += rows
    pick_lists(plan, grid[...], send, outs)


def embed_kernel(e_in, e_out, p_in, p_out, egeom, egeo, pgeom, pgeo, after, weights, eout, pout):
    stack_into(weights, (e_in, e_out, p_in, p_out))
    for geom, geo, out in ((egeom, egeo, eout), (pgeom, pgeo, pout)):
        for begin in range(0, out.shape[0], STEP):
            out[begin : begin + STEP, :] = embed_rows(geom[:, begin : begin + STEP], geo[...])


def cross_kernel(rows_whole, k_in, weights, lat, crossing, lat_out):
    lat_out[...] = lat[...]
    crossing[:rows_whole, :] = weights[:rows_whole, :]
    first, place = rows_whole, rows_whole
    for rows in (k_in, weights.shape[0] - rows_whole - k_in):
        half = rows // 2
        begin = pl.multiple_of(first + lax.axis_index("groups") * half, 64)
        crossing[place : place + half, :] = weights[pl.ds(begin, half), :]
        first, place = first + rows, place + half


def split_kernel(source, after, *outs):
    first = 0
    for out in outs:
        out[...] = source[first : first + out.shape[0], :]
        first += out.shape[0]


def concat_kernel(*refs):
    stack_into(refs[-1], refs[:-1])


def put_shard(target, source, first, step, part=0, parts=1):
    rows = target.shape[0] // (4 * parts)
    place = (lax.bitwise_xor(lax.axis_index("sub"), step) * parts + part) * rows
    target[pl.ds(pl.multiple_of(place, rows), rows), :] = source[first : first + rows, :]


def put_half(target, k, source, first=0, step=0, other=0):
    rows = target.shape[0] // 4
    which = lax.bitwise_xor(lax.axis_index("groups"), other)
    begin = lax.bitwise_xor(lax.axis_index("sub"), step) * rows
    for base, count in ((0, k // 2), (k // 2, (rows - k) // 2)):
        place = pl.multiple_of(begin + 2 * base + which * count, 64)
        target[pl.ds(place, count), :] = source[first + base : first + base + count, :]


def joined(stack, first, rows):
    step = stack.shape[0] // 4
    return jnp.concatenate([stack[k * step + first : k * step + first + rows, :] for k in range(4)], axis=0)


def halo_targets(plan, slots, node_rows, width):
    here = lax.axis_index("dom")
    lane = lax.broadcasted_iota(jnp.int32, (1, width), 1)
    target = jnp.full((1, width), -1, jnp.int32)
    for place, (pairs, sent, received) in enumerate(plan):
        region = by_index(received, here)
        first = jnp.where(region < 0, -4 * node_rows, node_rows + region * slots)
        inside = (lane >= place * slots) & (lane < (place + 1) * slots)
        target = jnp.where(inside, lane - place * slots + first, target)
    return target.astype(I16)


def columns(edges, first):
    pair = edges[:, first : first + STEP]
    zero = jnp.zeros((8 - pair.shape[0], STEP), jnp.int32)
    upright = jnp.transpose(jnp.concatenate([pair, zero], axis=0).astype(F32)).astype(jnp.int32).astype(I16)
    return upright[:, 0:1], upright[:, 1:2]


def edge_blocks(edges, live_edges, first_stage, w_out, messages, totals):
    count = edges.shape[1]
    row = lax.broadcasted_iota(I16, (totals.shape[0], 1), 0)
    quarter = lax.axis_index("sub")
    for first in range(0, count, STEP):
        hidden = silu(first_stage(first)).astype(BF16)
        message = layer_norm(dot(hidden, w_out))
        place = lax.broadcasted_iota(jnp.int32, (STEP, 1), 0) + (first + quarter * count)
        messages[first : first + STEP, :] = jnp.where(place < live_edges, message, 0.0).astype(BF16)
        done = first + STEP
        if done % GATHERED == 0 or done == count:
            begin = (first // GATHERED) * GATHERED
            collect = hot(row == edges[1:2, begin:done].astype(I16))
            part = dot(collect, messages[begin:done, :])
            if begin == 0:
                totals[...] = part
            else:
                totals[...] += part


def hand_out(totals, gain, keep, give):
    rows = totals.shape[0] // 4
    core = lax.rem(lax.axis_index("sub"), 2)
    for half in range(2):
        for out, which in ((keep, core), (give, 1 - core)):
            place = pl.multiple_of((2 * half + which) * rows, rows)
            out[half * rows : (half + 1) * rows, :] = (totals[pl.ds(place, rows), :] * gain[...]).astype(BF16)


def enc_kernel(
    plan, slots, grid_rows, mesh_rows, k_in, emb, edges, gain, l0, l1, l2, l3, o_in, o_out, b_in, b_out,
    across, round_, both, round_both, live, keep, give, own_mesh, full, stack, table, messages, totals,
):
    d = gain.shape[1]
    quarter = lax.axis_index("sub")
    width = l0.shape[1]
    for shard, step in zip((l0, l1, l2, l3), (0, 2, 1, 3)):
        place = pl.multiple_of(lax.bitwise_xor(quarter, step) * width, width)
        full[:, pl.ds(place, width)] = shard[...]
    step = k_in + d // 4
    for first, second, bit in ((o_in, o_out, 0), (b_in, b_out, 1)):
        place = lax.bitwise_xor(quarter, bit) * step
        stack[pl.ds(pl.multiple_of(place, 128), k_in), :] = first[...]
        stack[pl.ds(pl.multiple_of(place + k_in, 128), d // 4), :] = second[...]
    put_half(stack, k_in, across, 0, 2, 0)
    put_half(stack, k_in, round_, 0, 2, 1)
    put_half(stack, k_in, both, 0, 3, 0)
    put_half(stack, k_in, round_both, 0, 3, 1)
    rows = mesh_rows // 4
    core = lax.rem(quarter, 2)
    for half in range(2):
        place = pl.multiple_of(grid_rows + (2 * half + core) * rows, rows)
        own_mesh[half * rows : (half + 1) * rows, :] = full[pl.ds(place, rows), :]

    w_in = joined(stack, 0, k_in)
    halo_first, got = grid_rows + mesh_rows, full.shape[0] - grid_rows - mesh_rows
    table[:d, :] = w_in[:d, :]
    table[d : d + grid_rows, :] = dot(full[:grid_rows, :], w_in[d : 2 * d, :]).astype(BF16)
    base = d + grid_rows + mesh_rows
    table[d + grid_rows : base, :] = dot(full[grid_rows:halo_first, :], w_in[2 * d :, :]).astype(BF16)
    table[base : base + got, :] = dot(full[halo_first:, :], w_in[d : 2 * d, :]).astype(BF16)
    if base + got < table.shape[0]:
        table[base + got :, :] = jnp.zeros((table.shape[0] - base - got, d), BF16)
    targets = halo_targets(plan, slots, grid_rows, table.shape[0] - base)
    own = lax.broadcasted_iota(I16, (1, grid_rows), 1)
    mesh = lax.broadcasted_iota(I16, (1, mesh_rows), 1)

    def first_stage(first):
        senders, receivers = columns(edges, first)
        chosen = [emb[first : first + STEP, :], hot(own == senders), hot(mesh == receivers), hot(targets == senders)]
        return dot(jnp.concatenate(chosen, axis=1), table[...])

    edge_blocks(edges, live[0] * BLOCK, first_stage, joined(stack, k_in, d // 4), messages, totals)
    hand_out(totals, gain, keep, give)


def node_update(mesh, shares, w_in, w_out, gain):
    stacked = jnp.concatenate([mesh, shares], axis=1)
    hidden = silu(dot(stacked, w_in)).astype(BF16)
    update = layer_norm(dot(hidden, w_out)) * gain
    return (mesh.astype(F32) + update).astype(BF16)


def add(mine, theirs):
    return (mine.astype(F32) + theirs.astype(F32)).astype(BF16)


def add_kernel(mine, theirs, out):
    out[...] = add(mine[...], theirs[...])


def node_kernel(
    plan, k_in, k_out, mesh, mine, theirs, gain, n_in, n_out, w0, w1, w2, w3, w4, send, out, packed, *rest
):
    outs, stack = rest[:-1], rest[-1]
    for shard, bit in zip((w0, w1, w2), (0, 1, 2)):
        put_shard(stack, shard, 0, bit)
    put_shard(stack, w3, 0, 3, 0, 2)
    put_shard(stack, w4, 0, 3, 1, 2)
    w_in, w_out = joined(stack, 0, k_in), joined(stack, k_in, k_out)
    fresh = node_update(mesh[...], add(mine[...], theirs[...]), w_in, w_out, gain[...])
    out[...] = fresh
    half = fresh.shape[0] // 2
    core = lax.rem(lax.axis_index("sub"), 2)
    place = lax.broadcasted_iota(jnp.int32, (fresh.shape[0], 1), 0)
    rows = place + core * half + jnp.where(place < half, 0, half)
    pick_lists(plan, fresh, send, outs, rows.astype(I16))
    stack_into(packed, (n_in, n_out))


def proc_first_kernel(
    k_in, first_row, emb, mine, theirs, edges, w0, w1, across, both, round_, round_both,
    table, pre, w_source, w_out, stack, full,
):
    d = full.shape[1]
    node_rows = full.shape[0]
    rows = node_rows // 4
    core = lax.rem(lax.axis_index("sub"), 2)
    for half in range(2):
        for part, which in ((mine, core), (theirs, 1 - core)):
            place = pl.multiple_of((2 * half + which) * rows, rows)
            full[pl.ds(place, rows), :] = part[half * rows : (half + 1) * rows, :]
    put_shard(stack, w0, first_row, 0)
    put_shard(stack, w1, first_row, 1)
    put_half(stack, k_in, across, 0, 2, 0)
    put_half(stack, k_in, both, 0, 3, 0)
    put_half(stack, k_in, round_, 0, 2, 1)
    put_half(stack, k_in, round_both, 0, 3, 1)
    w_in = joined(stack, 0, k_in)
    w_out[...] = joined(stack, k_in, d // 4)
    w_source[...] = w_in[d : 2 * d, :]
    table[:d, :] = w_in[:d, :]
    table[d : d + node_rows, :] = dot(full[...], w_in[d : 2 * d, :]).astype(BF16)
    table[d + node_rows :, :] = dot(full[...], w_in[2 * d :, :]).astype(BF16)
    lane = lax.broadcasted_iota(I16, (1, node_rows), 1)
    for first in range(0, pre.shape[0], STEP):
        pre[first : first + STEP, :] = dot(own_chosen(emb, edges, lane, first), table[...])


def own_chosen(emb, edges, lane, first):
    senders, receivers = columns(edges, first)
    return jnp.concatenate([emb[first : first + STEP, :], hot(lane == senders), hot(lane == receivers)], axis=1)


def proc_second_kernel(
    plan, slots, node_rows, emb, edges, gain, table, pre, w_source, w_out, halo, halo_beside,
    live, keep, give, halo_table, messages, totals,
):
    d = pre.shape[1]
    got = halo[...] + halo_beside[...]
    halo_table[: got.shape[0], :] = dot(got, w_source[...]).astype(BF16)
    if got.shape[0] < halo_table.shape[0]:
        halo_table[got.shape[0] :, :] = jnp.zeros((halo_table.shape[0] - got.shape[0], d), BF16)
    targets = halo_targets(plan, slots, node_rows, halo_table.shape[0])
    lane = lax.broadcasted_iota(I16, (1, node_rows), 1)

    def first_stage(first):
        senders, receivers = columns(edges, first)
        remote = dot(hot(targets == senders), halo_table[...])
        if first < pre.shape[0]:
            return pre[first : first + STEP, :] + remote
        return dot(own_chosen(emb, edges, lane, first), table[...]) + remote

    edge_blocks(edges, live[0] * BLOCK, first_stage, w_out[...], messages, totals)
    hand_out(totals, gain, keep, give)


def fold_kernel(mine, theirs, keep, give):
    rows = mine.shape[0] // 2
    chip = lax.div(lax.axis_index("sub"), 2)
    for out, which in ((keep, chip), (give, 1 - chip)):
        place = pl.multiple_of(which * rows, rows)
        out[...] = add(mine[pl.ds(place, rows), :], theirs[pl.ds(place, rows), :])


def out_kernel(k_in, k_out, middle, mine, theirs, gain, w0, w1, w2, w3, out, stack):
    rows = mine.shape[0]
    chip = lax.div(lax.axis_index("sub"), 2)
    mesh = middle[pl.ds(pl.multiple_of(chip * rows, rows), rows), :]
    for shard, bit in zip((w0, w1, w2, w3), (0, 1, 2, 3)):
        put_shard(stack, shard, 0, bit)
    w_in, w_out = joined(stack, 0, k_in), joined(stack, k_in, k_out)
    out[...] = node_update(mesh, add(mine[...], theirs[...]), w_in, w_out, gain[...])


def to_chip(v):
    return lax.ppermute(v, "sub", [(i, i ^ 2) for i in range(4)])


def to_core(v):
    return lax.ppermute(v, "sub", [(i, i ^ 1) for i in range(4)])


def to_group(v):
    count = lax.axis_size("groups")
    return lax.ppermute(v, "groups", [(i, count - 1 - i) for i in range(count)])


def shape(rows, width, dtype=BF16):
    return jax.ShapeDtypeStruct((rows, width), dtype)


def padded(rows):
    return -(-rows // 128) * 128


def local(
    grid_lat,
    mesh_lat,
    grid_send,
    mesh_send,
    enc_edges,
    enc_geom,
    enc_blocks,
    proc_edges,
    proc_geom,
    proc_blocks,
    enc_geo,
    proc_geo,
    enc_edge_in,
    enc_edge_out,
    enc_node_in,
    enc_node_out,
    proc_edge_in,
    proc_edge_out,
    proc_node_in,
    proc_node_out,
    enc_edge_gain,
    enc_node_gain,
    proc_edge_gain,
    proc_node_gain,
):
    plan = halo_plan(lax.axis_size("dom"))
    d = enc_geo.shape[1]
    grid_rows, mesh_rows = grid_lat.shape[0], mesh_lat.shape[0]
    n_enc, n_proc = enc_edges.shape[1], proc_edges.shape[1]
    enc_edge_gain, enc_node_gain, proc_edge_gain, proc_node_gain = (
        g.reshape(1, d) for g in (enc_edge_gain, enc_node_gain, proc_edge_gain, proc_node_gain)
    )
    k_in, k_out = enc_edge_in.shape[0], enc_edge_out.shape[0]
    n_in, n_out = enc_node_in.shape[0], enc_node_out.shape[0]
    width = grid_lat.shape[1]

    slots = grid_send.shape[2]
    (token,) = call(begin_kernel, [shape(16, 128)], [], flops=LONG)
    edge_half, *outgoing = call(
        functools.partial(first_pack_kernel, plan),
        [shape((k_in + k_out) // 2, d)] + [shape(slots, width)] * len(plan),
        [grid_lat, grid_send, enc_edge_in, enc_edge_out, token],
    )
    edge_across = to_chip(edge_half)
    halos = [lax.ppermute(v, "dom", entry[0]) for v, entry in zip(outgoing, plan)]
    got = len(plan) * slots
    (lat,) = call(
        concat_kernel,
        [shape(grid_rows + mesh_rows + got, width)],
        [grid_lat, mesh_lat, *halos],
    )
    lat_across = to_chip(lat)
    lat_beside = to_core(lat)
    edge_beside = [to_core(enc_edge_in), to_core(enc_edge_out)]
    edge_round = to_group(edge_across)
    next_w, enc_emb, proc_emb = call(
        embed_kernel,
        [shape(n_in + n_out + k_in + k_out, d), shape(n_enc, d), shape(n_proc, d)],
        [
            enc_node_in, enc_node_out, proc_edge_in, proc_edge_out,
            enc_geom, enc_geo, proc_geom, proc_geo, lat,
        ],
        flops=2 * (n_enc + n_proc) * d * 128,
    )
    crossing, lat_sent = call(
        functools.partial(cross_kernel, n_in + n_out, k_in),
        [shape(n_in + n_out + (k_in + k_out) // 2, d), shape(lat.shape[0], width)],
        [next_w, lat_across],
    )
    lat_both = to_core(lat_sent)
    next_across = to_chip(crossing)
    next_beside = to_core(next_w)

    halo_rows = padded(got)
    half = mesh_rows // 2
    keep, give, own_mesh = call(
        functools.partial(enc_kernel, plan, slots, grid_rows, mesh_rows, k_in),
        [shape(half, d)] * 3,
        [
            enc_emb, enc_edges, enc_edge_gain, lat, lat_across, lat_beside, lat_both,
            enc_edge_in, enc_edge_out, *edge_beside,
            edge_across, edge_round, to_core(edge_across), to_core(edge_round), enc_blocks,
        ],
        scratch=[
            pltpu.VMEM((grid_rows + mesh_rows + got, d), BF16),
            pltpu.VMEM((4 * (k_in + k_out), d), BF16),
            pltpu.VMEM((d + grid_rows + mesh_rows + halo_rows, d), BF16),
            pltpu.VMEM((n_enc, d), BF16),
            pltpu.VMEM((mesh_rows, d), F32),
        ],
        flops=2 * n_enc * d * (3 * d + grid_rows + mesh_rows + halo_rows),
        smem=1,
    )
    (chip_sum,) = call(add_kernel, [shape(half, d)], [keep, to_core(give)])
    *node_across, proc_across = call(
        split_kernel,
        [shape((n_in + n_out) // 2, d)] * 2 + [shape((k_in + k_out) // 2, d)],
        [next_across, chip_sum],
    )
    node_both = [to_core(v) for v in node_across]
    proc_round = to_group(proc_across)
    slots = mesh_send.shape[2]
    mid_half, last_w, *outgoing = call(
        functools.partial(node_kernel, plan, n_in, n_out),
        [shape(half, d), shape(n_in + n_out, d)] + [shape(slots, d)] * len(plan),
        [
            own_mesh, chip_sum, to_chip(chip_sum), enc_node_gain, proc_node_in, proc_node_out,
            next_w, next_beside, next_across, *node_both, mesh_send,
        ],
        scratch=[pltpu.VMEM((4 * (n_in + n_out), d), BF16)],
        flops=2 * half * d * 3 * d,
    )
    halos = [lax.ppermute(v, "dom", entry[0]) for v, entry in zip(outgoing, plan)]
    (halo,) = call(concat_kernel, [shape(len(plan) * slots, d)], halos)
    halo_beside = to_core(halo)
    last_across, last_beside = to_chip(last_w), to_core(last_w)
    early = n_proc // 2
    table, pre, w_source, w_out = call(
        functools.partial(proc_first_kernel, k_in, n_in + n_out),
        [shape(d + 2 * mesh_rows, d), shape(early, d, F32), shape(d, d), shape(d, d)],
        [
            proc_emb, mid_half, to_core(mid_half), proc_edges, next_w, next_beside, proc_across, to_core(proc_across),
            proc_round, to_core(proc_round),
        ],
        scratch=[pltpu.VMEM((4 * (k_in + k_out), d), BF16), pltpu.VMEM((mesh_rows, d), BF16)],
        flops=2 * early * d * (d + 2 * mesh_rows),
    )
    halo_rows = padded(len(plan) * slots)
    keep, give = call(
        functools.partial(proc_second_kernel, plan, slots, mesh_rows),
        [shape(half, d), shape(half, d)],
        [proc_emb, proc_edges, proc_edge_gain, table, pre, w_source, w_out, halo, halo_beside, proc_blocks],
        scratch=[
            pltpu.VMEM((halo_rows, d), BF16),
            pltpu.VMEM((n_proc, d), BF16),
            pltpu.VMEM((mesh_rows, d), F32),
        ],
        flops=2 * n_proc * d * (2 * d + mesh_rows + halo_rows),
        smem=1,
    )
    quarter = mesh_rows // 4
    mine, other = call(fold_kernel, [shape(quarter, d)] * 2, [keep, to_core(give)])
    (result,) = call(
        functools.partial(out_kernel, n_in, n_out),
        [shape(quarter, d)],
        [mid_half, mine, to_chip(other), proc_node_gain, last_w, last_beside, last_across, to_core(last_across)],
        scratch=[pltpu.VMEM((4 * (n_in + n_out), d), BF16)],
        flops=2 * quarter * d * 3 * d,
    )
    return result


def solution(mesh):
    placed = (
        P(("groups", "dom"), "sub"),
        P(("groups", "dom"), "sub"),
        P("dom", None, None),
        P("dom", None, None),
        P(None, ("dom", "sub")),
        P(None, ("dom", "sub")),
        P("dom"),
        P(None, ("dom", "sub")),
        P(None, ("dom", "sub")),
        P("dom"),
        P(),
        P(),
        P("sub", None),
        P("sub", None),
        P("sub", None),
        P("sub", None),
        P("sub", None),
        P("sub", None),
        P("sub", None),
        P("sub", None),
        P(),
        P(),
        P(),
        P(),
    )
    return jax.shard_map(
        local,
        mesh=mesh,
        in_specs=placed,
        out_specs=P(("groups", "dom", "sub"), None),
        check_vma=False,
    )
```

```python
import functools

import jax
import jax.numpy as jnp
from jax import lax
from jax.experimental import pallas as pl
from jax.experimental.pallas import tpu as pltpu
from jax.sharding import PartitionSpec as P

BLOCK = 128
OFFSETS = (-2, -1, 1, 2)
STEP = 512
GATHERED = 1024
LONG = 30 * 10**9
BY_PART = ("dom",)
VMEM_BYTES = 24 * 1024 * 1024
I16 = jnp.int16
BF16 = jnp.bfloat16
F32 = jnp.float32


def silu(v):
    h = 0.5 * v
    return h + h * jnp.tanh(h)


def region_of(delta):
    return jnp.where(delta < 0, delta + 2, delta + 1)


def halo_plan(count):
    plan = []
    if count == 4:
        for bit in (1, 2, 3):
            pairs = [(d, d ^ bit) for d in range(4) if abs((d ^ bit) - d) <= 2]
            regions = [(OFFSETS.index((d ^ bit) - d) if abs((d ^ bit) - d) <= 2 else -1) for d in range(4)]
            plan.append((pairs, regions, regions))
    else:
        for region, offset in enumerate(OFFSETS):
            pairs = [(d, d + offset) for d in range(count) if 0 <= d + offset < count]
            plan.append((pairs, region, 3 - region))
    return plan


def by_index(choice, index):
    if isinstance(choice, int):
        return choice
    picked = jnp.int32(choice[0])
    for place in range(1, len(choice)):
        picked = jnp.where(index == place, choice[place], picked)
    return picked


def whole_refs(count):
    return [pl.BlockSpec(memory_space=pltpu.VMEM)] * count


def call(body, outs, args, scratch=(), flops=0, smem=0):
    moved = sum(a.size * a.dtype.itemsize for a in args) + sum(
        o.size * jnp.dtype(o.dtype).itemsize for o in outs
    )
    specs = whole_refs(len(args) - smem) + [pl.BlockSpec(memory_space=pltpu.SMEM)] * smem
    return pl.pallas_call(
        body,
        out_shape=tuple(outs),
        in_specs=specs,
        out_specs=tuple(whole_refs(len(outs))),
        scratch_shapes=list(scratch),
        compiler_params=pltpu.CompilerParams(vmem_limit_bytes=VMEM_BYTES),
        cost_estimate=pl.CostEstimate(flops=int(flops), bytes_accessed=int(moved), transcendentals=0),
    )(*args)


def dot(a, b):
    return jnp.dot(a, b, preferred_element_type=F32)


def dot_first(a, b):
    return lax.dot_general(a, b, (((0,), (0,)), ((), ())), preferred_element_type=F32)


def three_parts(v):
    a = v.astype(BF16)
    rest = v - a.astype(F32)
    b = rest.astype(BF16)
    c = (rest - b.astype(F32)).astype(BF16)
    return a, b, c


def embed_rows(geom, geo):
    a1, a2, a3 = three_parts(geom)
    b1, b2, b3 = three_parts(geo)
    left = jnp.concatenate([a1, a1, a2, a1, a2, a3], axis=0)
    right = jnp.concatenate([b1, b2, b1, b3, b2, b1], axis=0)
    return silu(dot_first(left, right)).astype(BF16)


def layer_norm(v):
    width = v.shape[-1]
    centered = v - jnp.sum(v, axis=-1, keepdims=True) * (1.0 / width)
    spread = jnp.sum(centered * centered, axis=-1, keepdims=True) * (1.0 / width)
    return centered * lax.rsqrt(spread + 1e-05)


def hot(cond):
    return jnp.where(cond, BF16(1), BF16(0))


def pick_rows(table, listed, rows=None):
    if rows is None:
        rows = lax.broadcasted_iota(I16, (table.shape[0], 1), 0)
    return dot_first(hot(rows == listed.astype(I16)), table).astype(BF16)


def pick_lists(plan, table, send, outs, rows=None):
    here = lax.axis_index("dom")
    for (pairs, sent, received), out in zip(plan, outs):
        region = jnp.maximum(by_index(sent, here), 0)
        out[...] = pick_rows(table, send[0, pl.ds(region, 1), :], rows)


def stack_into(out, parts):
    first = 0
    for part in parts:
        out[first : first + part.shape[0], :] = part[...]
        first += part.shape[0]


def begin_kernel(token):
    token[...] = jnp.zeros(token.shape, token.dtype)


def first_pack_kernel(plan, grid, send, w_in, w_out, token, half, *outs):
    place = 0
    for source in (w_in, w_out):
        rows = source.shape[0] // 2
        begin = pl.multiple_of(lax.axis_index("groups") * rows, 64)
        half[place : place + rows, :] = source[pl.ds(begin, rows), :]
        place += rows
    pick_lists(plan, grid[...], send, outs)


def embed_kernel(e_in, e_out, p_in, p_out, egeom, egeo, pgeom, pgeo, after, weights, eout, pout):
    stack_into(weights, (e_in, e_out, p_in, p_out))
    for geom, geo, out in ((egeom, egeo, eout), (pgeom, pgeo, pout)):
        for begin in range(0, out.shape[0], STEP):
            out[begin : begin + STEP, :] = embed_rows(geom[:, begin : begin + STEP], geo[...])


def cross_kernel(parts, weights, lat, crossing, lat_out):
    lat_out[...] = lat[...]
    first, place = 0, 0
    for rows, axes in parts:
        half = rows // 2
        begin = pl.multiple_of(first + parity(axes) * half, 64)
        crossing[place : place + half, :] = weights[pl.ds(begin, half), :]
        first, place = first + rows, place + half


def pair_kernel(first, second, after, out):
    stack_into(out, (first, second))


def split_kernel(source, after, *outs):
    first = 0
    for out in outs:
        out[...] = source[first : first + out.shape[0], :]
        first += out.shape[0]


def concat_kernel(*refs):
    stack_into(refs[-1], refs[:-1])


def put_shard(target, source, first, step, part=0, parts=1):
    rows = target.shape[0] // (4 * parts)
    place = (lax.bitwise_xor(lax.axis_index("sub"), step) * parts + part) * rows
    target[pl.ds(pl.multiple_of(place, rows), rows), :] = source[first : first + rows, :]


def parity(axes):
    return lax.rem(sum(lax.axis_index(axis) for axis in axes), 2)


def put_half(target, k, source, step, other, axes=("groups",)):
    rows = target.shape[0] // 4
    which = lax.bitwise_xor(parity(axes), other)
    begin = lax.bitwise_xor(lax.axis_index("sub"), step) * rows
    for base, count in ((0, k // 2), (k // 2, (rows - k) // 2)):
        place = pl.multiple_of(begin + 2 * base + which * count, 64)
        target[pl.ds(place, count), :] = source[base : base + count, :]


def joined(stack, first, rows):
    step = stack.shape[0] // 4
    return jnp.concatenate([stack[k * step + first : k * step + first + rows, :] for k in range(4)], axis=0)


def halo_targets(plan, slots, node_rows, width):
    here = lax.axis_index("dom")
    lane = lax.broadcasted_iota(jnp.int32, (1, width), 1)
    target = jnp.full((1, width), -1, jnp.int32)
    for place, (pairs, sent, received) in enumerate(plan):
        region = by_index(received, here)
        first = jnp.where(region < 0, -4 * node_rows, node_rows + region * slots)
        inside = (lane >= place * slots) & (lane < (place + 1) * slots)
        target = jnp.where(inside, lane - place * slots + first, target)
    return target.astype(I16)


def columns(edges, first):
    pair = edges[:, first : first + STEP]
    zero = jnp.zeros((8 - pair.shape[0], STEP), jnp.int32)
    upright = jnp.transpose(jnp.concatenate([pair, zero], axis=0).astype(F32)).astype(jnp.int32).astype(I16)
    return upright[:, 0:1], upright[:, 1:2]


def edge_blocks(edges, live_edges, first_stage, w_out, messages, totals):
    count = edges.shape[1]
    row = lax.broadcasted_iota(I16, (totals.shape[0], 1), 0)
    quarter = lax.axis_index("sub")
    for first in range(0, count, STEP):
        hidden = silu(first_stage(first)).astype(BF16)
        message = layer_norm(dot(hidden, w_out))
        place = lax.broadcasted_iota(jnp.int32, (STEP, 1), 0) + (first + quarter * count)
        messages[first : first + STEP, :] = jnp.where(place < live_edges, message, 0.0).astype(BF16)
        done = first + STEP
        if done % GATHERED == 0 or done == count:
            begin = (first // GATHERED) * GATHERED
            collect = hot(row == edges[1:2, begin:done].astype(I16))
            part = dot(collect, messages[begin:done, :])
            if begin == 0:
                totals[...] = part
            else:
                totals[...] += part


def hand_out(totals, gain, keep, give):
    rows = totals.shape[0] // 4
    core = lax.rem(lax.axis_index("sub"), 2)
    for half in range(2):
        for out, which in ((keep, core), (give, 1 - core)):
            place = pl.multiple_of((2 * half + which) * rows, rows)
            out[half * rows : (half + 1) * rows, :] = (totals[pl.ds(place, rows), :] * gain[...]).astype(BF16)


def enc_kernel(
    plan, slots, grid_rows, mesh_rows, k_in, emb, edges, gain, l0, l1, l2, l3, o_in, o_out, b_in, b_out,
    across, round_, both, round_both, live, keep, give, own_mesh, full, stack, table, messages, totals,
):
    d = gain.shape[1]
    quarter = lax.axis_index("sub")
    width = l0.shape[1]
    for shard, step in zip((l0, l1, l2, l3), (0, 2, 1, 3)):
        place = pl.multiple_of(lax.bitwise_xor(quarter, step) * width, width)
        full[:, pl.ds(place, width)] = shard[...]
    step = k_in + d // 4
    for first, second, bit in ((o_in, o_out, 0), (b_in, b_out, 1)):
        place = lax.bitwise_xor(quarter, bit) * step
        stack[pl.ds(pl.multiple_of(place, 128), k_in), :] = first[...]
        stack[pl.ds(pl.multiple_of(place + k_in, 128), d // 4), :] = second[...]
    put_half(stack, k_in, across, 2, 0)
    put_half(stack, k_in, round_, 2, 1)
    put_half(stack, k_in, both, 3, 0)
    put_half(stack, k_in, round_both, 3, 1)
    rows = mesh_rows // 4
    core = lax.rem(quarter, 2)
    for half in range(2):
        place = pl.multiple_of(grid_rows + (2 * half + core) * rows, rows)
        own_mesh[half * rows : (half + 1) * rows, :] = full[pl.ds(place, rows), :]

    w_in = joined(stack, 0, k_in)
    halo_first, got = grid_rows + mesh_rows, full.shape[0] - grid_rows - mesh_rows
    table[:d, :] = w_in[:d, :]
    table[d : d + grid_rows, :] = dot(full[:grid_rows, :], w_in[d : 2 * d, :]).astype(BF16)
    base = d + grid_rows + mesh_rows
    table[d + grid_rows : base, :] = dot(full[grid_rows:halo_first, :], w_in[2 * d :, :]).astype(BF16)
    table[base : base + got, :] = dot(full[halo_first:, :], w_in[d : 2 * d, :]).astype(BF16)
    if base + got < table.shape[0]:
        table[base + got :, :] = jnp.zeros((table.shape[0] - base - got, d), BF16)
    targets = halo_targets(plan, slots, grid_rows, table.shape[0] - base)
    own = lax.broadcasted_iota(I16, (1, grid_rows), 1)
    mesh = lax.broadcasted_iota(I16, (1, mesh_rows), 1)

    def first_stage(first):
        senders, receivers = columns(edges, first)
        chosen = [emb[first : first + STEP, :], hot(own == senders), hot(mesh == receivers), hot(targets == senders)]
        return dot(jnp.concatenate(chosen, axis=1), table[...])

    edge_blocks(edges, live[0] * BLOCK, first_stage, joined(stack, k_in, d // 4), messages, totals)
    hand_out(totals, gain, keep, give)


def node_update(mesh, shares, w_in, w_out, gain):
    stacked = jnp.concatenate([mesh, shares], axis=1)
    hidden = silu(dot(stacked, w_in)).astype(BF16)
    update = layer_norm(dot(hidden, w_out)) * gain
    return (mesh.astype(F32) + update).astype(BF16)


def add(mine, theirs):
    return (mine.astype(F32) + theirs.astype(F32)).astype(BF16)


def add_kernel(mine, theirs, out):
    out[...] = add(mine[...], theirs[...])


def node_kernel(
    plan, k_in, k_out, mesh, mine, theirs, gain, n_in, n_out, w0, w1, w2, w3, w4, w5, send, out, packed, *rest
):
    outs, stack = rest[:-1], rest[-1]
    put_shard(stack, w0, 0, 0)
    put_shard(stack, w1, 0, 1)
    put_half(stack, k_in, w2, 2, 0, BY_PART)
    put_half(stack, k_in, w3, 2, 1, BY_PART)
    put_half(stack, k_in, w4, 3, 0, BY_PART)
    put_half(stack, k_in, w5, 3, 1, BY_PART)
    w_in, w_out = joined(stack, 0, k_in), joined(stack, k_in, k_out)
    fresh = node_update(mesh[...], add(mine[...], theirs[...]), w_in, w_out, gain[...])
    out[...] = fresh
    half = fresh.shape[0] // 2
    core = lax.rem(lax.axis_index("sub"), 2)
    place = lax.broadcasted_iota(jnp.int32, (fresh.shape[0], 1), 0)
    rows = place + core * half + jnp.where(place < half, 0, half)
    pick_lists(plan, fresh, send, outs, rows.astype(I16))
    stack_into(packed, (n_in, n_out))


def proc_first_kernel(
    k_in, first_row, emb, mine, theirs, edges, w0, w1, pair, pair_beside,
    table, pre, w_source, w_out, stack, full,
):
    d = full.shape[1]
    node_rows = full.shape[0]
    rows = node_rows // 4
    core = lax.rem(lax.axis_index("sub"), 2)
    for half in range(2):
        for part, which in ((mine, core), (theirs, 1 - core)):
            place = pl.multiple_of((2 * half + which) * rows, rows)
            full[pl.ds(place, rows), :] = part[half * rows : (half + 1) * rows, :]
    put_shard(stack, w0, first_row, 0)
    put_shard(stack, w1, first_row, 1)
    rows = pair.shape[0] // 2
    for other in range(2):
        put_half(stack, k_in, pair.at[pl.ds(other * rows, rows), :], 2, other)
        put_half(stack, k_in, pair_beside.at[pl.ds(other * rows, rows), :], 3, other)
    w_in = joined(stack, 0, k_in)
    w_out[...] = joined(stack, k_in, d // 4)
    w_source[...] = w_in[d : 2 * d, :]
    table[:d, :] = w_in[:d, :]
    table[d : d + node_rows, :] = dot(full[...], w_in[d : 2 * d, :]).astype(BF16)
    table[d + node_rows :, :] = dot(full[...], w_in[2 * d :, :]).astype(BF16)
    lane = lax.broadcasted_iota(I16, (1, node_rows), 1)
    for first in range(0, pre.shape[0], STEP):
        pre[first : first + STEP, :] = dot(own_chosen(emb, edges, lane, first), table[...])


def own_chosen(emb, edges, lane, first):
    senders, receivers = columns(edges, first)
    return jnp.concatenate([emb[first : first + STEP, :], hot(lane == senders), hot(lane == receivers)], axis=1)


def proc_second_kernel(
    plan, slots, node_rows, emb, edges, gain, table, pre, w_source, w_out, halo, halo_beside,
    live, keep, give, halo_table, messages, totals,
):
    d = pre.shape[1]
    got = halo[...] + halo_beside[...]
    halo_table[: got.shape[0], :] = dot(got, w_source[...]).astype(BF16)
    if got.shape[0] < halo_table.shape[0]:
        halo_table[got.shape[0] :, :] = jnp.zeros((halo_table.shape[0] - got.shape[0], d), BF16)
    targets = halo_targets(plan, slots, node_rows, halo_table.shape[0])
    lane = lax.broadcasted_iota(I16, (1, node_rows), 1)

    def first_stage(first):
        senders, receivers = columns(edges, first)
        remote = dot(hot(targets == senders), halo_table[...])
        if first < pre.shape[0]:
            return pre[first : first + STEP, :] + remote
        return dot(own_chosen(emb, edges, lane, first), table[...]) + remote

    edge_blocks(edges, live[0] * BLOCK, first_stage, w_out[...], messages, totals)
    hand_out(totals, gain, keep, give)


def fold_kernel(mine, theirs, keep, give):
    rows = mine.shape[0] // 2
    chip = lax.div(lax.axis_index("sub"), 2)
    for out, which in ((keep, chip), (give, 1 - chip)):
        place = pl.multiple_of(which * rows, rows)
        out[...] = add(mine[pl.ds(place, rows), :], theirs[pl.ds(place, rows), :])


def out_kernel(k_in, k_out, middle, mine, theirs, gain, w0, w1, w2, w3, out, stack):
    rows = mine.shape[0]
    chip = lax.div(lax.axis_index("sub"), 2)
    mesh = middle[pl.ds(pl.multiple_of(chip * rows, rows), rows), :]
    for shard, bit in zip((w0, w1, w2, w3), (0, 1, 2, 3)):
        put_shard(stack, shard, 0, bit)
    w_in, w_out = joined(stack, 0, k_in), joined(stack, k_in, k_out)
    out[...] = node_update(mesh, add(mine[...], theirs[...]), w_in, w_out, gain[...])


def to_chip(v):
    return lax.ppermute(v, "sub", [(i, i ^ 2) for i in range(4)])


def to_core(v):
    return lax.ppermute(v, "sub", [(i, i ^ 1) for i in range(4)])


def to_group(v):
    count = lax.axis_size("groups")
    return lax.ppermute(v, "groups", [(i, count - 1 - i) for i in range(count)])


def to_partition(v):
    return lax.ppermute(v, "dom", [(i, i ^ 1) for i in range(lax.axis_size("dom"))])


def shape(rows, width, dtype=BF16):
    return jax.ShapeDtypeStruct((rows, width), dtype)


def padded(rows):
    return -(-rows // 128) * 128


def local(
    grid_lat,
    mesh_lat,
    grid_send,
    mesh_send,
    enc_edges,
    enc_geom,
    enc_blocks,
    proc_edges,
    proc_geom,
    proc_blocks,
    enc_geo,
    proc_geo,
    enc_edge_in,
    enc_edge_out,
    enc_node_in,
    enc_node_out,
    proc_edge_in,
    proc_edge_out,
    proc_node_in,
    proc_node_out,
    enc_edge_gain,
    enc_node_gain,
    proc_edge_gain,
    proc_node_gain,
):
    plan = halo_plan(lax.axis_size("dom"))
    d = enc_geo.shape[1]
    grid_rows, mesh_rows = grid_lat.shape[0], mesh_lat.shape[0]
    n_enc, n_proc = enc_edges.shape[1], proc_edges.shape[1]
    enc_edge_gain, enc_node_gain, proc_edge_gain, proc_node_gain = (
        g.reshape(1, d) for g in (enc_edge_gain, enc_node_gain, proc_edge_gain, proc_node_gain)
    )
    k_in, k_out = enc_edge_in.shape[0], enc_edge_out.shape[0]
    n_in, n_out = enc_node_in.shape[0], enc_node_out.shape[0]
    width = grid_lat.shape[1]

    slots = grid_send.shape[2]
    (token,) = call(begin_kernel, [shape(16, 128)], [], flops=LONG)
    edge_half, *outgoing = call(
        functools.partial(first_pack_kernel, plan),
        [shape((k_in + k_out) // 2, d)] + [shape(slots, width)] * len(plan),
        [grid_lat, grid_send, enc_edge_in, enc_edge_out, token],
    )
    edge_across = to_chip(edge_half)
    halos = [lax.ppermute(v, "dom", entry[0]) for v, entry in zip(outgoing, plan)]
    got = len(plan) * slots
    (lat,) = call(
        concat_kernel,
        [shape(grid_rows + mesh_rows + got, width)],
        [grid_lat, mesh_lat, *halos],
    )
    lat_across = to_chip(lat)
    lat_beside = to_core(lat)
    edge_beside = [to_core(enc_edge_in), to_core(enc_edge_out)]
    edge_round = to_group(edge_across)
    next_w, enc_emb, proc_emb = call(
        embed_kernel,
        [shape(n_in + n_out + k_in + k_out, d), shape(n_enc, d), shape(n_proc, d)],
        [
            enc_node_in, enc_node_out, proc_edge_in, proc_edge_out,
            enc_geom, enc_geo, proc_geom, proc_geo, lat,
        ],
        flops=2 * (n_enc + n_proc) * d * 128,
    )
    crossing, lat_sent = call(
        functools.partial(
            cross_kernel, ((n_in, BY_PART), (n_out, BY_PART), (k_in, ("groups",)), (k_out, ("groups",)))
        ),
        [shape((n_in + n_out + k_in + k_out) // 2, d), shape(lat.shape[0], width)],
        [next_w, lat_across],
    )
    lat_both = to_core(lat_sent)
    next_across = to_chip(crossing)
    next_beside = to_core(next_w)

    halo_rows = padded(got)
    half = mesh_rows // 2
    keep, give, own_mesh = call(
        functools.partial(enc_kernel, plan, slots, grid_rows, mesh_rows, k_in),
        [shape(half, d)] * 3,
        [
            enc_emb, enc_edges, enc_edge_gain, lat, lat_across, lat_beside, lat_both,
            enc_edge_in, enc_edge_out, *edge_beside,
            edge_across, edge_round, to_core(edge_across), to_core(edge_round), enc_blocks,
        ],
        scratch=[
            pltpu.VMEM((grid_rows + mesh_rows + got, d), BF16),
            pltpu.VMEM((4 * (k_in + k_out), d), BF16),
            pltpu.VMEM((d + grid_rows + mesh_rows + halo_rows, d), BF16),
            pltpu.VMEM((n_enc, d), BF16),
            pltpu.VMEM((mesh_rows, d), F32),
        ],
        flops=2 * n_enc * d * (3 * d + grid_rows + mesh_rows + halo_rows),
        smem=1,
    )
    (chip_sum,) = call(add_kernel, [shape(half, d)], [keep, to_core(give)])
    node_across, proc_across = call(
        split_kernel,
        [shape((n_in + n_out) // 2, d), shape((k_in + k_out) // 2, d)],
        [next_across, chip_sum],
    )
    node_round = to_partition(node_across)
    proc_round = to_group(proc_across)
    node_both = to_core(node_across)
    slots = mesh_send.shape[2]
    mid_half, last_w, *outgoing = call(
        functools.partial(node_kernel, plan, n_in, n_out),
        [shape(half, d), shape(n_in + n_out, d)] + [shape(slots, d)] * len(plan),
        [
            own_mesh, chip_sum, to_chip(chip_sum), enc_node_gain, proc_node_in, proc_node_out,
            next_w, next_beside, node_across, node_round, node_both, to_core(node_round), mesh_send,
        ],
        scratch=[pltpu.VMEM((4 * (n_in + n_out), d), BF16)],
        flops=2 * half * d * 3 * d,
    )
    (proc_pair,) = call(pair_kernel, [shape(k_in + k_out, d)], [proc_across, proc_round, mid_half])
    halos = [lax.ppermute(v, "dom", entry[0]) for v, entry in zip(outgoing, plan)]
    (halo,) = call(concat_kernel, [shape(len(plan) * slots, d)], halos)
    halo_beside = to_core(halo)
    last_across, last_beside = to_chip(last_w), to_core(last_w)
    early = n_proc // 2
    table, pre, w_source, w_out = call(
        functools.partial(proc_first_kernel, k_in, n_in + n_out),
        [shape(d + 2 * mesh_rows, d), shape(early, d, F32), shape(d, d), shape(d, d)],
        [
            proc_emb, mid_half, to_core(mid_half), proc_edges, next_w, next_beside, proc_pair, to_core(proc_pair),
        ],
        scratch=[pltpu.VMEM((4 * (k_in + k_out), d), BF16), pltpu.VMEM((mesh_rows, d), BF16)],
        flops=2 * early * d * (d + 2 * mesh_rows),
    )
    halo_rows = padded(len(plan) * slots)
    keep, give = call(
        functools.partial(proc_second_kernel, plan, slots, mesh_rows),
        [shape(half, d), shape(half, d)],
        [proc_emb, proc_edges, proc_edge_gain, table, pre, w_source, w_out, halo, halo_beside, proc_blocks],
        scratch=[
            pltpu.VMEM((halo_rows, d), BF16),
            pltpu.VMEM((n_proc, d), BF16),
            pltpu.VMEM((mesh_rows, d), F32),
        ],
        flops=2 * n_proc * d * (2 * d + mesh_rows + halo_rows),
        smem=1,
    )
    quarter = mesh_rows // 4
    mine, other = call(fold_kernel, [shape(quarter, d)] * 2, [keep, to_core(give)])
    (result,) = call(
        functools.partial(out_kernel, n_in, n_out),
        [shape(quarter, d)],
        [mid_half, mine, to_chip(other), proc_node_gain, last_w, last_beside, last_across, to_core(last_across)],
        scratch=[pltpu.VMEM((4 * (n_in + n_out), d), BF16)],
        flops=2 * quarter * d * 3 * d,
    )
    return result


def solution(mesh):
    placed = (
        P(("groups", "dom"), "sub"),
        P(("groups", "dom"), "sub"),
        P("dom", None, None),
        P("dom", None, None),
        P(None, ("dom", "sub")),
        P(None, ("dom", "sub")),
        P("dom"),
        P(None, ("dom", "sub")),
        P(None, ("dom", "sub")),
        P("dom"),
        P(),
        P(),
        P("sub", None),
        P("sub", None),
        P("sub", None),
        P("sub", None),
        P("sub", None),
        P("sub", None),
        P("sub", None),
        P("sub", None),
        P(),
        P(),
        P(),
        P(),
    )
    return jax.shard_map(
        local,
        mesh=mesh,
        in_specs=placed,
        out_specs=P(("groups", "dom", "sub"), None),
        check_vma=False,
    )
```

```python
import functools

import jax
import jax.numpy as jnp
from jax import lax
from jax.experimental import pallas as pl
from jax.experimental.pallas import tpu as pltpu
from jax.sharding import PartitionSpec as P

BLOCK = 128
OFFSETS = (-2, -1, 1, 2)
STEP = 512
GATHERED = 1024
LONG = 30 * 10**9
VMEM_BYTES = 24 * 1024 * 1024
I16 = jnp.int16
BF16 = jnp.bfloat16
F32 = jnp.float32


def silu(v):
    h = 0.5 * v
    return h + h * jnp.tanh(h)


def region_of(delta):
    return jnp.where(delta < 0, delta + 2, delta + 1)


def halo_plan(count):
    plan = []
    if count == 4:
        for bit in (1, 2, 3):
            pairs = [(d, d ^ bit) for d in range(4) if abs((d ^ bit) - d) <= 2]
            regions = [(OFFSETS.index((d ^ bit) - d) if abs((d ^ bit) - d) <= 2 else -1) for d in range(4)]
            plan.append((pairs, regions, regions))
    else:
        for region, offset in enumerate(OFFSETS):
            pairs = [(d, d + offset) for d in range(count) if 0 <= d + offset < count]
            plan.append((pairs, region, 3 - region))
    return plan


def by_index(choice, index):
    if isinstance(choice, int):
        return choice
    picked = jnp.int32(choice[0])
    for place in range(1, len(choice)):
        picked = jnp.where(index == place, choice[place], picked)
    return picked


def whole_refs(count):
    return [pl.BlockSpec(memory_space=pltpu.VMEM)] * count


def call(body, outs, args, scratch=(), flops=0, smem=0):
    moved = sum(a.size * a.dtype.itemsize for a in args) + sum(
        o.size * jnp.dtype(o.dtype).itemsize for o in outs
    )
    specs = whole_refs(len(args) - smem) + [pl.BlockSpec(memory_space=pltpu.SMEM)] * smem
    return pl.pallas_call(
        body,
        out_shape=tuple(outs),
        in_specs=specs,
        out_specs=tuple(whole_refs(len(outs))),
        scratch_shapes=list(scratch),
        compiler_params=pltpu.CompilerParams(vmem_limit_bytes=VMEM_BYTES),
        cost_estimate=pl.CostEstimate(flops=int(flops), bytes_accessed=int(moved), transcendentals=0),
    )(*args)


def dot(a, b):
    return jnp.dot(a, b, preferred_element_type=F32)


def dot_first(a, b):
    return lax.dot_general(a, b, (((0,), (0,)), ((), ())), preferred_element_type=F32)


def three_parts(v):
    a = v.astype(BF16)
    rest = v - a.astype(F32)
    b = rest.astype(BF16)
    c = (rest - b.astype(F32)).astype(BF16)
    return a, b, c


def embed_rows(geom, geo):
    a1, a2, a3 = three_parts(geom)
    b1, b2, b3 = three_parts(geo)
    left = jnp.concatenate([a1, a1, a2, a1, a2, a3], axis=0)
    right = jnp.concatenate([b1, b2, b1, b3, b2, b1], axis=0)
    return silu(dot_first(left, right)).astype(BF16)


def layer_norm(v):
    width = v.shape[-1]
    centered = v - jnp.sum(v, axis=-1, keepdims=True) * (1.0 / width)
    spread = jnp.sum(centered * centered, axis=-1, keepdims=True) * (1.0 / width)
    return centered * lax.rsqrt(spread + 1e-05)


def hot(cond):
    return jnp.where(cond, BF16(1), BF16(0))


def pick_rows(table, listed, rows=None):
    if rows is None:
        rows = lax.broadcasted_iota(I16, (table.shape[0], 1), 0)
    return dot_first(hot(rows == listed.astype(I16)), table).astype(BF16)


def pick_lists(plan, table, send, outs, rows=None):
    here = lax.axis_index("dom")
    for (pairs, sent, received), out in zip(plan, outs):
        region = jnp.maximum(by_index(sent, here), 0)
        out[...] = pick_rows(table, send[0, pl.ds(region, 1), :], rows)


def stack_into(out, parts):
    first = 0
    for part in parts:
        out[first : first + part.shape[0], :] = part[...]
        first += part.shape[0]


def begin_kernel(token):
    token[...] = jnp.zeros(token.shape, token.dtype)


def first_pack_kernel(plan, grid, send, w_in, w_out, token, half, *outs):
    place = 0
    for source in (w_in, w_out):
        rows = source.shape[0] // 2
        begin = pl.multiple_of(lax.axis_index("groups") * rows, 64)
        half[place : place + rows, :] = source[pl.ds(begin, rows), :]
        place += rows
    pick_lists(plan, grid[...], send, outs)


def embed_kernel(e_in, e_out, p_in, p_out, egeom, egeo, pgeom, pgeo, after, weights, eout, pout):
    stack_into(weights, (e_in, e_out, p_in, p_out))
    for geom, geo, out in ((egeom, egeo, eout), (pgeom, pgeo, pout)):
        for begin in range(0, out.shape[0], STEP):
            out[begin : begin + STEP, :] = embed_rows(geom[:, begin : begin + STEP], geo[...])


def cross_kernel(parts, weights, lat, lat_out, *crossing):
    lat_out[...] = lat[...]
    first = 0
    for stack, out in zip(parts, crossing):
        place = 0
        for rows in stack:
            half = rows // 2
            begin = pl.multiple_of(first + lax.axis_index("groups") * half, 64)
            out[place : place + half, :] = weights[pl.ds(begin, half), :]
            first, place = first + rows, place + half


def pair_kernel(first, second, after, out):
    stack_into(out, (first, second))


def hold_kernel(source, after, out):
    out[...] = source[...]


def concat_kernel(*refs):
    stack_into(refs[-1], refs[:-1])


def put_shard(target, source, first, step, part=0, parts=1):
    rows = target.shape[0] // (4 * parts)
    place = (lax.bitwise_xor(lax.axis_index("sub"), step) * parts + part) * rows
    target[pl.ds(pl.multiple_of(place, rows), rows), :] = source[first : first + rows, :]


def put_half(target, k, source, step, other):
    rows = target.shape[0] // 4
    which = lax.bitwise_xor(lax.axis_index("groups"), other)
    begin = lax.bitwise_xor(lax.axis_index("sub"), step) * rows
    for base, count in ((0, k // 2), (k // 2, (rows - k) // 2)):
        place = pl.multiple_of(begin + 2 * base + which * count, 64)
        target[pl.ds(place, count), :] = source[base : base + count, :]


def joined(stack, first, rows):
    step = stack.shape[0] // 4
    return jnp.concatenate([stack[k * step + first : k * step + first + rows, :] for k in range(4)], axis=0)


def halo_targets(plan, slots, node_rows, width):
    here = lax.axis_index("dom")
    lane = lax.broadcasted_iota(jnp.int32, (1, width), 1)
    target = jnp.full((1, width), -1, jnp.int32)
    for place, (pairs, sent, received) in enumerate(plan):
        region = by_index(received, here)
        first = jnp.where(region < 0, -4 * node_rows, node_rows + region * slots)
        inside = (lane >= place * slots) & (lane < (place + 1) * slots)
        target = jnp.where(inside, lane - place * slots + first, target)
    return target.astype(I16)


def columns(edges, first):
    pair = edges[:, first : first + STEP]
    zero = jnp.zeros((8 - pair.shape[0], STEP), jnp.int32)
    upright = jnp.transpose(jnp.concatenate([pair, zero], axis=0).astype(F32)).astype(jnp.int32).astype(I16)
    return upright[:, 0:1], upright[:, 1:2]


def edge_blocks(edges, live_edges, first_stage, w_out, messages, totals):
    count = edges.shape[1]
    row = lax.broadcasted_iota(I16, (totals.shape[0], 1), 0)
    quarter = lax.axis_index("sub")
    for first in range(0, count, STEP):
        hidden = silu(first_stage(first)).astype(BF16)
        message = layer_norm(dot(hidden, w_out))
        place = lax.broadcasted_iota(jnp.int32, (STEP, 1), 0) + (first + quarter * count)
        messages[first : first + STEP, :] = jnp.where(place < live_edges, message, 0.0).astype(BF16)
        done = first + STEP
        if done % GATHERED == 0 or done == count:
            begin = (first // GATHERED) * GATHERED
            collect = hot(row == edges[1:2, begin:done].astype(I16))
            part = dot(collect, messages[begin:done, :])
            if begin == 0:
                totals[...] = part
            else:
                totals[...] += part


def hand_out(totals, gain, keep, *give):
    rows = totals.shape[0] // 4
    core = lax.rem(lax.axis_index("sub"), 2)
    for half in range(2):
        kept = keep.at[pl.ds(half * rows, rows), :]
        given = give[0].at[pl.ds(half * rows, rows), :] if len(give) == 1 else give[half]
        for out, which in ((kept, core), (given, 1 - core)):
            place = pl.multiple_of((2 * half + which) * rows, rows)
            out[...] = (totals[pl.ds(place, rows), :] * gain[...]).astype(BF16)


def enc_kernel(
    plan, slots, grid_rows, mesh_rows, k_in, emb, edges, gain, l0, l1, l2, l3, o_in, o_out, b_in, b_out,
    across, round_, both, round_both, live, keep, give, give_more, own_mesh, full, stack, table, messages, totals,
):
    d = gain.shape[1]
    quarter = lax.axis_index("sub")
    width = l0.shape[1]
    for shard, step in zip((l0, l1, l2, l3), (0, 2, 1, 3)):
        place = pl.multiple_of(lax.bitwise_xor(quarter, step) * width, width)
        full[:, pl.ds(place, width)] = shard[...]
    step = k_in + d // 4
    for first, second, bit in ((o_in, o_out, 0), (b_in, b_out, 1)):
        place = lax.bitwise_xor(quarter, bit) * step
        stack[pl.ds(pl.multiple_of(place, 128), k_in), :] = first[...]
        stack[pl.ds(pl.multiple_of(place + k_in, 128), d // 4), :] = second[...]
    put_half(stack, k_in, across, 2, 0)
    put_half(stack, k_in, round_, 2, 1)
    put_half(stack, k_in, both, 3, 0)
    put_half(stack, k_in, round_both, 3, 1)
    rows = mesh_rows // 4
    core = lax.rem(quarter, 2)
    for half in range(2):
        place = pl.multiple_of(grid_rows + (2 * half + core) * rows, rows)
        own_mesh[half * rows : (half + 1) * rows, :] = full[pl.ds(place, rows), :]

    w_in = joined(stack, 0, k_in)
    halo_first, got = grid_rows + mesh_rows, full.shape[0] - grid_rows - mesh_rows
    table[:d, :] = w_in[:d, :]
    table[d : d + grid_rows, :] = dot(full[:grid_rows, :], w_in[d : 2 * d, :]).astype(BF16)
    base = d + grid_rows + mesh_rows
    table[d + grid_rows : base, :] = dot(full[grid_rows:halo_first, :], w_in[2 * d :, :]).astype(BF16)
    table[base : base + got, :] = dot(full[halo_first:, :], w_in[d : 2 * d, :]).astype(BF16)
    if base + got < table.shape[0]:
        table[base + got :, :] = jnp.zeros((table.shape[0] - base - got, d), BF16)
    targets = halo_targets(plan, slots, grid_rows, table.shape[0] - base)
    own = lax.broadcasted_iota(I16, (1, grid_rows), 1)
    mesh = lax.broadcasted_iota(I16, (1, mesh_rows), 1)

    def first_stage(first):
        senders, receivers = columns(edges, first)
        chosen = [emb[first : first + STEP, :], hot(own == senders), hot(mesh == receivers), hot(targets == senders)]
        return dot(jnp.concatenate(chosen, axis=1), table[...])

    edge_blocks(edges, live[0] * BLOCK, first_stage, joined(stack, k_in, d // 4), messages, totals)
    hand_out(totals, gain, keep, give, give_more)


def node_update(mesh, shares, w_in, w_out, gain):
    stacked = jnp.concatenate([mesh, shares], axis=1)
    hidden = silu(dot(stacked, w_in)).astype(BF16)
    update = layer_norm(dot(hidden, w_out)) * gain
    return (mesh.astype(F32) + update).astype(BF16)


def add(mine, theirs):
    return (mine.astype(F32) + theirs.astype(F32)).astype(BF16)


def add_kernel(mine, first, second, out):
    rows = first.shape[0]
    out[:rows, :] = add(mine[:rows, :], first[...])
    out[rows:, :] = add(mine[rows:, :], second[...])


def node_kernel(
    plan, k_in, k_out, mesh, mine, theirs, gain, n_in, n_out, w0, w1, w2, w3, w4, w5, send, out, packed, *rest
):
    outs, stack = rest[:-1], rest[-1]
    put_shard(stack, w0, 0, 0)
    put_shard(stack, w1, 0, 1)
    put_half(stack, k_in, w2, 2, 0)
    put_half(stack, k_in, w3, 2, 1)
    put_half(stack, k_in, w4, 3, 0)
    put_half(stack, k_in, w5, 3, 1)
    w_in, w_out = joined(stack, 0, k_in), joined(stack, k_in, k_out)
    fresh = node_update(mesh[...], add(mine[...], theirs[...]), w_in, w_out, gain[...])
    out[...] = fresh
    half = fresh.shape[0] // 2
    core = lax.rem(lax.axis_index("sub"), 2)
    place = lax.broadcasted_iota(jnp.int32, (fresh.shape[0], 1), 0)
    rows = place + core * half + jnp.where(place < half, 0, half)
    pick_lists(plan, fresh, send, outs, rows.astype(I16))
    stack_into(packed, (n_in, n_out))


def proc_first_kernel(
    k_in, first_row, emb, mine, theirs, edges, w0, w1, pair, pair_beside,
    table, pre, w_source, w_out, stack, full,
):
    d = full.shape[1]
    node_rows = full.shape[0]
    rows = node_rows // 4
    core = lax.rem(lax.axis_index("sub"), 2)
    for half in range(2):
        for part, which in ((mine, core), (theirs, 1 - core)):
            place = pl.multiple_of((2 * half + which) * rows, rows)
            full[pl.ds(place, rows), :] = part[half * rows : (half + 1) * rows, :]
    put_shard(stack, w0, first_row, 0)
    put_shard(stack, w1, first_row, 1)
    rows = pair.shape[0] // 2
    for other in range(2):
        put_half(stack, k_in, pair.at[pl.ds(other * rows, rows), :], 2, other)
        put_half(stack, k_in, pair_beside.at[pl.ds(other * rows, rows), :], 3, other)
    w_in = joined(stack, 0, k_in)
    w_out[...] = joined(stack, k_in, d // 4)
    w_source[...] = w_in[d : 2 * d, :]
    table[:d, :] = w_in[:d, :]
    table[d : d + node_rows, :] = dot(full[...], w_in[d : 2 * d, :]).astype(BF16)
    table[d + node_rows :, :] = dot(full[...], w_in[2 * d :, :]).astype(BF16)
    lane = lax.broadcasted_iota(I16, (1, node_rows), 1)
    for first in range(0, pre.shape[0], STEP):
        pre[first : first + STEP, :] = dot(own_chosen(emb, edges, lane, first), table[...])


def own_chosen(emb, edges, lane, first):
    senders, receivers = columns(edges, first)
    return jnp.concatenate([emb[first : first + STEP, :], hot(lane == senders), hot(lane == receivers)], axis=1)


def proc_second_kernel(
    plan, slots, node_rows, emb, edges, gain, table, pre, w_source, w_out, halo, halo_beside,
    live, keep, give, halo_table, messages, totals,
):
    d = pre.shape[1]
    got = halo[...] + halo_beside[...]
    halo_table[: got.shape[0], :] = dot(got, w_source[...]).astype(BF16)
    if got.shape[0] < halo_table.shape[0]:
        halo_table[got.shape[0] :, :] = jnp.zeros((halo_table.shape[0] - got.shape[0], d), BF16)
    targets = halo_targets(plan, slots, node_rows, halo_table.shape[0])
    lane = lax.broadcasted_iota(I16, (1, node_rows), 1)

    def first_stage(first):
        senders, receivers = columns(edges, first)
        remote = dot(hot(targets == senders), halo_table[...])
        if first < pre.shape[0]:
            return pre[first : first + STEP, :] + remote
        return dot(own_chosen(emb, edges, lane, first), table[...]) + remote

    edge_blocks(edges, live[0] * BLOCK, first_stage, w_out[...], messages, totals)
    hand_out(totals, gain, keep, give)


def fold_kernel(mine, theirs, keep, give):
    rows = mine.shape[0] // 2
    chip = lax.div(lax.axis_index("sub"), 2)
    for out, which in ((keep, chip), (give, 1 - chip)):
        place = pl.multiple_of(which * rows, rows)
        out[...] = add(mine[pl.ds(place, rows), :], theirs[pl.ds(place, rows), :])


def out_kernel(k_in, k_out, middle, mine, theirs, gain, w0, w1, w2, w3, out, stack):
    rows = mine.shape[0]
    chip = lax.div(lax.axis_index("sub"), 2)
    mesh = middle[pl.ds(pl.multiple_of(chip * rows, rows), rows), :]
    for shard, bit in zip((w0, w1, w2, w3), (0, 1, 2, 3)):
        put_shard(stack, shard, 0, bit)
    w_in, w_out = joined(stack, 0, k_in), joined(stack, k_in, k_out)
    out[...] = node_update(mesh, add(mine[...], theirs[...]), w_in, w_out, gain[...])


def to_chip(v):
    return lax.ppermute(v, "sub", [(i, i ^ 2) for i in range(4)])


def to_core(v):
    return lax.ppermute(v, "sub", [(i, i ^ 1) for i in range(4)])


def to_group(v):
    count = lax.axis_size("groups")
    return lax.ppermute(v, "groups", [(i, count - 1 - i) for i in range(count)])


def shape(rows, width, dtype=BF16):
    return jax.ShapeDtypeStruct((rows, width), dtype)


def call_hold(source, after):
    return call(hold_kernel, [shape(*source.shape)], [source, after])[0]


def padded(rows):
    return -(-rows // 128) * 128


def local(
    grid_lat,
    mesh_lat,
    grid_send,
    mesh_send,
    enc_edges,
    enc_geom,
    enc_blocks,
    proc_edges,
    proc_geom,
    proc_blocks,
    enc_geo,
    proc_geo,
    enc_edge_in,
    enc_edge_out,
    enc_node_in,
    enc_node_out,
    proc_edge_in,
    proc_edge_out,
    proc_node_in,
    proc_node_out,
    enc_edge_gain,
    enc_node_gain,
    proc_edge_gain,
    proc_node_gain,
):
    plan = halo_plan(lax.axis_size("dom"))
    d = enc_geo.shape[1]
    grid_rows, mesh_rows = grid_lat.shape[0], mesh_lat.shape[0]
    n_enc, n_proc = enc_edges.shape[1], proc_edges.shape[1]
    enc_edge_gain, enc_node_gain, proc_edge_gain, proc_node_gain = (
        g.reshape(1, d) for g in (enc_edge_gain, enc_node_gain, proc_edge_gain, proc_node_gain)
    )
    k_in, k_out = enc_edge_in.shape[0], enc_edge_out.shape[0]
    n_in, n_out = enc_node_in.shape[0], enc_node_out.shape[0]
    width = grid_lat.shape[1]

    slots = grid_send.shape[2]
    (token,) = call(begin_kernel, [shape(16, 128)], [], flops=LONG)
    edge_half, *outgoing = call(
        functools.partial(first_pack_kernel, plan),
        [shape((k_in + k_out) // 2, d)] + [shape(slots, width)] * len(plan),
        [grid_lat, grid_send, enc_edge_in, enc_edge_out, token],
    )
    edge_across = to_chip(edge_half)
    halos = [lax.ppermute(v, "dom", entry[0]) for v, entry in zip(outgoing, plan)]
    got = len(plan) * slots
    (lat,) = call(
        concat_kernel,
        [shape(grid_rows + mesh_rows + got, width)],
        [grid_lat, mesh_lat, *halos],
    )
    lat_across = to_chip(lat)
    lat_beside = to_core(lat)
    edge_beside = [to_core(enc_edge_in), to_core(enc_edge_out)]
    edge_round = to_group(edge_across)
    next_w, enc_emb, proc_emb = call(
        embed_kernel,
        [shape(n_in + n_out + k_in + k_out, d), shape(n_enc, d), shape(n_proc, d)],
        [
            enc_node_in, enc_node_out, proc_edge_in, proc_edge_out,
            enc_geom, enc_geo, proc_geom, proc_geo, lat,
        ],
        flops=2 * (n_enc + n_proc) * d * 128,
    )
    lat_sent, node_half, proc_half = call(
        functools.partial(cross_kernel, ((n_in, n_out), (k_in, k_out))),
        [shape(lat.shape[0], width), shape((n_in + n_out) // 2, d), shape((k_in + k_out) // 2, d)],
        [next_w, lat_across],
    )
    lat_both = to_core(lat_sent)
    node_came, proc_came = to_chip(node_half), to_chip(proc_half)
    next_beside = to_core(next_w)

    halo_rows = padded(got)
    half = mesh_rows // 2
    keep, give, give_more, own_mesh = call(
        functools.partial(enc_kernel, plan, slots, grid_rows, mesh_rows, k_in),
        [shape(half, d), shape(half // 2, d), shape(half // 2, d), shape(half, d)],
        [
            enc_emb, enc_edges, enc_edge_gain, lat, lat_across, lat_beside, lat_both,
            enc_edge_in, enc_edge_out, *edge_beside,
            edge_across, edge_round, to_core(edge_across), to_core(edge_round), enc_blocks,
        ],
        scratch=[
            pltpu.VMEM((grid_rows + mesh_rows + got, d), BF16),
            pltpu.VMEM((4 * (k_in + k_out), d), BF16),
            pltpu.VMEM((d + grid_rows + mesh_rows + halo_rows, d), BF16),
            pltpu.VMEM((n_enc, d), BF16),
            pltpu.VMEM((mesh_rows, d), F32),
        ],
        flops=2 * n_enc * d * (3 * d + grid_rows + mesh_rows + halo_rows),
        smem=1,
    )
    (chip_sum,) = call(add_kernel, [shape(half, d)], [keep, to_core(give), to_core(give_more)])
    node_across, proc_across = call_hold(node_came, chip_sum), call_hold(proc_came, chip_sum)
    node_round, proc_round = to_group(node_across), to_group(proc_across)
    node_both = to_core(node_across)
    slots = mesh_send.shape[2]
    mid_half, last_w, *outgoing = call(
        functools.partial(node_kernel, plan, n_in, n_out),
        [shape(half, d), shape(n_in + n_out, d)] + [shape(slots, d)] * len(plan),
        [
            own_mesh, chip_sum, to_chip(chip_sum), enc_node_gain, proc_node_in, proc_node_out,
            next_w, next_beside, node_across, node_round, node_both, to_core(node_round), mesh_send,
        ],
        scratch=[pltpu.VMEM((4 * (n_in + n_out), d), BF16)],
        flops=2 * half * d * 3 * d,
    )
    mid_beside = to_core(mid_half)
    halos = [lax.ppermute(v, "dom", entry[0]) for v, entry in zip(outgoing, plan)]
    (proc_pair,) = call(pair_kernel, [shape(k_in + k_out, d)], [proc_across, proc_round, halos[0]])
    (halo,) = call(concat_kernel, [shape(len(plan) * slots, d)], halos)
    halo_beside = to_core(halo)
    last_across, last_beside = to_chip(last_w), to_core(last_w)
    early = n_proc // 2
    table, pre, w_source, w_out = call(
        functools.partial(proc_first_kernel, k_in, n_in + n_out),
        [shape(d + 2 * mesh_rows, d), shape(early, d, F32), shape(d, d), shape(d, d)],
        [
            proc_emb, mid_half, mid_beside, proc_edges, next_w, next_beside, proc_pair, to_core(proc_pair),
        ],
        scratch=[pltpu.VMEM((4 * (k_in + k_out), d), BF16), pltpu.VMEM((mesh_rows, d), BF16)],
        flops=2 * early * d * (d + 2 * mesh_rows),
    )
    halo_rows = padded(len(plan) * slots)
    keep, give = call(
        functools.partial(proc_second_kernel, plan, slots, mesh_rows),
        [shape(half, d), shape(half, d)],
        [proc_emb, proc_edges, proc_edge_gain, table, pre, w_source, w_out, halo, halo_beside, proc_blocks],
        scratch=[
            pltpu.VMEM((halo_rows, d), BF16),
            pltpu.VMEM((n_proc, d), BF16),
            pltpu.VMEM((mesh_rows, d), F32),
        ],
        flops=2 * n_proc * d * (2 * d + mesh_rows + halo_rows),
        smem=1,
    )
    quarter = mesh_rows // 4
    mine, other = call(fold_kernel, [shape(quarter, d)] * 2, [keep, to_core(give)])
    (result,) = call(
        functools.partial(out_kernel, n_in, n_out),
        [shape(quarter, d)],
        [mid_half, mine, to_chip(other), proc_node_gain, last_w, last_beside, last_across, to_core(last_across)],
        scratch=[pltpu.VMEM((4 * (n_in + n_out), d), BF16)],
        flops=2 * quarter * d * 3 * d,
    )
    return result


def solution(mesh):
    placed = (
        P(("groups", "dom"), "sub"),
        P(("groups", "dom"), "sub"),
        P("dom", None, None),
        P("dom", None, None),
        P(None, ("dom", "sub")),
        P(None, ("dom", "sub")),
        P("dom"),
        P(None, ("dom", "sub")),
        P(None, ("dom", "sub")),
        P("dom"),
        P(),
        P(),
        P("sub", None),
        P("sub", None),
        P("sub", None),
        P("sub", None),
        P("sub", None),
        P("sub", None),
        P("sub", None),
        P("sub", None),
        P(),
        P(),
        P(),
        P(),
    )
    return jax.shard_map(
        local,
        mesh=mesh,
        in_specs=placed,
        out_specs=P(("groups", "dom", "sub"), None),
        check_vma=False,
    )
```

```python
import functools

import jax
import jax.numpy as jnp
from jax import lax
from jax.experimental import pallas as pl
from jax.experimental.pallas import tpu as pltpu
from jax.sharding import PartitionSpec as P

BLOCK = 128
OFFSETS = (-2, -1, 1, 2)
STEP = 512
GATHERED = 1024
LONG = 30 * 10**9
VMEM_BYTES = 24 * 1024 * 1024
I16 = jnp.int16
BF16 = jnp.bfloat16
F32 = jnp.float32


def silu(v):
    h = 0.5 * v
    return h + h * jnp.tanh(h)


def region_of(delta):
    return jnp.where(delta < 0, delta + 2, delta + 1)


def halo_plan(count):
    plan = []
    if count == 4:
        for bit in (1, 2, 3):
            pairs = [(d, d ^ bit) for d in range(4) if abs((d ^ bit) - d) <= 2]
            regions = [(OFFSETS.index((d ^ bit) - d) if abs((d ^ bit) - d) <= 2 else -1) for d in range(4)]
            plan.append((pairs, regions, regions))
    else:
        for region, offset in enumerate(OFFSETS):
            pairs = [(d, d + offset) for d in range(count) if 0 <= d + offset < count]
            plan.append((pairs, region, 3 - region))
    return plan


def by_index(choice, index):
    if isinstance(choice, int):
        return choice
    picked = jnp.int32(choice[0])
    for place in range(1, len(choice)):
        picked = jnp.where(index == place, choice[place], picked)
    return picked


def whole_refs(count):
    return [pl.BlockSpec(memory_space=pltpu.VMEM)] * count


def call(body, outs, args, scratch=(), flops=0, smem=0):
    moved = sum(a.size * a.dtype.itemsize for a in args) + sum(
        o.size * jnp.dtype(o.dtype).itemsize for o in outs
    )
    specs = whole_refs(len(args) - smem) + [pl.BlockSpec(memory_space=pltpu.SMEM)] * smem
    return pl.pallas_call(
        body,
        out_shape=tuple(outs),
        in_specs=specs,
        out_specs=tuple(whole_refs(len(outs))),
        scratch_shapes=list(scratch),
        compiler_params=pltpu.CompilerParams(vmem_limit_bytes=VMEM_BYTES),
        cost_estimate=pl.CostEstimate(flops=int(flops), bytes_accessed=int(moved), transcendentals=0),
    )(*args)


def dot(a, b):
    return jnp.dot(a, b, preferred_element_type=F32)


def dot_first(a, b):
    return lax.dot_general(a, b, (((0,), (0,)), ((), ())), preferred_element_type=F32)


def three_parts(v):
    a = v.astype(BF16)
    rest = v - a.astype(F32)
    b = rest.astype(BF16)
    c = (rest - b.astype(F32)).astype(BF16)
    return a, b, c


def embed_rows(geom, geo):
    a1, a2, a3 = three_parts(geom)
    b1, b2, b3 = three_parts(geo)
    left = jnp.concatenate([a1, a1, a2, a1, a2, a3], axis=0)
    right = jnp.concatenate([b1, b2, b1, b3, b2, b1], axis=0)
    return silu(dot_first(left, right)).astype(BF16)


def layer_norm(v):
    width = v.shape[-1]
    centered = v - jnp.sum(v, axis=-1, keepdims=True) * (1.0 / width)
    spread = jnp.sum(centered * centered, axis=-1, keepdims=True) * (1.0 / width)
    return centered * lax.rsqrt(spread + 1e-05)


def hot(cond):
    return jnp.where(cond, BF16(1), BF16(0))


def pick_rows(table, listed, rows=None):
    if rows is None:
        rows = lax.broadcasted_iota(I16, (table.shape[0], 1), 0)
    return dot_first(hot(rows == listed.astype(I16)), table).astype(BF16)


def pick_lists(plan, table, send, outs, rows=None):
    here = lax.axis_index("dom")
    for (pairs, sent, received), out in zip(plan, outs):
        region = jnp.maximum(by_index(sent, here), 0)
        out[...] = pick_rows(table, send[0, pl.ds(region, 1), :], rows)


def stack_into(out, parts):
    first = 0
    for part in parts:
        out[first : first + part.shape[0], :] = part[...]
        first += part.shape[0]


def begin_kernel(token):
    token[...] = jnp.zeros(token.shape, token.dtype)


def first_pack_kernel(plan, grid, send, w_in, w_out, token, half, *outs):
    place = 0
    for source in (w_in, w_out):
        rows = source.shape[0] // 2
        begin = pl.multiple_of(lax.axis_index("groups") * rows, 64)
        half[place : place + rows, :] = source[pl.ds(begin, rows), :]
        place += rows
    pick_lists(plan, grid[...], send, outs)


def embed_kernel(e_in, e_out, p_in, p_out, egeom, egeo, pgeom, pgeo, after, weights, eout, pout):
    stack_into(weights, (e_in, e_out, p_in, p_out))
    for geom, geo, out in ((egeom, egeo, eout), (pgeom, pgeo, pout)):
        for begin in range(0, out.shape[0], STEP):
            out[begin : begin + STEP, :] = embed_rows(geom[:, begin : begin + STEP], geo[...])


def cross_kernel(parts, weights, lat, lat_out, *crossing):
    lat_out[...] = lat[...]
    first = 0
    for stack, out in zip(parts, crossing):
        place = 0
        for rows in stack:
            half = rows // 2
            begin = pl.multiple_of(first + lax.axis_index("groups") * half, 64)
            out[place : place + half, :] = weights[pl.ds(begin, half), :]
            first, place = first + rows, place + half


def relay_kernel(across, round_, w_in, w_out, *refs):
    *parts, out, pair, packed = refs
    stack_into(out, parts)
    stack_into(pair, (across, round_))
    stack_into(packed, (w_in, w_out))


def hold_kernel(source, after, out):
    out[...] = source[...]


def concat_kernel(*refs):
    stack_into(refs[-1], refs[:-1])


def put_shard(target, source, first, step, part=0, parts=1):
    rows = target.shape[0] // (4 * parts)
    place = (lax.bitwise_xor(lax.axis_index("sub"), step) * parts + part) * rows
    target[pl.ds(pl.multiple_of(place, rows), rows), :] = source[first : first + rows, :]


def put_half(target, k, source, step, other):
    rows = target.shape[0] // 4
    which = lax.bitwise_xor(lax.axis_index("groups"), other)
    begin = lax.bitwise_xor(lax.axis_index("sub"), step) * rows
    for base, count in ((0, k // 2), (k // 2, (rows - k) // 2)):
        place = pl.multiple_of(begin + 2 * base + which * count, 64)
        target[pl.ds(place, count), :] = source[base : base + count, :]


def joined(stack, first, rows):
    step = stack.shape[0] // 4
    return jnp.concatenate([stack[k * step + first : k * step + first + rows, :] for k in range(4)], axis=0)


def halo_targets(plan, slots, node_rows, width):
    here = lax.axis_index("dom")
    lane = lax.broadcasted_iota(jnp.int32, (1, width), 1)
    target = jnp.full((1, width), -1, jnp.int32)
    for place, (pairs, sent, received) in enumerate(plan):
        region = by_index(received, here)
        first = jnp.where(region < 0, -4 * node_rows, node_rows + region * slots)
        inside = (lane >= place * slots) & (lane < (place + 1) * slots)
        target = jnp.where(inside, lane - place * slots + first, target)
    return target.astype(I16)


def columns(edges, first):
    pair = edges[:, first : first + STEP]
    zero = jnp.zeros((8 - pair.shape[0], STEP), jnp.int32)
    upright = jnp.transpose(jnp.concatenate([pair, zero], axis=0).astype(F32)).astype(jnp.int32).astype(I16)
    return upright[:, 0:1], upright[:, 1:2]


def edge_blocks(edges, live_edges, first_stage, w_out, messages, totals):
    count = edges.shape[1]
    row = lax.broadcasted_iota(I16, (totals.shape[0], 1), 0)
    quarter = lax.axis_index("sub")
    for first in range(0, count, STEP):
        hidden = silu(first_stage(first)).astype(BF16)
        message = layer_norm(dot(hidden, w_out))
        place = lax.broadcasted_iota(jnp.int32, (STEP, 1), 0) + (first + quarter * count)
        messages[first : first + STEP, :] = jnp.where(place < live_edges, message, 0.0).astype(BF16)
        done = first + STEP
        if done % GATHERED == 0 or done == count:
            begin = (first // GATHERED) * GATHERED
            collect = hot(row == edges[1:2, begin:done].astype(I16))
            part = dot(collect, messages[begin:done, :])
            if begin == 0:
                totals[...] = part
            else:
                totals[...] += part


def hand_out(totals, gain, keep, *give):
    rows = totals.shape[0] // 4
    core = lax.rem(lax.axis_index("sub"), 2)
    for half in range(2):
        kept = keep.at[pl.ds(half * rows, rows), :]
        given = give[0].at[pl.ds(half * rows, rows), :] if len(give) == 1 else give[half]
        for out, which in ((kept, core), (given, 1 - core)):
            place = pl.multiple_of((2 * half + which) * rows, rows)
            out[...] = (totals[pl.ds(place, rows), :] * gain[...]).astype(BF16)


def enc_kernel(
    plan, slots, grid_rows, mesh_rows, k_in, emb, edges, gain, l0, l1, l2, l3, o_in, o_out, b_in, b_out,
    across, round_, both, round_both, live, keep, give, give_more, own_mesh, full, stack, table, messages, totals,
):
    d = gain.shape[1]
    quarter = lax.axis_index("sub")
    width = l0.shape[1]
    for shard, step in zip((l0, l1, l2, l3), (0, 2, 1, 3)):
        place = pl.multiple_of(lax.bitwise_xor(quarter, step) * width, width)
        full[:, pl.ds(place, width)] = shard[...]
    step = k_in + d // 4
    for first, second, bit in ((o_in, o_out, 0), (b_in, b_out, 1)):
        place = lax.bitwise_xor(quarter, bit) * step
        stack[pl.ds(pl.multiple_of(place, 128), k_in), :] = first[...]
        stack[pl.ds(pl.multiple_of(place + k_in, 128), d // 4), :] = second[...]
    put_half(stack, k_in, across, 2, 0)
    put_half(stack, k_in, round_, 2, 1)
    put_half(stack, k_in, both, 3, 0)
    put_half(stack, k_in, round_both, 3, 1)
    rows = mesh_rows // 4
    core = lax.rem(quarter, 2)
    for half in range(2):
        place = pl.multiple_of(grid_rows + (2 * half + core) * rows, rows)
        own_mesh[half * rows : (half + 1) * rows, :] = full[pl.ds(place, rows), :]

    w_in = joined(stack, 0, k_in)
    halo_first, got = grid_rows + mesh_rows, full.shape[0] - grid_rows - mesh_rows
    table[:d, :] = w_in[:d, :]
    table[d : d + grid_rows, :] = dot(full[:grid_rows, :], w_in[d : 2 * d, :]).astype(BF16)
    base = d + grid_rows + mesh_rows
    table[d + grid_rows : base, :] = dot(full[grid_rows:halo_first, :], w_in[2 * d :, :]).astype(BF16)
    table[base : base + got, :] = dot(full[halo_first:, :], w_in[d : 2 * d, :]).astype(BF16)
    if base + got < table.shape[0]:
        table[base + got :, :] = jnp.zeros((table.shape[0] - base - got, d), BF16)
    targets = halo_targets(plan, slots, grid_rows, table.shape[0] - base)
    own = lax.broadcasted_iota(I16, (1, grid_rows), 1)
    mesh = lax.broadcasted_iota(I16, (1, mesh_rows), 1)

    def first_stage(first):
        senders, receivers = columns(edges, first)
        chosen = [emb[first : first + STEP, :], hot(own == senders), hot(mesh == receivers), hot(targets == senders)]
        return dot(jnp.concatenate(chosen, axis=1), table[...])

    edge_blocks(edges, live[0] * BLOCK, first_stage, joined(stack, k_in, d // 4), messages, totals)
    hand_out(totals, gain, keep, give, give_more)


def node_update(mesh, shares, w_in, w_out, gain):
    stacked = jnp.concatenate([mesh, shares], axis=1)
    hidden = silu(dot(stacked, w_in)).astype(BF16)
    update = layer_norm(dot(hidden, w_out)) * gain
    return (mesh.astype(F32) + update).astype(BF16)


def add(mine, theirs):
    return (mine.astype(F32) + theirs.astype(F32)).astype(BF16)


def add_kernel(mine, first, second, out):
    rows = first.shape[0]
    out[:rows, :] = add(mine[:rows, :], first[...])
    out[rows:, :] = add(mine[rows:, :], second[...])


def node_kernel(
    plan, k_in, k_out, mesh, mine, theirs, gain, w0, w1, w2, w3, w4, w5, send, out, *rest
):
    outs, stack = rest[:-1], rest[-1]
    put_shard(stack, w0, 0, 0)
    put_shard(stack, w1, 0, 1)
    put_half(stack, k_in, w2, 2, 0)
    put_half(stack, k_in, w3, 2, 1)
    put_half(stack, k_in, w4, 3, 0)
    put_half(stack, k_in, w5, 3, 1)
    w_in, w_out = joined(stack, 0, k_in), joined(stack, k_in, k_out)
    fresh = node_update(mesh[...], add(mine[...], theirs[...]), w_in, w_out, gain[...])
    out[...] = fresh
    half = fresh.shape[0] // 2
    core = lax.rem(lax.axis_index("sub"), 2)
    place = lax.broadcasted_iota(jnp.int32, (fresh.shape[0], 1), 0)
    rows = place + core * half + jnp.where(place < half, 0, half)
    pick_lists(plan, fresh, send, outs, rows.astype(I16))


def proc_first_kernel(
    k_in, first_row, emb, mine, theirs, edges, w0, w1, pair, pair_beside,
    table, pre, w_source, w_out, stack, full,
):
    d = full.shape[1]
    node_rows = full.shape[0]
    rows = node_rows // 4
    core = lax.rem(lax.axis_index("sub"), 2)
    for half in range(2):
        for part, which in ((mine, core), (theirs, 1 - core)):
            place = pl.multiple_of((2 * half + which) * rows, rows)
            full[pl.ds(place, rows), :] = part[half * rows : (half + 1) * rows, :]
    put_shard(stack, w0, first_row, 0)
    put_shard(stack, w1, first_row, 1)
    rows = pair.shape[0] // 2
    for other in range(2):
        put_half(stack, k_in, pair.at[pl.ds(other * rows, rows), :], 2, other)
        put_half(stack, k_in, pair_beside.at[pl.ds(other * rows, rows), :], 3, other)
    w_in = joined(stack, 0, k_in)
    w_out[...] = joined(stack, k_in, d // 4)
    w_source[...] = w_in[d : 2 * d, :]
    table[:d, :] = w_in[:d, :]
    table[d : d + node_rows, :] = dot(full[...], w_in[d : 2 * d, :]).astype(BF16)
    table[d + node_rows :, :] = dot(full[...], w_in[2 * d :, :]).astype(BF16)
    lane = lax.broadcasted_iota(I16, (1, node_rows), 1)
    for first in range(0, pre.shape[0], STEP):
        pre[first : first + STEP, :] = dot(own_chosen(emb, edges, lane, first), table[...])


def own_chosen(emb, edges, lane, first):
    senders, receivers = columns(edges, first)
    return jnp.concatenate([emb[first : first + STEP, :], hot(lane == senders), hot(lane == receivers)], axis=1)


def proc_second_kernel(
    plan, slots, node_rows, emb, edges, gain, table, pre, w_source, w_out, halo, halo_beside,
    live, keep, give, halo_table, messages, totals,
):
    d = pre.shape[1]
    got = halo[...] + halo_beside[...]
    halo_table[: got.shape[0], :] = dot(got, w_source[...]).astype(BF16)
    if got.shape[0] < halo_table.shape[0]:
        halo_table[got.shape[0] :, :] = jnp.zeros((halo_table.shape[0] - got.shape[0], d), BF16)
    targets = halo_targets(plan, slots, node_rows, halo_table.shape[0])
    lane = lax.broadcasted_iota(I16, (1, node_rows), 1)

    def first_stage(first):
        senders, receivers = columns(edges, first)
        remote = dot(hot(targets == senders), halo_table[...])
        if first < pre.shape[0]:
            return pre[first : first + STEP, :] + remote
        return dot(own_chosen(emb, edges, lane, first), table[...]) + remote

    edge_blocks(edges, live[0] * BLOCK, first_stage, w_out[...], messages, totals)
    hand_out(totals, gain, keep, give)


def fold_kernel(mine, theirs, keep, give):
    rows = mine.shape[0] // 2
    chip = lax.div(lax.axis_index("sub"), 2)
    for out, which in ((keep, chip), (give, 1 - chip)):
        place = pl.multiple_of(which * rows, rows)
        out[...] = add(mine[pl.ds(place, rows), :], theirs[pl.ds(place, rows), :])


def out_kernel(k_in, k_out, middle, mine, theirs, gain, w0, w1, w2, w3, out, stack):
    rows = mine.shape[0]
    chip = lax.div(lax.axis_index("sub"), 2)
    mesh = middle[pl.ds(pl.multiple_of(chip * rows, rows), rows), :]
    for shard, bit in zip((w0, w1, w2, w3), (0, 1, 2, 3)):
        put_shard(stack, shard, 0, bit)
    w_in, w_out = joined(stack, 0, k_in), joined(stack, k_in, k_out)
    out[...] = node_update(mesh, add(mine[...], theirs[...]), w_in, w_out, gain[...])


def to_chip(v):
    return lax.ppermute(v, "sub", [(i, i ^ 2) for i in range(4)])


def to_core(v):
    return lax.ppermute(v, "sub", [(i, i ^ 1) for i in range(4)])


def to_group(v):
    count = lax.axis_size("groups")
    return lax.ppermute(v, "groups", [(i, count - 1 - i) for i in range(count)])


def shape(rows, width, dtype=BF16):
    return jax.ShapeDtypeStruct((rows, width), dtype)


def call_hold(source, after):
    return call(hold_kernel, [shape(*source.shape)], [source, after])[0]


def padded(rows):
    return -(-rows // 128) * 128


def local(
    grid_lat,
    mesh_lat,
    grid_send,
    mesh_send,
    enc_edges,
    enc_geom,
    enc_blocks,
    proc_edges,
    proc_geom,
    proc_blocks,
    enc_geo,
    proc_geo,
    enc_edge_in,
    enc_edge_out,
    enc_node_in,
    enc_node_out,
    proc_edge_in,
    proc_edge_out,
    proc_node_in,
    proc_node_out,
    enc_edge_gain,
    enc_node_gain,
    proc_edge_gain,
    proc_node_gain,
):
    plan = halo_plan(lax.axis_size("dom"))
    d = enc_geo.shape[1]
    grid_rows, mesh_rows = grid_lat.shape[0], mesh_lat.shape[0]
    n_enc, n_proc = enc_edges.shape[1], proc_edges.shape[1]
    enc_edge_gain, enc_node_gain, proc_edge_gain, proc_node_gain = (
        g.reshape(1, d) for g in (enc_edge_gain, enc_node_gain, proc_edge_gain, proc_node_gain)
    )
    k_in, k_out = enc_edge_in.shape[0], enc_edge_out.shape[0]
    n_in, n_out = enc_node_in.shape[0], enc_node_out.shape[0]
    width = grid_lat.shape[1]

    slots = grid_send.shape[2]
    (token,) = call(begin_kernel, [shape(16, 128)], [], flops=LONG)
    edge_half, *outgoing = call(
        functools.partial(first_pack_kernel, plan),
        [shape((k_in + k_out) // 2, d)] + [shape(slots, width)] * len(plan),
        [grid_lat, grid_send, enc_edge_in, enc_edge_out, token],
    )
    edge_across = to_chip(edge_half)
    halos = [lax.ppermute(v, "dom", entry[0]) for v, entry in zip(outgoing, plan)]
    got = len(plan) * slots
    (lat,) = call(
        concat_kernel,
        [shape(grid_rows + mesh_rows + got, width)],
        [grid_lat, mesh_lat, *halos],
    )
    lat_across = to_chip(lat)
    lat_beside = to_core(lat)
    edge_beside = [to_core(enc_edge_in), to_core(enc_edge_out)]
    edge_round = to_group(edge_across)
    next_w, enc_emb, proc_emb = call(
        embed_kernel,
        [shape(n_in + n_out + k_in + k_out, d), shape(n_enc, d), shape(n_proc, d)],
        [
            enc_node_in, enc_node_out, proc_edge_in, proc_edge_out,
            enc_geom, enc_geo, proc_geom, proc_geo, lat,
        ],
        flops=2 * (n_enc + n_proc) * d * 128,
    )
    lat_sent, node_half, proc_half = call(
        functools.partial(cross_kernel, ((n_in, n_out), (k_in, k_out))),
        [shape(lat.shape[0], width), shape((n_in + n_out) // 2, d), shape((k_in + k_out) // 2, d)],
        [next_w, lat_across],
    )
    lat_both = to_core(lat_sent)
    node_came, proc_came = to_chip(node_half), to_chip(proc_half)
    next_beside = to_core(next_w)

    halo_rows = padded(got)
    half = mesh_rows // 2
    keep, give, give_more, own_mesh = call(
        functools.partial(enc_kernel, plan, slots, grid_rows, mesh_rows, k_in),
        [shape(half, d), shape(half // 2, d), shape(half // 2, d), shape(half, d)],
        [
            enc_emb, enc_edges, enc_edge_gain, lat, lat_across, lat_beside, lat_both,
            enc_edge_in, enc_edge_out, *edge_beside,
            edge_across, edge_round, to_core(edge_across), to_core(edge_round), enc_blocks,
        ],
        scratch=[
            pltpu.VMEM((grid_rows + mesh_rows + got, d), BF16),
            pltpu.VMEM((4 * (k_in + k_out), d), BF16),
            pltpu.VMEM((d + grid_rows + mesh_rows + halo_rows, d), BF16),
            pltpu.VMEM((n_enc, d), BF16),
            pltpu.VMEM((mesh_rows, d), F32),
        ],
        flops=2 * n_enc * d * (3 * d + grid_rows + mesh_rows + halo_rows),
        smem=1,
    )
    (chip_sum,) = call(add_kernel, [shape(half, d)], [keep, to_core(give), to_core(give_more)])
    node_across, proc_across = call_hold(node_came, chip_sum), call_hold(proc_came, chip_sum)
    node_round, proc_round = to_group(node_across), to_group(proc_across)
    node_both = to_core(node_across)
    slots = mesh_send.shape[2]
    mid_half, *outgoing = call(
        functools.partial(node_kernel, plan, n_in, n_out),
        [shape(half, d)] + [shape(slots, d)] * len(plan),
        [
            own_mesh, chip_sum, to_chip(chip_sum), enc_node_gain,
            next_w, next_beside, node_across, node_round, node_both, to_core(node_round), mesh_send,
        ],
        scratch=[pltpu.VMEM((4 * (n_in + n_out), d), BF16)],
        flops=2 * half * d * 3 * d,
    )
    mid_beside = to_core(mid_half)
    halos = [lax.ppermute(v, "dom", entry[0]) for v, entry in zip(outgoing, plan)]
    halo, proc_pair, last_w = call(
        relay_kernel,
        [shape(len(plan) * slots, d), shape(k_in + k_out, d), shape(n_in + n_out, d)],
        [proc_across, proc_round, proc_node_in, proc_node_out, *halos],
    )
    halo_beside = to_core(halo)
    last_across, last_beside = to_chip(last_w), to_core(last_w)
    early = n_proc // 2
    table, pre, w_source, w_out = call(
        functools.partial(proc_first_kernel, k_in, n_in + n_out),
        [shape(d + 2 * mesh_rows, d), shape(early, d, F32), shape(d, d), shape(d, d)],
        [
            proc_emb, mid_half, mid_beside, proc_edges, next_w, next_beside, proc_pair, to_core(proc_pair),
        ],
        scratch=[pltpu.VMEM((4 * (k_in + k_out), d), BF16), pltpu.VMEM((mesh_rows, d), BF16)],
        flops=2 * early * d * (d + 2 * mesh_rows),
    )
    halo_rows = padded(len(plan) * slots)
    keep, give = call(
        functools.partial(proc_second_kernel, plan, slots, mesh_rows),
        [shape(half, d), shape(half, d)],
        [proc_emb, proc_edges, proc_edge_gain, table, pre, w_source, w_out, halo, halo_beside, proc_blocks],
        scratch=[
            pltpu.VMEM((halo_rows, d), BF16),
            pltpu.VMEM((n_proc, d), BF16),
            pltpu.VMEM((mesh_rows, d), F32),
        ],
        flops=2 * n_proc * d * (2 * d + mesh_rows + halo_rows),
        smem=1,
    )
    quarter = mesh_rows // 4
    mine, other = call(fold_kernel, [shape(quarter, d)] * 2, [keep, to_core(give)])
    (result,) = call(
        functools.partial(out_kernel, n_in, n_out),
        [shape(quarter, d)],
        [mid_half, mine, to_chip(other), proc_node_gain, last_w, last_beside, last_across, to_core(last_across)],
        scratch=[pltpu.VMEM((4 * (n_in + n_out), d), BF16)],
        flops=2 * quarter * d * 3 * d,
    )
    return result


def solution(mesh):
    placed = (
        P(("groups", "dom"), "sub"),
        P(("groups", "dom"), "sub"),
        P("dom", None, None),
        P("dom", None, None),
        P(None, ("dom", "sub")),
        P(None, ("dom", "sub")),
        P("dom"),
        P(None, ("dom", "sub")),
        P(None, ("dom", "sub")),
        P("dom"),
        P(),
        P(),
        P("sub", None),
        P("sub", None),
        P("sub", None),
        P("sub", None),
        P("sub", None),
        P("sub", None),
        P("sub", None),
        P("sub", None),
        P(),
        P(),
        P(),
        P(),
    )
    return jax.shard_map(
        local,
        mesh=mesh,
        in_specs=placed,
        out_specs=P(("groups", "dom", "sub"), None),
        check_vma=False,
    )
```

```python
import functools

import jax
import jax.numpy as jnp
from jax import lax
from jax.experimental import pallas as pl
from jax.experimental.pallas import tpu as pltpu
from jax.sharding import PartitionSpec as P

BLOCK = 128
OFFSETS = (-2, -1, 1, 2)
STEP = 512
GATHERED = 1024
LONG = 30 * 10**9
VMEM_BYTES = 24 * 1024 * 1024
I16 = jnp.int16
BF16 = jnp.bfloat16
F32 = jnp.float32


def silu(v):
    h = 0.5 * v
    return h + h * jnp.tanh(h)


def region_of(delta):
    return jnp.where(delta < 0, delta + 2, delta + 1)


def halo_plan(count):
    plan = []
    if count == 4:
        for bit in (1, 2, 3):
            pairs = [(d, d ^ bit) for d in range(4) if abs((d ^ bit) - d) <= 2]
            regions = [(OFFSETS.index((d ^ bit) - d) if abs((d ^ bit) - d) <= 2 else -1) for d in range(4)]
            plan.append((pairs, regions, regions))
    else:
        for region, offset in enumerate(OFFSETS):
            pairs = [(d, d + offset) for d in range(count) if 0 <= d + offset < count]
            plan.append((pairs, region, 3 - region))
    return plan


def by_index(choice, index):
    if isinstance(choice, int):
        return choice
    picked = jnp.int32(choice[0])
    for place in range(1, len(choice)):
        picked = jnp.where(index == place, choice[place], picked)
    return picked


def whole_refs(count):
    return [pl.BlockSpec(memory_space=pltpu.VMEM)] * count


def call(body, outs, args, scratch=(), flops=0, smem=0):
    moved = sum(a.size * a.dtype.itemsize for a in args) + sum(
        o.size * jnp.dtype(o.dtype).itemsize for o in outs
    )
    specs = whole_refs(len(args) - smem) + [pl.BlockSpec(memory_space=pltpu.SMEM)] * smem
    return pl.pallas_call(
        body,
        out_shape=tuple(outs),
        in_specs=specs,
        out_specs=tuple(whole_refs(len(outs))),
        scratch_shapes=list(scratch),
        compiler_params=pltpu.CompilerParams(vmem_limit_bytes=VMEM_BYTES),
        cost_estimate=pl.CostEstimate(flops=int(flops), bytes_accessed=int(moved), transcendentals=0),
    )(*args)


def dot(a, b):
    return jnp.dot(a, b, preferred_element_type=F32)


def dot_first(a, b):
    return lax.dot_general(a, b, (((0,), (0,)), ((), ())), preferred_element_type=F32)


def three_parts(v):
    a = v.astype(BF16)
    rest = v - a.astype(F32)
    b = rest.astype(BF16)
    c = (rest - b.astype(F32)).astype(BF16)
    return a, b, c


def embed_rows(geom, geo):
    a1, a2, a3 = three_parts(geom)
    b1, b2, b3 = three_parts(geo)
    left = jnp.concatenate([a1, a1, a2, a1, a2, a3], axis=0)
    right = jnp.concatenate([b1, b2, b1, b3, b2, b1], axis=0)
    return silu(dot_first(left, right)).astype(BF16)


def layer_norm(v):
    width = v.shape[-1]
    centered = v - jnp.sum(v, axis=-1, keepdims=True) * (1.0 / width)
    spread = jnp.sum(centered * centered, axis=-1, keepdims=True) * (1.0 / width)
    return centered * lax.rsqrt(spread + 1e-05)


def hot(cond):
    return jnp.where(cond, BF16(1), BF16(0))


def pick_rows(table, listed, rows=None):
    if rows is None:
        rows = lax.broadcasted_iota(I16, (table.shape[0], 1), 0)
    return dot_first(hot(rows == listed.astype(I16)), table).astype(BF16)


def pick_lists(plan, table, send, outs, rows=None):
    here = lax.axis_index("dom")
    for (pairs, sent, received), out in zip(plan, outs):
        region = jnp.maximum(by_index(sent, here), 0)
        out[...] = pick_rows(table, send[0, pl.ds(region, 1), :], rows)


def stack_into(out, parts):
    first = 0
    for part in parts:
        out[first : first + part.shape[0], :] = part[...]
        first += part.shape[0]


def begin_kernel(token):
    token[...] = jnp.zeros(token.shape, token.dtype)


def first_pack_kernel(plan, grid, send, w_in, w_out, token, half, *outs):
    place = 0
    for source in (w_in, w_out):
        rows = source.shape[0] // 2
        begin = pl.multiple_of(lax.axis_index("groups") * rows, 64)
        half[place : place + rows, :] = source[pl.ds(begin, rows), :]
        place += rows
    pick_lists(plan, grid[...], send, outs)


def embed_kernel(e_in, e_out, p_in, p_out, egeom, egeo, pgeom, pgeo, after, weights, eout, pout):
    stack_into(weights, (e_in, e_out, p_in, p_out))
    for geom, geo, out in ((egeom, egeo, eout), (pgeom, pgeo, pout)):
        for begin in range(0, out.shape[0], STEP):
            out[begin : begin + STEP, :] = embed_rows(geom[:, begin : begin + STEP], geo[...])


def cross_kernel(parts, weights, lat, lat_out, *crossing):
    lat_out[...] = lat[...]
    first = 0
    for stack, out in zip(parts, crossing):
        place = 0
        for rows in stack:
            half = rows // 2
            begin = pl.multiple_of(first + lax.axis_index("groups") * half, 64)
            out[place : place + half, :] = weights[pl.ds(begin, half), :]
            first, place = first + rows, place + half


def hold_kernel(source, after, out):
    out[...] = source[...]


def concat_kernel(*refs):
    stack_into(refs[-1], refs[:-1])


def put_shard(target, source, first, step, part=0, parts=1):
    rows = target.shape[0] // (4 * parts)
    place = (lax.bitwise_xor(lax.axis_index("sub"), step) * parts + part) * rows
    target[pl.ds(pl.multiple_of(place, rows), rows), :] = source[first : first + rows, :]


def put_half(target, k, source, step, other):
    rows = target.shape[0] // 4
    which = lax.bitwise_xor(lax.axis_index("groups"), other)
    begin = lax.bitwise_xor(lax.axis_index("sub"), step) * rows
    for base, count in ((0, k // 2), (k // 2, (rows - k) // 2)):
        place = pl.multiple_of(begin + 2 * base + which * count, 64)
        target[pl.ds(place, count), :] = source[base : base + count, :]


def joined(stack, first, rows):
    step = stack.shape[0] // 4
    return jnp.concatenate([stack[k * step + first : k * step + first + rows, :] for k in range(4)], axis=0)


def halo_targets(firsts, slots, width):
    lane = lax.broadcasted_iota(jnp.int32, (1, width), 1)
    target = jnp.full((1, width), -1, jnp.int32)
    for place, first in enumerate(firsts):
        inside = (lane >= place * slots) & (lane < (place + 1) * slots)
        target = jnp.where(inside, lane - place * slots + first, target)
    return target.astype(I16)


def columns(edges, first):
    pair = edges[:, first : first + STEP]
    zero = jnp.zeros((8 - pair.shape[0], STEP), jnp.int32)
    upright = jnp.transpose(jnp.concatenate([pair, zero], axis=0).astype(F32)).astype(jnp.int32).astype(I16)
    return upright[:, 0:1], upright[:, 1:2]


def edge_blocks(edges, live_edges, first_stage, w_out, messages, totals):
    count = edges.shape[1]
    row = lax.broadcasted_iota(I16, (totals.shape[0], 1), 0)
    quarter = lax.axis_index("sub")
    for first in range(0, count, STEP):
        hidden = silu(first_stage(first)).astype(BF16)
        message = layer_norm(dot(hidden, w_out))
        place = lax.broadcasted_iota(jnp.int32, (STEP, 1), 0) + (first + quarter * count)
        messages[first : first + STEP, :] = jnp.where(place < live_edges, message, 0.0).astype(BF16)
        done = first + STEP
        if done % GATHERED == 0 or done == count:
            begin = (first // GATHERED) * GATHERED
            collect = hot(row == edges[1:2, begin:done].astype(I16))
            part = dot(collect, messages[begin:done, :])
            if begin == 0:
                totals[...] = part
            else:
                totals[...] += part


def hand_out(totals, gain, keep, *give):
    rows = totals.shape[0] // 4
    core = lax.rem(lax.axis_index("sub"), 2)
    for half in range(2):
        kept = keep.at[pl.ds(half * rows, rows), :]
        given = give[0].at[pl.ds(half * rows, rows), :] if len(give) == 1 else give[half]
        for out, which in ((kept, core), (given, 1 - core)):
            place = pl.multiple_of((2 * half + which) * rows, rows)
            out[...] = (totals[pl.ds(place, rows), :] * gain[...]).astype(BF16)


def enc_kernel(
    plan, slots, grid_rows, mesh_rows, k_in, emb, edges, gain, l0, l1, l2, l3, o_in, o_out, b_in, b_out,
    across, round_, both, round_both, live, keep, give, give_more, own_mesh, full, stack, table, messages, totals,
):
    d = gain.shape[1]
    quarter = lax.axis_index("sub")
    width = l0.shape[1]
    for shard, step in zip((l0, l1, l2, l3), (0, 2, 1, 3)):
        place = pl.multiple_of(lax.bitwise_xor(quarter, step) * width, width)
        full[:, pl.ds(place, width)] = shard[...]
    step = k_in + d // 4
    for first, second, bit in ((o_in, o_out, 0), (b_in, b_out, 1)):
        place = lax.bitwise_xor(quarter, bit) * step
        stack[pl.ds(pl.multiple_of(place, 128), k_in), :] = first[...]
        stack[pl.ds(pl.multiple_of(place + k_in, 128), d // 4), :] = second[...]
    put_half(stack, k_in, across, 2, 0)
    put_half(stack, k_in, round_, 2, 1)
    put_half(stack, k_in, both, 3, 0)
    put_half(stack, k_in, round_both, 3, 1)
    rows = mesh_rows // 4
    core = lax.rem(quarter, 2)
    for half in range(2):
        place = pl.multiple_of(grid_rows + (2 * half + core) * rows, rows)
        own_mesh[half * rows : (half + 1) * rows, :] = full[pl.ds(place, rows), :]

    w_in = joined(stack, 0, k_in)
    halo_first, got = grid_rows + mesh_rows, full.shape[0] - grid_rows - mesh_rows
    table[:d, :] = w_in[:d, :]
    table[d : d + grid_rows, :] = dot(full[:grid_rows, :], w_in[d : 2 * d, :]).astype(BF16)
    base = d + grid_rows + mesh_rows
    table[d + grid_rows : base, :] = dot(full[grid_rows:halo_first, :], w_in[2 * d :, :]).astype(BF16)
    table[base : base + got, :] = dot(full[halo_first:, :], w_in[d : 2 * d, :]).astype(BF16)
    if base + got < table.shape[0]:
        table[base + got :, :] = jnp.zeros((table.shape[0] - base - got, d), BF16)
    here = lax.axis_index("dom")
    firsts = []
    for pairs, sent, received in plan:
        region = by_index(received, here)
        firsts.append(jnp.where(region < 0, -4 * grid_rows, grid_rows + region * slots))
    targets = halo_targets(firsts, slots, table.shape[0] - base)
    own = lax.broadcasted_iota(I16, (1, grid_rows), 1)
    mesh = lax.broadcasted_iota(I16, (1, mesh_rows), 1)

    def first_stage(first):
        senders, receivers = columns(edges, first)
        chosen = [emb[first : first + STEP, :], hot(own == senders), hot(mesh == receivers), hot(targets == senders)]
        return dot(jnp.concatenate(chosen, axis=1), table[...])

    edge_blocks(edges, live[0] * BLOCK, first_stage, joined(stack, k_in, d // 4), messages, totals)
    hand_out(totals, gain, keep, give, give_more)


def node_update(mesh, shares, w_in, w_out, gain):
    stacked = jnp.concatenate([mesh, shares], axis=1)
    hidden = silu(dot(stacked, w_in)).astype(BF16)
    update = layer_norm(dot(hidden, w_out)) * gain
    return (mesh.astype(F32) + update).astype(BF16)


def add(mine, theirs):
    return (mine.astype(F32) + theirs.astype(F32)).astype(BF16)


def add_kernel(mine, first, second, out):
    rows = first.shape[0]
    out[:rows, :] = add(mine[:rows, :], first[...])
    out[rows:, :] = add(mine[rows:, :], second[...])


def node_kernel(
    k_in, k_out, mesh, mine, theirs, gain, n_in, n_out, w0, w1, w2, w3, w4, w5, out, packed, stack
):
    put_shard(stack, w0, 0, 0)
    put_shard(stack, w1, 0, 1)
    put_half(stack, k_in, w2, 2, 0)
    put_half(stack, k_in, w3, 2, 1)
    put_half(stack, k_in, w4, 3, 0)
    put_half(stack, k_in, w5, 3, 1)
    w_in, w_out = joined(stack, 0, k_in), joined(stack, k_in, k_out)
    fresh = node_update(mesh[...], add(mine[...], theirs[...]), w_in, w_out, gain[...])
    out[...] = fresh
    stack_into(packed, (n_in, n_out))


def middle_kernel(mine, theirs, send, across, round_, full, listed, pair):
    stack_into(pair, (across, round_))
    rows = mine.shape[0] // 2
    quarter = lax.axis_index("sub")
    core = lax.rem(quarter, 2)
    for half in range(2):
        for part, which in ((mine, core), (theirs, 1 - core)):
            place = pl.multiple_of((2 * half + which) * rows, rows)
            full[pl.ds(place, rows), :] = part[half * rows : (half + 1) * rows, :]
    listed[...] = pick_rows(full[...], send[0, pl.ds(quarter, 1), :])


def proc_first_kernel(
    k_in, first_row, emb, full, edges, w0, w1, pair, pair_beside, table, pre, w_source, w_out, stack
):
    d = full.shape[1]
    node_rows = full.shape[0]
    put_shard(stack, w0, first_row, 0)
    put_shard(stack, w1, first_row, 1)
    rows = pair.shape[0] // 2
    for other in range(2):
        put_half(stack, k_in, pair.at[pl.ds(other * rows, rows), :], 2, other)
        put_half(stack, k_in, pair_beside.at[pl.ds(other * rows, rows), :], 3, other)
    w_in = joined(stack, 0, k_in)
    w_out[...] = joined(stack, k_in, d // 4)
    w_source[...] = w_in[d : 2 * d, :]
    table[:d, :] = w_in[:d, :]
    table[d : d + node_rows, :] = dot(full[...], w_in[d : 2 * d, :]).astype(BF16)
    table[d + node_rows :, :] = dot(full[...], w_in[2 * d :, :]).astype(BF16)
    lane = lax.broadcasted_iota(I16, (1, node_rows), 1)
    for first in range(0, pre.shape[0], STEP):
        pre[first : first + STEP, :] = dot(own_chosen(emb, edges, lane, first), table[...])


def own_chosen(emb, edges, lane, first):
    senders, receivers = columns(edges, first)
    return jnp.concatenate([emb[first : first + STEP, :], hot(lane == senders), hot(lane == receivers)], axis=1)


def proc_second_kernel(
    slots, node_rows, emb, edges, gain, table, pre, w_source, w_out, halo, halo_beside,
    live, keep, give, halo_table, messages, totals,
):
    d = pre.shape[1]
    got = jnp.concatenate([halo[...], halo_beside[...]], axis=0)
    halo_table[: got.shape[0], :] = dot(got, w_source[...]).astype(BF16)
    if got.shape[0] < halo_table.shape[0]:
        halo_table[got.shape[0] :, :] = jnp.zeros((halo_table.shape[0] - got.shape[0], d), BF16)
    quarter = lax.axis_index("sub")
    firsts = [node_rows + (3 - lax.bitwise_xor(quarter, step)) * slots for step in (0, 2, 1, 3)]
    targets = halo_targets(firsts, slots, halo_table.shape[0])
    lane = lax.broadcasted_iota(I16, (1, node_rows), 1)

    def first_stage(first):
        senders, receivers = columns(edges, first)
        remote = dot(hot(targets == senders), halo_table[...])
        if first < pre.shape[0]:
            return pre[first : first + STEP, :] + remote
        return dot(own_chosen(emb, edges, lane, first), table[...]) + remote

    edge_blocks(edges, live[0] * BLOCK, first_stage, w_out[...], messages, totals)
    hand_out(totals, gain, keep, give)


def fold_kernel(mine, theirs, keep, give):
    rows = mine.shape[0] // 2
    chip = lax.div(lax.axis_index("sub"), 2)
    for out, which in ((keep, chip), (give, 1 - chip)):
        place = pl.multiple_of(which * rows, rows)
        out[...] = add(mine[pl.ds(place, rows), :], theirs[pl.ds(place, rows), :])


def out_kernel(k_in, k_out, middle, mine, theirs, gain, w0, w1, w2, w3, out, stack):
    rows = mine.shape[0]
    chip = lax.div(lax.axis_index("sub"), 2)
    mesh = middle[pl.ds(pl.multiple_of(chip * rows, rows), rows), :]
    for shard, bit in zip((w0, w1, w2, w3), (0, 1, 2, 3)):
        put_shard(stack, shard, 0, bit)
    w_in, w_out = joined(stack, 0, k_in), joined(stack, k_in, k_out)
    out[...] = node_update(mesh, add(mine[...], theirs[...]), w_in, w_out, gain[...])


def to_chip(v):
    return lax.ppermute(v, "sub", [(i, i ^ 2) for i in range(4)])


def to_offset(v, step):
    count, parts = lax.axis_size("dom"), lax.axis_size("sub")
    pairs = [
        (d * parts + s, (d + offset) * parts + (s ^ step))
        for d in range(count)
        for s, offset in enumerate(OFFSETS)
        if 0 <= d + offset < count
    ]
    return lax.ppermute(v, ("dom", "sub"), pairs)


def to_core(v):
    return lax.ppermute(v, "sub", [(i, i ^ 1) for i in range(4)])


def to_group(v):
    count = lax.axis_size("groups")
    return lax.ppermute(v, "groups", [(i, count - 1 - i) for i in range(count)])


def shape(rows, width, dtype=BF16):
    return jax.ShapeDtypeStruct((rows, width), dtype)


def call_hold(source, after):
    return call(hold_kernel, [shape(*source.shape)], [source, after])[0]


def padded(rows):
    return -(-rows // 128) * 128


def local(
    grid_lat,
    mesh_lat,
    grid_send,
    mesh_send,
    enc_edges,
    enc_geom,
    enc_blocks,
    proc_edges,
    proc_geom,
    proc_blocks,
    enc_geo,
    proc_geo,
    enc_edge_in,
    enc_edge_out,
    enc_node_in,
    enc_node_out,
    proc_edge_in,
    proc_edge_out,
    proc_node_in,
    proc_node_out,
    enc_edge_gain,
    enc_node_gain,
    proc_edge_gain,
    proc_node_gain,
):
    plan = halo_plan(lax.axis_size("dom"))
    d = enc_geo.shape[1]
    grid_rows, mesh_rows = grid_lat.shape[0], mesh_lat.shape[0]
    n_enc, n_proc = enc_edges.shape[1], proc_edges.shape[1]
    enc_edge_gain, enc_node_gain, proc_edge_gain, proc_node_gain = (
        g.reshape(1, d) for g in (enc_edge_gain, enc_node_gain, proc_edge_gain, proc_node_gain)
    )
    k_in, k_out = enc_edge_in.shape[0], enc_edge_out.shape[0]
    n_in, n_out = enc_node_in.shape[0], enc_node_out.shape[0]
    width = grid_lat.shape[1]

    slots = grid_send.shape[2]
    (token,) = call(begin_kernel, [shape(16, 128)], [], flops=LONG)
    edge_half, *outgoing = call(
        functools.partial(first_pack_kernel, plan),
        [shape((k_in + k_out) // 2, d)] + [shape(slots, width)] * len(plan),
        [grid_lat, grid_send, enc_edge_in, enc_edge_out, token],
    )
    edge_across = to_chip(edge_half)
    halos = [lax.ppermute(v, "dom", entry[0]) for v, entry in zip(outgoing, plan)]
    got = len(plan) * slots
    (lat,) = call(
        concat_kernel,
        [shape(grid_rows + mesh_rows + got, width)],
        [grid_lat, mesh_lat, *halos],
    )
    lat_across = to_chip(lat)
    lat_beside = to_core(lat)
    edge_beside = [to_core(enc_edge_in), to_core(enc_edge_out)]
    edge_round = to_group(edge_across)
    next_w, enc_emb, proc_emb = call(
        embed_kernel,
        [shape(n_in + n_out + k_in + k_out, d), shape(n_enc, d), shape(n_proc, d)],
        [
            enc_node_in, enc_node_out, proc_edge_in, proc_edge_out,
            enc_geom, enc_geo, proc_geom, proc_geo, lat,
        ],
        flops=2 * (n_enc + n_proc) * d * 128,
    )
    lat_sent, node_half, proc_half = call(
        functools.partial(cross_kernel, ((n_in, n_out), (k_in, k_out))),
        [shape(lat.shape[0], width), shape((n_in + n_out) // 2, d), shape((k_in + k_out) // 2, d)],
        [next_w, lat_across],
    )
    lat_both = to_core(lat_sent)
    node_came, proc_came = to_chip(node_half), to_chip(proc_half)
    next_beside = to_core(next_w)

    halo_rows = padded(got)
    half = mesh_rows // 2
    keep, give, give_more, own_mesh = call(
        functools.partial(enc_kernel, plan, slots, grid_rows, mesh_rows, k_in),
        [shape(half, d), shape(half // 2, d), shape(half // 2, d), shape(half, d)],
        [
            enc_emb, enc_edges, enc_edge_gain, lat, lat_across, lat_beside, lat_both,
            enc_edge_in, enc_edge_out, *edge_beside,
            edge_across, edge_round, to_core(edge_across), to_core(edge_round), enc_blocks,
        ],
        scratch=[
            pltpu.VMEM((grid_rows + mesh_rows + got, d), BF16),
            pltpu.VMEM((4 * (k_in + k_out), d), BF16),
            pltpu.VMEM((d + grid_rows + mesh_rows + halo_rows, d), BF16),
            pltpu.VMEM((n_enc, d), BF16),
            pltpu.VMEM((mesh_rows, d), F32),
        ],
        flops=2 * n_enc * d * (3 * d + grid_rows + mesh_rows + halo_rows),
        smem=1,
    )
    (chip_sum,) = call(add_kernel, [shape(half, d)], [keep, to_core(give), to_core(give_more)])
    node_across, proc_across = call_hold(node_came, chip_sum), call_hold(proc_came, chip_sum)
    node_round, proc_round = to_group(node_across), to_group(proc_across)
    node_both = to_core(node_across)
    slots = mesh_send.shape[2]
    mid_half, last_w = call(
        functools.partial(node_kernel, n_in, n_out),
        [shape(half, d), shape(n_in + n_out, d)],
        [
            own_mesh, chip_sum, to_chip(chip_sum), enc_node_gain, proc_node_in, proc_node_out,
            next_w, next_beside, node_across, node_round, node_both, to_core(node_round),
        ],
        scratch=[pltpu.VMEM((4 * (n_in + n_out), d), BF16)],
        flops=2 * half * d * 3 * d,
    )
    mid, listed, proc_pair = call(
        middle_kernel,
        [shape(mesh_rows, d), shape(slots, d), shape(k_in + k_out, d)],
        [mid_half, to_core(mid_half), mesh_send, proc_across, proc_round],
        flops=2 * slots * mesh_rows * d,
    )
    (halo,) = call(concat_kernel, [shape(2 * slots, d)], [to_offset(listed, 0), to_offset(listed, 2)])
    halo_beside = to_core(halo)
    last_across, last_beside = to_chip(last_w), to_core(last_w)
    early = n_proc // 2
    table, pre, w_source, w_out = call(
        functools.partial(proc_first_kernel, k_in, n_in + n_out),
        [shape(d + 2 * mesh_rows, d), shape(early, d, F32), shape(d, d), shape(d, d)],
        [
            proc_emb, mid, proc_edges, next_w, next_beside, proc_pair, to_core(proc_pair),
        ],
        scratch=[pltpu.VMEM((4 * (k_in + k_out), d), BF16)],
        flops=2 * early * d * (d + 2 * mesh_rows),
    )
    halo_rows = padded(4 * slots)
    keep, give = call(
        functools.partial(proc_second_kernel, slots, mesh_rows),
        [shape(half, d), shape(half, d)],
        [proc_emb, proc_edges, proc_edge_gain, table, pre, w_source, w_out, halo, halo_beside, proc_blocks],
        scratch=[
            pltpu.VMEM((halo_rows, d), BF16),
            pltpu.VMEM((n_proc, d), BF16),
            pltpu.VMEM((mesh_rows, d), F32),
        ],
        flops=2 * n_proc * d * (2 * d + mesh_rows + halo_rows),
        smem=1,
    )
    quarter = mesh_rows // 4
    mine, other = call(fold_kernel, [shape(quarter, d)] * 2, [keep, to_core(give)])
    (result,) = call(
        functools.partial(out_kernel, n_in, n_out),
        [shape(quarter, d)],
        [mid_half, mine, to_chip(other), proc_node_gain, last_w, last_beside, last_across, to_core(last_across)],
        scratch=[pltpu.VMEM((4 * (n_in + n_out), d), BF16)],
        flops=2 * quarter * d * 3 * d,
    )
    return result


def solution(mesh):
    placed = (
        P(("groups", "dom"), "sub"),
        P(("groups", "dom"), "sub"),
        P("dom", None, None),
        P("dom", None, None),
        P(None, ("dom", "sub")),
        P(None, ("dom", "sub")),
        P("dom"),
        P(None, ("dom", "sub")),
        P(None, ("dom", "sub")),
        P("dom"),
        P(),
        P(),
        P("sub", None),
        P("sub", None),
        P("sub", None),
        P("sub", None),
        P("sub", None),
        P("sub", None),
        P("sub", None),
        P("sub", None),
        P(),
        P(),
        P(),
        P(),
    )
    return jax.shard_map(
        local,
        mesh=mesh,
        in_specs=placed,
        out_specs=P(("groups", "dom", "sub"), None),
        check_vma=False,
    )
```

```python
import functools

import jax
import jax.numpy as jnp
from jax import lax
from jax.experimental import pallas as pl
from jax.experimental.pallas import tpu as pltpu
from jax.sharding import PartitionSpec as P

BLOCK = 128
OFFSETS = (-2, -1, 1, 2)
STEP = 512
GATHERED = 1024
LONG = 30 * 10**9
VMEM_BYTES = 24 * 1024 * 1024
I16 = jnp.int16
BF16 = jnp.bfloat16
F32 = jnp.float32


def silu(v):
    h = 0.5 * v
    return h + h * jnp.tanh(h)


def region_of(delta):
    return jnp.where(delta < 0, delta + 2, delta + 1)


def halo_plan(count):
    plan = []
    if count == 4:
        for bit in (1, 2, 3):
            pairs = [(d, d ^ bit) for d in range(4) if abs((d ^ bit) - d) <= 2]
            regions = [(OFFSETS.index((d ^ bit) - d) if abs((d ^ bit) - d) <= 2 else -1) for d in range(4)]
            plan.append((pairs, regions, regions))
    else:
        for region, offset in enumerate(OFFSETS):
            pairs = [(d, d + offset) for d in range(count) if 0 <= d + offset < count]
            plan.append((pairs, region, 3 - region))
    return plan


def by_index(choice, index):
    if isinstance(choice, int):
        return choice
    picked = jnp.int32(choice[0])
    for place in range(1, len(choice)):
        picked = jnp.where(index == place, choice[place], picked)
    return picked


def whole_refs(count):
    return [pl.BlockSpec(memory_space=pltpu.VMEM)] * count


def call(body, outs, args, scratch=(), flops=0, smem=0):
    moved = sum(a.size * a.dtype.itemsize for a in args) + sum(
        o.size * jnp.dtype(o.dtype).itemsize for o in outs
    )
    specs = whole_refs(len(args) - smem) + [pl.BlockSpec(memory_space=pltpu.SMEM)] * smem
    return pl.pallas_call(
        body,
        out_shape=tuple(outs),
        in_specs=specs,
        out_specs=tuple(whole_refs(len(outs))),
        scratch_shapes=list(scratch),
        compiler_params=pltpu.CompilerParams(vmem_limit_bytes=VMEM_BYTES),
        cost_estimate=pl.CostEstimate(flops=int(flops), bytes_accessed=int(moved), transcendentals=0),
    )(*args)


def dot(a, b):
    return jnp.dot(a, b, preferred_element_type=F32)


def dot_first(a, b):
    return lax.dot_general(a, b, (((0,), (0,)), ((), ())), preferred_element_type=F32)


def three_parts(v):
    a = v.astype(BF16)
    rest = v - a.astype(F32)
    b = rest.astype(BF16)
    c = (rest - b.astype(F32)).astype(BF16)
    return a, b, c


def embed_rows(geom, geo):
    a1, a2, a3 = three_parts(geom)
    b1, b2, b3 = three_parts(geo)
    left = jnp.concatenate([a1, a1, a2, a1, a2, a3], axis=0)
    right = jnp.concatenate([b1, b2, b1, b3, b2, b1], axis=0)
    return silu(dot_first(left, right)).astype(BF16)


def layer_norm(v):
    width = v.shape[-1]
    centered = v - jnp.sum(v, axis=-1, keepdims=True) * (1.0 / width)
    spread = jnp.sum(centered * centered, axis=-1, keepdims=True) * (1.0 / width)
    return centered * lax.rsqrt(spread + 1e-05)


def hot(cond):
    return jnp.where(cond, BF16(1), BF16(0))


def pick_rows(table, listed, rows=None):
    if rows is None:
        rows = lax.broadcasted_iota(I16, (table.shape[0], 1), 0)
    return dot_first(hot(rows == listed.astype(I16)), table).astype(BF16)


def pick_lists(plan, table, send, outs, rows=None):
    here = lax.axis_index("dom")
    for (pairs, sent, received), out in zip(plan, outs):
        region = jnp.maximum(by_index(sent, here), 0)
        out[...] = pick_rows(table, send[0, pl.ds(region, 1), :], rows)


def stack_into(out, parts):
    first = 0
    for part in parts:
        out[first : first + part.shape[0], :] = part[...]
        first += part.shape[0]


def begin_kernel(token):
    token[...] = jnp.zeros(token.shape, token.dtype)


def first_pack_kernel(plan, grid, send, w_in, w_out, n_in, n_out, token, half, *outs):
    place = 0
    for source in (w_in, w_out, n_in, n_out):
        rows = source.shape[0] // 2
        begin = pl.multiple_of(lax.axis_index("groups") * rows, 64)
        half[place : place + rows, :] = source[pl.ds(begin, rows), :]
        place += rows
    pick_lists(plan, grid[...], send, outs)


def embed_kernel(e_in, e_out, p_in, p_out, egeom, egeo, pgeom, pgeo, after, weights, eout, pout):
    stack_into(weights, (e_in, e_out, p_in, p_out))
    for geom, geo, out in ((egeom, egeo, eout), (pgeom, pgeo, pout)):
        for begin in range(0, out.shape[0], STEP):
            out[begin : begin + STEP, :] = embed_rows(geom[:, begin : begin + STEP], geo[...])


def cross_kernel(first, k_in, weights, lat, lat_out, crossing):
    lat_out[...] = lat[...]
    place = 0
    for rows in (k_in, weights.shape[0] - first - k_in):
        half = rows // 2
        begin = pl.multiple_of(first + lax.axis_index("groups") * half, 64)
        crossing[place : place + half, :] = weights[pl.ds(begin, half), :]
        first, place = first + rows, place + half


def relay_kernel(w_in, w_out, *refs):
    *parts, out, packed = refs
    stack_into(out, parts)
    stack_into(packed, (w_in, w_out))


def concat_kernel(*refs):
    stack_into(refs[-1], refs[:-1])


def split_kernel(source, *outs):
    first = 0
    for out in outs:
        out[...] = source[first : first + out.shape[0], :]
        first += out.shape[0]


def put_shard(target, source, first, step, part=0, parts=1):
    rows = target.shape[0] // (4 * parts)
    place = (lax.bitwise_xor(lax.axis_index("sub"), step) * parts + part) * rows
    target[pl.ds(pl.multiple_of(place, rows), rows), :] = source[first : first + rows, :]


def put_half(target, k, source, step, other):
    rows = target.shape[0] // 4
    which = lax.bitwise_xor(lax.axis_index("groups"), other)
    begin = lax.bitwise_xor(lax.axis_index("sub"), step) * rows
    for base, count in ((0, k // 2), (k // 2, (rows - k) // 2)):
        place = pl.multiple_of(begin + 2 * base + which * count, 64)
        target[pl.ds(place, count), :] = source[base : base + count, :]


def joined(stack, first, rows):
    step = stack.shape[0] // 4
    return jnp.concatenate([stack[k * step + first : k * step + first + rows, :] for k in range(4)], axis=0)


def halo_targets(plan, slots, node_rows, width):
    here = lax.axis_index("dom")
    lane = lax.broadcasted_iota(jnp.int32, (1, width), 1)
    target = jnp.full((1, width), -1, jnp.int32)
    for place, (pairs, sent, received) in enumerate(plan):
        region = by_index(received, here)
        first = jnp.where(region < 0, -4 * node_rows, node_rows + region * slots)
        inside = (lane >= place * slots) & (lane < (place + 1) * slots)
        target = jnp.where(inside, lane - place * slots + first, target)
    return target.astype(I16)


def columns(edges, first):
    pair = edges[:, first : first + STEP]
    zero = jnp.zeros((8 - pair.shape[0], STEP), jnp.int32)
    upright = jnp.transpose(jnp.concatenate([pair, zero], axis=0).astype(F32)).astype(jnp.int32).astype(I16)
    return upright[:, 0:1], upright[:, 1:2]


def edge_blocks(edges, live_edges, first_stage, w_out, messages, totals):
    count = edges.shape[1]
    row = lax.broadcasted_iota(I16, (totals.shape[0], 1), 0)
    quarter = lax.axis_index("sub")
    for first in range(0, count, STEP):
        hidden = silu(first_stage(first)).astype(BF16)
        message = layer_norm(dot(hidden, w_out))
        place = lax.broadcasted_iota(jnp.int32, (STEP, 1), 0) + (first + quarter * count)
        messages[first : first + STEP, :] = jnp.where(place < live_edges, message, 0.0).astype(BF16)
        done = first + STEP
        if done % GATHERED == 0 or done == count:
            begin = (first // GATHERED) * GATHERED
            collect = hot(row == edges[1:2, begin:done].astype(I16))
            part = dot(collect, messages[begin:done, :])
            if begin == 0:
                totals[...] = part
            else:
                totals[...] += part


def hand_out(totals, gain, keep, *give):
    rows = totals.shape[0] // 4
    core = lax.rem(lax.axis_index("sub"), 2)
    for half in range(2):
        kept = keep.at[pl.ds(half * rows, rows), :]
        given = give[0].at[pl.ds(half * rows, rows), :] if len(give) == 1 else give[half]
        for out, which in ((kept, core), (given, 1 - core)):
            place = pl.multiple_of((2 * half + which) * rows, rows)
            out[...] = (totals[pl.ds(place, rows), :] * gain[...]).astype(BF16)


def enc_kernel(
    plan, slots, grid_rows, mesh_rows, k_in, emb, edges, gain, l0, l1, l2, l3, o_in, o_out, b_in, b_out,
    across, round_, both, round_both, live, keep, give, give_more, own_mesh, full, stack, table, messages, totals,
):
    d = gain.shape[1]
    quarter = lax.axis_index("sub")
    width = l0.shape[1]
    for shard, step in zip((l0, l1, l2, l3), (0, 2, 1, 3)):
        place = pl.multiple_of(lax.bitwise_xor(quarter, step) * width, width)
        full[:, pl.ds(place, width)] = shard[...]
    step = k_in + d // 4
    for first, second, bit in ((o_in, o_out, 0), (b_in, b_out, 1)):
        place = lax.bitwise_xor(quarter, bit) * step
        stack[pl.ds(pl.multiple_of(place, 128), k_in), :] = first[...]
        stack[pl.ds(pl.multiple_of(place + k_in, 128), d // 4), :] = second[...]
    put_half(stack, k_in, across, 2, 0)
    put_half(stack, k_in, round_, 2, 1)
    put_half(stack, k_in, both, 3, 0)
    put_half(stack, k_in, round_both, 3, 1)
    rows = mesh_rows // 4
    core = lax.rem(quarter, 2)
    for half in range(2):
        place = pl.multiple_of(grid_rows + (2 * half + core) * rows, rows)
        own_mesh[half * rows : (half + 1) * rows, :] = full[pl.ds(place, rows), :]

    w_in = joined(stack, 0, k_in)
    halo_first, got = grid_rows + mesh_rows, full.shape[0] - grid_rows - mesh_rows
    table[:d, :] = w_in[:d, :]
    table[d : d + grid_rows, :] = dot(full[:grid_rows, :], w_in[d : 2 * d, :]).astype(BF16)
    base = d + grid_rows + mesh_rows
    table[d + grid_rows : base, :] = dot(full[grid_rows:halo_first, :], w_in[2 * d :, :]).astype(BF16)
    table[base : base + got, :] = dot(full[halo_first:, :], w_in[d : 2 * d, :]).astype(BF16)
    if base + got < table.shape[0]:
        table[base + got :, :] = jnp.zeros((table.shape[0] - base - got, d), BF16)
    targets = halo_targets(plan, slots, grid_rows, table.shape[0] - base)
    own = lax.broadcasted_iota(I16, (1, grid_rows), 1)
    mesh = lax.broadcasted_iota(I16, (1, mesh_rows), 1)

    def first_stage(first):
        senders, receivers = columns(edges, first)
        chosen = [emb[first : first + STEP, :], hot(own == senders), hot(mesh == receivers), hot(targets == senders)]
        return dot(jnp.concatenate(chosen, axis=1), table[...])

    edge_blocks(edges, live[0] * BLOCK, first_stage, joined(stack, k_in, d // 4), messages, totals)
    hand_out(totals, gain, keep, give, give_more)


def node_update(mesh, shares, w_in, w_out, gain):
    stacked = jnp.concatenate([mesh, shares], axis=1)
    hidden = silu(dot(stacked, w_in)).astype(BF16)
    update = layer_norm(dot(hidden, w_out)) * gain
    return (mesh.astype(F32) + update).astype(BF16)


def add(mine, theirs):
    return (mine.astype(F32) + theirs.astype(F32)).astype(BF16)


def add_kernel(mine, first, second, held_in, node_in, out, held, node):
    held[...] = held_in[...]
    node[...] = node_in[...]
    rows = first.shape[0]
    out[:rows, :] = add(mine[:rows, :], first[...])
    out[rows:, :] = add(mine[rows:, :], second[...])


def node_kernel(
    plan, k_in, k_out, mesh, mine, theirs, gain, w0, w1, w2, w3, w4, w5, across, round_, send, out, pair, *rest
):
    outs, stack = rest[:-1], rest[-1]
    stack_into(pair, (across, round_))
    put_shard(stack, w0, 0, 0)
    put_shard(stack, w1, 0, 1)
    put_half(stack, k_in, w2, 2, 0)
    put_half(stack, k_in, w3, 2, 1)
    put_half(stack, k_in, w4, 3, 0)
    put_half(stack, k_in, w5, 3, 1)
    w_in, w_out = joined(stack, 0, k_in), joined(stack, k_in, k_out)
    fresh = node_update(mesh[...], add(mine[...], theirs[...]), w_in, w_out, gain[...])
    out[...] = fresh
    half = fresh.shape[0] // 2
    core = lax.rem(lax.axis_index("sub"), 2)
    place = lax.broadcasted_iota(jnp.int32, (fresh.shape[0], 1), 0)
    rows = place + core * half + jnp.where(place < half, 0, half)
    pick_lists(plan, fresh, send, outs, rows.astype(I16))


def proc_first_kernel(
    k_in, first_row, emb, mine, theirs, edges, w0, w1, pair, pair_beside,
    table, pre, w_source, w_out, stack, full,
):
    d = full.shape[1]
    node_rows = full.shape[0]
    rows = node_rows // 4
    core = lax.rem(lax.axis_index("sub"), 2)
    for half in range(2):
        for part, which in ((mine, core), (theirs, 1 - core)):
            place = pl.multiple_of((2 * half + which) * rows, rows)
            full[pl.ds(place, rows), :] = part[half * rows : (half + 1) * rows, :]
    put_shard(stack, w0, first_row, 0)
    put_shard(stack, w1, first_row, 1)
    rows = pair.shape[0] // 2
    for other in range(2):
        put_half(stack, k_in, pair.at[pl.ds(other * rows, rows), :], 2, other)
        put_half(stack, k_in, pair_beside.at[pl.ds(other * rows, rows), :], 3, other)
    w_in = joined(stack, 0, k_in)
    w_out[...] = joined(stack, k_in, d // 4)
    w_source[...] = w_in[d : 2 * d, :]
    table[:d, :] = w_in[:d, :]
    table[d : d + node_rows, :] = dot(full[...], w_in[d : 2 * d, :]).astype(BF16)
    table[d + node_rows :, :] = dot(full[...], w_in[2 * d :, :]).astype(BF16)
    lane = lax.broadcasted_iota(I16, (1, node_rows), 1)
    for first in range(0, pre.shape[0], STEP):
        pre[first : first + STEP, :] = dot(own_chosen(emb, edges, lane, first), table[...])


def own_chosen(emb, edges, lane, first):
    senders, receivers = columns(edges, first)
    return jnp.concatenate([emb[first : first + STEP, :], hot(lane == senders), hot(lane == receivers)], axis=1)


def proc_second_kernel(
    plan, slots, node_rows, emb, edges, gain, table, pre, w_source, w_out, halo, halo_beside,
    live, keep, give, halo_table, messages, totals,
):
    d = pre.shape[1]
    got = halo[...] + halo_beside[...]
    halo_table[: got.shape[0], :] = dot(got, w_source[...]).astype(BF16)
    if got.shape[0] < halo_table.shape[0]:
        halo_table[got.shape[0] :, :] = jnp.zeros((halo_table.shape[0] - got.shape[0], d), BF16)
    targets = halo_targets(plan, slots, node_rows, halo_table.shape[0])
    lane = lax.broadcasted_iota(I16, (1, node_rows), 1)

    def first_stage(first):
        senders, receivers = columns(edges, first)
        remote = dot(hot(targets == senders), halo_table[...])
        if first < pre.shape[0]:
            return pre[first : first + STEP, :] + remote
        return dot(own_chosen(emb, edges, lane, first), table[...]) + remote

    edge_blocks(edges, live[0] * BLOCK, first_stage, w_out[...], messages, totals)
    hand_out(totals, gain, keep, give)


def fold_kernel(mine, theirs, keep, give):
    rows = mine.shape[0] // 2
    chip = lax.div(lax.axis_index("sub"), 2)
    for out, which in ((keep, chip), (give, 1 - chip)):
        place = pl.multiple_of(which * rows, rows)
        out[...] = add(mine[pl.ds(place, rows), :], theirs[pl.ds(place, rows), :])


def out_kernel(k_in, k_out, middle, mine, theirs, gain, w0, w1, w2, w3, out, stack):
    rows = mine.shape[0]
    chip = lax.div(lax.axis_index("sub"), 2)
    mesh = middle[pl.ds(pl.multiple_of(chip * rows, rows), rows), :]
    for shard, bit in zip((w0, w1, w2, w3), (0, 1, 2, 3)):
        put_shard(stack, shard, 0, bit)
    w_in, w_out = joined(stack, 0, k_in), joined(stack, k_in, k_out)
    out[...] = node_update(mesh, add(mine[...], theirs[...]), w_in, w_out, gain[...])


def to_chip(v):
    return lax.ppermute(v, "sub", [(i, i ^ 2) for i in range(4)])


def to_core(v):
    return lax.ppermute(v, "sub", [(i, i ^ 1) for i in range(4)])


def to_group(v):
    count = lax.axis_size("groups")
    return lax.ppermute(v, "groups", [(i, count - 1 - i) for i in range(count)])


def shape(rows, width, dtype=BF16):
    return jax.ShapeDtypeStruct((rows, width), dtype)


def padded(rows):
    return -(-rows // 128) * 128


def local(
    grid_lat,
    mesh_lat,
    grid_send,
    mesh_send,
    enc_edges,
    enc_geom,
    enc_blocks,
    proc_edges,
    proc_geom,
    proc_blocks,
    enc_geo,
    proc_geo,
    enc_edge_in,
    enc_edge_out,
    enc_node_in,
    enc_node_out,
    proc_edge_in,
    proc_edge_out,
    proc_node_in,
    proc_node_out,
    enc_edge_gain,
    enc_node_gain,
    proc_edge_gain,
    proc_node_gain,
):
    plan = halo_plan(lax.axis_size("dom"))
    d = enc_geo.shape[1]
    grid_rows, mesh_rows = grid_lat.shape[0], mesh_lat.shape[0]
    n_enc, n_proc = enc_edges.shape[1], proc_edges.shape[1]
    enc_edge_gain, enc_node_gain, proc_edge_gain, proc_node_gain = (
        g.reshape(1, d) for g in (enc_edge_gain, enc_node_gain, proc_edge_gain, proc_node_gain)
    )
    k_in, k_out = enc_edge_in.shape[0], enc_edge_out.shape[0]
    n_in, n_out = enc_node_in.shape[0], enc_node_out.shape[0]
    width = grid_lat.shape[1]

    slots = grid_send.shape[2]
    (token,) = call(begin_kernel, [shape(16, 128)], [], flops=LONG)
    edge_half, *outgoing = call(
        functools.partial(first_pack_kernel, plan),
        [shape((k_in + k_out + n_in + n_out) // 2, d)] + [shape(slots, width)] * len(plan),
        [grid_lat, grid_send, enc_edge_in, enc_edge_out, enc_node_in, enc_node_out, token],
    )
    first_across = to_chip(edge_half)
    halos = [lax.ppermute(v, "dom", entry[0]) for v, entry in zip(outgoing, plan)]
    got = len(plan) * slots
    (lat,) = call(concat_kernel, [shape(grid_rows + mesh_rows + got, width)], [grid_lat, mesh_lat, *halos])
    edge_across, node_across = call(
        split_kernel,
        [shape((k_in + k_out) // 2, d), shape((n_in + n_out) // 2, d)],
        [first_across],
    )
    lat_across = to_chip(lat)
    lat_beside = to_core(lat)
    edge_beside = [to_core(enc_edge_in), to_core(enc_edge_out)]
    edge_round = to_group(edge_across)
    next_w, enc_emb, proc_emb = call(
        embed_kernel,
        [shape(n_in + n_out + k_in + k_out, d), shape(n_enc, d), shape(n_proc, d)],
        [
            enc_node_in, enc_node_out, proc_edge_in, proc_edge_out,
            enc_geom, enc_geo, proc_geom, proc_geo, lat,
        ],
        flops=2 * (n_enc + n_proc) * d * 128,
    )
    lat_sent, proc_half = call(
        functools.partial(cross_kernel, n_in + n_out, k_in),
        [shape(lat.shape[0], width), shape((k_in + k_out) // 2, d)],
        [next_w, lat_across],
    )
    lat_both = to_core(lat_sent)
    proc_came = to_chip(proc_half)
    next_beside = to_core(next_w)

    halo_rows = padded(got)
    half = mesh_rows // 2
    keep, give, give_more, own_mesh = call(
        functools.partial(enc_kernel, plan, slots, grid_rows, mesh_rows, k_in),
        [shape(half, d), shape(half // 2, d), shape(half // 2, d), shape(half, d)],
        [
            enc_emb, enc_edges, enc_edge_gain, lat, lat_across, lat_beside, lat_both,
            enc_edge_in, enc_edge_out, *edge_beside,
            edge_across, edge_round, to_core(edge_across), to_core(edge_round), enc_blocks,
        ],
        scratch=[
            pltpu.VMEM((grid_rows + mesh_rows + got, d), BF16),
            pltpu.VMEM((4 * (k_in + k_out), d), BF16),
            pltpu.VMEM((d + grid_rows + mesh_rows + halo_rows, d), BF16),
            pltpu.VMEM((n_enc, d), BF16),
            pltpu.VMEM((mesh_rows, d), F32),
        ],
        flops=2 * n_enc * d * (3 * d + grid_rows + mesh_rows + halo_rows),
        smem=1,
    )
    chip_sum, proc_across, node_sent = call(
        add_kernel,
        [shape(half, d), shape(*proc_came.shape), shape(*node_across.shape)],
        [keep, to_core(give), to_core(give_more), proc_came, node_across],
    )
    node_round, proc_round = to_group(node_sent), to_group(proc_across)
    node_both = to_core(node_across)
    slots = mesh_send.shape[2]
    mid_half, proc_pair, *outgoing = call(
        functools.partial(node_kernel, plan, n_in, n_out),
        [shape(half, d), shape(k_in + k_out, d)] + [shape(slots, d)] * len(plan),
        [
            own_mesh, chip_sum, to_chip(chip_sum), enc_node_gain,
            next_w, next_beside, node_across, node_round, node_both, to_core(node_round),
            proc_across, proc_round, mesh_send,
        ],
        scratch=[pltpu.VMEM((4 * (n_in + n_out), d), BF16)],
        flops=2 * half * d * 3 * d,
    )
    mid_beside = to_core(mid_half)
    halos = [lax.ppermute(v, "dom", entry[0]) for v, entry in zip(outgoing, plan)]
    halo, last_w = call(
        relay_kernel,
        [shape(len(plan) * slots, d), shape(n_in + n_out, d)],
        [proc_node_in, proc_node_out, *halos],
    )
    halo_beside = to_core(halo)
    last_across, last_beside = to_chip(last_w), to_core(last_w)
    early = n_proc // 2
    table, pre, w_source, w_out = call(
        functools.partial(proc_first_kernel, k_in, n_in + n_out),
        [shape(d + 2 * mesh_rows, d), shape(early, d, F32), shape(d, d), shape(d, d)],
        [
            proc_emb, mid_half, mid_beside, proc_edges, next_w, next_beside, proc_pair, to_core(proc_pair),
        ],
        scratch=[pltpu.VMEM((4 * (k_in + k_out), d), BF16), pltpu.VMEM((mesh_rows, d), BF16)],
        flops=2 * early * d * (d + 2 * mesh_rows),
    )
    halo_rows = padded(len(plan) * slots)
    keep, give = call(
        functools.partial(proc_second_kernel, plan, slots, mesh_rows),
        [shape(half, d), shape(half, d)],
        [proc_emb, proc_edges, proc_edge_gain, table, pre, w_source, w_out, halo, halo_beside, proc_blocks],
        scratch=[
            pltpu.VMEM((halo_rows, d), BF16),
            pltpu.VMEM((n_proc, d), BF16),
            pltpu.VMEM((mesh_rows, d), F32),
        ],
        flops=2 * n_proc * d * (2 * d + mesh_rows + halo_rows),
        smem=1,
    )
    quarter = mesh_rows // 4
    mine, other = call(fold_kernel, [shape(quarter, d)] * 2, [keep, to_core(give)])
    (result,) = call(
        functools.partial(out_kernel, n_in, n_out),
        [shape(quarter, d)],
        [mid_half, mine, to_chip(other), proc_node_gain, last_w, last_beside, last_across, to_core(last_across)],
        scratch=[pltpu.VMEM((4 * (n_in + n_out), d), BF16)],
        flops=2 * quarter * d * 3 * d,
    )
    return result


def solution(mesh):
    placed = (
        P(("groups", "dom"), "sub"),
        P(("groups", "dom"), "sub"),
        P("dom", None, None),
        P("dom", None, None),
        P(None, ("dom", "sub")),
        P(None, ("dom", "sub")),
        P("dom"),
        P(None, ("dom", "sub")),
        P(None, ("dom", "sub")),
        P("dom"),
        P(),
        P(),
        P("sub", None),
        P("sub", None),
        P("sub", None),
        P("sub", None),
        P("sub", None),
        P("sub", None),
        P("sub", None),
        P("sub", None),
        P(),
        P(),
        P(),
        P(),
    )
    return jax.shard_map(
        local,
        mesh=mesh,
        in_specs=placed,
        out_specs=P(("groups", "dom", "sub"), None),
        check_vma=False,
    )
```

```python
import functools

import jax
import jax.numpy as jnp
from jax import lax
from jax.experimental import pallas as pl
from jax.experimental.pallas import tpu as pltpu
from jax.sharding import PartitionSpec as P

BLOCK = 128
OFFSETS = (-2, -1, 1, 2)
STEP = 512
GATHERED = 1024
LONG = 30 * 10**9
BY_GROUP = ("groups",)
BY_PART = ("dom",)
VMEM_BYTES = 24 * 1024 * 1024
I16 = jnp.int16
BF16 = jnp.bfloat16
F32 = jnp.float32


def silu(v):
    h = 0.5 * v
    return h + h * jnp.tanh(h)


def region_of(delta):
    return jnp.where(delta < 0, delta + 2, delta + 1)


def halo_plan(count):
    plan = []
    if count == 4:
        for bit in (1, 2, 3):
            pairs = [(d, d ^ bit) for d in range(4) if abs((d ^ bit) - d) <= 2]
            regions = [(OFFSETS.index((d ^ bit) - d) if abs((d ^ bit) - d) <= 2 else -1) for d in range(4)]
            plan.append((pairs, regions, regions))
    else:
        for region, offset in enumerate(OFFSETS):
            pairs = [(d, d + offset) for d in range(count) if 0 <= d + offset < count]
            plan.append((pairs, region, 3 - region))
    return plan


def by_index(choice, index):
    if isinstance(choice, int):
        return choice
    picked = jnp.int32(choice[0])
    for place in range(1, len(choice)):
        picked = jnp.where(index == place, choice[place], picked)
    return picked


def whole_refs(count):
    return [pl.BlockSpec(memory_space=pltpu.VMEM)] * count


def call(body, outs, args, scratch=(), flops=0, smem=0):
    moved = sum(a.size * a.dtype.itemsize for a in args) + sum(
        o.size * jnp.dtype(o.dtype).itemsize for o in outs
    )
    specs = whole_refs(len(args) - smem) + [pl.BlockSpec(memory_space=pltpu.SMEM)] * smem
    return pl.pallas_call(
        body,
        out_shape=tuple(outs),
        in_specs=specs,
        out_specs=tuple(whole_refs(len(outs))),
        scratch_shapes=list(scratch),
        compiler_params=pltpu.CompilerParams(vmem_limit_bytes=VMEM_BYTES),
        cost_estimate=pl.CostEstimate(flops=int(flops), bytes_accessed=int(moved), transcendentals=0),
    )(*args)


def dot(a, b):
    return jnp.dot(a, b, preferred_element_type=F32)


def dot_first(a, b):
    return lax.dot_general(a, b, (((0,), (0,)), ((), ())), preferred_element_type=F32)


def three_parts(v):
    a = v.astype(BF16)
    rest = v - a.astype(F32)
    b = rest.astype(BF16)
    c = (rest - b.astype(F32)).astype(BF16)
    return a, b, c


def embed_rows(geom, geo):
    a1, a2, a3 = three_parts(geom)
    b1, b2, b3 = three_parts(geo)
    left = jnp.concatenate([a1, a1, a2, a1, a2, a3], axis=0)
    right = jnp.concatenate([b1, b2, b1, b3, b2, b1], axis=0)
    return silu(dot_first(left, right)).astype(BF16)


def layer_norm(v):
    width = v.shape[-1]
    centered = v - jnp.sum(v, axis=-1, keepdims=True) * (1.0 / width)
    spread = jnp.sum(centered * centered, axis=-1, keepdims=True) * (1.0 / width)
    return centered * lax.rsqrt(spread + 1e-05)


def hot(cond):
    return jnp.where(cond, BF16(1), BF16(0))


def pick_rows(table, listed, rows=None):
    if rows is None:
        rows = lax.broadcasted_iota(I16, (table.shape[0], 1), 0)
    return dot_first(hot(rows == listed.astype(I16)), table).astype(BF16)


def pick_lists(plan, table, send, outs, rows=None):
    here = lax.axis_index("dom")
    for (pairs, sent, received), out in zip(plan, outs):
        region = jnp.maximum(by_index(sent, here), 0)
        out[...] = pick_rows(table, send[0, pl.ds(region, 1), :], rows)


def stack_into(out, parts):
    first = 0
    for part in parts:
        out[first : first + part.shape[0], :] = part[...]
        first += part.shape[0]


def begin_kernel(token):
    token[...] = jnp.zeros(token.shape, token.dtype)


def first_pack_kernel(plan, grid, send, w_in, w_out, n_out, p_out, token, half, *outs):
    place = 0
    for source, axes in ((w_in, BY_GROUP), (w_out, BY_GROUP), (n_out, BY_PART), (p_out, BY_GROUP)):
        rows = source.shape[0] // 2
        begin = pl.multiple_of(parity(axes) * rows, 64)
        half[place : place + rows, :] = source[pl.ds(begin, rows), :]
        place += rows
    pick_lists(plan, grid[...], send, outs)


def embed_kernel(e_in, e_out, p_in, p_out, egeom, egeo, pgeom, pgeo, after, weights, eout, pout):
    stack_into(weights, (e_in, e_out, p_in, p_out))
    for geom, geo, out in ((egeom, egeo, eout), (pgeom, pgeo, pout)):
        for begin in range(0, out.shape[0], STEP):
            out[begin : begin + STEP, :] = embed_rows(geom[:, begin : begin + STEP], geo[...])


def cross_kernel(parts, weights, lat, crossing, lat_out):
    lat_out[...] = lat[...]
    place = 0
    for first, rows, axes in parts:
        half = rows // 2
        begin = pl.multiple_of(first + parity(axes) * half, 64)
        crossing[place : place + half, :] = weights[pl.ds(begin, half), :]
        place += half


def rows_kernel(source, out):
    out[...] = source[: out.shape[0], :]


def pair_kernel(first, second, after, out):
    stack_into(out, (first, second))


def split_kernel(ins, early, source, after, node, proc):
    n, p = ins
    n_rest, p_rest = node.shape[0] - n, proc.shape[0] - p
    base = early.shape[0] - n_rest - p_rest
    stack_into(node, (source.at[pl.ds(0, n), :], early.at[pl.ds(base, n_rest), :]))
    stack_into(proc, (source.at[pl.ds(n, p), :], early.at[pl.ds(base + n_rest, p_rest), :]))


def concat_kernel(*refs):
    stack_into(refs[-1], refs[:-1])


def put_shard(target, source, first, step, part=0, parts=1):
    rows = target.shape[0] // (4 * parts)
    place = (lax.bitwise_xor(lax.axis_index("sub"), step) * parts + part) * rows
    target[pl.ds(pl.multiple_of(place, rows), rows), :] = source[first : first + rows, :]


def parity(axes):
    return lax.rem(sum(lax.axis_index(axis) for axis in axes), 2)


def put_half(target, k, source, step, other, axes=("groups",)):
    rows = target.shape[0] // 4
    which = lax.bitwise_xor(parity(axes), other)
    begin = lax.bitwise_xor(lax.axis_index("sub"), step) * rows
    for base, count in ((0, k // 2), (k // 2, (rows - k) // 2)):
        place = pl.multiple_of(begin + 2 * base + which * count, 64)
        target[pl.ds(place, count), :] = source[base : base + count, :]


def joined(stack, first, rows):
    step = stack.shape[0] // 4
    return jnp.concatenate([stack[k * step + first : k * step + first + rows, :] for k in range(4)], axis=0)


def halo_targets(plan, slots, node_rows, width):
    here = lax.axis_index("dom")
    lane = lax.broadcasted_iota(jnp.int32, (1, width), 1)
    target = jnp.full((1, width), -1, jnp.int32)
    for place, (pairs, sent, received) in enumerate(plan):
        region = by_index(received, here)
        first = jnp.where(region < 0, -4 * node_rows, node_rows + region * slots)
        inside = (lane >= place * slots) & (lane < (place + 1) * slots)
        target = jnp.where(inside, lane - place * slots + first, target)
    return target.astype(I16)


def columns(edges, first):
    pair = edges[:, first : first + STEP]
    zero = jnp.zeros((8 - pair.shape[0], STEP), jnp.int32)
    upright = jnp.transpose(jnp.concatenate([pair, zero], axis=0).astype(F32)).astype(jnp.int32).astype(I16)
    return upright[:, 0:1], upright[:, 1:2]


def edge_blocks(edges, live_edges, first_stage, w_out, messages, totals):
    count = edges.shape[1]
    row = lax.broadcasted_iota(I16, (totals.shape[0], 1), 0)
    quarter = lax.axis_index("sub")
    for first in range(0, count, STEP):
        hidden = silu(first_stage(first)).astype(BF16)
        message = layer_norm(dot(hidden, w_out))
        place = lax.broadcasted_iota(jnp.int32, (STEP, 1), 0) + (first + quarter * count)
        messages[first : first + STEP, :] = jnp.where(place < live_edges, message, 0.0).astype(BF16)
        done = first + STEP
        if done % GATHERED == 0 or done == count:
            begin = (first // GATHERED) * GATHERED
            collect = hot(row == edges[1:2, begin:done].astype(I16))
            part = dot(collect, messages[begin:done, :])
            if begin == 0:
                totals[...] = part
            else:
                totals[...] += part


def hand_out(totals, gain, keep, give):
    rows = totals.shape[0] // 4
    core = lax.rem(lax.axis_index("sub"), 2)
    for half in range(2):
        for out, which in ((keep, core), (give, 1 - core)):
            place = pl.multiple_of((2 * half + which) * rows, rows)
            out[half * rows : (half + 1) * rows, :] = (totals[pl.ds(place, rows), :] * gain[...]).astype(BF16)


def enc_kernel(
    plan, slots, grid_rows, mesh_rows, k_in, emb, edges, gain, l0, l1, l2, l3, o_in, o_out, b_in, b_out,
    across, round_, both, round_both, live, keep, give, own_mesh, full, stack, table, messages, totals,
):
    d = gain.shape[1]
    quarter = lax.axis_index("sub")
    width = l0.shape[1]
    for shard, step in zip((l0, l1, l2, l3), (0, 2, 1, 3)):
        place = pl.multiple_of(lax.bitwise_xor(quarter, step) * width, width)
        full[:, pl.ds(place, width)] = shard[...]
    step = k_in + d // 4
    for first, second, bit in ((o_in, o_out, 0), (b_in, b_out, 1)):
        place = lax.bitwise_xor(quarter, bit) * step
        stack[pl.ds(pl.multiple_of(place, 128), k_in), :] = first[...]
        stack[pl.ds(pl.multiple_of(place + k_in, 128), d // 4), :] = second[...]
    put_half(stack, k_in, across, 2, 0)
    put_half(stack, k_in, round_, 2, 1)
    put_half(stack, k_in, both, 3, 0)
    put_half(stack, k_in, round_both, 3, 1)
    rows = mesh_rows // 4
    core = lax.rem(quarter, 2)
    for half in range(2):
        place = pl.multiple_of(grid_rows + (2 * half + core) * rows, rows)
        own_mesh[half * rows : (half + 1) * rows, :] = full[pl.ds(place, rows), :]

    w_in = joined(stack, 0, k_in)
    halo_first, got = grid_rows + mesh_rows, full.shape[0] - grid_rows - mesh_rows
    table[:d, :] = w_in[:d, :]
    table[d : d + grid_rows, :] = dot(full[:grid_rows, :], w_in[d : 2 * d, :]).astype(BF16)
    base = d + grid_rows + mesh_rows
    table[d + grid_rows : base, :] = dot(full[grid_rows:halo_first, :], w_in[2 * d :, :]).astype(BF16)
    table[base : base + got, :] = dot(full[halo_first:, :], w_in[d : 2 * d, :]).astype(BF16)
    if base + got < table.shape[0]:
        table[base + got :, :] = jnp.zeros((table.shape[0] - base - got, d), BF16)
    targets = halo_targets(plan, slots, grid_rows, table.shape[0] - base)
    own = lax.broadcasted_iota(I16, (1, grid_rows), 1)
    mesh = lax.broadcasted_iota(I16, (1, mesh_rows), 1)

    def first_stage(first):
        senders, receivers = columns(edges, first)
        chosen = [emb[first : first + STEP, :], hot(own == senders), hot(mesh == receivers), hot(targets == senders)]
        return dot(jnp.concatenate(chosen, axis=1), table[...])

    edge_blocks(edges, live[0] * BLOCK, first_stage, joined(stack, k_in, d // 4), messages, totals)
    hand_out(totals, gain, keep, give)


def node_update(mesh, shares, w_in, w_out, gain):
    stacked = jnp.concatenate([mesh, shares], axis=1)
    hidden = silu(dot(stacked, w_in)).astype(BF16)
    update = layer_norm(dot(hidden, w_out)) * gain
    return (mesh.astype(F32) + update).astype(BF16)


def add(mine, theirs):
    return (mine.astype(F32) + theirs.astype(F32)).astype(BF16)


def add_kernel(mine, theirs, out):
    out[...] = add(mine[...], theirs[...])


def node_kernel(
    plan, k_in, k_out, mesh, mine, theirs, gain, n_in, n_out, w0, w1, w2, w3, w4, w5, send, out, packed, *rest
):
    outs, stack = rest[:-1], rest[-1]
    put_shard(stack, w0, 0, 0)
    put_shard(stack, w1, 0, 1)
    put_half(stack, k_in, w2, 2, 0, BY_PART)
    put_half(stack, k_in, w3, 2, 1, BY_PART)
    put_half(stack, k_in, w4, 3, 0, BY_PART)
    put_half(stack, k_in, w5, 3, 1, BY_PART)
    w_in, w_out = joined(stack, 0, k_in), joined(stack, k_in, k_out)
    fresh = node_update(mesh[...], add(mine[...], theirs[...]), w_in, w_out, gain[...])
    out[...] = fresh
    half = fresh.shape[0] // 2
    core = lax.rem(lax.axis_index("sub"), 2)
    place = lax.broadcasted_iota(jnp.int32, (fresh.shape[0], 1), 0)
    rows = place + core * half + jnp.where(place < half, 0, half)
    pick_lists(plan, fresh, send, outs, rows.astype(I16))
    stack_into(packed, (n_in, n_out))


def proc_first_kernel(
    k_in, first_row, emb, mine, theirs, edges, w0, w1, pair, pair_beside,
    table, pre, w_source, w_out, stack, full,
):
    d = full.shape[1]
    node_rows = full.shape[0]
    rows = node_rows // 4
    core = lax.rem(lax.axis_index("sub"), 2)
    for half in range(2):
        for part, which in ((mine, core), (theirs, 1 - core)):
            place = pl.multiple_of((2 * half + which) * rows, rows)
            full[pl.ds(place, rows), :] = part[half * rows : (half + 1) * rows, :]
    put_shard(stack, w0, first_row, 0)
    put_shard(stack, w1, first_row, 1)
    rows = pair.shape[0] // 2
    for other in range(2):
        put_half(stack, k_in, pair.at[pl.ds(other * rows, rows), :], 2, other)
        put_half(stack, k_in, pair_beside.at[pl.ds(other * rows, rows), :], 3, other)
    w_in = joined(stack, 0, k_in)
    w_out[...] = joined(stack, k_in, d // 4)
    w_source[...] = w_in[d : 2 * d, :]
    table[:d, :] = w_in[:d, :]
    table[d : d + node_rows, :] = dot(full[...], w_in[d : 2 * d, :]).astype(BF16)
    table[d + node_rows :, :] = dot(full[...], w_in[2 * d :, :]).astype(BF16)
    lane = lax.broadcasted_iota(I16, (1, node_rows), 1)
    for first in range(0, pre.shape[0], STEP):
        pre[first : first + STEP, :] = dot(own_chosen(emb, edges, lane, first), table[...])


def own_chosen(emb, edges, lane, first):
    senders, receivers = columns(edges, first)
    return jnp.concatenate([emb[first : first + STEP, :], hot(lane == senders), hot(lane == receivers)], axis=1)


def proc_second_kernel(
    plan, slots, node_rows, emb, edges, gain, table, pre, w_source, w_out, halo, halo_beside,
    live, keep, give, halo_table, messages, totals,
):
    d = pre.shape[1]
    got = halo[...] + halo_beside[...]
    halo_table[: got.shape[0], :] = dot(got, w_source[...]).astype(BF16)
    if got.shape[0] < halo_table.shape[0]:
        halo_table[got.shape[0] :, :] = jnp.zeros((halo_table.shape[0] - got.shape[0], d), BF16)
    targets = halo_targets(plan, slots, node_rows, halo_table.shape[0])
    lane = lax.broadcasted_iota(I16, (1, node_rows), 1)

    def first_stage(first):
        senders, receivers = columns(edges, first)
        remote = dot(hot(targets == senders), halo_table[...])
        if first < pre.shape[0]:
            return pre[first : first + STEP, :] + remote
        return dot(own_chosen(emb, edges, lane, first), table[...]) + remote

    edge_blocks(edges, live[0] * BLOCK, first_stage, w_out[...], messages, totals)
    hand_out(totals, gain, keep, give)


def fold_kernel(mine, theirs, keep, give):
    rows = mine.shape[0] // 2
    chip = lax.div(lax.axis_index("sub"), 2)
    for out, which in ((keep, chip), (give, 1 - chip)):
        place = pl.multiple_of(which * rows, rows)
        out[...] = add(mine[pl.ds(place, rows), :], theirs[pl.ds(place, rows), :])


def out_kernel(k_in, k_out, middle, mine, theirs, gain, w0, w1, w2, w3, out, stack):
    rows = mine.shape[0]
    chip = lax.div(lax.axis_index("sub"), 2)
    mesh = middle[pl.ds(pl.multiple_of(chip * rows, rows), rows), :]
    for shard, bit in zip((w0, w1, w2, w3), (0, 1, 2, 3)):
        put_shard(stack, shard, 0, bit)
    w_in, w_out = joined(stack, 0, k_in), joined(stack, k_in, k_out)
    out[...] = node_update(mesh, add(mine[...], theirs[...]), w_in, w_out, gain[...])


def to_chip(v):
    return lax.ppermute(v, "sub", [(i, i ^ 2) for i in range(4)])


def to_core(v):
    return lax.ppermute(v, "sub", [(i, i ^ 1) for i in range(4)])


def to_group(v):
    count = lax.axis_size("groups")
    return lax.ppermute(v, "groups", [(i, count - 1 - i) for i in range(count)])


def to_partition(v):
    return lax.ppermute(v, "dom", [(i, i ^ 1) for i in range(lax.axis_size("dom"))])


def shape(rows, width, dtype=BF16):
    return jax.ShapeDtypeStruct((rows, width), dtype)


def padded(rows):
    return -(-rows // 128) * 128


def local(
    grid_lat,
    mesh_lat,
    grid_send,
    mesh_send,
    enc_edges,
    enc_geom,
    enc_blocks,
    proc_edges,
    proc_geom,
    proc_blocks,
    enc_geo,
    proc_geo,
    enc_edge_in,
    enc_edge_out,
    enc_node_in,
    enc_node_out,
    proc_edge_in,
    proc_edge_out,
    proc_node_in,
    proc_node_out,
    enc_edge_gain,
    enc_node_gain,
    proc_edge_gain,
    proc_node_gain,
):
    plan = halo_plan(lax.axis_size("dom"))
    d = enc_geo.shape[1]
    grid_rows, mesh_rows = grid_lat.shape[0], mesh_lat.shape[0]
    n_enc, n_proc = enc_edges.shape[1], proc_edges.shape[1]
    enc_edge_gain, enc_node_gain, proc_edge_gain, proc_node_gain = (
        g.reshape(1, d) for g in (enc_edge_gain, enc_node_gain, proc_edge_gain, proc_node_gain)
    )
    k_in, k_out = enc_edge_in.shape[0], enc_edge_out.shape[0]
    n_in, n_out = enc_node_in.shape[0], enc_node_out.shape[0]
    width = grid_lat.shape[1]

    slots = grid_send.shape[2]
    (token,) = call(begin_kernel, [shape(16, 128)], [], flops=LONG)
    edge_half, *outgoing = call(
        functools.partial(first_pack_kernel, plan),
        [shape((k_in + 2 * k_out + n_out) // 2, d)] + [shape(slots, width)] * len(plan),
        [grid_lat, grid_send, enc_edge_in, enc_edge_out, enc_node_out, proc_edge_out, token],
    )
    first_across = to_chip(edge_half)
    (edge_across,) = call(rows_kernel, [shape((k_in + k_out) // 2, d)], [first_across])
    halos = [lax.ppermute(v, "dom", entry[0]) for v, entry in zip(outgoing, plan)]
    got = len(plan) * slots
    (lat,) = call(
        concat_kernel,
        [shape(grid_rows + mesh_rows + got, width)],
        [grid_lat, mesh_lat, *halos],
    )
    lat_across = to_chip(lat)
    lat_beside = to_core(lat)
    edge_beside = [to_core(enc_edge_in), to_core(enc_edge_out)]
    edge_round = to_group(edge_across)
    next_w, enc_emb, proc_emb = call(
        embed_kernel,
        [shape(n_in + n_out + k_in + k_out, d), shape(n_enc, d), shape(n_proc, d)],
        [
            enc_node_in, enc_node_out, proc_edge_in, proc_edge_out,
            enc_geom, enc_geo, proc_geom, proc_geo, lat,
        ],
        flops=2 * (n_enc + n_proc) * d * 128,
    )
    crossing, lat_sent = call(
        functools.partial(cross_kernel, ((0, n_in, BY_PART), (n_in + n_out, k_in, BY_GROUP))),
        [shape((n_in + k_in) // 2, d), shape(lat.shape[0], width)],
        [next_w, lat_across],
    )
    lat_both = to_core(lat_sent)
    next_across = to_chip(crossing)
    next_beside = to_core(next_w)

    halo_rows = padded(got)
    half = mesh_rows // 2
    keep, give, own_mesh = call(
        functools.partial(enc_kernel, plan, slots, grid_rows, mesh_rows, k_in),
        [shape(half, d)] * 3,
        [
            enc_emb, enc_edges, enc_edge_gain, lat, lat_across, lat_beside, lat_both,
            enc_edge_in, enc_edge_out, *edge_beside,
            edge_across, edge_round, to_core(edge_across), to_core(edge_round), enc_blocks,
        ],
        scratch=[
            pltpu.VMEM((grid_rows + mesh_rows + got, d), BF16),
            pltpu.VMEM((4 * (k_in + k_out), d), BF16),
            pltpu.VMEM((d + grid_rows + mesh_rows + halo_rows, d), BF16),
            pltpu.VMEM((n_enc, d), BF16),
            pltpu.VMEM((mesh_rows, d), F32),
        ],
        flops=2 * n_enc * d * (3 * d + grid_rows + mesh_rows + halo_rows),
        smem=1,
    )
    (chip_sum,) = call(add_kernel, [shape(half, d)], [keep, to_core(give)])
    node_across, proc_across = call(
        functools.partial(split_kernel, (n_in // 2, k_in // 2)),
        [shape((n_in + n_out) // 2, d), shape((k_in + k_out) // 2, d)],
        [first_across, next_across, chip_sum],
    )
    node_round = to_partition(node_across)
    proc_round = to_group(proc_across)
    node_both = to_core(node_across)
    slots = mesh_send.shape[2]
    mid_half, last_w, *outgoing = call(
        functools.partial(node_kernel, plan, n_in, n_out),
        [shape(half, d), shape(n_in + n_out, d)] + [shape(slots, d)] * len(plan),
        [
            own_mesh, chip_sum, to_chip(chip_sum), enc_node_gain, proc_node_in, proc_node_out,
            next_w, next_beside, node_across, node_round, node_both, to_core(node_round), mesh_send,
        ],
        scratch=[pltpu.VMEM((4 * (n_in + n_out), d), BF16)],
        flops=2 * half * d * 3 * d,
    )
    (proc_pair,) = call(pair_kernel, [shape(k_in + k_out, d)], [proc_across, proc_round, mid_half])
    halos = [lax.ppermute(v, "dom", entry[0]) for v, entry in zip(outgoing, plan)]
    (halo,) = call(concat_kernel, [shape(len(plan) * slots, d)], halos)
    halo_beside = to_core(halo)
    last_across, last_beside = to_chip(last_w), to_core(last_w)
    early = n_proc // 2
    table, pre, w_source, w_out = call(
        functools.partial(proc_first_kernel, k_in, n_in + n_out),
        [shape(d + 2 * mesh_rows, d), shape(early, d, F32), shape(d, d), shape(d, d)],
        [
            proc_emb, mid_half, to_core(mid_half), proc_edges, next_w, next_beside, proc_pair, to_core(proc_pair),
        ],
        scratch=[pltpu.VMEM((4 * (k_in + k_out), d), BF16), pltpu.VMEM((mesh_rows, d), BF16)],
        flops=2 * early * d * (d + 2 * mesh_rows),
    )
    halo_rows = padded(len(plan) * slots)
    keep, give = call(
        functools.partial(proc_second_kernel, plan, slots, mesh_rows),
        [shape(half, d), shape(half, d)],
        [proc_emb, proc_edges, proc_edge_gain, table, pre, w_source, w_out, halo, halo_beside, proc_blocks],
        scratch=[
            pltpu.VMEM((halo_rows, d), BF16),
            pltpu.VMEM((n_proc, d), BF16),
            pltpu.VMEM((mesh_rows, d), F32),
        ],
        flops=2 * n_proc * d * (2 * d + mesh_rows + halo_rows),
        smem=1,
    )
    quarter = mesh_rows // 4
    mine, other = call(fold_kernel, [shape(quarter, d)] * 2, [keep, to_core(give)])
    (result,) = call(
        functools.partial(out_kernel, n_in, n_out),
        [shape(quarter, d)],
        [mid_half, mine, to_chip(other), proc_node_gain, last_w, last_beside, last_across, to_core(last_across)],
        scratch=[pltpu.VMEM((4 * (n_in + n_out), d), BF16)],
        flops=2 * quarter * d * 3 * d,
    )
    return result


def solution(mesh):
    placed = (
        P(("groups", "dom"), "sub"),
        P(("groups", "dom"), "sub"),
        P("dom", None, None),
        P("dom", None, None),
        P(None, ("dom", "sub")),
        P(None, ("dom", "sub")),
        P("dom"),
        P(None, ("dom", "sub")),
        P(None, ("dom", "sub")),
        P("dom"),
        P(),
        P(),
        P("sub", None),
        P("sub", None),
        P("sub", None),
        P("sub", None),
        P("sub", None),
        P("sub", None),
        P("sub", None),
        P("sub", None),
        P(),
        P(),
        P(),
        P(),
    )
    return jax.shard_map(
        local,
        mesh=mesh,
        in_specs=placed,
        out_specs=P(("groups", "dom", "sub"), None),
        check_vma=False,
    )
```

```python
import functools

import jax
import jax.numpy as jnp
from jax import lax
from jax.experimental import pallas as pl
from jax.experimental.pallas import tpu as pltpu
from jax.sharding import PartitionSpec as P

BLOCK = 128
OFFSETS = (-2, -1, 1, 2)
STEP = 512
GATHERED = 1024
LONG = 30 * 10**9
BY_GROUP = ("groups",)
BY_PART = ("dom",)
VMEM_BYTES = 24 * 1024 * 1024
I16 = jnp.int16
BF16 = jnp.bfloat16
F32 = jnp.float32


def silu_of_half(h):
    return h + h * jnp.tanh(h)


def silu(v):
    return silu_of_half(0.5 * v)


def halved(v):
    return (v.astype(F32) * 0.5).astype(BF16)


def region_of(delta):
    return jnp.where(delta < 0, delta + 2, delta + 1)


def halo_plan(count):
    plan = []
    if count == 4:
        for bit in (1, 2, 3):
            pairs = [(d, d ^ bit) for d in range(4) if abs((d ^ bit) - d) <= 2]
            regions = [(OFFSETS.index((d ^ bit) - d) if abs((d ^ bit) - d) <= 2 else -1) for d in range(4)]
            plan.append((pairs, regions, regions))
    else:
        for region, offset in enumerate(OFFSETS):
            pairs = [(d, d + offset) for d in range(count) if 0 <= d + offset < count]
            plan.append((pairs, region, 3 - region))
    return plan


def by_index(choice, index):
    if isinstance(choice, int):
        return choice
    picked = jnp.int32(choice[0])
    for place in range(1, len(choice)):
        picked = jnp.where(index == place, choice[place], picked)
    return picked


def whole_refs(count):
    return [pl.BlockSpec(memory_space=pltpu.VMEM)] * count


def call(body, outs, args, scratch=(), flops=0, smem=0):
    moved = sum(a.size * a.dtype.itemsize for a in args) + sum(
        o.size * jnp.dtype(o.dtype).itemsize for o in outs
    )
    specs = whole_refs(len(args) - smem) + [pl.BlockSpec(memory_space=pltpu.SMEM)] * smem
    return pl.pallas_call(
        body,
        out_shape=tuple(outs),
        in_specs=specs,
        out_specs=tuple(whole_refs(len(outs))),
        scratch_shapes=list(scratch),
        compiler_params=pltpu.CompilerParams(vmem_limit_bytes=VMEM_BYTES),
        cost_estimate=pl.CostEstimate(flops=int(flops), bytes_accessed=int(moved), transcendentals=0),
    )(*args)


def dot(a, b):
    return jnp.dot(a, b, preferred_element_type=F32)


def dot_first(a, b):
    return lax.dot_general(a, b, (((0,), (0,)), ((), ())), preferred_element_type=F32)


def three_parts(v):
    a = v.astype(BF16)
    rest = v - a.astype(F32)
    b = rest.astype(BF16)
    c = (rest - b.astype(F32)).astype(BF16)
    return a, b, c


def embed_rows(geom, geo):
    a1, a2, a3 = three_parts(geom)
    b1, b2, b3 = three_parts(geo)
    left = jnp.concatenate([a1, a1, a2, a1, a2, a3], axis=0)
    right = jnp.concatenate([b1, b2, b1, b3, b2, b1], axis=0)
    return silu(dot_first(left, right)).astype(BF16)


def layer_norm(v, live=None):
    width = v.shape[-1]
    centered = v - jnp.sum(v, axis=-1, keepdims=True) * (1.0 / width)
    spread = jnp.sum(centered * centered, axis=-1, keepdims=True) * (1.0 / width)
    factor = lax.rsqrt(spread + 1e-05)
    if live is not None:
        factor = jnp.where(live, factor, 0.0)
    return centered * factor


def hot(cond):
    return jnp.where(cond, BF16(1), BF16(0))


def pick_rows(table, listed, rows=None):
    if rows is None:
        rows = lax.broadcasted_iota(I16, (table.shape[0], 1), 0)
    return dot_first(hot(rows == listed.astype(I16)), table).astype(BF16)


def pick_lists(plan, table, send, outs, rows=None):
    here = lax.axis_index("dom")
    for (pairs, sent, received), out in zip(plan, outs):
        region = jnp.maximum(by_index(sent, here), 0)
        out[...] = pick_rows(table, send[0, pl.ds(region, 1), :], rows)


def stack_into(out, parts):
    first = 0
    for part in parts:
        out[first : first + part.shape[0], :] = part[...]
        first += part.shape[0]


def begin_kernel(token):
    token[...] = jnp.zeros(token.shape, token.dtype)


def first_pack_kernel(plan, grid, send, w_in, w_out, n_out, p_out, token, half, *outs):
    place = 0
    for source, axes in ((w_in, BY_GROUP), (w_out, BY_GROUP), (n_out, BY_PART), (p_out, BY_GROUP)):
        rows = source.shape[0] // 2
        begin = pl.multiple_of(parity(axes) * rows, 64)
        half[place : place + rows, :] = source[pl.ds(begin, rows), :]
        place += rows
    pick_lists(plan, grid[...], send, outs)


def embed_kernel(e_in, e_out, p_in, p_out, egeom, egeo, pgeom, pgeo, after, weights, eout, pout):
    stack_into(weights, (e_in, e_out, p_in, p_out))
    for geom, geo, out in ((egeom, egeo, eout), (pgeom, pgeo, pout)):
        for begin in range(0, out.shape[0], STEP):
            out[begin : begin + STEP, :] = embed_rows(geom[:, begin : begin + STEP], geo[...])


def cross_kernel(parts, weights, lat, crossing, lat_out):
    lat_out[...] = lat[...]
    place = 0
    for first, rows, axes in parts:
        half = rows // 2
        begin = pl.multiple_of(first + parity(axes) * half, 64)
        crossing[place : place + half, :] = weights[pl.ds(begin, half), :]
        place += half


def rows_kernel(source, out):
    out[...] = source[: out.shape[0], :]


def pair_kernel(first, second, after, out):
    stack_into(out, (first, second))


def split_kernel(ins, early, source, after, node, proc):
    n, p = ins
    n_rest, p_rest = node.shape[0] - n, proc.shape[0] - p
    base = early.shape[0] - n_rest - p_rest
    stack_into(node, (source.at[pl.ds(0, n), :], early.at[pl.ds(base, n_rest), :]))
    stack_into(proc, (source.at[pl.ds(n, p), :], early.at[pl.ds(base + n_rest, p_rest), :]))


def concat_kernel(*refs):
    stack_into(refs[-1], refs[:-1])


def put_shard(target, source, first, step, part=0, parts=1):
    rows = target.shape[0] // (4 * parts)
    place = (lax.bitwise_xor(lax.axis_index("sub"), step) * parts + part) * rows
    target[pl.ds(pl.multiple_of(place, rows), rows), :] = source[first : first + rows, :]


def parity(axes):
    return lax.rem(sum(lax.axis_index(axis) for axis in axes), 2)


def put_half(target, k, source, step, other, axes=("groups",)):
    rows = target.shape[0] // 4
    which = lax.bitwise_xor(parity(axes), other)
    begin = lax.bitwise_xor(lax.axis_index("sub"), step) * rows
    for base, count in ((0, k // 2), (k // 2, (rows - k) // 2)):
        place = pl.multiple_of(begin + 2 * base + which * count, 64)
        target[pl.ds(place, count), :] = source[base : base + count, :]


def joined(stack, first, rows):
    step = stack.shape[0] // 4
    return jnp.concatenate([stack[k * step + first : k * step + first + rows, :] for k in range(4)], axis=0)


def halo_targets(plan, slots, node_rows, width):
    here = lax.axis_index("dom")
    lane = lax.broadcasted_iota(jnp.int32, (1, width), 1)
    target = jnp.full((1, width), -1, jnp.int32)
    for place, (pairs, sent, received) in enumerate(plan):
        region = by_index(received, here)
        first = jnp.where(region < 0, -4 * node_rows, node_rows + region * slots)
        inside = (lane >= place * slots) & (lane < (place + 1) * slots)
        target = jnp.where(inside, lane - place * slots + first, target)
    return target.astype(I16)


def columns(edges, first):
    pair = edges[:, first : first + STEP]
    zero = jnp.zeros((8 - pair.shape[0], STEP), jnp.int32)
    upright = jnp.transpose(jnp.concatenate([pair, zero], axis=0).astype(F32)).astype(jnp.int32).astype(I16)
    return upright[:, 0:1], upright[:, 1:2]


def edge_blocks(edges, live_edges, first_stage, w_out, messages, totals):
    count = edges.shape[1]
    steps = count // STEP
    row = lax.broadcasted_iota(I16, (totals.shape[0], 1), 0)
    quarter = lax.axis_index("sub")
    sums, raw = {}, {}
    for turn in range(steps + 2):
        if turn < steps:
            sums[turn] = first_stage(turn * STEP)
        if 0 <= turn - 1 < steps:
            raw[turn - 1] = dot(silu_of_half(sums.pop(turn - 1)).astype(BF16), w_out)
        if turn < 2:
            continue
        first = (turn - 2) * STEP
        place = lax.broadcasted_iota(jnp.int32, (STEP, 1), 0) + (first + quarter * count)
        message = layer_norm(raw.pop(turn - 2), place < live_edges)
        messages[first : first + STEP, :] = message.astype(BF16)
        done = first + STEP
        if done % GATHERED == 0 or done == count:
            begin = (first // GATHERED) * GATHERED
            collect = hot(row == edges[1:2, begin:done].astype(I16))
            part = dot(collect, messages[begin:done, :])
            if begin == 0:
                totals[...] = part
            else:
                totals[...] += part


def hand_out(totals, gain, keep, give):
    rows = totals.shape[0] // 4
    core = lax.rem(lax.axis_index("sub"), 2)
    for half in range(2):
        for out, which in ((keep, core), (give, 1 - core)):
            place = pl.multiple_of((2 * half + which) * rows, rows)
            out[half * rows : (half + 1) * rows, :] = (totals[pl.ds(place, rows), :] * gain[...]).astype(BF16)


def enc_kernel(
    plan, slots, grid_rows, mesh_rows, k_in, emb, edges, gain, l0, l1, l2, l3, o_in, o_out, b_in, b_out,
    across, round_, both, round_both, live, keep, give, own_mesh, full, stack, table, messages, totals,
):
    d = gain.shape[1]
    quarter = lax.axis_index("sub")
    width = l0.shape[1]
    for shard, step in zip((l0, l1, l2, l3), (0, 2, 1, 3)):
        place = pl.multiple_of(lax.bitwise_xor(quarter, step) * width, width)
        full[:, pl.ds(place, width)] = shard[...]
    step = k_in + d // 4
    for first, second, bit in ((o_in, o_out, 0), (b_in, b_out, 1)):
        place = lax.bitwise_xor(quarter, bit) * step
        stack[pl.ds(pl.multiple_of(place, 128), k_in), :] = first[...]
        stack[pl.ds(pl.multiple_of(place + k_in, 128), d // 4), :] = second[...]
    put_half(stack, k_in, across, 2, 0)
    put_half(stack, k_in, round_, 2, 1)
    put_half(stack, k_in, both, 3, 0)
    put_half(stack, k_in, round_both, 3, 1)
    rows = mesh_rows // 4
    core = lax.rem(quarter, 2)
    for half in range(2):
        place = pl.multiple_of(grid_rows + (2 * half + core) * rows, rows)
        own_mesh[half * rows : (half + 1) * rows, :] = full[pl.ds(place, rows), :]

    w_in = joined(stack, 0, k_in)
    halo_first, got = grid_rows + mesh_rows, full.shape[0] - grid_rows - mesh_rows
    table[:d, :] = halved(w_in[:d, :])
    table[d : d + grid_rows, :] = halved(dot(full[:grid_rows, :], w_in[d : 2 * d, :]))
    base = d + grid_rows + mesh_rows
    table[d + grid_rows : base, :] = halved(dot(full[grid_rows:halo_first, :], w_in[2 * d :, :]))
    table[base : base + got, :] = halved(dot(full[halo_first:, :], w_in[d : 2 * d, :]))
    if base + got < table.shape[0]:
        table[base + got :, :] = jnp.zeros((table.shape[0] - base - got, d), BF16)
    targets = halo_targets(plan, slots, grid_rows, table.shape[0] - base)
    own = lax.broadcasted_iota(I16, (1, grid_rows), 1)
    mesh = lax.broadcasted_iota(I16, (1, mesh_rows), 1)

    def first_stage(first):
        senders, receivers = columns(edges, first)
        chosen = [emb[first : first + STEP, :], hot(own == senders), hot(mesh == receivers), hot(targets == senders)]
        return dot(jnp.concatenate(chosen, axis=1), table[...])

    edge_blocks(edges, live[0] * BLOCK, first_stage, joined(stack, k_in, d // 4), messages, totals)
    hand_out(totals, gain, keep, give)


def node_update(mesh, shares, w_in, w_out, gain):
    stacked = jnp.concatenate([mesh, shares], axis=1)
    hidden = silu(dot(stacked, w_in)).astype(BF16)
    update = layer_norm(dot(hidden, w_out)) * gain
    return (mesh.astype(F32) + update).astype(BF16)


def add(mine, theirs):
    return (mine.astype(F32) + theirs.astype(F32)).astype(BF16)


def add_kernel(mine, theirs, out):
    out[...] = add(mine[...], theirs[...])


def node_kernel(
    plan, k_in, k_out, mesh, mine, theirs, gain, n_in, n_out, w0, w1, w2, w3, w4, w5, send, out, packed, *rest
):
    outs, stack = rest[:-1], rest[-1]
    put_shard(stack, w0, 0, 0)
    put_shard(stack, w1, 0, 1)
    put_half(stack, k_in, w2, 2, 0, BY_PART)
    put_half(stack, k_in, w3, 2, 1, BY_PART)
    put_half(stack, k_in, w4, 3, 0, BY_PART)
    put_half(stack, k_in, w5, 3, 1, BY_PART)
    w_in, w_out = joined(stack, 0, k_in), joined(stack, k_in, k_out)
    fresh = node_update(mesh[...], add(mine[...], theirs[...]), w_in, w_out, gain[...])
    out[...] = fresh
    half = fresh.shape[0] // 2
    core = lax.rem(lax.axis_index("sub"), 2)
    place = lax.broadcasted_iota(jnp.int32, (fresh.shape[0], 1), 0)
    rows = place + core * half + jnp.where(place < half, 0, half)
    pick_lists(plan, fresh, send, outs, rows.astype(I16))
    stack_into(packed, (n_in, n_out))


def proc_first_kernel(
    k_in, first_row, emb, mine, theirs, edges, w0, w1, pair, pair_beside,
    table, pre, w_source, w_out, stack, full,
):
    d = full.shape[1]
    node_rows = full.shape[0]
    rows = node_rows // 4
    core = lax.rem(lax.axis_index("sub"), 2)
    for half in range(2):
        for part, which in ((mine, core), (theirs, 1 - core)):
            place = pl.multiple_of((2 * half + which) * rows, rows)
            full[pl.ds(place, rows), :] = part[half * rows : (half + 1) * rows, :]
    put_shard(stack, w0, first_row, 0)
    put_shard(stack, w1, first_row, 1)
    rows = pair.shape[0] // 2
    for other in range(2):
        put_half(stack, k_in, pair.at[pl.ds(other * rows, rows), :], 2, other)
        put_half(stack, k_in, pair_beside.at[pl.ds(other * rows, rows), :], 3, other)
    w_in = joined(stack, 0, k_in)
    w_out[...] = joined(stack, k_in, d // 4)
    w_source[...] = w_in[d : 2 * d, :]
    table[:d, :] = halved(w_in[:d, :])
    table[d : d + node_rows, :] = halved(dot(full[...], w_in[d : 2 * d, :]))
    table[d + node_rows :, :] = halved(dot(full[...], w_in[2 * d :, :]))
    lane = lax.broadcasted_iota(I16, (1, node_rows), 1)
    for first in range(0, pre.shape[0], STEP):
        pre[first : first + STEP, :] = dot(own_chosen(emb, edges, lane, first), table[...])


def own_chosen(emb, edges, lane, first):
    senders, receivers = columns(edges, first)
    return jnp.concatenate([emb[first : first + STEP, :], hot(lane == senders), hot(lane == receivers)], axis=1)


def proc_second_kernel(
    plan, slots, node_rows, emb, edges, gain, table, pre, w_source, w_out, halo, halo_beside,
    live, keep, give, halo_table, messages, totals,
):
    d = pre.shape[1]
    got = halo[...] + halo_beside[...]
    halo_table[: got.shape[0], :] = halved(dot(got, w_source[...]))
    if got.shape[0] < halo_table.shape[0]:
        halo_table[got.shape[0] :, :] = jnp.zeros((halo_table.shape[0] - got.shape[0], d), BF16)
    targets = halo_targets(plan, slots, node_rows, halo_table.shape[0])
    lane = lax.broadcasted_iota(I16, (1, node_rows), 1)

    def first_stage(first):
        senders, receivers = columns(edges, first)
        remote = dot(hot(targets == senders), halo_table[...])
        if first < pre.shape[0]:
            return pre[first : first + STEP, :] + remote
        return dot(own_chosen(emb, edges, lane, first), table[...]) + remote

    edge_blocks(edges, live[0] * BLOCK, first_stage, w_out[...], messages, totals)
    hand_out(totals, gain, keep, give)


def fold_kernel(mine, theirs, keep, give):
    rows = mine.shape[0] // 2
    chip = lax.div(lax.axis_index("sub"), 2)
    for out, which in ((keep, chip), (give, 1 - chip)):
        place = pl.multiple_of(which * rows, rows)
        out[...] = add(mine[pl.ds(place, rows), :], theirs[pl.ds(place, rows), :])


def out_kernel(k_in, k_out, middle, mine, theirs, gain, w0, w1, w2, w3, out, stack):
    rows = mine.shape[0]
    chip = lax.div(lax.axis_index("sub"), 2)
    mesh = middle[pl.ds(pl.multiple_of(chip * rows, rows), rows), :]
    for shard, bit in zip((w0, w1, w2, w3), (0, 1, 2, 3)):
        put_shard(stack, shard, 0, bit)
    w_in, w_out = joined(stack, 0, k_in), joined(stack, k_in, k_out)
    out[...] = node_update(mesh, add(mine[...], theirs[...]), w_in, w_out, gain[...])


def to_chip(v):
    return lax.ppermute(v, "sub", [(i, i ^ 2) for i in range(4)])


def to_core(v):
    return lax.ppermute(v, "sub", [(i, i ^ 1) for i in range(4)])


def to_group(v):
    count = lax.axis_size("groups")
    return lax.ppermute(v, "groups", [(i, count - 1 - i) for i in range(count)])


def to_partition(v):
    return lax.ppermute(v, "dom", [(i, i ^ 1) for i in range(lax.axis_size("dom"))])


def shape(rows, width, dtype=BF16):
    return jax.ShapeDtypeStruct((rows, width), dtype)


def padded(rows):
    return -(-rows // 128) * 128


def local(
    grid_lat,
    mesh_lat,
    grid_send,
    mesh_send,
    enc_edges,
    enc_geom,
    enc_blocks,
    proc_edges,
    proc_geom,
    proc_blocks,
    enc_geo,
    proc_geo,
    enc_edge_in,
    enc_edge_out,
    enc_node_in,
    enc_node_out,
    proc_edge_in,
    proc_edge_out,
    proc_node_in,
    proc_node_out,
    enc_edge_gain,
    enc_node_gain,
    proc_edge_gain,
    proc_node_gain,
):
    plan = halo_plan(lax.axis_size("dom"))
    d = enc_geo.shape[1]
    grid_rows, mesh_rows = grid_lat.shape[0], mesh_lat.shape[0]
    n_enc, n_proc = enc_edges.shape[1], proc_edges.shape[1]
    enc_edge_gain, enc_node_gain, proc_edge_gain, proc_node_gain = (
        g.reshape(1, d) for g in (enc_edge_gain, enc_node_gain, proc_edge_gain, proc_node_gain)
    )
    k_in, k_out = enc_edge_in.shape[0], enc_edge_out.shape[0]
    n_in, n_out = enc_node_in.shape[0], enc_node_out.shape[0]
    width = grid_lat.shape[1]

    slots = grid_send.shape[2]
    (token,) = call(begin_kernel, [shape(16, 128)], [], flops=LONG)
    edge_half, *outgoing = call(
        functools.partial(first_pack_kernel, plan),
        [shape((k_in + 2 * k_out + n_out) // 2, d)] + [shape(slots, width)] * len(plan),
        [grid_lat, grid_send, enc_edge_in, enc_edge_out, enc_node_out, proc_edge_out, token],
    )
    first_across = to_chip(edge_half)
    (edge_across,) = call(rows_kernel, [shape((k_in + k_out) // 2, d)], [first_across])
    halos = [lax.ppermute(v, "dom", entry[0]) for v, entry in zip(outgoing, plan)]
    got = len(plan) * slots
    (lat,) = call(
        concat_kernel,
        [shape(grid_rows + mesh_rows + got, width)],
        [grid_lat, mesh_lat, *halos],
    )
    lat_across = to_chip(lat)
    lat_beside = to_core(lat)
    edge_beside = [to_core(enc_edge_in), to_core(enc_edge_out)]
    edge_round = to_group(edge_across)
    next_w, enc_emb, proc_emb = call(
        embed_kernel,
        [shape(n_in + n_out + k_in + k_out, d), shape(n_enc, d), shape(n_proc, d)],
        [
            enc_node_in, enc_node_out, proc_edge_in, proc_edge_out,
            enc_geom, enc_geo, proc_geom, proc_geo, lat,
        ],
        flops=2 * (n_enc + n_proc) * d * 128,
    )
    crossing, lat_sent = call(
        functools.partial(cross_kernel, ((0, n_in, BY_PART), (n_in + n_out, k_in, BY_GROUP))),
        [shape((n_in + k_in) // 2, d), shape(lat.shape[0], width)],
        [next_w, lat_across],
    )
    lat_both = to_core(lat_sent)
    next_across = to_chip(crossing)
    next_beside = to_core(next_w)

    halo_rows = padded(got)
    half = mesh_rows // 2
    keep, give, own_mesh = call(
        functools.partial(enc_kernel, plan, slots, grid_rows, mesh_rows, k_in),
        [shape(half, d)] * 3,
        [
            enc_emb, enc_edges, enc_edge_gain, lat, lat_across, lat_beside, lat_both,
            enc_edge_in, enc_edge_out, *edge_beside,
            edge_across, edge_round, to_core(edge_across), to_core(edge_round), enc_blocks,
        ],
        scratch=[
            pltpu.VMEM((grid_rows + mesh_rows + got, d), BF16),
            pltpu.VMEM((4 * (k_in + k_out), d), BF16),
            pltpu.VMEM((d + grid_rows + mesh_rows + halo_rows, d), BF16),
            pltpu.VMEM((n_enc, d), BF16),
            pltpu.VMEM((mesh_rows, d), F32),
        ],
        flops=2 * n_enc * d * (3 * d + grid_rows + mesh_rows + halo_rows),
        smem=1,
    )
    (chip_sum,) = call(add_kernel, [shape(half, d)], [keep, to_core(give)])
    node_across, proc_across = call(
        functools.partial(split_kernel, (n_in // 2, k_in // 2)),
        [shape((n_in + n_out) // 2, d), shape((k_in + k_out) // 2, d)],
        [first_across, next_across, chip_sum],
    )
    node_round = to_partition(node_across)
    proc_round = to_group(proc_across)
    node_both = to_core(node_across)
    slots = mesh_send.shape[2]
    mid_half, last_w, *outgoing = call(
        functools.partial(node_kernel, plan, n_in, n_out),
        [shape(half, d), shape(n_in + n_out, d)] + [shape(slots, d)] * len(plan),
        [
            own_mesh, chip_sum, to_chip(chip_sum), enc_node_gain, proc_node_in, proc_node_out,
            next_w, next_beside, node_across, node_round, node_both, to_core(node_round), mesh_send,
        ],
        scratch=[pltpu.VMEM((4 * (n_in + n_out), d), BF16)],
        flops=2 * half * d * 3 * d,
    )
    (proc_pair,) = call(pair_kernel, [shape(k_in + k_out, d)], [proc_across, proc_round, mid_half])
    halos = [lax.ppermute(v, "dom", entry[0]) for v, entry in zip(outgoing, plan)]
    (halo,) = call(concat_kernel, [shape(len(plan) * slots, d)], halos)
    halo_beside = to_core(halo)
    last_across, last_beside = to_chip(last_w), to_core(last_w)
    early = n_proc // 2
    table, pre, w_source, w_out = call(
        functools.partial(proc_first_kernel, k_in, n_in + n_out),
        [shape(d + 2 * mesh_rows, d), shape(early, d, F32), shape(d, d), shape(d, d)],
        [
            proc_emb, mid_half, to_core(mid_half), proc_edges, next_w, next_beside, proc_pair, to_core(proc_pair),
        ],
        scratch=[pltpu.VMEM((4 * (k_in + k_out), d), BF16), pltpu.VMEM((mesh_rows, d), BF16)],
        flops=2 * early * d * (d + 2 * mesh_rows),
    )
    halo_rows = padded(len(plan) * slots)
    keep, give = call(
        functools.partial(proc_second_kernel, plan, slots, mesh_rows),
        [shape(half, d), shape(half, d)],
        [proc_emb, proc_edges, proc_edge_gain, table, pre, w_source, w_out, halo, halo_beside, proc_blocks],
        scratch=[
            pltpu.VMEM((halo_rows, d), BF16),
            pltpu.VMEM((n_proc, d), BF16),
            pltpu.VMEM((mesh_rows, d), F32),
        ],
        flops=2 * n_proc * d * (2 * d + mesh_rows + halo_rows),
        smem=1,
    )
    quarter = mesh_rows // 4
    mine, other = call(fold_kernel, [shape(quarter, d)] * 2, [keep, to_core(give)])
    (result,) = call(
        functools.partial(out_kernel, n_in, n_out),
        [shape(quarter, d)],
        [mid_half, mine, to_chip(other), proc_node_gain, last_w, last_beside, last_across, to_core(last_across)],
        scratch=[pltpu.VMEM((4 * (n_in + n_out), d), BF16)],
        flops=2 * quarter * d * 3 * d,
    )
    return result


def solution(mesh):
    placed = (
        P(("groups", "dom"), "sub"),
        P(("groups", "dom"), "sub"),
        P("dom", None, None),
        P("dom", None, None),
        P(None, ("dom", "sub")),
        P(None, ("dom", "sub")),
        P("dom"),
        P(None, ("dom", "sub")),
        P(None, ("dom", "sub")),
        P("dom"),
        P(),
        P(),
        P("sub", None),
        P("sub", None),
        P("sub", None),
        P("sub", None),
        P("sub", None),
        P("sub", None),
        P("sub", None),
        P("sub", None),
        P(),
        P(),
        P(),
        P(),
    )
    return jax.shard_map(
        local,
        mesh=mesh,
        in_specs=placed,
        out_specs=P(("groups", "dom", "sub"), None),
        check_vma=False,
    )
```

```python
import functools

import jax
import jax.numpy as jnp
from jax import lax
from jax.experimental import pallas as pl
from jax.experimental.pallas import tpu as pltpu
from jax.sharding import PartitionSpec as P

BLOCK = 128
OFFSETS = (-2, -1, 1, 2)
STEP = 512
GATHERED = 1024
LONG = 30 * 10**9
BY_GROUP = ("groups",)
BY_PART = ("dom",)
VMEM_BYTES = 24 * 1024 * 1024
I16 = jnp.int16
BF16 = jnp.bfloat16
F32 = jnp.float32


def silu_of_half(h):
    return h + h * jnp.tanh(h)


def silu(v):
    return silu_of_half(0.5 * v)


def halved(v):
    return (v.astype(F32) * 0.5).astype(BF16)


def region_of(delta):
    return jnp.where(delta < 0, delta + 2, delta + 1)


def halo_plan(count):
    plan = []
    if count == 4:
        for bit in (1, 2, 3):
            pairs = [(d, d ^ bit) for d in range(4) if abs((d ^ bit) - d) <= 2]
            regions = [(OFFSETS.index((d ^ bit) - d) if abs((d ^ bit) - d) <= 2 else -1) for d in range(4)]
            plan.append((pairs, regions, regions))
    else:
        for region, offset in enumerate(OFFSETS):
            pairs = [(d, d + offset) for d in range(count) if 0 <= d + offset < count]
            plan.append((pairs, region, 3 - region))
    return plan


def by_index(choice, index):
    if isinstance(choice, int):
        return choice
    picked = jnp.int32(choice[0])
    for place in range(1, len(choice)):
        picked = jnp.where(index == place, choice[place], picked)
    return picked


def whole_refs(count):
    return [pl.BlockSpec(memory_space=pltpu.VMEM)] * count


def call(body, outs, args, scratch=(), flops=0, smem=0):
    moved = sum(a.size * a.dtype.itemsize for a in args) + sum(
        o.size * jnp.dtype(o.dtype).itemsize for o in outs
    )
    specs = whole_refs(len(args) - smem) + [pl.BlockSpec(memory_space=pltpu.SMEM)] * smem
    return pl.pallas_call(
        body,
        out_shape=tuple(outs),
        in_specs=specs,
        out_specs=tuple(whole_refs(len(outs))),
        scratch_shapes=list(scratch),
        compiler_params=pltpu.CompilerParams(vmem_limit_bytes=VMEM_BYTES),
        cost_estimate=pl.CostEstimate(flops=int(flops), bytes_accessed=int(moved), transcendentals=0),
    )(*args)


def dot(a, b):
    return jnp.dot(a, b, preferred_element_type=F32)


def dot_first(a, b):
    return lax.dot_general(a, b, (((0,), (0,)), ((), ())), preferred_element_type=F32)


def three_parts(v):
    a = v.astype(BF16)
    rest = v - a.astype(F32)
    b = rest.astype(BF16)
    c = (rest - b.astype(F32)).astype(BF16)
    return a, b, c


def embed_rows(geom, geo):
    a1, a2, a3 = three_parts(geom)
    b1, b2, b3 = three_parts(geo)
    left = jnp.concatenate([a1, a1, a2, a1, a2, a3], axis=0)
    right = jnp.concatenate([b1, b2, b1, b3, b2, b1], axis=0)
    return silu(dot_first(left, right)).astype(BF16)


def layer_norm(v, live=None):
    width = v.shape[-1]
    centered = v - jnp.sum(v, axis=-1, keepdims=True) * (1.0 / width)
    spread = jnp.sum(centered * centered, axis=-1, keepdims=True) * (1.0 / width)
    factor = lax.rsqrt(spread + 1e-05)
    if live is not None:
        factor = jnp.where(live, factor, 0.0)
    return centered * factor


def hot(cond):
    return jnp.where(cond, BF16(1), BF16(0))


def pick_rows(table, listed, rows=None):
    if rows is None:
        rows = lax.broadcasted_iota(I16, (table.shape[0], 1), 0)
    return dot_first(hot(rows == listed.astype(I16)), table).astype(BF16)


def pick_lists(plan, table, send, outs, rows=None):
    here = lax.axis_index("dom")
    for (pairs, sent, received), out in zip(plan, outs):
        region = jnp.maximum(by_index(sent, here), 0)
        out[...] = pick_rows(table, send[0, pl.ds(region, 1), :], rows)


def stack_into(out, parts):
    first = 0
    for part in parts:
        out[first : first + part.shape[0], :] = part[...]
        first += part.shape[0]


def begin_kernel(token):
    token[...] = jnp.zeros(token.shape, token.dtype)


def first_pack_kernel(plan, grid, send, w_in, w_out, n_out, p_out, token, half, *outs):
    place = 0
    for source, axes in ((w_in, BY_GROUP), (w_out, BY_GROUP), (n_out, BY_PART), (p_out, BY_GROUP)):
        rows = source.shape[0] // 2
        begin = pl.multiple_of(parity(axes) * rows, 64)
        half[place : place + rows, :] = source[pl.ds(begin, rows), :]
        place += rows
    pick_lists(plan, grid[...], send, outs)


def embed_kernel(e_in, e_out, p_in, p_out, egeom, egeo, pgeom, pgeo, after, node, proc, eout, pout):
    stack_into(node, (e_in, e_out))
    stack_into(proc, (p_in, p_out))
    for geom, geo, out in ((egeom, egeo, eout), (pgeom, pgeo, pout)):
        for begin in range(0, out.shape[0], STEP):
            out[begin : begin + STEP, :] = embed_rows(geom[:, begin : begin + STEP], geo[...])


def cross_kernel(counts, node, proc, lat, crossing, lat_out):
    lat_out[...] = lat[...]
    place = 0
    for stack, rows, axes in ((node, counts[0], BY_PART), (proc, counts[1], BY_GROUP)):
        half = rows // 2
        begin = pl.multiple_of(parity(axes) * half, 64)
        crossing[place : place + half, :] = stack[pl.ds(begin, half), :]
        place += half


def rows_kernel(source, out):
    out[...] = source[: out.shape[0], :]


def pair_kernel(first, second, after, out):
    stack_into(out, (first, second))


def split_kernel(ins, early, source, after, node, proc):
    n, p = ins
    n_rest, p_rest = node.shape[0] - n, proc.shape[0] - p
    base = early.shape[0] - n_rest - p_rest
    stack_into(node, (source.at[pl.ds(0, n), :], early.at[pl.ds(base, n_rest), :]))
    stack_into(proc, (source.at[pl.ds(n, p), :], early.at[pl.ds(base + n_rest, p_rest), :]))


def concat_kernel(*refs):
    stack_into(refs[-1], refs[:-1])


def put_shard(target, source, first, step, part=0, parts=1):
    rows = target.shape[0] // (4 * parts)
    place = (lax.bitwise_xor(lax.axis_index("sub"), step) * parts + part) * rows
    target[pl.ds(pl.multiple_of(place, rows), rows), :] = source[first : first + rows, :]


def parity(axes):
    return lax.rem(sum(lax.axis_index(axis) for axis in axes), 2)


def put_half(target, k, source, step, other, axes=("groups",)):
    rows = target.shape[0] // 4
    which = lax.bitwise_xor(parity(axes), other)
    begin = lax.bitwise_xor(lax.axis_index("sub"), step) * rows
    for base, count in ((0, k // 2), (k // 2, (rows - k) // 2)):
        place = pl.multiple_of(begin + 2 * base + which * count, 64)
        target[pl.ds(place, count), :] = source[base : base + count, :]


def joined(stack, first, rows):
    step = stack.shape[0] // 4
    return jnp.concatenate([stack[k * step + first : k * step + first + rows, :] for k in range(4)], axis=0)


def halo_targets(plan, slots, node_rows, width):
    here = lax.axis_index("dom")
    lane = lax.broadcasted_iota(jnp.int32, (1, width), 1)
    target = jnp.full((1, width), -1, jnp.int32)
    for place, (pairs, sent, received) in enumerate(plan):
        region = by_index(received, here)
        first = jnp.where(region < 0, -4 * node_rows, node_rows + region * slots)
        inside = (lane >= place * slots) & (lane < (place + 1) * slots)
        target = jnp.where(inside, lane - place * slots + first, target)
    return target.astype(I16)


def columns(edges, first):
    pair = edges[:, first : first + STEP]
    zero = jnp.zeros((8 - pair.shape[0], STEP), jnp.int32)
    upright = jnp.transpose(jnp.concatenate([pair, zero], axis=0).astype(F32)).astype(jnp.int32).astype(I16)
    return upright[:, 0:1], upright[:, 1:2]


def edge_blocks(edges, live_edges, first_stage, w_out, messages, totals):
    count = edges.shape[1]
    steps = count // STEP
    row = lax.broadcasted_iota(I16, (totals.shape[0], 1), 0)
    quarter = lax.axis_index("sub")
    sums, raw = {}, {}
    for turn in range(steps + 2):
        if turn < steps:
            sums[turn] = first_stage(turn * STEP)
        if 0 <= turn - 1 < steps:
            raw[turn - 1] = dot(silu_of_half(sums.pop(turn - 1)).astype(BF16), w_out)
        if turn < 2:
            continue
        first = (turn - 2) * STEP
        place = lax.broadcasted_iota(jnp.int32, (STEP, 1), 0) + (first + quarter * count)
        message = layer_norm(raw.pop(turn - 2), place < live_edges)
        messages[first : first + STEP, :] = message.astype(BF16)
        done = first + STEP
        if done % GATHERED == 0 or done == count:
            begin = (first // GATHERED) * GATHERED
            collect = hot(row == edges[1:2, begin:done].astype(I16))
            part = dot(collect, messages[begin:done, :])
            if begin == 0:
                totals[...] = part
            else:
                totals[...] += part


def hand_out(totals, gain, keep, give):
    rows = totals.shape[0] // 4
    core = lax.rem(lax.axis_index("sub"), 2)
    for half in range(2):
        for out, which in ((keep, core), (give, 1 - core)):
            place = pl.multiple_of((2 * half + which) * rows, rows)
            out[half * rows : (half + 1) * rows, :] = (totals[pl.ds(place, rows), :] * gain[...]).astype(BF16)


def enc_kernel(
    plan, slots, grid_rows, mesh_rows, k_in, emb, edges, gain, l0, l1, l2, l3, o_in, o_out, b_in, b_out,
    across, round_, both, round_both, live, keep, give, own_mesh, full, stack, table, messages, totals,
):
    d = gain.shape[1]
    quarter = lax.axis_index("sub")
    width = l0.shape[1]
    for shard, step in zip((l0, l1, l2, l3), (0, 2, 1, 3)):
        place = pl.multiple_of(lax.bitwise_xor(quarter, step) * width, width)
        full[:, pl.ds(place, width)] = shard[...]
    step = k_in + d // 4
    for first, second, bit in ((o_in, o_out, 0), (b_in, b_out, 1)):
        place = lax.bitwise_xor(quarter, bit) * step
        stack[pl.ds(pl.multiple_of(place, 128), k_in), :] = first[...]
        stack[pl.ds(pl.multiple_of(place + k_in, 128), d // 4), :] = second[...]
    put_half(stack, k_in, across, 2, 0)
    put_half(stack, k_in, round_, 2, 1)
    put_half(stack, k_in, both, 3, 0)
    put_half(stack, k_in, round_both, 3, 1)
    rows = mesh_rows // 4
    core = lax.rem(quarter, 2)
    for half in range(2):
        place = pl.multiple_of(grid_rows + (2 * half + core) * rows, rows)
        own_mesh[half * rows : (half + 1) * rows, :] = full[pl.ds(place, rows), :]

    w_in = joined(stack, 0, k_in)
    halo_first, got = grid_rows + mesh_rows, full.shape[0] - grid_rows - mesh_rows
    table[:d, :] = halved(w_in[:d, :])
    table[d : d + grid_rows, :] = halved(dot(full[:grid_rows, :], w_in[d : 2 * d, :]))
    base = d + grid_rows + mesh_rows
    table[d + grid_rows : base, :] = halved(dot(full[grid_rows:halo_first, :], w_in[2 * d :, :]))
    table[base : base + got, :] = halved(dot(full[halo_first:, :], w_in[d : 2 * d, :]))
    if base + got < table.shape[0]:
        table[base + got :, :] = jnp.zeros((table.shape[0] - base - got, d), BF16)
    targets = halo_targets(plan, slots, grid_rows, table.shape[0] - base)
    own = lax.broadcasted_iota(I16, (1, grid_rows), 1)
    mesh = lax.broadcasted_iota(I16, (1, mesh_rows), 1)

    def first_stage(first):
        senders, receivers = columns(edges, first)
        chosen = [emb[first : first + STEP, :], hot(own == senders), hot(mesh == receivers), hot(targets == senders)]
        return dot(jnp.concatenate(chosen, axis=1), table[...])

    edge_blocks(edges, live[0] * BLOCK, first_stage, joined(stack, k_in, d // 4), messages, totals)
    hand_out(totals, gain, keep, give)


def node_update(mesh, shares, w_in, w_out, gain):
    stacked = jnp.concatenate([mesh, shares], axis=1)
    hidden = silu(dot(stacked, w_in)).astype(BF16)
    update = layer_norm(dot(hidden, w_out)) * gain
    return (mesh.astype(F32) + update).astype(BF16)


def add(mine, theirs):
    return (mine.astype(F32) + theirs.astype(F32)).astype(BF16)


def add_kernel(mine, theirs, out):
    out[...] = add(mine[...], theirs[...])


def node_kernel(
    plan, k_in, k_out, mesh, mine, theirs, gain, n_in, n_out, w0, w1, w2, w3, w4, w5, send, after, out, packed, *rest
):
    outs, stack = rest[:-1], rest[-1]
    put_shard(stack, w0, 0, 0)
    put_shard(stack, w1, 0, 1)
    put_half(stack, k_in, w2, 2, 0, BY_PART)
    put_half(stack, k_in, w3, 2, 1, BY_PART)
    put_half(stack, k_in, w4, 3, 0, BY_PART)
    put_half(stack, k_in, w5, 3, 1, BY_PART)
    w_in, w_out = joined(stack, 0, k_in), joined(stack, k_in, k_out)
    fresh = node_update(mesh[...], add(mine[...], theirs[...]), w_in, w_out, gain[...])
    out[...] = fresh
    half = fresh.shape[0] // 2
    core = lax.rem(lax.axis_index("sub"), 2)
    place = lax.broadcasted_iota(jnp.int32, (fresh.shape[0], 1), 0)
    rows = place + core * half + jnp.where(place < half, 0, half)
    pick_lists(plan, fresh, send, outs, rows.astype(I16))
    stack_into(packed, (n_in, n_out))


def proc_first_kernel(
    k_in, emb, mine, theirs, edges, w0, w1, pair, pair_beside,
    table, pre, w_source, w_out, stack, full,
):
    d = full.shape[1]
    node_rows = full.shape[0]
    rows = node_rows // 4
    core = lax.rem(lax.axis_index("sub"), 2)
    for half in range(2):
        for part, which in ((mine, core), (theirs, 1 - core)):
            place = pl.multiple_of((2 * half + which) * rows, rows)
            full[pl.ds(place, rows), :] = part[half * rows : (half + 1) * rows, :]
    put_shard(stack, w0, 0, 0)
    put_shard(stack, w1, 0, 1)
    rows = pair.shape[0] // 2
    for other in range(2):
        put_half(stack, k_in, pair.at[pl.ds(other * rows, rows), :], 2, other)
        put_half(stack, k_in, pair_beside.at[pl.ds(other * rows, rows), :], 3, other)
    w_in = joined(stack, 0, k_in)
    w_out[...] = joined(stack, k_in, d // 4)
    w_source[...] = w_in[d : 2 * d, :]
    table[:d, :] = halved(w_in[:d, :])
    table[d : d + node_rows, :] = halved(dot(full[...], w_in[d : 2 * d, :]))
    table[d + node_rows :, :] = halved(dot(full[...], w_in[2 * d :, :]))
    lane = lax.broadcasted_iota(I16, (1, node_rows), 1)
    for first in range(0, pre.shape[0], STEP):
        pre[first : first + STEP, :] = dot(own_chosen(emb, edges, lane, first), table[...])


def own_chosen(emb, edges, lane, first):
    senders, receivers = columns(edges, first)
    return jnp.concatenate([emb[first : first + STEP, :], hot(lane == senders), hot(lane == receivers)], axis=1)


def proc_second_kernel(
    plan, slots, node_rows, emb, edges, gain, table, pre, w_source, w_out, halo, halo_beside,
    live, keep, give, halo_table, messages, totals,
):
    d = pre.shape[1]
    got = halo[...] + halo_beside[...]
    halo_table[: got.shape[0], :] = halved(dot(got, w_source[...]))
    if got.shape[0] < halo_table.shape[0]:
        halo_table[got.shape[0] :, :] = jnp.zeros((halo_table.shape[0] - got.shape[0], d), BF16)
    targets = halo_targets(plan, slots, node_rows, halo_table.shape[0])
    lane = lax.broadcasted_iota(I16, (1, node_rows), 1)

    def first_stage(first):
        senders, receivers = columns(edges, first)
        remote = dot(hot(targets == senders), halo_table[...])
        if first < pre.shape[0]:
            return pre[first : first + STEP, :] + remote
        return dot(own_chosen(emb, edges, lane, first), table[...]) + remote

    edge_blocks(edges, live[0] * BLOCK, first_stage, w_out[...], messages, totals)
    hand_out(totals, gain, keep, give)


def fold_kernel(mine, theirs, keep, give):
    rows = mine.shape[0] // 2
    chip = lax.div(lax.axis_index("sub"), 2)
    for out, which in ((keep, chip), (give, 1 - chip)):
        place = pl.multiple_of(which * rows, rows)
        out[...] = add(mine[pl.ds(place, rows), :], theirs[pl.ds(place, rows), :])


def out_kernel(k_in, k_out, middle, mine, theirs, gain, w0, w1, w2, w3, out, stacked, hidden):
    rows, d = out.shape
    quarter = lax.axis_index("sub")
    chip = lax.div(quarter, 2)
    mesh = middle[pl.ds(pl.multiple_of(chip * rows, rows), rows), :]
    stacked[:, :d] = mesh
    stacked[:, d:] = add(mine[...], theirs[...])
    shards = (w0, w1, w2, w3)

    def columns_of(ref, step, count):
        return ref[:, pl.ds(pl.multiple_of(lax.bitwise_xor(quarter, step) * count, count), count)]

    left = jnp.concatenate([columns_of(stacked, step, k_in) for step in range(4)], axis=1)
    right = jnp.concatenate([w[:k_in, :] for w in shards], axis=0)
    hidden[...] = silu(dot(left, right)).astype(BF16)
    left = jnp.concatenate([columns_of(hidden, step, k_out) for step in range(4)], axis=1)
    right = jnp.concatenate([w[k_in:, :] for w in shards], axis=0)
    update = layer_norm(dot(left, right)) * gain[...]
    out[...] = (mesh.astype(F32) + update).astype(BF16)


def to_chip(v):
    return lax.ppermute(v, "sub", [(i, i ^ 2) for i in range(4)])


def to_core(v):
    return lax.ppermute(v, "sub", [(i, i ^ 1) for i in range(4)])


def to_group(v):
    count = lax.axis_size("groups")
    return lax.ppermute(v, "groups", [(i, count - 1 - i) for i in range(count)])


def to_partition(v):
    return lax.ppermute(v, "dom", [(i, i ^ 1) for i in range(lax.axis_size("dom"))])


def shape(rows, width, dtype=BF16):
    return jax.ShapeDtypeStruct((rows, width), dtype)


def padded(rows):
    return -(-rows // 128) * 128


def local(
    grid_lat,
    mesh_lat,
    grid_send,
    mesh_send,
    enc_edges,
    enc_geom,
    enc_blocks,
    proc_edges,
    proc_geom,
    proc_blocks,
    enc_geo,
    proc_geo,
    enc_edge_in,
    enc_edge_out,
    enc_node_in,
    enc_node_out,
    proc_edge_in,
    proc_edge_out,
    proc_node_in,
    proc_node_out,
    enc_edge_gain,
    enc_node_gain,
    proc_edge_gain,
    proc_node_gain,
):
    plan = halo_plan(lax.axis_size("dom"))
    d = enc_geo.shape[1]
    grid_rows, mesh_rows = grid_lat.shape[0], mesh_lat.shape[0]
    n_enc, n_proc = enc_edges.shape[1], proc_edges.shape[1]
    enc_edge_gain, enc_node_gain, proc_edge_gain, proc_node_gain = (
        g.reshape(1, d) for g in (enc_edge_gain, enc_node_gain, proc_edge_gain, proc_node_gain)
    )
    k_in, k_out = enc_edge_in.shape[0], enc_edge_out.shape[0]
    n_in, n_out = enc_node_in.shape[0], enc_node_out.shape[0]
    width = grid_lat.shape[1]

    slots = grid_send.shape[2]
    (token,) = call(begin_kernel, [shape(16, 128)], [], flops=LONG)
    edge_half, *outgoing = call(
        functools.partial(first_pack_kernel, plan),
        [shape((k_in + 2 * k_out + n_out) // 2, d)] + [shape(slots, width)] * len(plan),
        [grid_lat, grid_send, enc_edge_in, enc_edge_out, enc_node_out, proc_edge_out, token],
    )
    first_across = to_chip(edge_half)
    (edge_across,) = call(rows_kernel, [shape((k_in + k_out) // 2, d)], [first_across])
    halos = [lax.ppermute(v, "dom", entry[0]) for v, entry in zip(outgoing, plan)]
    got = len(plan) * slots
    (lat,) = call(
        concat_kernel,
        [shape(grid_rows + mesh_rows + got, width)],
        [grid_lat, mesh_lat, *halos],
    )
    lat_across = to_chip(lat)
    lat_beside = to_core(lat)
    edge_beside = [to_core(enc_edge_in), to_core(enc_edge_out)]
    edge_round = to_group(edge_across)
    node_w, proc_w, enc_emb, proc_emb = call(
        embed_kernel,
        [shape(n_in + n_out, d), shape(k_in + k_out, d), shape(n_enc, d), shape(n_proc, d)],
        [
            enc_node_in, enc_node_out, proc_edge_in, proc_edge_out,
            enc_geom, enc_geo, proc_geom, proc_geo, lat,
        ],
        flops=2 * (n_enc + n_proc) * d * 128,
    )
    crossing, lat_sent = call(
        functools.partial(cross_kernel, (n_in, k_in)),
        [shape((n_in + k_in) // 2, d), shape(lat.shape[0], width)],
        [node_w, proc_w, lat_across],
    )
    lat_both = to_core(lat_sent)
    next_across = to_chip(crossing)
    node_beside, proc_beside = to_core(node_w), to_core(proc_w)

    halo_rows = padded(got)
    half = mesh_rows // 2
    keep, give, own_mesh = call(
        functools.partial(enc_kernel, plan, slots, grid_rows, mesh_rows, k_in),
        [shape(half, d)] * 3,
        [
            enc_emb, enc_edges, enc_edge_gain, lat, lat_across, lat_beside, lat_both,
            enc_edge_in, enc_edge_out, *edge_beside,
            edge_across, edge_round, to_core(edge_across), to_core(edge_round), enc_blocks,
        ],
        scratch=[
            pltpu.VMEM((grid_rows + mesh_rows + got, d), BF16),
            pltpu.VMEM((4 * (k_in + k_out), d), BF16),
            pltpu.VMEM((d + grid_rows + mesh_rows + halo_rows, d), BF16),
            pltpu.VMEM((n_enc, d), BF16),
            pltpu.VMEM((mesh_rows, d), F32),
        ],
        flops=2 * n_enc * d * (3 * d + grid_rows + mesh_rows + halo_rows),
        smem=1,
    )
    (chip_sum,) = call(add_kernel, [shape(half, d)], [keep, to_core(give)])
    node_across, proc_across = call(
        functools.partial(split_kernel, (n_in // 2, k_in // 2)),
        [shape((n_in + n_out) // 2, d), shape((k_in + k_out) // 2, d)],
        [first_across, next_across, chip_sum],
    )
    node_round = to_partition(node_across)
    proc_round = to_group(proc_across)
    node_both = to_core(node_across)
    slots = mesh_send.shape[2]
    mid_half, last_w, *outgoing = call(
        functools.partial(node_kernel, plan, n_in, n_out),
        [shape(half, d), shape(n_in + n_out, d)] + [shape(slots, d)] * len(plan),
        [
            own_mesh, chip_sum, to_chip(chip_sum), enc_node_gain, proc_node_in, proc_node_out,
            node_w, node_beside, node_across, node_round, node_both, to_core(node_round), mesh_send, proc_beside,
        ],
        scratch=[pltpu.VMEM((4 * (n_in + n_out), d), BF16)],
        flops=2 * half * d * 3 * d,
    )
    (proc_pair,) = call(pair_kernel, [shape(k_in + k_out, d)], [proc_across, proc_round, mid_half])
    halos = [lax.ppermute(v, "dom", entry[0]) for v, entry in zip(outgoing, plan)]
    (halo,) = call(concat_kernel, [shape(len(plan) * slots, d)], halos)
    halo_beside = to_core(halo)
    last_across, last_beside = to_chip(last_w), to_core(last_w)
    early = n_proc // 2
    table, pre, w_source, w_out = call(
        functools.partial(proc_first_kernel, k_in),
        [shape(d + 2 * mesh_rows, d), shape(early, d, F32), shape(d, d), shape(d, d)],
        [
            proc_emb, mid_half, to_core(mid_half), proc_edges, proc_w, proc_beside, proc_pair, to_core(proc_pair),
        ],
        scratch=[pltpu.VMEM((4 * (k_in + k_out), d), BF16), pltpu.VMEM((mesh_rows, d), BF16)],
        flops=2 * early * d * (d + 2 * mesh_rows),
    )
    halo_rows = padded(len(plan) * slots)
    keep, give = call(
        functools.partial(proc_second_kernel, plan, slots, mesh_rows),
        [shape(half, d), shape(half, d)],
        [proc_emb, proc_edges, proc_edge_gain, table, pre, w_source, w_out, halo, halo_beside, proc_blocks],
        scratch=[
            pltpu.VMEM((halo_rows, d), BF16),
            pltpu.VMEM((n_proc, d), BF16),
            pltpu.VMEM((mesh_rows, d), F32),
        ],
        flops=2 * n_proc * d * (2 * d + mesh_rows + halo_rows),
        smem=1,
    )
    quarter = mesh_rows // 4
    mine, other = call(fold_kernel, [shape(quarter, d)] * 2, [keep, to_core(give)])
    (result,) = call(
        functools.partial(out_kernel, n_in, n_out),
        [shape(quarter, d)],
        [mid_half, mine, to_chip(other), proc_node_gain, last_w, last_beside, last_across, to_core(last_across)],
        scratch=[pltpu.VMEM((quarter, 4 * n_in), BF16), pltpu.VMEM((quarter, 4 * n_out), BF16)],
        flops=2 * quarter * d * 3 * d,
    )
    return result


def solution(mesh):
    placed = (
        P(("groups", "dom"), "sub"),
        P(("groups", "dom"), "sub"),
        P("dom", None, None),
        P("dom", None, None),
        P(None, ("dom", "sub")),
        P(None, ("dom", "sub")),
        P("dom"),
        P(None, ("dom", "sub")),
        P(None, ("dom", "sub")),
        P("dom"),
        P(),
        P(),
        P("sub", None),
        P("sub", None),
        P("sub", None),
        P("sub", None),
        P("sub", None),
        P("sub", None),
        P("sub", None),
        P("sub", None),
        P(),
        P(),
        P(),
        P(),
    )
    return jax.shard_map(
        local,
        mesh=mesh,
        in_specs=placed,
        out_specs=P(("groups", "dom", "sub"), None),
        check_vma=False,
    )
```

```python
import functools

import jax
import jax.numpy as jnp
from jax import lax
from jax.experimental import pallas as pl
from jax.experimental.pallas import tpu as pltpu
from jax.sharding import PartitionSpec as P

BLOCK = 128
OFFSETS = (-2, -1, 1, 2)
STEP = 512
GATHERED = 1024
LONG = 30 * 10**9
BY_GROUP = ("groups",)
BY_PART = ("dom",)
VMEM_BYTES = 24 * 1024 * 1024
I16 = jnp.int16
BF16 = jnp.bfloat16
F32 = jnp.float32


def silu_of_half(h):
    return h + h * jnp.tanh(h)


def silu(v):
    return silu_of_half(0.5 * v)


def halved(v):
    return (v.astype(F32) * 0.5).astype(BF16)


def region_of(delta):
    return jnp.where(delta < 0, delta + 2, delta + 1)


def halo_plan(count):
    plan = []
    if count == 4:
        for bit in (1, 2, 3):
            pairs = [(d, d ^ bit) for d in range(4) if abs((d ^ bit) - d) <= 2]
            regions = [(OFFSETS.index((d ^ bit) - d) if abs((d ^ bit) - d) <= 2 else -1) for d in range(4)]
            plan.append((pairs, regions, regions))
    else:
        for region, offset in enumerate(OFFSETS):
            pairs = [(d, d + offset) for d in range(count) if 0 <= d + offset < count]
            plan.append((pairs, region, 3 - region))
    return plan


def by_index(choice, index):
    if isinstance(choice, int):
        return choice
    picked = jnp.int32(choice[0])
    for place in range(1, len(choice)):
        picked = jnp.where(index == place, choice[place], picked)
    return picked


def whole_refs(count):
    return [pl.BlockSpec(memory_space=pltpu.VMEM)] * count


def call(body, outs, args, scratch=(), flops=0, smem=0):
    moved = sum(a.size * a.dtype.itemsize for a in args) + sum(
        o.size * jnp.dtype(o.dtype).itemsize for o in outs
    )
    specs = whole_refs(len(args) - smem) + [pl.BlockSpec(memory_space=pltpu.SMEM)] * smem
    return pl.pallas_call(
        body,
        out_shape=tuple(outs),
        in_specs=specs,
        out_specs=tuple(whole_refs(len(outs))),
        scratch_shapes=list(scratch),
        compiler_params=pltpu.CompilerParams(vmem_limit_bytes=VMEM_BYTES),
        cost_estimate=pl.CostEstimate(flops=int(flops), bytes_accessed=int(moved), transcendentals=0),
    )(*args)


def dot(a, b):
    return jnp.dot(a, b, preferred_element_type=F32)


def dot_first(a, b):
    return lax.dot_general(a, b, (((0,), (0,)), ((), ())), preferred_element_type=F32)


def three_parts(v):
    a = v.astype(BF16)
    rest = v - a.astype(F32)
    b = rest.astype(BF16)
    c = (rest - b.astype(F32)).astype(BF16)
    return a, b, c


def embed_rows(geom, geo):
    a1, a2, a3 = three_parts(geom)
    b1, b2, b3 = three_parts(geo)
    left = jnp.concatenate([a1, a1, a2, a1, a2, a3], axis=0)
    right = jnp.concatenate([b1, b2, b1, b3, b2, b1], axis=0)
    return silu(dot_first(left, right)).astype(BF16)


def layer_norm(v, live=None):
    width = v.shape[-1]
    centered = v - jnp.sum(v, axis=-1, keepdims=True) * (1.0 / width)
    spread = jnp.sum(centered * centered, axis=-1, keepdims=True) * (1.0 / width)
    factor = lax.rsqrt(spread + 1e-05)
    if live is not None:
        factor = jnp.where(live, factor, 0.0)
    return centered * factor


def hot(cond):
    return jnp.where(cond, BF16(1), BF16(0))


def pick_rows(table, listed, rows=None):
    if rows is None:
        rows = lax.broadcasted_iota(I16, (table.shape[0], 1), 0)
    return dot_first(hot(rows == listed.astype(I16)), table).astype(BF16)


def pick_lists(plan, table, send, outs, rows=None):
    here = lax.axis_index("dom")
    for (pairs, sent, received), out in zip(plan, outs):
        region = jnp.maximum(by_index(sent, here), 0)
        out[...] = pick_rows(table, send[0, pl.ds(region, 1), :], rows)


def stack_into(out, parts):
    first = 0
    for part in parts:
        out[first : first + part.shape[0], :] = part[...]
        first += part.shape[0]


def begin_kernel(token):
    token[...] = jnp.zeros(token.shape, token.dtype)


def first_pack_kernel(plan, grid, send, w_in, w_out, n_out, p_out, p_in, token, half, *outs):
    place = 0
    for source, axes in ((w_in, BY_GROUP), (w_out, BY_GROUP), (n_out, BY_PART), (p_out, BY_GROUP)):
        rows = source.shape[0] // 2
        begin = pl.multiple_of(parity(axes) * rows, 64)
        half[place : place + rows, :] = source[pl.ds(begin, rows), :]
        place += rows
    rows = half.shape[0] - place
    begin = pl.multiple_of(lax.axis_index("groups") * (p_in.shape[0] // 2), 64)
    half[place:, :] = p_in[pl.ds(begin, rows), :]
    pick_lists(plan, grid[...], send, outs)


def embed_kernel(e_in, e_out, p_in, p_out, egeom, egeo, pgeom, pgeo, after, node, proc, eout, pout):
    stack_into(node, (e_in, e_out))
    stack_into(proc, (p_in, p_out))
    for geom, geo, out in ((egeom, egeo, eout), (pgeom, pgeo, pout)):
        for begin in range(0, out.shape[0], STEP):
            out[begin : begin + STEP, :] = embed_rows(geom[:, begin : begin + STEP], geo[...])


def cross_kernel(counts, skipped, node, proc, lat, crossing, lat_out):
    lat_out[...] = lat[...]
    place = 0
    for stack, rows, axes, gone in ((node, counts[0], BY_PART, 0), (proc, counts[1], BY_GROUP, skipped)):
        half = rows // 2
        begin = pl.multiple_of(parity(axes) * half + gone, 32)
        crossing[place : place + half - gone, :] = stack[pl.ds(begin, half - gone), :]
        place += half - gone


def rows_kernel(source, out):
    out[...] = source[: out.shape[0], :]


def pair_kernel(first, second, after, out):
    stack_into(out, (first, second))


def split_kernel(n, early_rows, early, source, after, node, proc):
    rest = source.shape[0] - n
    n_out = node.shape[0] - n
    p_out = proc.shape[0] - rest - early_rows
    base = early.shape[0] - n_out - p_out - early_rows
    stack_into(node, (source.at[pl.ds(0, n), :], early.at[pl.ds(base, n_out), :]))
    first = early.at[pl.ds(base + n_out + p_out, early_rows), :]
    stack_into(proc, (first, source.at[pl.ds(n, rest), :], early.at[pl.ds(base + n_out, p_out), :]))


def concat_kernel(*refs):
    stack_into(refs[-1], refs[:-1])


def put_shard(target, source, first, step, part=0, parts=1):
    rows = target.shape[0] // (4 * parts)
    place = (lax.bitwise_xor(lax.axis_index("sub"), step) * parts + part) * rows
    target[pl.ds(pl.multiple_of(place, rows), rows), :] = source[first : first + rows, :]


def parity(axes):
    return lax.rem(sum(lax.axis_index(axis) for axis in axes), 2)


def put_half(target, k, source, step, other, axes=("groups",)):
    rows = target.shape[0] // 4
    which = lax.bitwise_xor(parity(axes), other)
    begin = lax.bitwise_xor(lax.axis_index("sub"), step) * rows
    for base, count in ((0, k // 2), (k // 2, (rows - k) // 2)):
        place = pl.multiple_of(begin + 2 * base + which * count, 64)
        target[pl.ds(place, count), :] = source[base : base + count, :]


def joined(stack, first, rows):
    step = stack.shape[0] // 4
    return jnp.concatenate([stack[k * step + first : k * step + first + rows, :] for k in range(4)], axis=0)


def halo_targets(plan, slots, node_rows, width):
    here = lax.axis_index("dom")
    lane = lax.broadcasted_iota(jnp.int32, (1, width), 1)
    target = jnp.full((1, width), -1, jnp.int32)
    for place, (pairs, sent, received) in enumerate(plan):
        region = by_index(received, here)
        first = jnp.where(region < 0, -4 * node_rows, node_rows + region * slots)
        inside = (lane >= place * slots) & (lane < (place + 1) * slots)
        target = jnp.where(inside, lane - place * slots + first, target)
    return target.astype(I16)


def columns(edges, first):
    pair = edges[:, first : first + STEP]
    zero = jnp.zeros((8 - pair.shape[0], STEP), jnp.int32)
    upright = jnp.transpose(jnp.concatenate([pair, zero], axis=0).astype(F32)).astype(jnp.int32).astype(I16)
    return upright[:, 0:1], upright[:, 1:2]


def edge_blocks(edges, live_edges, first_stage, w_out, messages, totals):
    count = edges.shape[1]
    steps = count // STEP
    row = lax.broadcasted_iota(I16, (totals.shape[0], 1), 0)
    quarter = lax.axis_index("sub")
    sums, raw = {}, {}
    for turn in range(steps + 2):
        if turn < steps:
            sums[turn] = first_stage(turn * STEP)
        if 0 <= turn - 1 < steps:
            raw[turn - 1] = dot(silu_of_half(sums.pop(turn - 1)).astype(BF16), w_out)
        if turn < 2:
            continue
        first = (turn - 2) * STEP
        place = lax.broadcasted_iota(jnp.int32, (STEP, 1), 0) + (first + quarter * count)
        message = layer_norm(raw.pop(turn - 2), place < live_edges)
        messages[first : first + STEP, :] = message.astype(BF16)
        done = first + STEP
        if done % GATHERED == 0 or done == count:
            begin = (first // GATHERED) * GATHERED
            collect = hot(row == edges[1:2, begin:done].astype(I16))
            part = dot(collect, messages[begin:done, :])
            if begin == 0:
                totals[...] = part
            else:
                totals[...] += part


def hand_out(totals, gain, keep, *give):
    rows = totals.shape[0] // 4
    core = lax.rem(lax.axis_index("sub"), 2)
    for half in range(2):
        kept = keep.at[pl.ds(half * rows, rows), :]
        given = give[0].at[pl.ds(half * rows, rows), :] if len(give) == 1 else give[half]
        for out, which in ((kept, core), (given, 1 - core)):
            place = pl.multiple_of((2 * half + which) * rows, rows)
            out[...] = (totals[pl.ds(place, rows), :] * gain[...]).astype(BF16)


def enc_kernel(
    plan, slots, grid_rows, mesh_rows, k_in, emb, edges, gain, l0, l1, l2, l3, o_in, o_out, b_in, b_out,
    across, round_, both, round_both, live, keep, give, give_more, own_mesh, full, stack, table, messages, totals,
):
    d = gain.shape[1]
    quarter = lax.axis_index("sub")
    width = l0.shape[1]
    for shard, step in zip((l0, l1, l2, l3), (0, 2, 1, 3)):
        place = pl.multiple_of(lax.bitwise_xor(quarter, step) * width, width)
        full[:, pl.ds(place, width)] = shard[...]
    step = k_in + d // 4
    for first, second, bit in ((o_in, o_out, 0), (b_in, b_out, 1)):
        place = lax.bitwise_xor(quarter, bit) * step
        stack[pl.ds(pl.multiple_of(place, 128), k_in), :] = first[...]
        stack[pl.ds(pl.multiple_of(place + k_in, 128), d // 4), :] = second[...]
    put_half(stack, k_in, across, 2, 0)
    put_half(stack, k_in, round_, 2, 1)
    put_half(stack, k_in, both, 3, 0)
    put_half(stack, k_in, round_both, 3, 1)
    rows = mesh_rows // 4
    core = lax.rem(quarter, 2)
    for half in range(2):
        place = pl.multiple_of(grid_rows + (2 * half + core) * rows, rows)
        own_mesh[half * rows : (half + 1) * rows, :] = full[pl.ds(place, rows), :]

    w_in = joined(stack, 0, k_in)
    halo_first, got = grid_rows + mesh_rows, full.shape[0] - grid_rows - mesh_rows
    table[:d, :] = halved(w_in[:d, :])
    table[d : d + grid_rows, :] = halved(dot(full[:grid_rows, :], w_in[d : 2 * d, :]))
    base = d + grid_rows + mesh_rows
    table[d + grid_rows : base, :] = halved(dot(full[grid_rows:halo_first, :], w_in[2 * d :, :]))
    table[base : base + got, :] = halved(dot(full[halo_first:, :], w_in[d : 2 * d, :]))
    if base + got < table.shape[0]:
        table[base + got :, :] = jnp.zeros((table.shape[0] - base - got, d), BF16)
    targets = halo_targets(plan, slots, grid_rows, table.shape[0] - base)
    own = lax.broadcasted_iota(I16, (1, grid_rows), 1)
    mesh = lax.broadcasted_iota(I16, (1, mesh_rows), 1)

    def first_stage(first):
        senders, receivers = columns(edges, first)
        chosen = [emb[first : first + STEP, :], hot(own == senders), hot(mesh == receivers), hot(targets == senders)]
        return dot(jnp.concatenate(chosen, axis=1), table[...])

    edge_blocks(edges, live[0] * BLOCK, first_stage, joined(stack, k_in, d // 4), messages, totals)
    hand_out(totals, gain, keep, give, give_more)


def node_update(mesh, shares, w_in, w_out, gain):
    stacked = jnp.concatenate([mesh, shares], axis=1)
    hidden = silu(dot(stacked, w_in)).astype(BF16)
    update = layer_norm(dot(hidden, w_out)) * gain
    return (mesh.astype(F32) + update).astype(BF16)


def add(mine, theirs):
    return (mine.astype(F32) + theirs.astype(F32)).astype(BF16)


def add_kernel(mine, first, second, out):
    rows = first.shape[0]
    out[:rows, :] = add(mine[:rows, :], first[...])
    out[rows:, :] = add(mine[rows:, :], second[...])


def node_kernel(
    plan, k_in, k_out, mesh, mine, theirs, gain, n_in, n_out, w0, w1, w2, w3, w4, w5, send, after, out, packed, *rest
):
    outs, stack = rest[:-1], rest[-1]
    put_shard(stack, w0, 0, 0)
    put_shard(stack, w1, 0, 1)
    put_half(stack, k_in, w2, 2, 0, BY_PART)
    put_half(stack, k_in, w3, 2, 1, BY_PART)
    put_half(stack, k_in, w4, 3, 0, BY_PART)
    put_half(stack, k_in, w5, 3, 1, BY_PART)
    w_in, w_out = joined(stack, 0, k_in), joined(stack, k_in, k_out)
    fresh = node_update(mesh[...], add(mine[...], theirs[...]), w_in, w_out, gain[...])
    out[...] = fresh
    half = fresh.shape[0] // 2
    core = lax.rem(lax.axis_index("sub"), 2)
    place = lax.broadcasted_iota(jnp.int32, (fresh.shape[0], 1), 0)
    rows = place + core * half + jnp.where(place < half, 0, half)
    pick_lists(plan, fresh, send, outs, rows.astype(I16))
    stack_into(packed, (n_in, n_out))


def proc_first_kernel(
    k_in, emb, mine, theirs, edges, w0, w1, pair, pair_beside,
    table, pre, w_source, w_out, stack, full,
):
    d = full.shape[1]
    node_rows = full.shape[0]
    rows = node_rows // 4
    core = lax.rem(lax.axis_index("sub"), 2)
    for half in range(2):
        for part, which in ((mine, core), (theirs, 1 - core)):
            place = pl.multiple_of((2 * half + which) * rows, rows)
            full[pl.ds(place, rows), :] = part[half * rows : (half + 1) * rows, :]
    put_shard(stack, w0, 0, 0)
    put_shard(stack, w1, 0, 1)
    rows = pair.shape[0] // 2
    for other in range(2):
        put_half(stack, k_in, pair.at[pl.ds(other * rows, rows), :], 2, other)
        put_half(stack, k_in, pair_beside.at[pl.ds(other * rows, rows), :], 3, other)
    w_in = joined(stack, 0, k_in)
    w_out[...] = joined(stack, k_in, d // 4)
    w_source[...] = w_in[d : 2 * d, :]
    table[:d, :] = halved(w_in[:d, :])
    table[d : d + node_rows, :] = halved(dot(full[...], w_in[d : 2 * d, :]))
    table[d + node_rows :, :] = halved(dot(full[...], w_in[2 * d :, :]))
    lane = lax.broadcasted_iota(I16, (1, node_rows), 1)
    for first in range(0, pre.shape[0], STEP):
        pre[first : first + STEP, :] = dot(own_chosen(emb, edges, lane, first), table[...])


def own_chosen(emb, edges, lane, first):
    senders, receivers = columns(edges, first)
    return jnp.concatenate([emb[first : first + STEP, :], hot(lane == senders), hot(lane == receivers)], axis=1)


def proc_second_kernel(
    plan, slots, node_rows, emb, edges, gain, table, pre, w_source, w_out, halo, halo_beside,
    live, keep, give, halo_table, messages, totals,
):
    d = pre.shape[1]
    got = halo[...] + halo_beside[...]
    halo_table[: got.shape[0], :] = halved(dot(got, w_source[...]))
    if got.shape[0] < halo_table.shape[0]:
        halo_table[got.shape[0] :, :] = jnp.zeros((halo_table.shape[0] - got.shape[0], d), BF16)
    targets = halo_targets(plan, slots, node_rows, halo_table.shape[0])
    lane = lax.broadcasted_iota(I16, (1, node_rows), 1)

    def first_stage(first):
        senders, receivers = columns(edges, first)
        remote = dot(hot(targets == senders), halo_table[...])
        if first < pre.shape[0]:
            return pre[first : first + STEP, :] + remote
        return dot(own_chosen(emb, edges, lane, first), table[...]) + remote

    edge_blocks(edges, live[0] * BLOCK, first_stage, w_out[...], messages, totals)
    hand_out(totals, gain, keep, give)


def fold_kernel(mine, theirs, keep, give):
    rows = mine.shape[0] // 2
    chip = lax.div(lax.axis_index("sub"), 2)
    for out, which in ((keep, chip), (give, 1 - chip)):
        place = pl.multiple_of(which * rows, rows)
        out[...] = add(mine[pl.ds(place, rows), :], theirs[pl.ds(place, rows), :])


def out_kernel(k_in, k_out, middle, mine, theirs, gain, w0, w1, w2, w3, out, stacked, hidden):
    rows, d = out.shape
    quarter = lax.axis_index("sub")
    chip = lax.div(quarter, 2)
    mesh = middle[pl.ds(pl.multiple_of(chip * rows, rows), rows), :]
    stacked[:, :d] = mesh
    stacked[:, d:] = add(mine[...], theirs[...])
    shards = (w0, w1, w2, w3)

    def columns_of(ref, step, count):
        return ref[:, pl.ds(pl.multiple_of(lax.bitwise_xor(quarter, step) * count, count), count)]

    left = jnp.concatenate([columns_of(stacked, step, k_in) for step in range(4)], axis=1)
    right = jnp.concatenate([w[:k_in, :] for w in shards], axis=0)
    hidden[...] = silu(dot(left, right)).astype(BF16)
    left = jnp.concatenate([columns_of(hidden, step, k_out) for step in range(4)], axis=1)
    right = jnp.concatenate([w[k_in:, :] for w in shards], axis=0)
    update = layer_norm(dot(left, right)) * gain[...]
    out[...] = (mesh.astype(F32) + update).astype(BF16)


def to_chip(v):
    return lax.ppermute(v, "sub", [(i, i ^ 2) for i in range(4)])


def to_core(v):
    return lax.ppermute(v, "sub", [(i, i ^ 1) for i in range(4)])


def to_group(v):
    count = lax.axis_size("groups")
    return lax.ppermute(v, "groups", [(i, count - 1 - i) for i in range(count)])


def to_partition(v):
    return lax.ppermute(v, "dom", [(i, i ^ 1) for i in range(lax.axis_size("dom"))])


def shape(rows, width, dtype=BF16):
    return jax.ShapeDtypeStruct((rows, width), dtype)


def padded(rows):
    return -(-rows // 128) * 128


def local(
    grid_lat,
    mesh_lat,
    grid_send,
    mesh_send,
    enc_edges,
    enc_geom,
    enc_blocks,
    proc_edges,
    proc_geom,
    proc_blocks,
    enc_geo,
    proc_geo,
    enc_edge_in,
    enc_edge_out,
    enc_node_in,
    enc_node_out,
    proc_edge_in,
    proc_edge_out,
    proc_node_in,
    proc_node_out,
    enc_edge_gain,
    enc_node_gain,
    proc_edge_gain,
    proc_node_gain,
):
    plan = halo_plan(lax.axis_size("dom"))
    d = enc_geo.shape[1]
    grid_rows, mesh_rows = grid_lat.shape[0], mesh_lat.shape[0]
    n_enc, n_proc = enc_edges.shape[1], proc_edges.shape[1]
    enc_edge_gain, enc_node_gain, proc_edge_gain, proc_node_gain = (
        g.reshape(1, d) for g in (enc_edge_gain, enc_node_gain, proc_edge_gain, proc_node_gain)
    )
    k_in, k_out = enc_edge_in.shape[0], enc_edge_out.shape[0]
    n_in, n_out = enc_node_in.shape[0], enc_node_out.shape[0]
    width = grid_lat.shape[1]

    slots = grid_send.shape[2]
    early_rows = k_in // 4
    (token,) = call(begin_kernel, [shape(16, 128)], [], flops=LONG)
    edge_half, *outgoing = call(
        functools.partial(first_pack_kernel, plan),
        [shape((k_in + 2 * k_out + n_out) // 2 + early_rows, d)] + [shape(slots, width)] * len(plan),
        [grid_lat, grid_send, enc_edge_in, enc_edge_out, enc_node_out, proc_edge_out, proc_edge_in, token],
    )
    first_across = to_chip(edge_half)
    (edge_across,) = call(rows_kernel, [shape((k_in + k_out) // 2, d)], [first_across])
    halos = [lax.ppermute(v, "dom", entry[0]) for v, entry in zip(outgoing, plan)]
    got = len(plan) * slots
    (lat,) = call(
        concat_kernel,
        [shape(grid_rows + mesh_rows + got, width)],
        [grid_lat, mesh_lat, *halos],
    )
    lat_across = to_chip(lat)
    lat_beside = to_core(lat)
    edge_beside = [to_core(enc_edge_in), to_core(enc_edge_out)]
    edge_round = to_group(edge_across)
    node_w, proc_w, enc_emb, proc_emb = call(
        embed_kernel,
        [shape(n_in + n_out, d), shape(k_in + k_out, d), shape(n_enc, d), shape(n_proc, d)],
        [
            enc_node_in, enc_node_out, proc_edge_in, proc_edge_out,
            enc_geom, enc_geo, proc_geom, proc_geo, lat,
        ],
        flops=2 * (n_enc + n_proc) * d * 128,
    )
    crossing, lat_sent = call(
        functools.partial(cross_kernel, (n_in, k_in), early_rows),
        [shape((n_in + k_in) // 2 - early_rows, d), shape(lat.shape[0], width)],
        [node_w, proc_w, lat_across],
    )
    lat_both = to_core(lat_sent)
    next_across = to_chip(crossing)
    node_beside, proc_beside = to_core(node_w), to_core(proc_w)

    halo_rows = padded(got)
    half = mesh_rows // 2
    keep, give, give_more, own_mesh = call(
        functools.partial(enc_kernel, plan, slots, grid_rows, mesh_rows, k_in),
        [shape(half, d), shape(half // 2, d), shape(half // 2, d), shape(half, d)],
        [
            enc_emb, enc_edges, enc_edge_gain, lat, lat_across, lat_beside, lat_both,
            enc_edge_in, enc_edge_out, *edge_beside,
            edge_across, edge_round, to_core(edge_across), to_core(edge_round), enc_blocks,
        ],
        scratch=[
            pltpu.VMEM((grid_rows + mesh_rows + got, d), BF16),
            pltpu.VMEM((4 * (k_in + k_out), d), BF16),
            pltpu.VMEM((d + grid_rows + mesh_rows + halo_rows, d), BF16),
            pltpu.VMEM((n_enc, d), BF16),
            pltpu.VMEM((mesh_rows, d), F32),
        ],
        flops=2 * n_enc * d * (3 * d + grid_rows + mesh_rows + halo_rows),
        smem=1,
    )
    (chip_sum,) = call(add_kernel, [shape(half, d)], [keep, to_core(give), to_core(give_more)])
    node_across, proc_across = call(
        functools.partial(split_kernel, n_in // 2, early_rows),
        [shape((n_in + n_out) // 2, d), shape((k_in + k_out) // 2, d)],
        [first_across, next_across, chip_sum],
    )
    node_round = to_partition(node_across)
    proc_round = to_group(proc_across)
    node_both = to_core(node_across)
    slots = mesh_send.shape[2]
    mid_half, last_w, *outgoing = call(
        functools.partial(node_kernel, plan, n_in, n_out),
        [shape(half, d), shape(n_in + n_out, d)] + [shape(slots, d)] * len(plan),
        [
            own_mesh, chip_sum, to_chip(chip_sum), enc_node_gain, proc_node_in, proc_node_out,
            node_w, node_beside, node_across, node_round, node_both, to_core(node_round), mesh_send, proc_beside,
        ],
        scratch=[pltpu.VMEM((4 * (n_in + n_out), d), BF16)],
        flops=2 * half * d * 3 * d,
    )
    (proc_pair,) = call(pair_kernel, [shape(k_in + k_out, d)], [proc_across, proc_round, mid_half])
    halos = [lax.ppermute(v, "dom", entry[0]) for v, entry in zip(outgoing, plan)]
    (halo,) = call(concat_kernel, [shape(len(plan) * slots, d)], halos)
    halo_beside = to_core(halo)
    last_across, last_beside = to_chip(last_w), to_core(last_w)
    early = n_proc // 2
    table, pre, w_source, w_out = call(
        functools.partial(proc_first_kernel, k_in),
        [shape(d + 2 * mesh_rows, d), shape(early, d, F32), shape(d, d), shape(d, d)],
        [
            proc_emb, mid_half, to_core(mid_half), proc_edges, proc_w, proc_beside, proc_pair, to_core(proc_pair),
        ],
        scratch=[pltpu.VMEM((4 * (k_in + k_out), d), BF16), pltpu.VMEM((mesh_rows, d), BF16)],
        flops=2 * early * d * (d + 2 * mesh_rows),
    )
    halo_rows = padded(len(plan) * slots)
    keep, give = call(
        functools.partial(proc_second_kernel, plan, slots, mesh_rows),
        [shape(half, d), shape(half, d)],
        [proc_emb, proc_edges, proc_edge_gain, table, pre, w_source, w_out, halo, halo_beside, proc_blocks],
        scratch=[
            pltpu.VMEM((halo_rows, d), BF16),
            pltpu.VMEM((n_proc, d), BF16),
            pltpu.VMEM((mesh_rows, d), F32),
        ],
        flops=2 * n_proc * d * (2 * d + mesh_rows + halo_rows),
        smem=1,
    )
    quarter = mesh_rows // 4
    mine, other = call(fold_kernel, [shape(quarter, d)] * 2, [keep, to_core(give)])
    (result,) = call(
        functools.partial(out_kernel, n_in, n_out),
        [shape(quarter, d)],
        [mid_half, mine, to_chip(other), proc_node_gain, last_w, last_beside, last_across, to_core(last_across)],
        scratch=[pltpu.VMEM((quarter, 4 * n_in), BF16), pltpu.VMEM((quarter, 4 * n_out), BF16)],
        flops=2 * quarter * d * 3 * d,
    )
    return result


def solution(mesh):
    placed = (
        P(("groups", "dom"), "sub"),
        P(("groups", "dom"), "sub"),
        P("dom", None, None),
        P("dom", None, None),
        P(None, ("dom", "sub")),
        P(None, ("dom", "sub")),
        P("dom"),
        P(None, ("dom", "sub")),
        P(None, ("dom", "sub")),
        P("dom"),
        P(),
        P(),
        P("sub", None),
        P("sub", None),
        P("sub", None),
        P("sub", None),
        P("sub", None),
        P("sub", None),
        P("sub", None),
        P("sub", None),
        P(),
        P(),
        P(),
        P(),
    )
    return jax.shard_map(
        local,
        mesh=mesh,
        in_specs=placed,
        out_specs=P(("groups", "dom", "sub"), None),
        check_vma=False,
    )
```

```python
import functools

import jax
import jax.numpy as jnp
from jax import lax
from jax.experimental import pallas as pl
from jax.experimental.pallas import tpu as pltpu
from jax.sharding import PartitionSpec as P

BLOCK = 128
OFFSETS = (-2, -1, 1, 2)
STEP = 512
GATHERED = 1024
LONG = 30 * 10**9
BY_GROUP = ("groups",)
BY_PART = ("dom",)
VMEM_BYTES = 24 * 1024 * 1024
I16 = jnp.int16
BF16 = jnp.bfloat16
F32 = jnp.float32


def silu_of_half(h):
    return h + h * jnp.tanh(h)


def silu(v):
    return silu_of_half(0.5 * v)


def halved(v):
    return (v.astype(F32) * 0.5).astype(BF16)


def region_of(delta):
    return jnp.where(delta < 0, delta + 2, delta + 1)


def halo_plan(count):
    plan = []
    if count == 4:
        for bit in (1, 2, 3):
            pairs = [(d, d ^ bit) for d in range(4) if abs((d ^ bit) - d) <= 2]
            regions = [(OFFSETS.index((d ^ bit) - d) if abs((d ^ bit) - d) <= 2 else -1) for d in range(4)]
            plan.append((pairs, regions, regions))
    else:
        for region, offset in enumerate(OFFSETS):
            pairs = [(d, d + offset) for d in range(count) if 0 <= d + offset < count]
            plan.append((pairs, region, 3 - region))
    return plan


def by_index(choice, index):
    if isinstance(choice, int):
        return choice
    picked = jnp.int32(choice[0])
    for place in range(1, len(choice)):
        picked = jnp.where(index == place, choice[place], picked)
    return picked


def whole_refs(count):
    return [pl.BlockSpec(memory_space=pltpu.VMEM)] * count


def call(body, outs, args, scratch=(), flops=0):
    moved = sum(a.size * a.dtype.itemsize for a in args) + sum(
        o.size * jnp.dtype(o.dtype).itemsize for o in outs
    )
    specs = whole_refs(len(args))
    return pl.pallas_call(
        body,
        out_shape=tuple(outs),
        in_specs=specs,
        out_specs=tuple(whole_refs(len(outs))),
        scratch_shapes=list(scratch),
        compiler_params=pltpu.CompilerParams(vmem_limit_bytes=VMEM_BYTES),
        cost_estimate=pl.CostEstimate(flops=int(flops), bytes_accessed=int(moved), transcendentals=0),
    )(*args)


def dot(a, b):
    return jnp.dot(a, b, preferred_element_type=F32)


def dot_first(a, b):
    return lax.dot_general(a, b, (((0,), (0,)), ((), ())), preferred_element_type=F32)


def three_parts(v):
    a = v.astype(BF16)
    rest = v - a.astype(F32)
    b = rest.astype(BF16)
    c = (rest - b.astype(F32)).astype(BF16)
    return a, b, c


def embed_rows(geom, geo):
    a1, a2, a3 = three_parts(geom)
    b1, b2, b3 = three_parts(geo)
    left = jnp.concatenate([a1, a1, a2, a1, a2, a3], axis=0)
    right = jnp.concatenate([b1, b2, b1, b3, b2, b1], axis=0)
    return silu(dot_first(left, right)).astype(BF16)


def layer_norm(v, live=None):
    width = v.shape[-1]
    centered = v - jnp.sum(v, axis=-1, keepdims=True) * (1.0 / width)
    spread = jnp.sum(centered * centered, axis=-1, keepdims=True) * (1.0 / width)
    factor = lax.rsqrt(spread + 1e-05)
    if live is not None:
        factor = jnp.where(live, factor, 0.0)
    return centered * factor


def hot(cond):
    return jnp.where(cond, BF16(1), BF16(0))


def pick_rows(table, listed, rows=None):
    if rows is None:
        rows = lax.broadcasted_iota(I16, (table.shape[0], 1), 0)
    return dot_first(hot(rows == listed.astype(I16)), table).astype(BF16)


def pick_lists(plan, table, send, outs, rows=None):
    here = lax.axis_index("dom")
    for (pairs, sent, received), out in zip(plan, outs):
        region = jnp.maximum(by_index(sent, here), 0)
        out[...] = pick_rows(table, send[0, pl.ds(region, 1), :], rows)


def stack_into(out, parts):
    first = 0
    for part in parts:
        out[first : first + part.shape[0], :] = part[...]
        first += part.shape[0]


def begin_kernel(token):
    token[...] = jnp.zeros(token.shape, token.dtype)


def first_pack_kernel(plan, grid, send, w_in, w_out, n_out, p_out, token, half, *outs):
    place = 0
    for source, axes in ((w_in, BY_GROUP), (w_out, BY_GROUP), (n_out, BY_PART), (p_out, BY_GROUP)):
        rows = source.shape[0] // 2
        begin = pl.multiple_of(parity(axes) * rows, 64)
        half[place : place + rows, :] = source[pl.ds(begin, rows), :]
        place += rows
    pick_lists(plan, grid[...], send, outs)


def embed_kernel(e_in, e_out, p_in, p_out, egeom, egeo, pgeom, pgeo, elive, plive, after, node, proc, eout, pout, lives):
    lives[0:1, :] = jnp.broadcast_to(elive[...], (1, lives.shape[1]))
    lives[1:2, :] = jnp.broadcast_to(plive[...], (1, lives.shape[1]))
    stack_into(node, (e_in, e_out))
    stack_into(proc, (p_in, p_out))
    for geom, geo, out in ((egeom, egeo, eout), (pgeom, pgeo, pout)):
        for begin in range(0, out.shape[0], STEP):
            out[begin : begin + STEP, :] = embed_rows(geom[:, begin : begin + STEP], geo[...])


def cross_kernel(counts, node, proc, lat, crossing, lat_out):
    lat_out[...] = lat[...]
    place = 0
    for stack, rows, axes in ((node, counts[0], BY_PART), (proc, counts[1], BY_GROUP)):
        half = rows // 2
        begin = pl.multiple_of(parity(axes) * half, 64)
        crossing[place : place + half, :] = stack[pl.ds(begin, half), :]
        place += half


def rows_kernel(source, out):
    out[...] = source[: out.shape[0], :]


def pair_kernel(first, second, after, out):
    stack_into(out, (first, second))


def split_kernel(ins, early, source, after, node, proc):
    n, p = ins
    n_rest, p_rest = node.shape[0] - n, proc.shape[0] - p
    base = early.shape[0] - n_rest - p_rest
    stack_into(node, (source.at[pl.ds(0, n), :], early.at[pl.ds(base, n_rest), :]))
    stack_into(proc, (source.at[pl.ds(n, p), :], early.at[pl.ds(base + n_rest, p_rest), :]))


def concat_kernel(*refs):
    stack_into(refs[-1], refs[:-1])


def put_shard(target, source, first, step, part=0, parts=1):
    rows = target.shape[0] // (4 * parts)
    place = (lax.bitwise_xor(lax.axis_index("sub"), step) * parts + part) * rows
    target[pl.ds(pl.multiple_of(place, rows), rows), :] = source[first : first + rows, :]


def parity(axes):
    return lax.rem(sum(lax.axis_index(axis) for axis in axes), 2)


def put_half(target, k, source, step, other, axes=("groups",)):
    rows = target.shape[0] // 4
    which = lax.bitwise_xor(parity(axes), other)
    begin = lax.bitwise_xor(lax.axis_index("sub"), step) * rows
    for base, count in ((0, k // 2), (k // 2, (rows - k) // 2)):
        place = pl.multiple_of(begin + 2 * base + which * count, 64)
        target[pl.ds(place, count), :] = source[base : base + count, :]


def joined(stack, first, rows):
    step = stack.shape[0] // 4
    return jnp.concatenate([stack[k * step + first : k * step + first + rows, :] for k in range(4)], axis=0)


def halo_targets(plan, slots, node_rows, width):
    here = lax.axis_index("dom")
    lane = lax.broadcasted_iota(jnp.int32, (1, width), 1)
    target = jnp.full((1, width), -1, jnp.int32)
    for place, (pairs, sent, received) in enumerate(plan):
        region = by_index(received, here)
        first = jnp.where(region < 0, -4 * node_rows, node_rows + region * slots)
        inside = (lane >= place * slots) & (lane < (place + 1) * slots)
        target = jnp.where(inside, lane - place * slots + first, target)
    return target.astype(I16)


def columns(edges, first):
    pair = edges[:, first : first + STEP]
    zero = jnp.zeros((8 - pair.shape[0], STEP), jnp.int32)
    upright = jnp.transpose(jnp.concatenate([pair, zero], axis=0).astype(F32)).astype(jnp.int32).astype(I16)
    return upright[:, 0:1], upright[:, 1:2]


def edge_blocks(edges, live_edges, first_stage, w_out, messages, totals):
    count = edges.shape[1]
    steps = count // STEP
    row = lax.broadcasted_iota(I16, (totals.shape[0], 1), 0)
    quarter = lax.axis_index("sub")
    sums, raw = {}, {}
    for turn in range(steps + 2):
        if turn < steps:
            sums[turn] = first_stage(turn * STEP)
        if 0 <= turn - 1 < steps:
            raw[turn - 1] = dot(silu_of_half(sums.pop(turn - 1)).astype(BF16), w_out)
        if turn < 2:
            continue
        first = (turn - 2) * STEP
        place = lax.broadcasted_iota(jnp.int32, (STEP, 1), 0) + (first + quarter * count)
        message = layer_norm(raw.pop(turn - 2), place < live_edges)
        messages[first : first + STEP, :] = message.astype(BF16)
        done = first + STEP
        if done % GATHERED == 0 or done == count:
            begin = (first // GATHERED) * GATHERED
            collect = hot(row == edges[1:2, begin:done].astype(I16))
            part = dot(collect, messages[begin:done, :])
            if begin == 0:
                totals[...] = part
            else:
                totals[...] += part


def hand_out(totals, gain, keep, give):
    rows = totals.shape[0] // 4
    core = lax.rem(lax.axis_index("sub"), 2)
    for half in range(2):
        for out, which in ((keep, core), (give, 1 - core)):
            place = pl.multiple_of((2 * half + which) * rows, rows)
            out[half * rows : (half + 1) * rows, :] = (totals[pl.ds(place, rows), :] * gain[...]).astype(BF16)


def enc_kernel(
    plan, slots, grid_rows, mesh_rows, k_in, emb, edges, gain, l0, l1, l2, l3, o_in, o_out, b_in, b_out,
    across, round_, both, round_both, live, keep, give, own_mesh, full, stack, table, messages, totals,
):
    d = gain.shape[1]
    quarter = lax.axis_index("sub")
    width = l0.shape[1]
    for shard, step in zip((l0, l1, l2, l3), (0, 2, 1, 3)):
        place = pl.multiple_of(lax.bitwise_xor(quarter, step) * width, width)
        full[:, pl.ds(place, width)] = shard[...]
    step = k_in + d // 4
    for first, second, bit in ((o_in, o_out, 0), (b_in, b_out, 1)):
        place = lax.bitwise_xor(quarter, bit) * step
        stack[pl.ds(pl.multiple_of(place, 128), k_in), :] = first[...]
        stack[pl.ds(pl.multiple_of(place + k_in, 128), d // 4), :] = second[...]
    put_half(stack, k_in, across, 2, 0)
    put_half(stack, k_in, round_, 2, 1)
    put_half(stack, k_in, both, 3, 0)
    put_half(stack, k_in, round_both, 3, 1)
    rows = mesh_rows // 4
    core = lax.rem(quarter, 2)
    for half in range(2):
        place = pl.multiple_of(grid_rows + (2 * half + core) * rows, rows)
        own_mesh[half * rows : (half + 1) * rows, :] = full[pl.ds(place, rows), :]

    w_in = joined(stack, 0, k_in)
    halo_first, got = grid_rows + mesh_rows, full.shape[0] - grid_rows - mesh_rows
    table[:d, :] = halved(w_in[:d, :])
    table[d : d + grid_rows, :] = halved(dot(full[:grid_rows, :], w_in[d : 2 * d, :]))
    base = d + grid_rows + mesh_rows
    table[d + grid_rows : base, :] = halved(dot(full[grid_rows:halo_first, :], w_in[2 * d :, :]))
    table[base : base + got, :] = halved(dot(full[halo_first:, :], w_in[d : 2 * d, :]))
    if base + got < table.shape[0]:
        table[base + got :, :] = jnp.zeros((table.shape[0] - base - got, d), BF16)
    targets = halo_targets(plan, slots, grid_rows, table.shape[0] - base)
    own = lax.broadcasted_iota(I16, (1, grid_rows), 1)
    mesh = lax.broadcasted_iota(I16, (1, mesh_rows), 1)

    def first_stage(first):
        senders, receivers = columns(edges, first)
        chosen = [emb[first : first + STEP, :], hot(own == senders), hot(mesh == receivers), hot(targets == senders)]
        return dot(jnp.concatenate(chosen, axis=1), table[...])

    edge_blocks(edges, live[0:1, 0:1] * BLOCK, first_stage, joined(stack, k_in, d // 4), messages, totals)
    hand_out(totals, gain, keep, give)


def node_update(mesh, shares, w_in, w_out, gain):
    stacked = jnp.concatenate([mesh, shares], axis=1)
    hidden = silu(dot(stacked, w_in)).astype(BF16)
    update = layer_norm(dot(hidden, w_out)) * gain
    return (mesh.astype(F32) + update).astype(BF16)


def add(mine, theirs):
    return (mine.astype(F32) + theirs.astype(F32)).astype(BF16)


def add_kernel(mine, theirs, out):
    out[...] = add(mine[...], theirs[...])


def node_kernel(
    plan, k_in, k_out, mesh, mine, theirs, gain, n_in, n_out, w0, w1, w2, w3, w4, w5, send, after, out, packed, *rest
):
    outs, stack = rest[:-1], rest[-1]
    put_shard(stack, w0, 0, 0)
    put_shard(stack, w1, 0, 1)
    put_half(stack, k_in, w2, 2, 0, BY_PART)
    put_half(stack, k_in, w3, 2, 1, BY_PART)
    put_half(stack, k_in, w4, 3, 0, BY_PART)
    put_half(stack, k_in, w5, 3, 1, BY_PART)
    w_in, w_out = joined(stack, 0, k_in), joined(stack, k_in, k_out)
    fresh = node_update(mesh[...], add(mine[...], theirs[...]), w_in, w_out, gain[...])
    out[...] = fresh
    half = fresh.shape[0] // 2
    core = lax.rem(lax.axis_index("sub"), 2)
    place = lax.broadcasted_iota(jnp.int32, (fresh.shape[0], 1), 0)
    rows = place + core * half + jnp.where(place < half, 0, half)
    pick_lists(plan, fresh, send, outs, rows.astype(I16))
    stack_into(packed, (n_in, n_out))


def proc_first_kernel(
    k_in, emb, mine, theirs, edges, w0, w1, pair, pair_beside,
    table, pre, w_source, w_out, stack, full,
):
    d = full.shape[1]
    node_rows = full.shape[0]
    rows = node_rows // 4
    core = lax.rem(lax.axis_index("sub"), 2)
    for half in range(2):
        for part, which in ((mine, core), (theirs, 1 - core)):
            place = pl.multiple_of((2 * half + which) * rows, rows)
            full[pl.ds(place, rows), :] = part[half * rows : (half + 1) * rows, :]
    put_shard(stack, w0, 0, 0)
    put_shard(stack, w1, 0, 1)
    rows = pair.shape[0] // 2
    for other in range(2):
        put_half(stack, k_in, pair.at[pl.ds(other * rows, rows), :], 2, other)
        put_half(stack, k_in, pair_beside.at[pl.ds(other * rows, rows), :], 3, other)
    w_in = joined(stack, 0, k_in)
    w_out[...] = joined(stack, k_in, d // 4)
    w_source[...] = w_in[d : 2 * d, :]
    table[:d, :] = halved(w_in[:d, :])
    table[d : d + node_rows, :] = halved(dot(full[...], w_in[d : 2 * d, :]))
    table[d + node_rows :, :] = halved(dot(full[...], w_in[2 * d :, :]))
    lane = lax.broadcasted_iota(I16, (1, node_rows), 1)
    for first in range(0, pre.shape[0], STEP):
        pre[first : first + STEP, :] = dot(own_chosen(emb, edges, lane, first), table[...])


def own_chosen(emb, edges, lane, first):
    senders, receivers = columns(edges, first)
    return jnp.concatenate([emb[first : first + STEP, :], hot(lane == senders), hot(lane == receivers)], axis=1)


def proc_second_kernel(
    plan, slots, node_rows, emb, edges, gain, table, pre, w_source, w_out, halo, halo_beside,
    live, keep, give, halo_table, messages, totals,
):
    d = pre.shape[1]
    got = halo[...] + halo_beside[...]
    halo_table[: got.shape[0], :] = halved(dot(got, w_source[...]))
    if got.shape[0] < halo_table.shape[0]:
        halo_table[got.shape[0] :, :] = jnp.zeros((halo_table.shape[0] - got.shape[0], d), BF16)
    targets = halo_targets(plan, slots, node_rows, halo_table.shape[0])
    lane = lax.broadcasted_iota(I16, (1, node_rows), 1)

    def first_stage(first):
        senders, receivers = columns(edges, first)
        remote = dot(hot(targets == senders), halo_table[...])
        if first < pre.shape[0]:
            return pre[first : first + STEP, :] + remote
        return dot(own_chosen(emb, edges, lane, first), table[...]) + remote

    edge_blocks(edges, live[1:2, 0:1] * BLOCK, first_stage, w_out[...], messages, totals)
    hand_out(totals, gain, keep, give)


def fold_kernel(mine, theirs, keep, give):
    rows = mine.shape[0] // 2
    chip = lax.div(lax.axis_index("sub"), 2)
    for out, which in ((keep, chip), (give, 1 - chip)):
        place = pl.multiple_of(which * rows, rows)
        out[...] = add(mine[pl.ds(place, rows), :], theirs[pl.ds(place, rows), :])


def out_kernel(k_in, k_out, middle, mine, theirs, gain, w0, w1, w2, w3, out, stacked, hidden):
    rows, d = out.shape
    quarter = lax.axis_index("sub")
    chip = lax.div(quarter, 2)
    mesh = middle[pl.ds(pl.multiple_of(chip * rows, rows), rows), :]
    stacked[:, :d] = mesh
    stacked[:, d:] = add(mine[...], theirs[...])
    shards = (w0, w1, w2, w3)

    def columns_of(ref, step, count):
        return ref[:, pl.ds(pl.multiple_of(lax.bitwise_xor(quarter, step) * count, count), count)]

    left = jnp.concatenate([columns_of(stacked, step, k_in) for step in range(4)], axis=1)
    right = jnp.concatenate([w[:k_in, :] for w in shards], axis=0)
    hidden[...] = silu(dot(left, right)).astype(BF16)
    left = jnp.concatenate([columns_of(hidden, step, k_out) for step in range(4)], axis=1)
    right = jnp.concatenate([w[k_in:, :] for w in shards], axis=0)
    update = layer_norm(dot(left, right)) * gain[...]
    out[...] = (mesh.astype(F32) + update).astype(BF16)


def to_chip(v):
    return lax.ppermute(v, "sub", [(i, i ^ 2) for i in range(4)])


def to_core(v):
    return lax.ppermute(v, "sub", [(i, i ^ 1) for i in range(4)])


def to_group(v):
    count = lax.axis_size("groups")
    return lax.ppermute(v, "groups", [(i, count - 1 - i) for i in range(count)])


def to_partition(v):
    return lax.ppermute(v, "dom", [(i, i ^ 1) for i in range(lax.axis_size("dom"))])


def shape(rows, width, dtype=BF16):
    return jax.ShapeDtypeStruct((rows, width), dtype)


def padded(rows):
    return -(-rows // 128) * 128


def local(
    grid_lat,
    mesh_lat,
    grid_send,
    mesh_send,
    enc_edges,
    enc_geom,
    enc_blocks,
    proc_edges,
    proc_geom,
    proc_blocks,
    enc_geo,
    proc_geo,
    enc_edge_in,
    enc_edge_out,
    enc_node_in,
    enc_node_out,
    proc_edge_in,
    proc_edge_out,
    proc_node_in,
    proc_node_out,
    enc_edge_gain,
    enc_node_gain,
    proc_edge_gain,
    proc_node_gain,
):
    plan = halo_plan(lax.axis_size("dom"))
    d = enc_geo.shape[1]
    grid_rows, mesh_rows = grid_lat.shape[0], mesh_lat.shape[0]
    n_enc, n_proc = enc_edges.shape[1], proc_edges.shape[1]
    enc_edge_gain, enc_node_gain, proc_edge_gain, proc_node_gain = (
        g.reshape(1, d) for g in (enc_edge_gain, enc_node_gain, proc_edge_gain, proc_node_gain)
    )
    k_in, k_out = enc_edge_in.shape[0], enc_edge_out.shape[0]
    n_in, n_out = enc_node_in.shape[0], enc_node_out.shape[0]
    width = grid_lat.shape[1]

    slots = grid_send.shape[2]
    (token,) = call(begin_kernel, [shape(16, 128)], [], flops=LONG)
    edge_half, *outgoing = call(
        functools.partial(first_pack_kernel, plan),
        [shape((k_in + 2 * k_out + n_out) // 2, d)] + [shape(slots, width)] * len(plan),
        [grid_lat, grid_send, enc_edge_in, enc_edge_out, enc_node_out, proc_edge_out, token],
    )
    first_across = to_chip(edge_half)
    (edge_across,) = call(rows_kernel, [shape((k_in + k_out) // 2, d)], [first_across])
    halos = [lax.ppermute(v, "dom", entry[0]) for v, entry in zip(outgoing, plan)]
    got = len(plan) * slots
    (lat,) = call(
        concat_kernel,
        [shape(grid_rows + mesh_rows + got, width)],
        [grid_lat, mesh_lat, *halos],
    )
    lat_across = to_chip(lat)
    lat_beside = to_core(lat)
    edge_beside = [to_core(enc_edge_in), to_core(enc_edge_out)]
    edge_round = to_group(edge_across)
    node_w, proc_w, enc_emb, proc_emb, lives = call(
        embed_kernel,
        [
            shape(n_in + n_out, d), shape(k_in + k_out, d), shape(n_enc, d), shape(n_proc, d),
            shape(8, 128, jnp.int32),
        ],
        [
            enc_node_in, enc_node_out, proc_edge_in, proc_edge_out,
            enc_geom, enc_geo, proc_geom, proc_geo, enc_blocks.reshape(1, 1), proc_blocks.reshape(1, 1), lat,
        ],
        flops=2 * (n_enc + n_proc) * d * 128,
    )
    crossing, lat_sent = call(
        functools.partial(cross_kernel, (n_in, k_in)),
        [shape((n_in + k_in) // 2, d), shape(lat.shape[0], width)],
        [node_w, proc_w, lat_across],
    )
    lat_both = to_core(lat_sent)
    next_across = to_chip(crossing)
    node_beside, proc_beside = to_core(node_w), to_core(proc_w)

    halo_rows = padded(got)
    half = mesh_rows // 2
    keep, give, own_mesh = call(
        functools.partial(enc_kernel, plan, slots, grid_rows, mesh_rows, k_in),
        [shape(half, d)] * 3,
        [
            enc_emb, enc_edges, enc_edge_gain, lat, lat_across, lat_beside, lat_both,
            enc_edge_in, enc_edge_out, *edge_beside,
            edge_across, edge_round, to_core(edge_across), to_core(edge_round), lives,
        ],
        scratch=[
            pltpu.VMEM((grid_rows + mesh_rows + got, d), BF16),
            pltpu.VMEM((4 * (k_in + k_out), d), BF16),
            pltpu.VMEM((d + grid_rows + mesh_rows + halo_rows, d), BF16),
            pltpu.VMEM((n_enc, d), BF16),
            pltpu.VMEM((mesh_rows, d), F32),
        ],
        flops=2 * n_enc * d * (3 * d + grid_rows + mesh_rows + halo_rows),
    )
    (chip_sum,) = call(add_kernel, [shape(half, d)], [keep, to_core(give)])
    node_across, proc_across = call(
        functools.partial(split_kernel, (n_in // 2, k_in // 2)),
        [shape((n_in + n_out) // 2, d), shape((k_in + k_out) // 2, d)],
        [first_across, next_across, chip_sum],
    )
    node_round = to_partition(node_across)
    proc_round = to_group(proc_across)
    node_both = to_core(node_across)
    slots = mesh_send.shape[2]
    mid_half, last_w, *outgoing = call(
        functools.partial(node_kernel, plan, n_in, n_out),
        [shape(half, d), shape(n_in + n_out, d)] + [shape(slots, d)] * len(plan),
        [
            own_mesh, chip_sum, to_chip(chip_sum), enc_node_gain, proc_node_in, proc_node_out,
            node_w, node_beside, node_across, node_round, node_both, to_core(node_round), mesh_send, proc_beside,
        ],
        scratch=[pltpu.VMEM((4 * (n_in + n_out), d), BF16)],
        flops=2 * half * d * 3 * d,
    )
    (proc_pair,) = call(pair_kernel, [shape(k_in + k_out, d)], [proc_across, proc_round, mid_half])
    halos = [lax.ppermute(v, "dom", entry[0]) for v, entry in zip(outgoing, plan)]
    (halo,) = call(concat_kernel, [shape(len(plan) * slots, d)], halos)
    halo_beside = to_core(halo)
    last_across, last_beside = to_chip(last_w), to_core(last_w)
    early = n_proc // 2
    table, pre, w_source, w_out = call(
        functools.partial(proc_first_kernel, k_in),
        [shape(d + 2 * mesh_rows, d), shape(early, d, F32), shape(d, d), shape(d, d)],
        [
            proc_emb, mid_half, to_core(mid_half), proc_edges, proc_w, proc_beside, proc_pair, to_core(proc_pair),
        ],
        scratch=[pltpu.VMEM((4 * (k_in + k_out), d), BF16), pltpu.VMEM((mesh_rows, d), BF16)],
        flops=2 * early * d * (d + 2 * mesh_rows),
    )
    halo_rows = padded(len(plan) * slots)
    keep, give = call(
        functools.partial(proc_second_kernel, plan, slots, mesh_rows),
        [shape(half, d), shape(half, d)],
        [proc_emb, proc_edges, proc_edge_gain, table, pre, w_source, w_out, halo, halo_beside, lives],
        scratch=[
            pltpu.VMEM((halo_rows, d), BF16),
            pltpu.VMEM((n_proc, d), BF16),
            pltpu.VMEM((mesh_rows, d), F32),
        ],
        flops=2 * n_proc * d * (2 * d + mesh_rows + halo_rows),
    )
    quarter = mesh_rows // 4
    mine, other = call(fold_kernel, [shape(quarter, d)] * 2, [keep, to_core(give)])
    (result,) = call(
        functools.partial(out_kernel, n_in, n_out),
        [shape(quarter, d)],
        [mid_half, mine, to_chip(other), proc_node_gain, last_w, last_beside, last_across, to_core(last_across)],
        scratch=[pltpu.VMEM((quarter, 4 * n_in), BF16), pltpu.VMEM((quarter, 4 * n_out), BF16)],
        flops=2 * quarter * d * 3 * d,
    )
    return result


def solution(mesh):
    placed = (
        P(("groups", "dom"), "sub"),
        P(("groups", "dom"), "sub"),
        P("dom", None, None),
        P("dom", None, None),
        P(None, ("dom", "sub")),
        P(None, ("dom", "sub")),
        P("dom"),
        P(None, ("dom", "sub")),
        P(None, ("dom", "sub")),
        P("dom"),
        P(),
        P(),
        P("sub", None),
        P("sub", None),
        P("sub", None),
        P("sub", None),
        P("sub", None),
        P("sub", None),
        P("sub", None),
        P("sub", None),
        P(),
        P(),
        P(),
        P(),
    )
    return jax.shard_map(
        local,
        mesh=mesh,
        in_specs=placed,
        out_specs=P(("groups", "dom", "sub"), None),
        check_vma=False,
    )
```

```python
import functools

import jax
import jax.numpy as jnp
from jax import lax
from jax.experimental import pallas as pl
from jax.experimental.pallas import tpu as pltpu
from jax.sharding import PartitionSpec as P

BLOCK = 128
OFFSETS = (-2, -1, 1, 2)
STEP = 512
GATHERED = 2048
LONG = 30 * 10**9
BY_GROUP = ("groups",)
BY_PART = ("dom",)
VMEM_BYTES = 24 * 1024 * 1024
I16 = jnp.int16
BF16 = jnp.bfloat16
F32 = jnp.float32


def silu_of_half(h):
    return h + h * jnp.tanh(h)


def silu(v):
    return silu_of_half(0.5 * v)


def halved(v):
    return (v.astype(F32) * 0.5).astype(BF16)


def region_of(delta):
    return jnp.where(delta < 0, delta + 2, delta + 1)


def halo_plan(count):
    plan = []
    if count == 4:
        for bit in (1, 2, 3):
            pairs = [(d, d ^ bit) for d in range(4) if abs((d ^ bit) - d) <= 2]
            regions = [(OFFSETS.index((d ^ bit) - d) if abs((d ^ bit) - d) <= 2 else -1) for d in range(4)]
            plan.append((pairs, regions, regions))
    else:
        for region, offset in enumerate(OFFSETS):
            pairs = [(d, d + offset) for d in range(count) if 0 <= d + offset < count]
            plan.append((pairs, region, 3 - region))
    return plan


def by_index(choice, index):
    if isinstance(choice, int):
        return choice
    picked = jnp.int32(choice[0])
    for place in range(1, len(choice)):
        picked = jnp.where(index == place, choice[place], picked)
    return picked


def whole_refs(count):
    return [pl.BlockSpec(memory_space=pltpu.VMEM)] * count


def call(body, outs, args, scratch=(), flops=0):
    moved = sum(a.size * a.dtype.itemsize for a in args) + sum(
        o.size * jnp.dtype(o.dtype).itemsize for o in outs
    )
    specs = whole_refs(len(args))
    return pl.pallas_call(
        body,
        out_shape=tuple(outs),
        in_specs=specs,
        out_specs=tuple(whole_refs(len(outs))),
        scratch_shapes=list(scratch),
        compiler_params=pltpu.CompilerParams(vmem_limit_bytes=VMEM_BYTES),
        cost_estimate=pl.CostEstimate(flops=int(flops), bytes_accessed=int(moved), transcendentals=0),
    )(*args)


def dot(a, b):
    return jnp.dot(a, b, preferred_element_type=F32)


def dot_first(a, b):
    return lax.dot_general(a, b, (((0,), (0,)), ((), ())), preferred_element_type=F32)


def three_parts(v):
    a = v.astype(BF16)
    rest = v - a.astype(F32)
    b = rest.astype(BF16)
    c = (rest - b.astype(F32)).astype(BF16)
    return a, b, c


def embed_rows(geom, geo):
    a1, a2, a3 = three_parts(geom)
    b1, b2, b3 = three_parts(geo)
    left = jnp.concatenate([a1, a1, a2, a1, a2, a3], axis=0)
    right = jnp.concatenate([b1, b2, b1, b3, b2, b1], axis=0)
    return silu(dot_first(left, right)).astype(BF16)


def layer_norm(v, live=None):
    width = v.shape[-1]
    centered = v - jnp.sum(v, axis=-1, keepdims=True) * (1.0 / width)
    spread = jnp.sum(centered * centered, axis=-1, keepdims=True) * (1.0 / width)
    factor = lax.rsqrt(spread + 1e-05)
    if live is not None:
        factor = jnp.where(live, factor, 0.0)
    return centered * factor


def hot(cond):
    return jnp.where(cond, BF16(1), BF16(0))


def pick_rows(table, listed, rows=None):
    if rows is None:
        rows = lax.broadcasted_iota(I16, (table.shape[0], 1), 0)
    return dot_first(hot(rows == listed.astype(I16)), table).astype(BF16)


def pick_lists(plan, table, send, outs, rows=None):
    here = lax.axis_index("dom")
    for (pairs, sent, received), out in zip(plan, outs):
        region = jnp.maximum(by_index(sent, here), 0)
        out[...] = pick_rows(table, send[0, pl.ds(region, 1), :], rows)


def stack_into(out, parts):
    first = 0
    for part in parts:
        out[first : first + part.shape[0], :] = part[...]
        first += part.shape[0]


def begin_kernel(token):
    token[...] = jnp.zeros(token.shape, token.dtype)


def first_pack_kernel(plan, grid, send, w_in, w_out, n_out, p_out, token, half, *outs):
    place = 0
    for source, axes in ((w_in, BY_GROUP), (w_out, BY_GROUP), (n_out, BY_PART), (p_out, BY_GROUP)):
        rows = source.shape[0] // 2
        begin = pl.multiple_of(parity(axes) * rows, 64)
        half[place : place + rows, :] = source[pl.ds(begin, rows), :]
        place += rows
    pick_lists(plan, grid[...], send, outs)


def embed_kernel(e_in, e_out, p_in, p_out, egeom, egeo, pgeom, pgeo, elive, plive, after, node, proc, eout, pout, lives):
    lives[0:1, :] = jnp.broadcast_to(elive[...], (1, lives.shape[1]))
    lives[1:2, :] = jnp.broadcast_to(plive[...], (1, lives.shape[1]))
    stack_into(node, (e_in, e_out))
    stack_into(proc, (p_in, p_out))
    for geom, geo, out in ((egeom, egeo, eout), (pgeom, pgeo, pout)):
        for begin in range(0, out.shape[0], STEP):
            out[begin : begin + STEP, :] = embed_rows(geom[:, begin : begin + STEP], geo[...])


def cross_kernel(counts, node, proc, lat, crossing, lat_out):
    lat_out[...] = lat[...]
    place = 0
    for stack, rows, axes in ((node, counts[0], BY_PART), (proc, counts[1], BY_GROUP)):
        half = rows // 2
        begin = pl.multiple_of(parity(axes) * half, 64)
        crossing[place : place + half, :] = stack[pl.ds(begin, half), :]
        place += half


def rows_kernel(source, out):
    out[...] = source[: out.shape[0], :]


def pair_kernel(first, second, after, out):
    stack_into(out, (first, second))


def split_kernel(ins, early, source, after, node, proc):
    n, p = ins
    n_rest, p_rest = node.shape[0] - n, proc.shape[0] - p
    base = early.shape[0] - n_rest - p_rest
    stack_into(node, (source.at[pl.ds(0, n), :], early.at[pl.ds(base, n_rest), :]))
    stack_into(proc, (source.at[pl.ds(n, p), :], early.at[pl.ds(base + n_rest, p_rest), :]))


def concat_kernel(*refs):
    stack_into(refs[-1], refs[:-1])


def put_shard(target, source, first, step, part=0, parts=1):
    rows = target.shape[0] // (4 * parts)
    place = (lax.bitwise_xor(lax.axis_index("sub"), step) * parts + part) * rows
    target[pl.ds(pl.multiple_of(place, rows), rows), :] = source[first : first + rows, :]


def parity(axes):
    return lax.rem(sum(lax.axis_index(axis) for axis in axes), 2)


def put_half(target, k, source, step, other, axes=("groups",)):
    rows = target.shape[0] // 4
    which = lax.bitwise_xor(parity(axes), other)
    begin = lax.bitwise_xor(lax.axis_index("sub"), step) * rows
    for base, count in ((0, k // 2), (k // 2, (rows - k) // 2)):
        place = pl.multiple_of(begin + 2 * base + which * count, 64)
        target[pl.ds(place, count), :] = source[base : base + count, :]


def joined(stack, first, rows):
    step = stack.shape[0] // 4
    return jnp.concatenate([stack[k * step + first : k * step + first + rows, :] for k in range(4)], axis=0)


def halo_targets(plan, slots, node_rows, width):
    here = lax.axis_index("dom")
    lane = lax.broadcasted_iota(jnp.int32, (1, width), 1)
    target = jnp.full((1, width), -1, jnp.int32)
    for place, (pairs, sent, received) in enumerate(plan):
        region = by_index(received, here)
        first = jnp.where(region < 0, -4 * node_rows, node_rows + region * slots)
        inside = (lane >= place * slots) & (lane < (place + 1) * slots)
        target = jnp.where(inside, lane - place * slots + first, target)
    return target.astype(I16)


def columns(edges, first):
    pair = edges[:, first : first + STEP]
    zero = jnp.zeros((8 - pair.shape[0], STEP), jnp.int32)
    upright = jnp.transpose(jnp.concatenate([pair, zero], axis=0).astype(F32)).astype(jnp.int32).astype(I16)
    return upright[:, 0:1], upright[:, 1:2]


def edge_blocks(edges, live_edges, first_stage, w_out, messages, totals):
    count = edges.shape[1]
    steps = count // STEP
    row = lax.broadcasted_iota(I16, (totals.shape[0], 1), 0)
    quarter = lax.axis_index("sub")
    sums, raw = {}, {}
    for turn in range(steps + 2):
        if turn < steps:
            sums[turn] = first_stage(turn * STEP)
        if 0 <= turn - 1 < steps:
            raw[turn - 1] = dot(silu_of_half(sums.pop(turn - 1)).astype(BF16), w_out)
        if turn < 2:
            continue
        first = (turn - 2) * STEP
        place = lax.broadcasted_iota(jnp.int32, (STEP, 1), 0) + (first + quarter * count)
        message = layer_norm(raw.pop(turn - 2), place < live_edges)
        messages[first : first + STEP, :] = message.astype(BF16)
        done = first + STEP
        if done % GATHERED == 0 or done == count:
            begin = (first // GATHERED) * GATHERED
            collect = hot(row == edges[1:2, begin:done].astype(I16))
            part = dot(collect, messages[begin:done, :])
            if begin == 0:
                totals[...] = part
            else:
                totals[...] += part


def hand_out(totals, gain, keep, give):
    rows = totals.shape[0] // 4
    core = lax.rem(lax.axis_index("sub"), 2)
    for half in range(2):
        for out, which in ((keep, core), (give, 1 - core)):
            place = pl.multiple_of((2 * half + which) * rows, rows)
            out[half * rows : (half + 1) * rows, :] = (totals[pl.ds(place, rows), :] * gain[...]).astype(BF16)


def enc_kernel(
    plan, slots, grid_rows, mesh_rows, k_in, emb, edges, gain, l0, l1, l2, l3, o_in, o_out, b_in, b_out,
    across, round_, both, round_both, live, keep, give, own_mesh, full, stack, table, messages, totals,
):
    d = gain.shape[1]
    quarter = lax.axis_index("sub")
    width = l0.shape[1]
    for shard, step in zip((l0, l1, l2, l3), (0, 2, 1, 3)):
        place = pl.multiple_of(lax.bitwise_xor(quarter, step) * width, width)
        full[:, pl.ds(place, width)] = shard[...]
    step = k_in + d // 4
    for first, second, bit in ((o_in, o_out, 0), (b_in, b_out, 1)):
        place = lax.bitwise_xor(quarter, bit) * step
        stack[pl.ds(pl.multiple_of(place, 128), k_in), :] = first[...]
        stack[pl.ds(pl.multiple_of(place + k_in, 128), d // 4), :] = second[...]
    put_half(stack, k_in, across, 2, 0)
    put_half(stack, k_in, round_, 2, 1)
    put_half(stack, k_in, both, 3, 0)
    put_half(stack, k_in, round_both, 3, 1)
    rows = mesh_rows // 4
    core = lax.rem(quarter, 2)
    for half in range(2):
        place = pl.multiple_of(grid_rows + (2 * half + core) * rows, rows)
        own_mesh[half * rows : (half + 1) * rows, :] = full[pl.ds(place, rows), :]

    w_in = joined(stack, 0, k_in)
    halo_first, got = grid_rows + mesh_rows, full.shape[0] - grid_rows - mesh_rows
    table[:d, :] = halved(w_in[:d, :])
    table[d : d + grid_rows, :] = halved(dot(full[:grid_rows, :], w_in[d : 2 * d, :]))
    base = d + grid_rows + mesh_rows
    table[d + grid_rows : base, :] = halved(dot(full[grid_rows:halo_first, :], w_in[2 * d :, :]))
    table[base : base + got, :] = halved(dot(full[halo_first:, :], w_in[d : 2 * d, :]))
    if base + got < table.shape[0]:
        table[base + got :, :] = jnp.zeros((table.shape[0] - base - got, d), BF16)
    targets = halo_targets(plan, slots, grid_rows, table.shape[0] - base)
    own = lax.broadcasted_iota(I16, (1, grid_rows), 1)
    mesh = lax.broadcasted_iota(I16, (1, mesh_rows), 1)

    def first_stage(first):
        senders, receivers = columns(edges, first)
        chosen = [emb[first : first + STEP, :], hot(own == senders), hot(mesh == receivers), hot(targets == senders)]
        return dot(jnp.concatenate(chosen, axis=1), table[...])

    edge_blocks(edges, live[0:1, 0:1] * BLOCK, first_stage, joined(stack, k_in, d // 4), messages, totals)
    hand_out(totals, gain, keep, give)


def node_update(mesh, shares, w_in, w_out, gain):
    stacked = jnp.concatenate([mesh, shares], axis=1)
    hidden = silu(dot(stacked, w_in)).astype(BF16)
    update = layer_norm(dot(hidden, w_out)) * gain
    return (mesh.astype(F32) + update).astype(BF16)


def add(mine, theirs):
    return (mine.astype(F32) + theirs.astype(F32)).astype(BF16)


def add_kernel(mine, theirs, out):
    out[...] = add(mine[...], theirs[...])


def node_kernel(
    plan, k_in, k_out, mesh, mine, theirs, gain, n_in, n_out, w0, w1, w2, w3, w4, w5, send, after, out, packed, *rest
):
    outs, stack = rest[:-1], rest[-1]
    put_shard(stack, w0, 0, 0)
    put_shard(stack, w1, 0, 1)
    put_half(stack, k_in, w2, 2, 0, BY_PART)
    put_half(stack, k_in, w3, 2, 1, BY_PART)
    put_half(stack, k_in, w4, 3, 0, BY_PART)
    put_half(stack, k_in, w5, 3, 1, BY_PART)
    w_in, w_out = joined(stack, 0, k_in), joined(stack, k_in, k_out)
    fresh = node_update(mesh[...], add(mine[...], theirs[...]), w_in, w_out, gain[...])
    out[...] = fresh
    half = fresh.shape[0] // 2
    core = lax.rem(lax.axis_index("sub"), 2)
    place = lax.broadcasted_iota(jnp.int32, (fresh.shape[0], 1), 0)
    rows = place + core * half + jnp.where(place < half, 0, half)
    pick_lists(plan, fresh, send, outs, rows.astype(I16))
    stack_into(packed, (n_in, n_out))


def proc_first_kernel(
    k_in, emb, mine, theirs, edges, w0, w1, pair, pair_beside,
    table, pre, w_source, w_out, stack, full,
):
    d = full.shape[1]
    node_rows = full.shape[0]
    rows = node_rows // 4
    core = lax.rem(lax.axis_index("sub"), 2)
    for half in range(2):
        for part, which in ((mine, core), (theirs, 1 - core)):
            place = pl.multiple_of((2 * half + which) * rows, rows)
            full[pl.ds(place, rows), :] = part[half * rows : (half + 1) * rows, :]
    put_shard(stack, w0, 0, 0)
    put_shard(stack, w1, 0, 1)
    rows = pair.shape[0] // 2
    for other in range(2):
        put_half(stack, k_in, pair.at[pl.ds(other * rows, rows), :], 2, other)
        put_half(stack, k_in, pair_beside.at[pl.ds(other * rows, rows), :], 3, other)
    w_in = joined(stack, 0, k_in)
    w_out[...] = joined(stack, k_in, d // 4)
    w_source[...] = w_in[d : 2 * d, :]
    table[:d, :] = halved(w_in[:d, :])
    table[d : d + node_rows, :] = halved(dot(full[...], w_in[d : 2 * d, :]))
    table[d + node_rows :, :] = halved(dot(full[...], w_in[2 * d :, :]))
    lane = lax.broadcasted_iota(I16, (1, node_rows), 1)
    for first in range(0, pre.shape[0], STEP):
        pre[first : first + STEP, :] = dot(own_chosen(emb, edges, lane, first), table[...])


def own_chosen(emb, edges, lane, first):
    senders, receivers = columns(edges, first)
    return jnp.concatenate([emb[first : first + STEP, :], hot(lane == senders), hot(lane == receivers)], axis=1)


def proc_second_kernel(
    plan, slots, node_rows, emb, edges, gain, table, pre, w_source, w_out, halo, halo_beside,
    live, keep, give, halo_table, messages, totals,
):
    d = pre.shape[1]
    got = halo[...] + halo_beside[...]
    halo_table[: got.shape[0], :] = halved(dot(got, w_source[...]))
    if got.shape[0] < halo_table.shape[0]:
        halo_table[got.shape[0] :, :] = jnp.zeros((halo_table.shape[0] - got.shape[0], d), BF16)
    targets = halo_targets(plan, slots, node_rows, halo_table.shape[0])
    lane = lax.broadcasted_iota(I16, (1, node_rows), 1)

    def first_stage(first):
        senders, receivers = columns(edges, first)
        remote = dot(hot(targets == senders), halo_table[...])
        if first < pre.shape[0]:
            return pre[first : first + STEP, :] + remote
        return dot(own_chosen(emb, edges, lane, first), table[...]) + remote

    edge_blocks(edges, live[1:2, 0:1] * BLOCK, first_stage, w_out[...], messages, totals)
    hand_out(totals, gain, keep, give)


def fold_kernel(mine, theirs, keep, give):
    rows = mine.shape[0] // 2
    chip = lax.div(lax.axis_index("sub"), 2)
    for out, which in ((keep, chip), (give, 1 - chip)):
        place = pl.multiple_of(which * rows, rows)
        out[...] = add(mine[pl.ds(place, rows), :], theirs[pl.ds(place, rows), :])


def out_kernel(k_in, k_out, middle, mine, theirs, gain, w0, w1, w2, w3, out, stacked, hidden):
    rows, d = out.shape
    quarter = lax.axis_index("sub")
    chip = lax.div(quarter, 2)
    mesh = middle[pl.ds(pl.multiple_of(chip * rows, rows), rows), :]
    stacked[:, :d] = mesh
    stacked[:, d:] = add(mine[...], theirs[...])
    shards = (w0, w1, w2, w3)

    def columns_of(ref, step, count):
        return ref[:, pl.ds(pl.multiple_of(lax.bitwise_xor(quarter, step) * count, count), count)]

    left = jnp.concatenate([columns_of(stacked, step, k_in) for step in range(4)], axis=1)
    right = jnp.concatenate([w[:k_in, :] for w in shards], axis=0)
    hidden[...] = silu(dot(left, right)).astype(BF16)
    left = jnp.concatenate([columns_of(hidden, step, k_out) for step in range(4)], axis=1)
    right = jnp.concatenate([w[k_in:, :] for w in shards], axis=0)
    update = layer_norm(dot(left, right)) * gain[...]
    out[...] = (mesh.astype(F32) + update).astype(BF16)


def to_chip(v):
    return lax.ppermute(v, "sub", [(i, i ^ 2) for i in range(4)])


def to_core(v):
    return lax.ppermute(v, "sub", [(i, i ^ 1) for i in range(4)])


def to_group(v):
    count = lax.axis_size("groups")
    return lax.ppermute(v, "groups", [(i, count - 1 - i) for i in range(count)])


def to_partition(v):
    return lax.ppermute(v, "dom", [(i, i ^ 1) for i in range(lax.axis_size("dom"))])


def shape(rows, width, dtype=BF16):
    return jax.ShapeDtypeStruct((rows, width), dtype)


def padded(rows):
    return -(-rows // 128) * 128


def local(
    grid_lat,
    mesh_lat,
    grid_send,
    mesh_send,
    enc_edges,
    enc_geom,
    enc_blocks,
    proc_edges,
    proc_geom,
    proc_blocks,
    enc_geo,
    proc_geo,
    enc_edge_in,
    enc_edge_out,
    enc_node_in,
    enc_node_out,
    proc_edge_in,
    proc_edge_out,
    proc_node_in,
    proc_node_out,
    enc_edge_gain,
    enc_node_gain,
    proc_edge_gain,
    proc_node_gain,
):
    plan = halo_plan(lax.axis_size("dom"))
    d = enc_geo.shape[1]
    grid_rows, mesh_rows = grid_lat.shape[0], mesh_lat.shape[0]
    n_enc, n_proc = enc_edges.shape[1], proc_edges.shape[1]
    enc_edge_gain, enc_node_gain, proc_edge_gain, proc_node_gain = (
        g.reshape(1, d) for g in (enc_edge_gain, enc_node_gain, proc_edge_gain, proc_node_gain)
    )
    k_in, k_out = enc_edge_in.shape[0], enc_edge_out.shape[0]
    n_in, n_out = enc_node_in.shape[0], enc_node_out.shape[0]
    width = grid_lat.shape[1]

    slots = grid_send.shape[2]
    (token,) = call(begin_kernel, [shape(16, 128)], [], flops=LONG)
    edge_half, *outgoing = call(
        functools.partial(first_pack_kernel, plan),
        [shape((k_in + 2 * k_out + n_out) // 2, d)] + [shape(slots, width)] * len(plan),
        [grid_lat, grid_send, enc_edge_in, enc_edge_out, enc_node_out, proc_edge_out, token],
    )
    first_across = to_chip(edge_half)
    (edge_across,) = call(rows_kernel, [shape((k_in + k_out) // 2, d)], [first_across])
    halos = [lax.ppermute(v, "dom", entry[0]) for v, entry in zip(outgoing, plan)]
    got = len(plan) * slots
    (lat,) = call(
        concat_kernel,
        [shape(grid_rows + mesh_rows + got, width)],
        [grid_lat, mesh_lat, *halos],
    )
    lat_across = to_chip(lat)
    lat_beside = to_core(lat)
    edge_beside = [to_core(enc_edge_in), to_core(enc_edge_out)]
    edge_round = to_group(edge_across)
    node_w, proc_w, enc_emb, proc_emb, lives = call(
        embed_kernel,
        [
            shape(n_in + n_out, d), shape(k_in + k_out, d), shape(n_enc, d), shape(n_proc, d),
            shape(8, 128, jnp.int32),
        ],
        [
            enc_node_in, enc_node_out, proc_edge_in, proc_edge_out,
            enc_geom, enc_geo, proc_geom, proc_geo, enc_blocks.reshape(1, 1), proc_blocks.reshape(1, 1), lat,
        ],
        flops=2 * (n_enc + n_proc) * d * 128,
    )
    crossing, lat_sent = call(
        functools.partial(cross_kernel, (n_in, k_in)),
        [shape((n_in + k_in) // 2, d), shape(lat.shape[0], width)],
        [node_w, proc_w, lat_across],
    )
    lat_both = to_core(lat_sent)
    next_across = to_chip(crossing)
    node_beside, proc_beside = to_core(node_w), to_core(proc_w)

    halo_rows = padded(got)
    half = mesh_rows // 2
    keep, give, own_mesh = call(
        functools.partial(enc_kernel, plan, slots, grid_rows, mesh_rows, k_in),
        [shape(half, d)] * 3,
        [
            enc_emb, enc_edges, enc_edge_gain, lat, lat_across, lat_beside, lat_both,
            enc_edge_in, enc_edge_out, *edge_beside,
            edge_across, edge_round, to_core(edge_across), to_core(edge_round), lives,
        ],
        scratch=[
            pltpu.VMEM((grid_rows + mesh_rows + got, d), BF16),
            pltpu.VMEM((4 * (k_in + k_out), d), BF16),
            pltpu.VMEM((d + grid_rows + mesh_rows + halo_rows, d), BF16),
            pltpu.VMEM((n_enc, d), BF16),
            pltpu.VMEM((mesh_rows, d), F32),
        ],
        flops=2 * n_enc * d * (3 * d + grid_rows + mesh_rows + halo_rows),
    )
    (chip_sum,) = call(add_kernel, [shape(half, d)], [keep, to_core(give)])
    node_across, proc_across = call(
        functools.partial(split_kernel, (n_in // 2, k_in // 2)),
        [shape((n_in + n_out) // 2, d), shape((k_in + k_out) // 2, d)],
        [first_across, next_across, chip_sum],
    )
    node_round = to_partition(node_across)
    proc_round = to_group(proc_across)
    node_both = to_core(node_across)
    slots = mesh_send.shape[2]
    mid_half, last_w, *outgoing = call(
        functools.partial(node_kernel, plan, n_in, n_out),
        [shape(half, d), shape(n_in + n_out, d)] + [shape(slots, d)] * len(plan),
        [
            own_mesh, chip_sum, to_chip(chip_sum), enc_node_gain, proc_node_in, proc_node_out,
            node_w, node_beside, node_across, node_round, node_both, to_core(node_round), mesh_send, proc_beside,
        ],
        scratch=[pltpu.VMEM((4 * (n_in + n_out), d), BF16)],
        flops=2 * half * d * 3 * d,
    )
    (proc_pair,) = call(pair_kernel, [shape(k_in + k_out, d)], [proc_across, proc_round, mid_half])
    halos = [lax.ppermute(v, "dom", entry[0]) for v, entry in zip(outgoing, plan)]
    (halo,) = call(concat_kernel, [shape(len(plan) * slots, d)], halos)
    halo_beside = to_core(halo)
    last_across, last_beside = to_chip(last_w), to_core(last_w)
    early = n_proc // 2
    table, pre, w_source, w_out = call(
        functools.partial(proc_first_kernel, k_in),
        [shape(d + 2 * mesh_rows, d), shape(early, d, F32), shape(d, d), shape(d, d)],
        [
            proc_emb, mid_half, to_core(mid_half), proc_edges, proc_w, proc_beside, proc_pair, to_core(proc_pair),
        ],
        scratch=[pltpu.VMEM((4 * (k_in + k_out), d), BF16), pltpu.VMEM((mesh_rows, d), BF16)],
        flops=2 * early * d * (d + 2 * mesh_rows),
    )
    halo_rows = padded(len(plan) * slots)
    keep, give = call(
        functools.partial(proc_second_kernel, plan, slots, mesh_rows),
        [shape(half, d), shape(half, d)],
        [proc_emb, proc_edges, proc_edge_gain, table, pre, w_source, w_out, halo, halo_beside, lives],
        scratch=[
            pltpu.VMEM((halo_rows, d), BF16),
            pltpu.VMEM((n_proc, d), BF16),
            pltpu.VMEM((mesh_rows, d), F32),
        ],
        flops=2 * n_proc * d * (2 * d + mesh_rows + halo_rows),
    )
    quarter = mesh_rows // 4
    mine, other = call(fold_kernel, [shape(quarter, d)] * 2, [keep, to_core(give)])
    (result,) = call(
        functools.partial(out_kernel, n_in, n_out),
        [shape(quarter, d)],
        [mid_half, mine, to_chip(other), proc_node_gain, last_w, last_beside, last_across, to_core(last_across)],
        scratch=[pltpu.VMEM((quarter, 4 * n_in), BF16), pltpu.VMEM((quarter, 4 * n_out), BF16)],
        flops=2 * quarter * d * 3 * d,
    )
    return result


def solution(mesh):
    placed = (
        P(("groups", "dom"), "sub"),
        P(("groups", "dom"), "sub"),
        P("dom", None, None),
        P("dom", None, None),
        P(None, ("dom", "sub")),
        P(None, ("dom", "sub")),
        P("dom"),
        P(None, ("dom", "sub")),
        P(None, ("dom", "sub")),
        P("dom"),
        P(),
        P(),
        P("sub", None),
        P("sub", None),
        P("sub", None),
        P("sub", None),
        P("sub", None),
        P("sub", None),
        P("sub", None),
        P("sub", None),
        P(),
        P(),
        P(),
        P(),
    )
    return jax.shard_map(
        local,
        mesh=mesh,
        in_specs=placed,
        out_specs=P(("groups", "dom", "sub"), None),
        check_vma=False,
    )
```
